32 devices in a mesh: oct: 32 (over z, y, x, core).
Axes of the slice: x: 2, y: 2, z: 4, core: 2. Of those that a mesh axis runs over, the one named last changes fastest.
Arguments:
- points: float32 [2048, 3, 128], P('oct'), may hold values from -6 to 6
- dens: float32 [2048, 32, 128], P('oct'), may hold values from -6 to 6
- surface: float32 [2048, 3, 152], P('oct'), may hold values from -6 to 6
- counts: int32 [2048], P('oct'), may hold values from 1 to 128, as said below
- ulist: int32 [2048, 27], P('oct'), may hold values from -1 to 2047, as said below
- vlist: int32 [256, 316], P('oct'), may hold values from -1 to 255, as said below
- up_inverse: float32 [152, 152], replicated, may hold values from -0.5 to 0.5
- down_inverse: float32 [152, 152], replicated, may hold values from -0.5 to 0.5
- shift_up: float32 [8, 152, 152], replicated, may hold values from -0.15625 to 0.15625
- shift_down: float32 [8, 152, 152], replicated, may hold values from -0.5 to 0.5
- coarse: float32 [8, 152, 152], replicated, may hold values from -0.25 to 0.25
- translate: bfloat16 [316, 152, 152], replicated, may hold values from -0.0390625 to 0.0390625
Outputs:
- potential: float32 [2048, 32, 128], P('oct')
The draws below stay inside these ranges and needn't reach their ends.
Inputs may be any that keep to these rules, and one draw needn't show every extreme that they name: `counts`: each leaf has 1 to 128 stations in use; the first leaf of every slab of 64 leaves is full. `ulist`: slot 0 holds the leaf itself; slots 1 to 8 hold -1 or leaves of the next lower slab of 64 leaves, slots 9 to 17 -1 or leaves of the leaf's own slab, slots 18 to 26 -1 or leaves of the next upper slab. `vlist`: every id is -1 or a node of the same slab of 8 nodes or of an adjacent one.
All inputs are finite; a program needn't handle non-finite values.
Results may differ from the reference program's by a relative error of at most 0.0017.
Values may be sent and summed in bfloat16 or wider, within the bound.
No kernel may reach another device: no remote copies, remote signals or barrier semaphores. Data moves between devices by JAX's collectives and lax.ppermute only.
A program may use at most 192 MiB of HBM per device.

```python
import jax
import jax.numpy as jnp
from jax import lax

Q = 32
EQ = 152
NTYPE = 316
NU = 27
LEAF_DEV = 64
PTS = 128
NODE_DEV = 8
LEAVES = 2048
NODES = 256
N_OCT = 32


def draw_counts(key, part):
    drawn = jax.random.randint(key, (LEAVES,), 1, PTS + 1)
    leaf_ids = jnp.arange(LEAVES)
    return jnp.where(leaf_ids % LEAF_DEV == 0, PTS, drawn).astype(jnp.int32)


def draw_ulist(key, part):
    key_list = jax.random.split(key, 2)
    leaf_ids = jnp.arange(LEAVES)
    slab_ids = leaf_ids // LEAF_DEV
    slot_ids = jnp.arange(NU)
    lower_end = 1 + (NU - 1) // 3
    upper_start = lower_end + (NU - lower_end) // 2
    slot_offsets = jnp.where(slot_ids < lower_end, -1, jnp.where(slot_ids < upper_start, 0, 1))
    offsets = jnp.broadcast_to(slot_offsets[None, :], (LEAVES, NU))
    within_slab = jax.random.randint(key_list[0], (LEAVES, NU), 0, LEAF_DEV)
    keep_draw = jax.random.randint(key_list[1], (LEAVES, NU), 0, 5)
    target_slab = slab_ids[:, None] + offsets
    chosen = target_slab * LEAF_DEV + within_slab
    usable = (target_slab >= 0) & (target_slab < LEAVES // LEAF_DEV) & (keep_draw > 0)
    chosen = jnp.where(usable, chosen, -1)
    chosen = chosen.at[:, 0].set(leaf_ids)
    chosen = chosen.at[0, NU - 1].set(-1)
    return chosen.astype(jnp.int32)


def draw_vlist(key, part):
    key_list = jax.random.split(key, 3)
    node_ids = jnp.arange(NODES)
    slab_ids = node_ids // NODE_DEV
    offsets = jax.random.randint(key_list[0], (NODES, NTYPE), -1, 2)
    within_slab = jax.random.randint(key_list[1], (NODES, NTYPE), 0, NODE_DEV)
    keep_draw = jax.random.randint(key_list[2], (NODES, NTYPE), 0, 5)
    target_slab = slab_ids[:, None] + offsets
    chosen = target_slab * NODE_DEV + within_slab
    usable = (target_slab >= 0) & (target_slab < NODES // NODE_DEV) & (keep_draw > 1)
    chosen = jnp.where(usable, chosen, -1)
    chosen = chosen.at[0, 0].set(-1)
    chosen = chosen.at[NODES - 2, 1].set(NODES - 1)
    return chosen.astype(jnp.int32)


def levels(stream_key, dims, shards, least, top_value):
    factor_of, own = 1.0, jax.random.fold_in(stream_key, 6)
    for dim, parts in shards:
        heights = jnp.exp(jax.random.uniform(jax.random.fold_in(own, dim), (parts,), jnp.float32, least / len(shards), top_value / len(shards)))
        factor_of = factor_of * jnp.repeat(heights, dims[dim] // parts).reshape([-1 if axis == dim else 1 for axis in range(len(dims))])
    return factor_of


def scatter_about(rng, dims, spread, bound, cuts=(), dtype=jnp.bfloat16):
    values = spread * jax.random.normal(rng, dims, jnp.float32)
    if cuts:
        values = values * levels(rng, dims, cuts, -0.22, 0.18)
    return jnp.clip(values, -bound, bound).astype(dtype)


def setup_inputs(seed: int = 0) -> dict:
    streams_of = jax.random.split(jax.random.key(seed), 13)
    return {
        "points": scatter_about(streams_of[0], (LEAVES, 3, PTS), 1.0, 6.0, ((0, 32),), jnp.float32),
        "dens": scatter_about(streams_of[1], (LEAVES, Q, PTS), 1.0, 6.0, ((0, 32),), jnp.float32),
        "surface": scatter_about(streams_of[2], (LEAVES, 3, EQ), 1.0, 6.0, ((0, 32),), jnp.float32),
        "counts": draw_counts(jax.random.fold_in(streams_of[12], 71), 0),
        "ulist": draw_ulist(jax.random.fold_in(streams_of[12], 71), 0),
        "vlist": draw_vlist(jax.random.fold_in(streams_of[12], 71), 0),
        "up_inverse": scatter_about(streams_of[6], (EQ, EQ), EQ ** -0.5, 0.5, (), jnp.float32),
        "down_inverse": scatter_about(streams_of[7], (EQ, EQ), EQ ** -0.5, 0.5, (), jnp.float32),
        "shift_up": scatter_about(streams_of[8], (8, EQ, EQ), (8 * EQ) ** -0.5, 0.15625, (), jnp.float32),
        "shift_down": scatter_about(streams_of[9], (8, EQ, EQ), EQ ** -0.5, 0.5, (), jnp.float32),
        "coarse": scatter_about(streams_of[10], (8, EQ, EQ), (3 * EQ) ** -0.5, 0.25, (), jnp.float32),
        "translate": scatter_about(streams_of[11], (NTYPE, EQ, EQ), (EQ * NTYPE // 2) ** -0.5, 0.0390625),
    }


HIGHEST = lax.Precision.HIGHEST


def kernel(left_pts, right_pts):
    total_sq = jnp.zeros((left_pts.shape[1], right_pts.shape[1]), jnp.float32)
    for coord_index in range(3):
        offset = left_pts[coord_index][:, None] - right_pts[coord_index][None, :]
        total_sq = total_sq + offset * offset
    return jnp.exp(-0.5 * total_sq)


def near_field(target_pts, target_ids, source_base, sources):
    source_count = sources.shape[0]
    local_ids = target_ids - source_base
    usable = (target_ids >= 0) & (local_ids >= 0) & (local_ids < source_count)
    safe_ids = jnp.clip(local_ids, 0, source_count - 1).astype(jnp.int32)

    def one_leaf(leaf_pts, leaf_ids, leaf_usable):
        picked = sources[leaf_ids]
        weights = jnp.where(leaf_usable[:, None, None], picked[:, 3:, :], 0.0)
        kernels = jax.vmap(kernel, in_axes=(0, None))(picked[:, :3, :], leaf_pts)
        slot_count, q_width, p_width = weights.shape
        flat_weights = jnp.transpose(weights, (1, 0, 2)).reshape(q_width, slot_count * p_width)
        return jnp.dot(flat_weights, kernels.reshape(slot_count * p_width, leaf_pts.shape[1]),
                       precision=HIGHEST, preferred_element_type=jnp.float32)

    def block_fn(block):
        return jax.vmap(one_leaf)(block[0], block[1], block[2])

    leaf_count = target_pts.shape[0]
    blocked = (target_pts.reshape((leaf_count // 4, 4) + target_pts.shape[1:]),
               safe_ids.reshape(leaf_count // 4, 4, -1),
               usable.reshape(leaf_count // 4, 4, -1))
    result = lax.map(block_fn, blocked)
    return result.reshape(leaf_count, sources.shape[1] - 3, target_pts.shape[2])


def reference(points, dens, surface, counts, ulist, vlist, up_inverse, down_inverse, shift_up, shift_down, coarse, translate):
    leaf_total, q_width, p_width = dens.shape
    eq_width = surface.shape[2]
    slots = jnp.arange(p_width).astype(jnp.int32)
    mask = (slots[None, :] < counts[:, None]).astype(jnp.float32)[:, None, :]
    masked = dens * mask
    up_kernel = jax.vmap(kernel)(points, surface)
    check = jnp.einsum("lqp,lpe->lqe", masked, up_kernel, precision=HIGHEST)
    leaf_eq = jnp.dot(check.reshape(-1, eq_width), up_inverse, precision=HIGHEST,
                      preferred_element_type=jnp.float32).reshape(leaf_total, q_width, eq_width)
    node_eq = jnp.einsum("ncqe,cef->nqf", leaf_eq.reshape(-1, 8, q_width, eq_width), shift_up, precision=HIGHEST)
    node_send = node_eq.astype(jnp.bfloat16)
    current = jnp.einsum("ncqe,cef->nqf", node_eq.reshape(-1, 8, q_width, eq_width), shift_up, precision=HIGHEST)
    bit_count = N_OCT.bit_length() - 1
    device_ids = jnp.arange(N_OCT).astype(jnp.int32)
    slab_local = jnp.zeros((N_OCT, q_width, eq_width), jnp.float32)
    for level_start in range(0, bit_count, 3):
        width_bits = min(3, bit_count - level_start)
        group_size = 2 ** width_bits
        current = jnp.einsum("mcqe,cef->mqf", current.reshape(-1, group_size, q_width, eq_width),
                             shift_up[:group_size], precision=HIGHEST)
        parents = current[jnp.right_shift(device_ids, level_start + width_bits)]
        child_slot = jnp.right_shift(device_ids, level_start) & 7
        slab_local = slab_local + jnp.einsum("mqe,mef->mqf", parents, coarse[child_slot], precision=HIGHEST)
    translate_wide = translate.astype(jnp.float32)

    def far_block(block_ids):
        usable = block_ids >= 0
        safe_ids = jnp.clip(block_ids, 0, node_send.shape[0] - 1).astype(jnp.int32)
        picked = jnp.where(usable[:, :, None, None], node_send[safe_ids].astype(jnp.float32), 0.0)
        return jnp.einsum("ntqe,tef->nqf", picked, translate_wide, precision=HIGHEST)

    node_dev = vlist.shape[0] // N_OCT
    far_node = lax.map(far_block, vlist.reshape(N_OCT, node_dev, -1)).reshape(-1, q_width, eq_width)
    parent_part = jnp.einsum("mqe,cef->mcqf", slab_local, shift_down, precision=HIGHEST).reshape(-1, q_width, eq_width)
    node_local = far_node + parent_part
    leaf_local = jnp.einsum("nqe,cef->ncqf", node_local, shift_down, precision=HIGHEST).reshape(leaf_total, q_width, eq_width)
    leaf_down = jnp.dot(leaf_local.reshape(-1, eq_width), down_inverse, precision=HIGHEST,
                        preferred_element_type=jnp.float32).reshape(leaf_total, q_width, eq_width)
    far_pot = jnp.einsum("lqe,lpe->lqp", leaf_down, up_kernel, precision=HIGHEST)
    sources = jnp.concatenate([points, masked], axis=1)
    near = near_field(points, ulist, 0, sources)
    return (far_pot + near) * mask
```

```python
import math

import jax
import jax.numpy as jnp
from jax import lax
from jax.experimental import pallas as pl
from jax.experimental.pallas import tpu as pltpu
from jax.sharding import PartitionSpec as P

F32 = jnp.float32
BF16 = jnp.bfloat16
HIGHEST = lax.Precision.HIGHEST
SCALE = math.sqrt(math.log2(math.e))
VMEM_LIMIT = 56 * 1024 * 1024
NT = (((1,), (1,)), ((), ()))
TN = (((0,), (0,)), ((), ()))
BLOCK = 256
UNROLL = 4
SOURCES = 32


def dot(left, right):
    return jnp.dot(left, right, preferred_element_type=F32)


def dot_nt(left, right):
    return lax.dot_general(left, right, NT, preferred_element_type=F32)


def dot_tn(left, right):
    return lax.dot_general(left, right, TN, preferred_element_type=F32)


def halves(value):
    high = value.astype(BF16)
    low = (value - high.astype(F32)).astype(BF16)
    return high, low


def dot3(left, right):
    left_high, left_low = halves(left)
    right_high, right_low = halves(right)
    return dot(left_high, right_high) + dot(left_high, right_low) + dot(left_low, right_high)


def iota(shape, dim):
    return lax.broadcasted_iota(jnp.int32, shape, dim)


def coords_of(ref, leaf):
    width = ref.shape[2]
    row = iota((8, width), 0)
    value = jnp.zeros((8, width), F32)
    for dim in range(3):
        line = jnp.broadcast_to(ref[dim, pl.ds(leaf, 1), :], (8, width))
        value = jnp.where(row == dim, line, value)
    return value


def pieces(coords):
    row = iota(coords.shape, 0)
    used = row < 3
    scaled = jnp.where(used, coords, 0.0) * SCALE
    high = scaled.astype(BF16).astype(F32)
    rest = scaled - high
    mid = rest.astype(BF16).astype(F32)
    low = (rest - mid).astype(BF16).astype(F32)
    norm = -0.5 * jnp.sum(scaled * scaled, axis=0, keepdims=True)
    norm_high = norm.astype(BF16).astype(F32)
    norm_rest = norm - norm_high
    norm_mid = norm_rest.astype(BF16).astype(F32)
    norm_low = norm_rest - norm_mid
    norms = jnp.where(row == 0, norm_high, jnp.where(row == 1, norm_mid, jnp.where(row == 2, norm_low, 0.0)))
    ones = jnp.where(used, 1.0, 0.0)
    return high, mid, low, norms, ones


def left_rows(parts):
    high, mid, low, norms, ones = parts
    return jnp.concatenate([high, high, mid, mid, high, low, ones, norms], axis=0)


def right_rows(parts):
    high, mid, low, norms, ones = parts
    return jnp.concatenate([high, mid, high, mid, low, high, norms, ones], axis=0)


def padded_left(parts):
    rows = left_rows(parts)
    return jnp.concatenate([jnp.zeros_like(rows), rows], axis=0).astype(BF16)


def packed_rows(weights, parts):
    weights_high = weights.astype(BF16).astype(F32)
    return jnp.concatenate([weights_high, weights - weights_high, right_rows(parts)], axis=0).astype(BF16)


def upward_kernel(
    points_ref, dens_ref, surface_ref, counts_ref, up_ref, shift_ref, pack_ref, target_ref, message_ref, send_ref,
    slab_ref, check_ref
):
    leaf_count, q_width, p_width = dens_ref.shape
    eq_width = surface_ref.shape[2]
    node_count = leaf_count // 8
    lane = iota((q_width, p_width), 1)
    row = iota((8, p_width), 0)

    def node_step(node, carry):
        for child in range(8):
            leaf = node * 8 + child
            count = counts_ref[leaf]
            weights = jnp.where(lane < count, dens_ref[leaf], 0.0)
            coords = coords_of(points_ref, leaf)
            message_ref[leaf, :q_width, :] = weights
            message_ref[leaf, q_width:, :] = jnp.where(row == 3, count.astype(F32), coords)
            parts = pieces(coords)
            rows = packed_rows(weights, parts)
            pack = rows.T
            pack_ref[leaf] = pack
            target_ref[leaf] = padded_left(parts).T
            values = jnp.exp2(dot(pack, padded_left(pieces(coords_of(surface_ref, leaf)))))
            values_high, values_low = halves(values)
            both = dot(rows[: 2 * q_width], values_high)
            check = both[:q_width] + both[q_width:] + dot(rows[:q_width], values_low)
            check_ref[child, pl.ds(pl.multiple_of(node * q_width, q_width), q_width), :] = check
        return carry

    lax.fori_loop(0, node_count, node_step, 0)

    def child_step(child, total):
        leaf_eq = dot3(check_ref[child], up_ref[...])
        return total + dot3(leaf_eq, shift_ref[child])

    node_eq = lax.fori_loop(0, 8, child_step, jnp.zeros((node_count * q_width, eq_width), F32))
    send_ref[: node_count * q_width, :] = node_eq.astype(BF16)
    slab_eq = jnp.zeros((q_width, eq_width), F32)
    for child in range(8):
        slab_eq = slab_eq + dot3(node_eq[child * q_width : (child + 1) * q_width], shift_ref[child])
    index = lax.axis_index("oct")
    slab = dot3(slab_eq, shift_ref[index & 7])
    slab_ref[...] = slab
    high, rest = halves(slab)
    low = (slab - high.astype(F32) - rest.astype(F32)).astype(BF16)
    for place, part in enumerate((high, rest, low)):
        start = node_count * q_width + place * q_width
        send_ref[start : start + q_width, :] = part


def far_kernel(lower_ref, own_ref, upper_ref, vlist_ref, table_hbm, out_ref, table_ref, wide_ref, total_ref, sems):
    node_count, type_count = vlist_ref.shape
    eq_width = own_ref.shape[1]
    q_width = out_ref.shape[0] // node_count
    lanes = node_count * q_width
    chunk = 8
    chunk_count = eq_width // chunk

    def copy_of(number):
        span = pl.ds(number * chunk, chunk)
        return pltpu.make_async_copy(table_hbm.at[span], table_ref.at[span], sems.at[number])

    for number in range(chunk_count):
        copy_of(number).start()

    index = lax.axis_index("oct")
    tile = 128 // q_width
    repeat = (iota((q_width, 128), 1) % q_width == iota((q_width, 128), 0)).astype(BF16)
    for part, source in enumerate((lower_ref, own_ref, upper_ref)):
        for node in range(node_count):
            spread = dot_tn(source[node * q_width : (node + 1) * q_width, :], repeat)
            wide_ref[pl.ds(part * node_count + node, eq_width, stride=SOURCES), :] = spread
    for place in range(3 * node_count, SOURCES):
        wide_ref[pl.ds(place, eq_width, stride=SOURCES), :] = jnp.zeros((eq_width, 128), F32)

    ids = vlist_ref[...]
    places = jnp.where(ids >= 0, ids - (index - 1) * node_count, -1).astype(F32).astype(BF16)
    spread = (iota((node_count, lanes), 1) // SOURCES == iota((node_count, lanes), 0)).astype(BF16)
    wanted = dot_tn(places, spread)
    chosen = (wanted == (iota((type_count, lanes), 1) % SOURCES).astype(F32)).astype(BF16)
    lane_node = iota((SOURCES, 128), 1) // q_width
    nothing = jnp.zeros((SOURCES, 128), F32)
    total_ref[...] = jnp.zeros_like(total_ref)

    def chunk_step(number, carry):
        copy_of(number).wait()
        total = jnp.zeros((eq_width, lanes), F32)
        for step in range(chunk):
            row = number * chunk + step
            summed = dot(table_ref[row], chosen)
            high = summed.astype(BF16).astype(F32)
            both = jnp.concatenate([high, summed - high], axis=0).astype(BF16)
            sent = wide_ref[pl.ds(pl.multiple_of(row * SOURCES, SOURCES), SOURCES), :]
            parts = [jnp.where(lane_node == place, sent, 0.0) for place in range(tile)]
            blocks = []
            for node in range(node_count):
                line = [parts[node % tile] if place == node // tile else nothing for place in range(node_count // tile)]
                blocks.append(jnp.concatenate(line, axis=1))
            product = dot(both, jnp.concatenate(blocks, axis=0).astype(BF16))
            total = total + product[:eq_width] + product[eq_width:]
        total_ref[...] += total
        return carry

    lax.fori_loop(0, chunk_count, chunk_step, 0)
    out_ref[...] = total_ref[...].T


def near_kernel(sides, ulist_ref, counts_ref, pack_ref, target_ref, out_ref, gather_ref, value_ref, total_ref, owner_ref):
    leaf_count, q_width, p_width = out_ref.shape
    slot_count = sum(end - first for first, end, _, _ in sides)
    index = lax.axis_index("oct")

    def gather(leaf, member, block):
        offset = block * BLOCK
        for first, end, slab, start in sides:
            base = (index + slab) * leaf_count - start
            for slot in range(first, end):
                leaf_id = ulist_ref[slot, leaf]
                place = jnp.where(leaf_id >= 0, leaf_id - base, start)
                length = jnp.where(leaf_id >= 0, jnp.bitwise_and(counts_ref[place] + 15, -16), 0)
                gather_ref[pl.ds(pl.multiple_of(offset, 16), p_width), :] = pack_ref[place]
                offset = offset + length
        gather_ref[pl.ds(pl.multiple_of(offset, 16), BLOCK), :] = jnp.zeros((BLOCK, 128), BF16)
        for number in range(-(-slot_count * p_width // BLOCK)):
            owner_ref[UNROLL + block + number] = member
        return lax.div(offset + (BLOCK - 1), BLOCK)

    for number in range(UNROLL):
        owner_ref[number] = 8

    def group_step(group, carry):
        block_count = lax.fori_loop(0, 8, lambda member, block: gather(group * 8 + member, member, block), 0)
        for number in range(2 * UNROLL):
            owner_ref[UNROLL + block_count + number] = 8
        total_ref[...] = jnp.zeros_like(total_ref)

        def sources_of(block):
            return gather_ref[pl.ds(pl.multiple_of(block * BLOCK, BLOCK), BLOCK), :]

        def blocks_step(step, inner):
            slot = jnp.bitwise_and(step, 1) * UNROLL
            for part in range(UNROLL):
                block = jnp.maximum(step - 1, 0) * UNROLL + part
                member = owner_ref[step * UNROLL + part]
                total_ref[member] += dot(value_ref[UNROLL - slot + part], sources_of(block))
            for part in range(UNROLL):
                block = step * UNROLL + part
                member = owner_ref[UNROLL + block]
                targets = target_ref[group * 8 + jnp.minimum(member, 7)]
                value_ref[slot + part] = jnp.exp2(dot_nt(targets, sources_of(block))).astype(BF16)
            return inner

        lax.fori_loop(0, lax.div(block_count + (2 * UNROLL - 1), UNROLL), blocks_step, 0)

        for member in range(8):
            turned = total_ref[member].T
            out_ref[group * 8 + member] = turned[:q_width] + turned[q_width : 2 * q_width]
        return carry

    lax.fori_loop(0, leaf_count // 8, group_step, 0)


def near_call(sides, ulist, counts, pack, targets, q_width, name):
    leaf_count, p_width = targets.shape[:2]
    slot_count = sum(end - first for first, end, _, _ in sides)
    member_blocks = -(-slot_count * p_width // BLOCK)
    vmem = pl.BlockSpec(memory_space=pltpu.VMEM)
    smem = pl.BlockSpec(memory_space=pltpu.SMEM)
    return pl.pallas_call(
        lambda *refs: near_kernel(sides, *refs),
        out_shape=jax.ShapeDtypeStruct((leaf_count, q_width, p_width), F32),
        in_specs=[smem, smem, vmem, vmem],
        out_specs=vmem,
        scratch_shapes=[
            pltpu.VMEM(((8 * member_blocks + 2 * UNROLL + 2) * BLOCK, 128), BF16),
            pltpu.VMEM((2 * UNROLL, p_width, BLOCK), BF16),
            pltpu.VMEM((9, p_width, 128), F32),
            pltpu.SMEM((9 * member_blocks + 4 * UNROLL,), jnp.int32),
        ],
        compiler_params=pltpu.CompilerParams(vmem_limit_bytes=VMEM_LIMIT),
        name=name,
    )(ulist, counts, pack, targets)


def pack_kernel(lower_ref, upper_ref, sum_ref, pair_ref, shift_ref, pack_ref, counts_ref, top_ref, next_ref):
    leaf_count, rows, p_width = lower_ref.shape
    q_width = rows - 8
    index = lax.axis_index("oct")
    top = sum_ref[...] + pair_ref[...]
    top_ref[...] = top
    next_ref[...] = dot3(top, shift_ref[jnp.right_shift(index, 3) & 7])
    lane = iota((1, p_width), 1)

    def pack_step(step, counts):
        lower_counts, upper_counts = counts
        for part in range(4):
            leaf = step * 4 + part
            for side, source in ((0, lower_ref), (1, upper_ref)):
                packed = packed_rows(source[leaf, :q_width, :], pieces(source[leaf, q_width:, :]))
                pack_ref[side * leaf_count + leaf] = packed.T
            lower_counts = jnp.where(lane == leaf, lower_ref[leaf, q_width + 3 : q_width + 4, :], lower_counts)
            upper_counts = jnp.where(lane == leaf, upper_ref[leaf, q_width + 3 : q_width + 4, :], upper_counts)
        return lower_counts, upper_counts

    nothing = jnp.zeros((1, p_width), F32)
    lower_counts, upper_counts = lax.fori_loop(0, leaf_count // 4, pack_step, (nothing, nothing))
    counts_ref[0:1, :] = lower_counts.astype(jnp.int32)
    counts_ref[1:2, :] = upper_counts.astype(jnp.int32)


def final_kernel(
    level_count, pack_ref, surface_ref, counts_ref, own_near_ref, side_near_ref, far_ref, coarse_ref, shift_ref,
    down_ref, *rest
):
    top_refs, (out_ref, node_ref, down_leaf_ref) = rest[:level_count], rest[level_count:]
    leaf_count, q_width, p_width = out_ref.shape
    eq_width = far_ref.shape[1]
    node_count = leaf_count // 8
    index = lax.axis_index("oct")
    slab_local = jnp.zeros((q_width, eq_width), F32)
    for level, top_ref in enumerate(top_refs):
        slab_local = slab_local + dot3(top_ref[...], coarse_ref[jnp.right_shift(index, 3 * level) & 7])
    for node in range(node_count):
        rows = slice(node * q_width, (node + 1) * q_width)
        node_ref[rows, :] = far_ref[rows, :] + dot3(slab_local, shift_ref[node])

    def child_step(child, carry):
        down_leaf_ref[child] = dot3(dot3(node_ref[...], shift_ref[child]), down_ref[...])
        return carry

    lax.fori_loop(0, 8, child_step, 0)
    lane = iota((q_width, p_width), 1)

    def node_step(node, carry):
        for child in range(8):
            leaf = node * 8 + child
            values = jnp.exp2(dot(pack_ref[leaf], padded_left(pieces(coords_of(surface_ref, leaf)))))
            values_high, values_low = halves(values)
            down = down_leaf_ref[child, pl.ds(pl.multiple_of(node * q_width, q_width), q_width), :]
            down_high = down.astype(BF16).astype(F32)
            empty = jnp.zeros((128 - 2 * q_width, eq_width), F32)
            down_rows = jnp.concatenate([down_high, down - down_high, empty], axis=0).astype(BF16)
            down_first = jnp.concatenate([down_high, jnp.zeros_like(down_high), empty], axis=0).astype(BF16)
            turned = (dot_nt(values_high, down_rows) + dot_nt(values_low, down_first)).T
            summed = turned[:q_width] + turned[q_width : 2 * q_width] + own_near_ref[leaf] + side_near_ref[leaf]
            out_ref[leaf] = jnp.where(lane < counts_ref[leaf], summed, 0.0)
        return carry

    lax.fori_loop(0, node_count, node_step, 0)


def shifted(value, size):
    up = [(i, i + 1) for i in range(size - 1)]
    down = [(j, i) for i, j in up]
    return lax.ppermute(value, "oct", up), lax.ppermute(value, "oct", down)


def swapped(value, size, bit):
    return lax.ppermute(value, "oct", [(source, source ^ (1 << bit)) for source in range(size)])


def local(
    points,
    dens,
    surface,
    counts,
    ulist,
    vlist,
    up_inverse,
    down_inverse,
    shift_up,
    shift_down,
    coarse,
    translate,
):
    leaf_count, q_width, p_width = dens.shape
    eq_width = surface.shape[2]
    node_count, type_count = vlist.shape
    node_rows = node_count * q_width
    size = lax.axis_size("oct")
    bits = size.bit_length() - 1
    index = lax.axis_index("oct")
    vmem = pl.BlockSpec(memory_space=pltpu.VMEM)
    smem = pl.BlockSpec(memory_space=pltpu.SMEM)
    hbm = pl.BlockSpec(memory_space=pl.ANY)
    params = pltpu.CompilerParams(vmem_limit_bytes=VMEM_LIMIT)
    points = jnp.transpose(points, (1, 0, 2))
    surface = jnp.transpose(surface, (1, 0, 2))
    ulist = ulist.T
    table = jnp.transpose(translate, (1, 2, 0))

    pack, targets, message, send, slab = pl.pallas_call(
        upward_kernel,
        out_shape=(
            jax.ShapeDtypeStruct((leaf_count, p_width, 128), BF16),
            jax.ShapeDtypeStruct((leaf_count, p_width, 128), BF16),
            jax.ShapeDtypeStruct((leaf_count, q_width + 8, p_width), F32),
            jax.ShapeDtypeStruct((node_rows + 3 * q_width, eq_width), BF16),
            jax.ShapeDtypeStruct((q_width, eq_width), F32),
        ),
        in_specs=[vmem, vmem, vmem, smem, vmem, vmem],
        out_specs=(vmem,) * 5,
        scratch_shapes=[pltpu.VMEM((8, node_rows, eq_width), F32)],
        compiler_params=params,
        name="upward",
    )(points, dens, surface, counts, up_inverse, shift_up)

    send_lower, send_upper = shifted(send, size)
    lower, upper = shifted(message, size)

    partner = jnp.where(index & 1 == 1, send_lower[node_rows:], send_upper[node_rows:]).astype(F32)
    total = slab + (partner[:q_width] + partner[q_width : 2 * q_width] + partner[2 * q_width :])
    total = total + swapped(total, size, 1)
    pair = swapped(total, size, 2)

    near_own = near_call(
        ((0, 1, 0, 0), (9, 18, 0, 0)), ulist, counts, pack, targets, q_width, "near_own"
    )

    far_node = pl.pallas_call(
        far_kernel,
        out_shape=jax.ShapeDtypeStruct((node_rows, eq_width), F32),
        in_specs=[vmem, vmem, vmem, vmem, hbm],
        out_specs=vmem,
        scratch_shapes=[
            pltpu.VMEM((eq_width, eq_width, type_count), BF16),
            pltpu.VMEM((eq_width * SOURCES, 128), F32),
            pltpu.VMEM((eq_width, node_rows), F32),
            pltpu.SemaphoreType.DMA((eq_width // 8,)),
        ],
        compiler_params=params,
        name="far",
    )(send_lower, send, send_upper, vlist, table)

    side_pack, side_counts, top, current = pl.pallas_call(
        pack_kernel,
        out_shape=(
            jax.ShapeDtypeStruct((2 * leaf_count, p_width, 128), BF16),
            jax.ShapeDtypeStruct((2, p_width), jnp.int32),
            jax.ShapeDtypeStruct((q_width, eq_width), F32),
            jax.ShapeDtypeStruct((q_width, eq_width), F32),
        ),
        in_specs=[vmem] * 5,
        out_specs=(vmem,) * 4,
        compiler_params=params,
        name="pack",
    )(lower, upper, total, pair, shift_up)

    tops = [top]
    for level in range(3, bits, 3):
        if level > 3:
            current = jnp.dot(current, shift_up[jnp.right_shift(index, level) & 7], precision=HIGHEST)
        for bit in range(level, min(level + 3, bits)):
            current = current + swapped(current, size, bit)
        tops.append(current)

    side_counts = side_counts[:, :leaf_count].reshape(-1)
    near_side = near_call(
        ((1, 9, -1, 0), (18, 27, 1, leaf_count)), ulist, side_counts, side_pack, targets, q_width, "near_side"
    )

    return pl.pallas_call(
        lambda *refs: final_kernel(len(tops), *refs),
        out_shape=jax.ShapeDtypeStruct((leaf_count, q_width, p_width), F32),
        in_specs=[vmem, vmem, smem] + [vmem] * (6 + len(tops)),
        out_specs=vmem,
        scratch_shapes=[
            pltpu.VMEM((node_rows, eq_width), F32),
            pltpu.VMEM((8, node_rows, eq_width), F32),
        ],
        compiler_params=params,
        name="final",
    )(pack, surface, counts, near_own, near_side, far_node, coarse, shift_down, down_inverse, *tops)


def solution(mesh):
    placed = (
        P("oct", None, None),
        P("oct", None, None),
        P("oct", None, None),
        P("oct"),
        P("oct", None),
        P("oct", None),
        P(),
        P(),
        P(),
        P(),
        P(),
        P(),
    )
    return jax.shard_map(
        local, mesh=mesh, in_specs=placed, out_specs=P("oct", None, None), check_vma=False
    )
```

```python
import math

import jax
import jax.numpy as jnp
from jax import lax
from jax.experimental import pallas as pl
from jax.experimental.pallas import tpu as pltpu
from jax.sharding import PartitionSpec as P

F32 = jnp.float32
BF16 = jnp.bfloat16
HIGHEST = lax.Precision.HIGHEST
SCALE = math.sqrt(math.log2(math.e))
VMEM_LIMIT = 56 * 1024 * 1024
NT = (((1,), (1,)), ((), ()))
TN = (((0,), (0,)), ((), ()))
BLOCK = 256
UNROLL = 4
SOURCES = 32


def dot(left, right):
    return jnp.dot(left, right, preferred_element_type=F32)


def dot_nt(left, right):
    return lax.dot_general(left, right, NT, preferred_element_type=F32)


def dot_tn(left, right):
    return lax.dot_general(left, right, TN, preferred_element_type=F32)


def halves(value):
    high = value.astype(BF16)
    low = (value - high.astype(F32)).astype(BF16)
    return high, low


def dot3(left, right):
    left_high, left_low = halves(left)
    right_high, right_low = halves(right)
    return dot(left_high, right_high) + dot(left_high, right_low) + dot(left_low, right_high)


def iota(shape, dim):
    return lax.broadcasted_iota(jnp.int32, shape, dim)


def coords_of(ref, leaf):
    width = ref.shape[2]
    row = iota((8, width), 0)
    value = jnp.zeros((8, width), F32)
    for dim in range(3):
        line = jnp.broadcast_to(ref[dim, pl.ds(leaf, 1), :], (8, width))
        value = jnp.where(row == dim, line, value)
    return value


def pieces(coords):
    row = iota(coords.shape, 0)
    used = row < 3
    scaled = jnp.where(used, coords, 0.0) * SCALE
    high = scaled.astype(BF16).astype(F32)
    rest = scaled - high
    mid = rest.astype(BF16).astype(F32)
    low = (rest - mid).astype(BF16).astype(F32)
    norm = -0.5 * jnp.sum(scaled * scaled, axis=0, keepdims=True)
    norm_high = norm.astype(BF16).astype(F32)
    norm_rest = norm - norm_high
    norm_mid = norm_rest.astype(BF16).astype(F32)
    norm_low = norm_rest - norm_mid
    norms = jnp.where(row == 0, norm_high, jnp.where(row == 1, norm_mid, jnp.where(row == 2, norm_low, 0.0)))
    ones = jnp.where(used, 1.0, 0.0)
    return high, mid, low, norms, ones


def left_rows(parts):
    high, mid, low, norms, ones = parts
    return jnp.concatenate([high, high, mid, mid, high, low, ones, norms], axis=0)


def right_rows(parts):
    high, mid, low, norms, ones = parts
    return jnp.concatenate([high, mid, high, mid, low, high, norms, ones], axis=0)


def padded_left(parts):
    rows = left_rows(parts)
    return jnp.concatenate([jnp.zeros_like(rows), rows], axis=0).astype(BF16)


def packed_rows(weights, parts):
    weights_high = weights.astype(BF16).astype(F32)
    return jnp.concatenate([weights_high, weights - weights_high, right_rows(parts)], axis=0).astype(BF16)


def upward_kernel(
    points_ref, dens_ref, surface_ref, counts_ref, up_ref, shift_ref, pack_ref, target_ref, message_ref, send_ref,
    slab_ref, check_ref
):
    leaf_count, q_width, p_width = dens_ref.shape
    eq_width = surface_ref.shape[2]
    node_count = leaf_count // 8
    lane = iota((q_width, p_width), 1)
    row = iota((8, p_width), 0)

    def node_step(node, carry):
        for child in range(8):
            leaf = node * 8 + child
            count = counts_ref[leaf]
            weights = jnp.where(lane < count, dens_ref[leaf], 0.0)
            coords = coords_of(points_ref, leaf)
            message_ref[leaf, :q_width, :] = weights
            message_ref[leaf, q_width:, :] = jnp.where(row == 3, count.astype(F32), coords)
            parts = pieces(coords)
            rows = packed_rows(weights, parts)
            pack = rows.T
            pack_ref[leaf] = pack
            target_ref[leaf] = padded_left(parts).T
            values = jnp.exp2(dot(pack, padded_left(pieces(coords_of(surface_ref, leaf)))))
            values_high, values_low = halves(values)
            both = dot(rows[: 2 * q_width], values_high)
            check = both[:q_width] + both[q_width:] + dot(rows[:q_width], values_low)
            check_ref[child, pl.ds(pl.multiple_of(node * q_width, q_width), q_width), :] = check
        return carry

    lax.fori_loop(0, node_count, node_step, 0)

    def child_step(child, total):
        leaf_eq = dot3(check_ref[child], up_ref[...])
        return total + dot3(leaf_eq, shift_ref[child])

    node_eq = lax.fori_loop(0, 8, child_step, jnp.zeros((node_count * q_width, eq_width), F32))
    send_ref[: node_count * q_width, :] = node_eq.astype(BF16)
    slab_eq = jnp.zeros((q_width, eq_width), F32)
    for child in range(8):
        slab_eq = slab_eq + dot3(node_eq[child * q_width : (child + 1) * q_width], shift_ref[child])
    index = lax.axis_index("oct")
    slab = dot3(slab_eq, shift_ref[index & 7])
    slab_ref[...] = slab
    high, rest = halves(slab)
    low = (slab - high.astype(F32) - rest.astype(F32)).astype(BF16)
    for place, part in enumerate((high, rest, low)):
        start = node_count * q_width + place * q_width
        send_ref[start : start + q_width, :] = part


def far_kernel(
    lower_ref, own_ref, upper_ref, vlist_ref, table_hbm, out_ref, table_ref, tail_ref, wide_ref, total_ref, sems
):
    node_count, type_count = vlist_ref.shape
    eq_width = own_ref.shape[1]
    q_width = out_ref.shape[0] // node_count
    lanes = node_count * q_width
    tile = 128 // q_width
    chunk = 8
    chunk_rows = chunk * eq_width
    chunk_count = eq_width // chunk
    full = type_count // 128

    def copies_of(number):
        span = pl.ds(number * chunk_rows, chunk_rows)
        copies = []
        for part in range(full):
            source = table_hbm.at[span, pl.ds(part * 128, 128)]
            copies.append(pltpu.make_async_copy(source, table_ref.at[part, span], sems.at[number, part]))
        source = table_hbm.at[span, pl.ds(full * 128, type_count - full * 128)]
        copies.append(pltpu.make_async_copy(source, tail_ref.at[span], sems.at[number, full]))
        return copies

    for number in range(chunk_count):
        for copy in copies_of(number):
            copy.start()

    index = lax.axis_index("oct")
    repeat = (iota((q_width, 128), 1) % q_width == iota((q_width, 128), 0)).astype(BF16)
    for part, source in enumerate((lower_ref, own_ref, upper_ref)):
        for node in range(node_count):
            spread = dot_tn(source[node * q_width : (node + 1) * q_width, :], repeat)
            wide_ref[pl.ds(part * node_count + node, eq_width, stride=SOURCES), :] = spread
    for place in range(3 * node_count, SOURCES):
        wide_ref[pl.ds(place, eq_width, stride=SOURCES), :] = jnp.zeros((eq_width, 128), F32)

    ids = vlist_ref[...]
    places = jnp.where(ids >= 0, ids - (index - 1) * node_count, -1).astype(F32).astype(BF16)
    spread = (iota((node_count, lanes), 1) // SOURCES == iota((node_count, lanes), 0)).astype(BF16)
    wanted = dot_tn(places, spread)
    chosen = (wanted == (iota((type_count, lanes), 1) % SOURCES).astype(F32)).astype(F32)
    chosen_full = chosen[: full * 128].astype(BF16)
    chosen_tail = chosen[full * 128 :].astype(BF16)
    lane_node = iota((SOURCES, 128), 1) // q_width
    nothing = jnp.zeros((SOURCES, 128), F32)
    total_ref[...] = jnp.zeros_like(total_ref)

    def chunk_step(number, carry):
        for copy in copies_of(number):
            copy.wait()
        span = pl.ds(pl.multiple_of(number * chunk_rows, chunk_rows), chunk_rows)
        left = jnp.concatenate([table_ref[part, span, :] for part in range(full)], axis=1)
        summed = dot(left, chosen_full) + dot(tail_ref[span, :], chosen_tail)
        lefts, rights = [], []
        for step in range(chunk):
            value = summed[step * eq_width : (step + 1) * eq_width]
            high = value.astype(BF16).astype(F32)
            lefts.append(jnp.concatenate([high, value - high], axis=0).astype(BF16))
            row = number * chunk + step
            sent = wide_ref[pl.ds(pl.multiple_of(row * SOURCES, SOURCES), SOURCES), :]
            parts = [jnp.where(lane_node == place, sent, 0.0) for place in range(tile)]
            for node in range(node_count):
                line = [parts[node % tile] if place == node // tile else nothing for place in range(node_count // tile)]
                rights.append(jnp.concatenate(line, axis=1))
        product = dot(jnp.concatenate(lefts, axis=1), jnp.concatenate(rights, axis=0).astype(BF16))
        total_ref[...] += product[:eq_width] + product[eq_width:]
        return carry

    lax.fori_loop(0, chunk_count, chunk_step, 0)
    out_ref[...] = total_ref[...].T


def near_kernel(
    ulist_ref, counts_ref, side_counts_ref, own_pack_ref, side_pack_ref, target_ref, out_ref, first_ref, second_ref,
    value_ref, total_ref, owner_ref
):
    leaf_count, q_width, p_width = out_ref.shape
    slot_count = ulist_ref.shape[0]
    member_blocks = -(-slot_count * p_width // BLOCK)
    spare_block = 8 * member_blocks + 10 * UNROLL
    group_count = leaf_count // 8
    index = lax.axis_index("oct")
    buffers = (first_ref, second_ref)

    def source_of(slot, leaf):
        leaf_id = ulist_ref[slot, leaf]
        side = 0 if slot == 0 else (-1 if slot < 9 else (0 if slot < 18 else 1))
        place = jnp.where(leaf_id >= 0, leaf_id - (index + side) * leaf_count, 0)
        if side == 0:
            count, pack = counts_ref[place], own_pack_ref[place]
        else:
            half = (side + 1) // 2
            count, pack = side_counts_ref[half, place], side_pack_ref[half * leaf_count + place]
        return jnp.where(leaf_id >= 0, jnp.bitwise_and(count + 15, -16), 0), pack

    def gather(half, leaf, member, block):
        gather_ref = buffers[half]
        offset = block * BLOCK
        for slot in range(slot_count):
            length, pack = source_of(slot, leaf)
            gather_ref[pl.ds(pl.multiple_of(offset, 16), p_width), :] = pack
            offset = offset + length
        gather_ref[pl.ds(pl.multiple_of(offset, 16), BLOCK), :] = jnp.zeros((BLOCK, 128), BF16)
        for number in range(member_blocks):
            owner_ref[half, UNROLL + block + number] = member
        return lax.shift_right_logical(offset + (BLOCK - 1), BLOCK.bit_length() - 1)

    for half in range(2):
        for number in range(UNROLL):
            owner_ref[half, number] = 8

    first_count = lax.fori_loop(0, 8, lambda member, block: gather(0, member, member, block), 0)

    def group_step(group, half, block_count):
        for number in range(10 * UNROLL):
            owner_ref[half, UNROLL + block_count + number] = 8
        total_ref[...] = jnp.zeros_like(total_ref)
        later = jnp.minimum(group + 1, group_count - 1)

        def sources_of(block):
            return buffers[half][pl.ds(pl.multiple_of(block * BLOCK, BLOCK), BLOCK), :]

        def blocks_step(step, later_block):
            slot = jnp.bitwise_and(step, 1) * UNROLL
            for part in range(UNROLL):
                block = jnp.maximum(step - 1, 0) * UNROLL + part
                member = owner_ref[half, step * UNROLL + part]
                values = jnp.concatenate([value_ref[UNROLL - slot + part, side] for side in range(2)], axis=1)
                total_ref[member] += dot(values, sources_of(block))
            for part in range(UNROLL):
                block = step * UNROLL + part
                member = owner_ref[half, UNROLL + block]
                targets = target_ref[group * 8 + jnp.minimum(member, 7)]
                values = jnp.exp2(dot_nt(targets, sources_of(block))).astype(BF16)
                for side in range(2):
                    value_ref[slot + part, side] = values[:, side * 128 : (side + 1) * 128]
            live = step < 8
            member = jnp.minimum(step, 7)
            place = jnp.where(live, later_block, spare_block)
            following = gather(1 - half, later * 8 + member, member, place)
            return jnp.where(live, following, later_block)

        steps = jnp.maximum(lax.div(block_count + (2 * UNROLL - 1), UNROLL), 8)
        later_count = lax.fori_loop(0, steps, blocks_step, 0)

        for member in range(8):
            turned = total_ref[member].T
            out_ref[group * 8 + member] = turned[:q_width] + turned[q_width : 2 * q_width]
        return later_count

    def pair_step(pair, block_count):
        return group_step(2 * pair + 1, 1, group_step(2 * pair, 0, block_count))

    lax.fori_loop(0, group_count // 2, pair_step, first_count)


def pack_kernel(lower_ref, upper_ref, sum_ref, pair_ref, shift_ref, pack_ref, counts_ref, top_ref, next_ref):
    leaf_count, rows, p_width = lower_ref.shape
    q_width = rows - 8
    index = lax.axis_index("oct")
    top = sum_ref[...] + pair_ref[...]
    top_ref[...] = top
    next_ref[...] = dot3(top, shift_ref[jnp.right_shift(index, 3) & 7])
    lane = iota((1, p_width), 1)

    def pack_step(step, counts):
        lower_counts, upper_counts = counts
        for part in range(4):
            leaf = step * 4 + part
            for side, source in ((0, lower_ref), (1, upper_ref)):
                packed = packed_rows(source[leaf, :q_width, :], pieces(source[leaf, q_width:, :]))
                pack_ref[side * leaf_count + leaf] = packed.T
            lower_counts = jnp.where(lane == leaf, lower_ref[leaf, q_width + 3 : q_width + 4, :], lower_counts)
            upper_counts = jnp.where(lane == leaf, upper_ref[leaf, q_width + 3 : q_width + 4, :], upper_counts)
        return lower_counts, upper_counts

    nothing = jnp.zeros((1, p_width), F32)
    lower_counts, upper_counts = lax.fori_loop(0, leaf_count // 4, pack_step, (nothing, nothing))
    counts_ref[0:1, :] = lower_counts.astype(jnp.int32)
    counts_ref[1:2, :] = upper_counts.astype(jnp.int32)


def final_kernel(
    level_count, pack_ref, surface_ref, counts_ref, near_ref, far_ref, coarse_ref, shift_ref,
    down_ref, *rest
):
    top_refs, (out_ref, node_ref, down_leaf_ref) = rest[:level_count], rest[level_count:]
    leaf_count, q_width, p_width = out_ref.shape
    eq_width = far_ref.shape[1]
    node_count = leaf_count // 8
    index = lax.axis_index("oct")
    slab_local = jnp.zeros((q_width, eq_width), F32)
    for level, top_ref in enumerate(top_refs):
        slab_local = slab_local + dot3(top_ref[...], coarse_ref[jnp.right_shift(index, 3 * level) & 7])
    for node in range(node_count):
        rows = slice(node * q_width, (node + 1) * q_width)
        node_ref[rows, :] = far_ref[rows, :] + dot3(slab_local, shift_ref[node])

    def child_step(child, carry):
        down_leaf_ref[child] = dot3(dot3(node_ref[...], shift_ref[child]), down_ref[...])
        return carry

    lax.fori_loop(0, 8, child_step, 0)
    lane = iota((q_width, p_width), 1)

    def node_step(node, carry):
        for child in range(8):
            leaf = node * 8 + child
            values = jnp.exp2(dot(pack_ref[leaf], padded_left(pieces(coords_of(surface_ref, leaf)))))
            values_high, values_low = halves(values)
            down = down_leaf_ref[child, pl.ds(pl.multiple_of(node * q_width, q_width), q_width), :]
            down_high = down.astype(BF16).astype(F32)
            down_rows = jnp.concatenate([down_high, down - down_high], axis=0).astype(BF16)
            down_first = jnp.concatenate([down_high, jnp.zeros_like(down_high)], axis=0).astype(BF16)
            turned = (dot_nt(values_high, down_rows) + dot_nt(values_low, down_first)).T
            summed = turned[:q_width] + turned[q_width : 2 * q_width] + near_ref[leaf]
            out_ref[leaf] = jnp.where(lane < counts_ref[leaf], summed, 0.0)
        return carry

    lax.fori_loop(0, node_count, node_step, 0)


def shifted(value, size):
    up = [(i, i + 1) for i in range(size - 1)]
    down = [(j, i) for i, j in up]
    return lax.ppermute(value, "oct", up), lax.ppermute(value, "oct", down)


def swapped(value, size, bit):
    return lax.ppermute(value, "oct", [(source, source ^ (1 << bit)) for source in range(size)])


def local(
    points,
    dens,
    surface,
    counts,
    ulist,
    vlist,
    up_inverse,
    down_inverse,
    shift_up,
    shift_down,
    coarse,
    translate,
):
    leaf_count, q_width, p_width = dens.shape
    eq_width = surface.shape[2]
    node_count, type_count = vlist.shape
    node_rows = node_count * q_width
    size = lax.axis_size("oct")
    bits = size.bit_length() - 1
    index = lax.axis_index("oct")
    vmem = pl.BlockSpec(memory_space=pltpu.VMEM)
    smem = pl.BlockSpec(memory_space=pltpu.SMEM)
    hbm = pl.BlockSpec(memory_space=pl.ANY)
    params = pltpu.CompilerParams(vmem_limit_bytes=VMEM_LIMIT)
    points = jnp.transpose(points, (1, 0, 2))
    surface = jnp.transpose(surface, (1, 0, 2))
    ulist = ulist.T
    table = jnp.transpose(translate, (1, 2, 0))

    pack, targets, message, send, slab = pl.pallas_call(
        upward_kernel,
        out_shape=(
            jax.ShapeDtypeStruct((leaf_count, p_width, 128), BF16),
            jax.ShapeDtypeStruct((leaf_count, p_width, 128), BF16),
            jax.ShapeDtypeStruct((leaf_count, q_width + 8, p_width), F32),
            jax.ShapeDtypeStruct((node_rows + 3 * q_width, eq_width), BF16),
            jax.ShapeDtypeStruct((q_width, eq_width), F32),
        ),
        in_specs=[vmem, vmem, vmem, smem, vmem, vmem],
        out_specs=(vmem,) * 5,
        scratch_shapes=[pltpu.VMEM((8, node_rows, eq_width), F32)],
        compiler_params=params,
        name="upward",
    )(points, dens, surface, counts, up_inverse, shift_up)

    send_lower, send_upper = shifted(send, size)
    partner = jnp.where(index & 1 == 1, send_lower[node_rows:], send_upper[node_rows:]).astype(F32)
    total = slab + (partner[:q_width] + partner[q_width : 2 * q_width] + partner[2 * q_width :])
    message, total = lax.optimization_barrier((message, total))
    lower, upper = shifted(message, size)
    total = total + swapped(total, size, 1)
    pair = swapped(total, size, 2)
    send_lower, total = lax.optimization_barrier((send_lower, total))

    table = table.reshape(eq_width * eq_width, type_count)
    far_node = pl.pallas_call(
        far_kernel,
        out_shape=jax.ShapeDtypeStruct((node_rows, eq_width), F32),
        in_specs=[vmem, vmem, vmem, vmem, hbm],
        out_specs=vmem,
        scratch_shapes=[
            pltpu.VMEM((type_count // 128, eq_width * eq_width, 128), BF16),
            pltpu.VMEM((eq_width * eq_width, type_count % 128), BF16),
            pltpu.VMEM((eq_width * SOURCES, 128), F32),
            pltpu.VMEM((eq_width, node_rows), F32),
            pltpu.SemaphoreType.DMA((eq_width // 8, type_count // 128 + 1)),
        ],
        compiler_params=params,
        cost_estimate=pl.CostEstimate(flops=2 * 10**10, bytes_accessed=18 * 10**6, transcendentals=0),
        name="far",
    )(send_lower, send, send_upper, vlist, table)
    far_node, lower, upper = lax.optimization_barrier((far_node, lower, upper))

    side_pack, side_counts, top, current = pl.pallas_call(
        pack_kernel,
        out_shape=(
            jax.ShapeDtypeStruct((2 * leaf_count, p_width, 128), BF16),
            jax.ShapeDtypeStruct((2, p_width), jnp.int32),
            jax.ShapeDtypeStruct((q_width, eq_width), F32),
            jax.ShapeDtypeStruct((q_width, eq_width), F32),
        ),
        in_specs=[vmem] * 5,
        out_specs=(vmem,) * 4,
        compiler_params=params,
        name="pack",
    )(lower, upper, total, pair, shift_up)

    tops = [top]
    for level in range(3, bits, 3):
        if level > 3:
            current = jnp.dot(current, shift_up[jnp.right_shift(index, level) & 7], precision=HIGHEST)
        for bit in range(level, min(level + 3, bits)):
            current = current + swapped(current, size, bit)
        tops.append(current)

    member_blocks = -(-ulist.shape[0] * p_width // BLOCK)
    gather_rows = (9 * member_blocks + 10 * UNROLL + 2) * BLOCK
    near = pl.pallas_call(
        near_kernel,
        out_shape=jax.ShapeDtypeStruct((leaf_count, q_width, p_width), F32),
        in_specs=[smem, smem, smem, vmem, vmem, vmem],
        out_specs=vmem,
        scratch_shapes=[
            pltpu.VMEM((gather_rows, 128), BF16),
            pltpu.VMEM((gather_rows, 128), BF16),
            pltpu.VMEM((2 * UNROLL, 2, p_width, 128), BF16),
            pltpu.VMEM((9, p_width, 128), F32),
            pltpu.SMEM((2, 9 * member_blocks + 12 * UNROLL), jnp.int32),
        ],
        compiler_params=params,
        cost_estimate=pl.CostEstimate(flops=3 * 10**10, bytes_accessed=10**7, transcendentals=0),
        name="near",
    )(ulist, counts, side_counts, pack, side_pack, targets)

    return pl.pallas_call(
        lambda *refs: final_kernel(len(tops), *refs),
        out_shape=jax.ShapeDtypeStruct((leaf_count, q_width, p_width), F32),
        in_specs=[vmem, vmem, smem] + [vmem] * (5 + len(tops)),
        out_specs=vmem,
        scratch_shapes=[
            pltpu.VMEM((node_rows, eq_width), F32),
            pltpu.VMEM((8, node_rows, eq_width), F32),
        ],
        compiler_params=params,
        name="final",
    )(pack, surface, counts, near, far_node, coarse, shift_down, down_inverse, *tops)


def solution(mesh):
    placed = (
        P("oct", None, None),
        P("oct", None, None),
        P("oct", None, None),
        P("oct"),
        P("oct", None),
        P("oct", None),
        P(),
        P(),
        P(),
        P(),
        P(),
        P(),
    )
    return jax.shard_map(
        local, mesh=mesh, in_specs=placed, out_specs=P("oct", None, None), check_vma=False
    )
```

```python
import math

import jax
import jax.numpy as jnp
from jax import lax
from jax.experimental import pallas as pl
from jax.experimental.pallas import tpu as pltpu
from jax.sharding import PartitionSpec as P

F32 = jnp.float32
BF16 = jnp.bfloat16
HIGHEST = lax.Precision.HIGHEST
SCALE = math.sqrt(math.log2(math.e))
NT = (((1,), (1,)), ((), ()))
TN = (((0,), (0,)), ((), ()))
BLOCK = 256
UNROLL = 4
PIECE = 32
SOURCES = 32


def dot(left, right):
    return jnp.dot(left, right, preferred_element_type=F32)


def dot_nt(left, right):
    return lax.dot_general(left, right, NT, preferred_element_type=F32)


def dot_tn(left, right):
    return lax.dot_general(left, right, TN, preferred_element_type=F32)


def halves(value):
    high = value.astype(BF16)
    low = (value - high.astype(F32)).astype(BF16)
    return high, low


def dot3(left, right):
    left_high, left_low = halves(left)
    right_high, right_low = halves(right)
    return dot(left_high, right_high) + dot(left_high, right_low) + dot(left_low, right_high)


def grant(mebibytes):
    return pltpu.CompilerParams(vmem_limit_bytes=mebibytes * 1024 * 1024)


def iota(shape, dim):
    return lax.broadcasted_iota(jnp.int32, shape, dim)


def coords_of(ref, leaf):
    width = ref.shape[2]
    row = iota((8, width), 0)
    value = jnp.zeros((8, width), F32)
    for dim in range(3):
        line = jnp.broadcast_to(ref[dim, pl.ds(leaf, 1), :], (8, width))
        value = jnp.where(row == dim, line, value)
    return value


def pieces(coords):
    row = iota(coords.shape, 0)
    used = row < 3
    scaled = jnp.where(used, coords, 0.0) * SCALE
    high = scaled.astype(BF16).astype(F32)
    rest = scaled - high
    mid = rest.astype(BF16).astype(F32)
    low = (rest - mid).astype(BF16).astype(F32)
    norm = -0.5 * jnp.sum(scaled * scaled, axis=0, keepdims=True)
    norm_high = norm.astype(BF16).astype(F32)
    norm_rest = norm - norm_high
    norm_mid = norm_rest.astype(BF16).astype(F32)
    norm_low = norm_rest - norm_mid
    norms = jnp.where(row == 0, norm_high, jnp.where(row == 1, norm_mid, jnp.where(row == 2, norm_low, 0.0)))
    ones = jnp.where(used, 1.0, 0.0)
    return high, mid, low, norms, ones


LEFT = (0, 0, 1, 1, 0, 2, 4, 3)
RIGHT = (0, 1, 0, 1, 2, 0, 3, 4)


def selector(order):
    row = iota((32, 40), 0)
    column = iota((32, 40), 1)
    picked = jnp.zeros((32, 40), F32)
    for group, piece in enumerate(order):
        shift = 8 * piece - 3 * group
        inside = (row >= 3 * group) & (row < 3 * group + 3)
        picked = jnp.where(inside & (column == row + shift), 1.0, picked)
    return picked.astype(BF16)


def stacked(coords):
    return jnp.concatenate(pieces(coords), axis=0).astype(BF16)


def weight_rows(weights):
    high = weights.astype(BF16).astype(F32)
    return high, weights - high


def kernel_rows(surface_ref, leaf, right, select_left):
    left = dot(select_left, stacked(coords_of(surface_ref, leaf))).astype(BF16)
    return halves(jnp.exp2(dot_tn(left, right.astype(BF16))))


def upward_kernel(
    points_ref, dens_ref, surface_ref, counts_ref, up_ref, shift_ref, pack_ref, target_ref, message_ref, send_ref,
    slab_ref, check_ref
):
    leaf_count, q_width, p_width = dens_ref.shape
    eq_width = surface_ref.shape[2]
    node_count = leaf_count // 8
    lane = iota((q_width, p_width), 1)
    row = iota((8, p_width), 0)
    column = iota((p_width, 128), 1)
    select_left, select_right = selector(LEFT), selector(RIGHT)

    def node_step(node, carry):
        for child in range(8):
            leaf = node * 8 + child
            count = counts_ref[leaf]
            weights = jnp.where(lane < count, dens_ref[leaf], 0.0)
            coords = coords_of(points_ref, leaf)
            message_ref[leaf, :q_width, :] = weights
            message_ref[leaf, q_width:, :] = jnp.where(row == 3, count.astype(F32), coords)
            base = stacked(coords)
            left, right = dot(select_left, base), dot(select_right, base)
            high, low = weight_rows(weights)
            turned = jnp.concatenate([high, low, right, left], axis=0).T
            pack_ref[leaf] = turned.astype(BF16)
            moved = pltpu.roll(turned, 96, 1)
            target_ref[leaf] = jnp.where((column >= 64) & (column < 96), moved, 0.0).astype(BF16)
            values_high, values_low = kernel_rows(surface_ref, leaf, right, select_left)
            both = dot_nt(jnp.concatenate([high, low], axis=0).astype(BF16), values_high)
            check = both[:q_width] + both[q_width:] + dot_nt(high.astype(BF16), values_low)
            check_ref[child, pl.ds(pl.multiple_of(node * q_width, q_width), q_width), :] = check
        return carry

    lax.fori_loop(0, node_count, node_step, 0)

    def child_step(child, total):
        leaf_eq = dot3(check_ref[child], up_ref[...])
        return total + dot3(leaf_eq, shift_ref[child])

    node_eq = lax.fori_loop(0, 8, child_step, jnp.zeros((node_count * q_width, eq_width), F32))
    send_ref[: node_count * q_width, :] = node_eq.astype(BF16)
    slab_eq = jnp.zeros((q_width, eq_width), F32)
    for child in range(8):
        slab_eq = slab_eq + dot3(node_eq[child * q_width : (child + 1) * q_width], shift_ref[child])
    index = lax.axis_index("oct")
    slab = dot3(slab_eq, shift_ref[index & 7])
    slab_ref[...] = slab
    high, rest = halves(slab)
    low = (slab - high.astype(F32) - rest.astype(F32)).astype(BF16)
    for place, part in enumerate((high, rest, low)):
        start = node_count * q_width + place * q_width
        send_ref[start : start + q_width, :] = part


def far_kernel(
    lower_ref, own_ref, upper_ref, vlist_ref, table_hbm, out_ref, table_ref, tail_ref, wide_ref, total_ref, sems
):
    node_count, type_count = vlist_ref.shape
    eq_width = own_ref.shape[1]
    q_width = out_ref.shape[0] // node_count
    lanes = node_count * q_width
    tile = 128 // q_width
    chunk = 8
    chunk_rows = chunk * eq_width
    chunk_count = eq_width // chunk
    full = type_count // 128

    def copies_of(number):
        span = pl.ds(number * chunk_rows, chunk_rows)
        copies = []
        for part in range(full):
            source = table_hbm.at[span, pl.ds(part * 128, 128)]
            copies.append(pltpu.make_async_copy(source, table_ref.at[part, span], sems.at[number, part]))
        source = table_hbm.at[span, pl.ds(full * 128, type_count - full * 128)]
        copies.append(pltpu.make_async_copy(source, tail_ref.at[span], sems.at[number, full]))
        return copies

    for number in range(chunk_count):
        for copy in copies_of(number):
            copy.start()

    index = lax.axis_index("oct")
    repeat = (iota((q_width, 128), 1) % q_width == iota((q_width, 128), 0)).astype(BF16)
    for part, source in enumerate((lower_ref, own_ref, upper_ref)):
        for node in range(node_count):
            spread = dot_tn(source[node * q_width : (node + 1) * q_width, :], repeat)
            wide_ref[pl.ds(part * node_count + node, eq_width, stride=SOURCES), :] = spread
    for place in range(3 * node_count, SOURCES):
        wide_ref[pl.ds(place, eq_width, stride=SOURCES), :] = jnp.zeros((eq_width, 128), F32)

    ids = vlist_ref[...]
    places = jnp.where(ids >= 0, ids - (index - 1) * node_count, -1).astype(F32).astype(BF16)
    spread = (iota((node_count, lanes), 1) // SOURCES == iota((node_count, lanes), 0)).astype(BF16)
    wanted = dot_tn(places, spread)
    chosen = (wanted == (iota((type_count, lanes), 1) % SOURCES).astype(F32)).astype(F32)
    chosen_full = chosen[: full * 128].astype(BF16)
    chosen_tail = chosen[full * 128 :].astype(BF16)
    lane_node = iota((SOURCES, 128), 1) // q_width
    nothing = jnp.zeros((SOURCES, 128), F32)
    total_ref[...] = jnp.zeros_like(total_ref)

    def chunk_step(number, carry):
        for copy in copies_of(number):
            copy.wait()
        span = pl.ds(pl.multiple_of(number * chunk_rows, chunk_rows), chunk_rows)
        left = jnp.concatenate([table_ref[part, span, :] for part in range(full)], axis=1)
        summed = dot(left, chosen_full) + dot(tail_ref[span, :], chosen_tail)
        lefts, rights = [], []
        for step in range(chunk):
            value = summed[step * eq_width : (step + 1) * eq_width]
            high = value.astype(BF16).astype(F32)
            lefts.append(jnp.concatenate([high, value - high], axis=0).astype(BF16))
            row = number * chunk + step
            sent = wide_ref[pl.ds(pl.multiple_of(row * SOURCES, SOURCES), SOURCES), :]
            parts = [jnp.where(lane_node == place, sent, 0.0) for place in range(tile)]
            for node in range(node_count):
                line = [parts[node % tile] if place == node // tile else nothing for place in range(node_count // tile)]
                rights.append(jnp.concatenate(line, axis=1))
        product = dot(jnp.concatenate(lefts, axis=1), jnp.concatenate(rights, axis=0).astype(BF16))
        total_ref[...] += product[:eq_width] + product[eq_width:]
        return carry

    lax.fori_loop(0, chunk_count, chunk_step, 0)
    out_ref[...] = total_ref[...].T


def near_kernel(
    ulist_ref, counts_ref, pack_ref, target_ref, out_ref, value_ref, total_ref, first_list, second_list, owner_ref,
    order_ref
):
    leaf_count, q_width, p_width = out_ref.shape
    slot_count = ulist_ref.shape[0]
    leaf_pieces = p_width // PIECE
    block_pieces = BLOCK // PIECE
    member_blocks = -(-slot_count * p_width // BLOCK)
    spare_block = 8 * member_blocks + 10 * UNROLL
    zero_piece = 3 * leaf_count * leaf_pieces
    group_count = leaf_count // 8
    index = lax.axis_index("oct")
    lists = (first_list, second_list)

    def class_of(leaf):
        return lax.shift_right_logical(counts_ref[1, leaf] - 1, 5)

    def tally(leaf, totals):
        own = class_of(leaf)
        return tuple(total + (own == number).astype(jnp.int32) for number, total in enumerate(totals))

    zero = jnp.int32(0)
    totals = lax.fori_loop(0, leaf_count, tally, (zero,) * 4)

    def assign(leaf, places):
        own = class_of(leaf)
        place = places[0]
        for number in range(1, 4):
            place = jnp.where(own == number, places[number], place)
        order_ref[place] = leaf
        return tuple(value + (own == number).astype(jnp.int32) for number, value in enumerate(places))

    starts = (zero, totals[0], totals[0] + totals[1], totals[0] + totals[1] + totals[2])
    lax.fori_loop(0, leaf_count, assign, starts)

    def enlist(half, leaf, member, block):
        list_ref = lists[half]
        place = block * block_pieces
        for slot in range(slot_count):
            side = 1 if slot == 0 else (0 if slot < 9 else (1 if slot < 18 else 2))
            leaf_id = ulist_ref[slot, leaf]
            near = jnp.where(leaf_id >= 0, leaf_id - (index + (side - 1)) * leaf_count, 0)
            length = lax.shift_right_logical(counts_ref[side, near] + (PIECE - 1), PIECE.bit_length() - 1)
            piece = (near + side * leaf_count) * leaf_pieces
            for number in range(leaf_pieces):
                list_ref[place + number] = piece + number
            place = place + jnp.where(leaf_id >= 0, length, 0)
        for number in range(block_pieces):
            list_ref[place + number] = zero_piece
        for number in range(member_blocks):
            owner_ref[half, UNROLL + block + number] = member
        return lax.shift_right_logical(place + (block_pieces - 1), block_pieces.bit_length() - 1)

    for half in range(2):
        for number in range(UNROLL):
            owner_ref[half, number] = 8

        def clear(number, carry, half=half):
            lists[half][number] = zero_piece
            return carry

        lax.fori_loop(0, lists[half].shape[0], clear, 0)

    first_count = lax.fori_loop(0, 8, lambda member, block: enlist(0, order_ref[member], member, block), 0)

    def group_step(group, half, block_count):
        for number in range(10 * UNROLL):
            owner_ref[half, UNROLL + block_count + number] = 8
        total_ref[...] = jnp.zeros_like(total_ref)
        later = jnp.minimum(group + 1, group_count - 1) * 8

        def sources_of(block):
            rows = []
            for number in range(block_pieces):
                piece = lists[half][block * block_pieces + number]
                rows.append(pack_ref[pl.ds(pl.multiple_of(piece * PIECE, PIECE), PIECE), :])
            return jnp.concatenate(rows, axis=0)

        def run(rows):
            def blocks_step(step, later_block):
                slot = jnp.bitwise_and(step, 1) * UNROLL
                for part in range(UNROLL):
                    block = jnp.maximum(step - 1, 0) * UNROLL + part
                    member = owner_ref[half, step * UNROLL + part]
                    values = [value_ref[UNROLL - slot + part, side, :rows] for side in range(2)]
                    total_ref[member, :rows] += dot(jnp.concatenate(values, axis=1), sources_of(block))
                for part in range(UNROLL):
                    block = step * UNROLL + part
                    member = owner_ref[half, UNROLL + block]
                    leaf = order_ref[group * 8 + jnp.minimum(member, 7)]
                    targets = target_ref[leaf, :rows]
                    values = jnp.exp2(dot_nt(targets, sources_of(block))).astype(BF16)
                    for side in range(2):
                        value_ref[slot + part, side, :rows] = values[:, side * 128 : (side + 1) * 128]
                live = step < 8
                member = jnp.minimum(step, 7)
                place = jnp.where(live, later_block, spare_block)
                following = enlist(1 - half, order_ref[later + member], member, place)
                return jnp.where(live, following, later_block)

            steps = jnp.maximum(lax.div(block_count + (2 * UNROLL - 1), UNROLL), 8)
            return lax.fori_loop(0, steps, blocks_step, 0)

        largest = class_of(order_ref[group * 8 + 7])
        later_count = lax.switch(largest, [lambda rows=rows: run(rows) for rows in (32, 64, 96, 128)])

        for member in range(8):
            turned = total_ref[member, :, : 2 * q_width].T
            out_ref[order_ref[group * 8 + member]] = turned[:q_width] + turned[q_width:]
        return later_count

    def pair_step(pair, block_count):
        return group_step(2 * pair + 1, 1, group_step(2 * pair, 0, block_count))

    lax.fori_loop(0, group_count // 2, pair_step, first_count)


def pack_kernel(
    lower_ref, upper_ref, own_ref, own_counts_ref, sum_ref, pair_ref, shift_ref, pack_ref, counts_ref, top_ref, next_ref
):
    leaf_count, rows, p_width = lower_ref.shape
    q_width = rows - 8
    leaf_rows = leaf_count * p_width
    index = lax.axis_index("oct")
    top = sum_ref[...] + pair_ref[...]
    top_ref[...] = top
    next_ref[...] = dot3(top, shift_ref[jnp.right_shift(index, 3) & 7])
    lane = iota((1, p_width), 1)
    select_right = selector(RIGHT)
    blank = jnp.zeros((p_width - 2 * q_width - 32, p_width), F32)
    pack_ref[leaf_rows : 2 * leaf_rows, :] = own_ref[...].reshape(leaf_rows, 128)
    pack_ref[3 * leaf_rows :, :] = jnp.zeros((PIECE, 128), BF16)

    def pack_step(step, counts):
        side_counts = list(counts)
        for part in range(4):
            leaf = step * 4 + part
            for side, source in ((0, lower_ref), (2, upper_ref)):
                high, low = weight_rows(source[leaf, :q_width, :])
                tail = source[leaf, q_width:, :]
                right = dot(select_right, stacked(tail))
                packed = jnp.concatenate([high, low, right, blank], axis=0).T.astype(BF16)
                start = pl.multiple_of(side * leaf_rows + leaf * p_width, p_width)
                pack_ref[pl.ds(start, p_width), :] = packed
                side_counts[side // 2] = jnp.where(lane == leaf, tail[3:4], side_counts[side // 2])
        return tuple(side_counts)

    nothing = jnp.zeros((1, p_width), F32)
    lower_counts, upper_counts = lax.fori_loop(0, leaf_count // 4, pack_step, (nothing, nothing))
    counts_ref[0:1, :] = lower_counts.astype(jnp.int32)
    counts_ref[1:2, :leaf_count] = own_counts_ref[...]
    counts_ref[2:3, :] = upper_counts.astype(jnp.int32)


def final_kernel(
    level_count, points_ref, surface_ref, counts_ref, near_ref, far_ref, coarse_ref, shift_ref, down_ref, *rest
):
    top_refs, (out_ref, node_ref, down_leaf_ref) = rest[:level_count], rest[level_count:]
    leaf_count, q_width, p_width = out_ref.shape
    eq_width = far_ref.shape[1]
    node_count = leaf_count // 8
    index = lax.axis_index("oct")
    select_left, select_right = selector(LEFT), selector(RIGHT)
    slab_local = jnp.zeros((q_width, eq_width), F32)
    for level, top_ref in enumerate(top_refs):
        slab_local = slab_local + dot3(top_ref[...], coarse_ref[jnp.right_shift(index, 3 * level) & 7])
    for node in range(node_count):
        rows = slice(node * q_width, (node + 1) * q_width)
        node_ref[rows, :] = far_ref[rows, :] + dot3(slab_local, shift_ref[node])

    def child_step(child, carry):
        down_leaf_ref[child] = dot3(dot3(node_ref[...], shift_ref[child]), down_ref[...])
        return carry

    lax.fori_loop(0, 8, child_step, 0)
    lane = iota((q_width, p_width), 1)

    def node_step(node, carry):
        for child in range(8):
            leaf = node * 8 + child
            right = dot(select_right, stacked(coords_of(points_ref, leaf)))
            values_high, values_low = kernel_rows(surface_ref, leaf, right, select_left)
            down = down_leaf_ref[child, pl.ds(pl.multiple_of(node * q_width, q_width), q_width), :]
            high, low = weight_rows(down)
            both = dot(jnp.concatenate([high, low], axis=0).astype(BF16), values_high)
            far = both[:q_width] + both[q_width:] + dot(high.astype(BF16), values_low)
            out_ref[leaf] = jnp.where(lane < counts_ref[leaf], far + near_ref[leaf], 0.0)
        return carry

    lax.fori_loop(0, node_count, node_step, 0)


def shifted(value, size):
    up = [(i, i + 1) for i in range(size - 1)]
    down = [(j, i) for i, j in up]
    return lax.ppermute(value, "oct", up), lax.ppermute(value, "oct", down)


def swapped(value, size, bit):
    return lax.ppermute(value, "oct", [(source, source ^ (1 << bit)) for source in range(size)])


def local(
    points,
    dens,
    surface,
    counts,
    ulist,
    vlist,
    up_inverse,
    down_inverse,
    shift_up,
    shift_down,
    coarse,
    translate,
):
    leaf_count, q_width, p_width = dens.shape
    eq_width = surface.shape[2]
    node_count, type_count = vlist.shape
    node_rows = node_count * q_width
    size = lax.axis_size("oct")
    bits = size.bit_length() - 1
    index = lax.axis_index("oct")
    vmem = pl.BlockSpec(memory_space=pltpu.VMEM)
    smem = pl.BlockSpec(memory_space=pltpu.SMEM)
    hbm = pl.BlockSpec(memory_space=pl.ANY)
    points = jnp.transpose(points, (1, 0, 2))
    surface = jnp.transpose(surface, (1, 0, 2))
    ulist = ulist.T
    table = jnp.transpose(translate, (1, 2, 0))

    pack, targets, message, send, slab = pl.pallas_call(
        upward_kernel,
        out_shape=(
            jax.ShapeDtypeStruct((leaf_count, p_width, 128), BF16),
            jax.ShapeDtypeStruct((leaf_count, p_width, 128), BF16),
            jax.ShapeDtypeStruct((leaf_count, q_width + 8, p_width), F32),
            jax.ShapeDtypeStruct((node_rows + 3 * q_width, eq_width), BF16),
            jax.ShapeDtypeStruct((q_width, eq_width), F32),
        ),
        in_specs=[vmem, vmem, vmem, smem, vmem, vmem],
        out_specs=(vmem,) * 5,
        scratch_shapes=[pltpu.VMEM((8, node_rows, eq_width), F32)],
        compiler_params=grant(24),
        name="upward",
    )(points, dens, surface, counts, up_inverse, shift_up)

    send_lower, send_upper = shifted(send, size)
    partner = jnp.where(index & 1 == 1, send_lower[node_rows:], send_upper[node_rows:]).astype(F32)
    total = slab + (partner[:q_width] + partner[q_width : 2 * q_width] + partner[2 * q_width :])
    message, total = lax.optimization_barrier((message, total))
    lower, upper = shifted(message, size)
    total = total + swapped(total, size, 1)
    pair = swapped(total, size, 2)
    send_lower, total = lax.optimization_barrier((send_lower, total))

    table = table.reshape(eq_width * eq_width, type_count)
    far_node = pl.pallas_call(
        far_kernel,
        out_shape=jax.ShapeDtypeStruct((node_rows, eq_width), F32),
        in_specs=[vmem, vmem, vmem, vmem, hbm],
        out_specs=vmem,
        scratch_shapes=[
            pltpu.VMEM((type_count // 128, eq_width * eq_width, 128), BF16),
            pltpu.VMEM((eq_width * eq_width, type_count % 128), BF16),
            pltpu.VMEM((eq_width * SOURCES, 128), F32),
            pltpu.VMEM((eq_width, node_rows), F32),
            pltpu.SemaphoreType.DMA((eq_width // 8, type_count // 128 + 1)),
        ],
        compiler_params=grant(36),
        cost_estimate=pl.CostEstimate(flops=2 * 10**10, bytes_accessed=18 * 10**6, transcendentals=0),
        name="far",
    )(send_lower, send, send_upper, vlist, table)
    far_node, lower, upper = lax.optimization_barrier((far_node, lower, upper))

    all_pack, all_counts, top, current = pl.pallas_call(
        pack_kernel,
        out_shape=(
            jax.ShapeDtypeStruct((3 * leaf_count * p_width + PIECE, 128), BF16),
            jax.ShapeDtypeStruct((3, p_width), jnp.int32),
            jax.ShapeDtypeStruct((q_width, eq_width), F32),
            jax.ShapeDtypeStruct((q_width, eq_width), F32),
        ),
        in_specs=[vmem] * 7,
        out_specs=(vmem,) * 4,
        compiler_params=grant(20),
        name="pack",
    )(lower, upper, pack, counts.reshape(1, leaf_count), total, pair, shift_up)

    tops = [top]
    for level in range(3, bits, 3):
        if level > 3:
            current = jnp.dot(current, shift_up[jnp.right_shift(index, level) & 7], precision=HIGHEST)
        for bit in range(level, min(level + 3, bits)):
            current = current + swapped(current, size, bit)
        tops.append(current)

    member_blocks = -(-ulist.shape[0] * p_width // BLOCK)
    list_blocks = 9 * member_blocks + 10 * UNROLL + 2
    near = pl.pallas_call(
        near_kernel,
        out_shape=jax.ShapeDtypeStruct((leaf_count, q_width, p_width), F32),
        in_specs=[smem, smem, vmem, vmem],
        out_specs=vmem,
        scratch_shapes=[
            pltpu.VMEM((2 * UNROLL, 2, p_width, 128), BF16),
            pltpu.VMEM((9, p_width, 128), F32),
            pltpu.SMEM((list_blocks * (BLOCK // PIECE),), jnp.int32),
            pltpu.SMEM((list_blocks * (BLOCK // PIECE),), jnp.int32),
            pltpu.SMEM((2, list_blocks + 2 * UNROLL), jnp.int32),
            pltpu.SMEM((leaf_count,), jnp.int32),
        ],
        compiler_params=grant(24),
        cost_estimate=pl.CostEstimate(flops=3 * 10**10, bytes_accessed=10**7, transcendentals=0),
        name="near",
    )(ulist, all_counts, all_pack, targets)

    return pl.pallas_call(
        lambda *refs: final_kernel(len(tops), *refs),
        out_shape=jax.ShapeDtypeStruct((leaf_count, q_width, p_width), F32),
        in_specs=[vmem, vmem, smem] + [vmem] * (5 + len(tops)),
        out_specs=vmem,
        scratch_shapes=[
            pltpu.VMEM((node_rows, eq_width), F32),
            pltpu.VMEM((8, node_rows, eq_width), F32),
        ],
        compiler_params=grant(20),
        name="final",
    )(points, surface, counts, near, far_node, coarse, shift_down, down_inverse, *tops)


def solution(mesh):
    placed = (
        P("oct", None, None),
        P("oct", None, None),
        P("oct", None, None),
        P("oct"),
        P("oct", None),
        P("oct", None),
        P(),
        P(),
        P(),
        P(),
        P(),
        P(),
    )
    return jax.shard_map(
        local, mesh=mesh, in_specs=placed, out_specs=P("oct", None, None), check_vma=False
    )
```

```python
import math

import jax
import jax.numpy as jnp
from jax import lax
from jax.experimental import pallas as pl
from jax.experimental.pallas import tpu as pltpu
from jax.sharding import PartitionSpec as P

F32 = jnp.float32
BF16 = jnp.bfloat16
HIGHEST = lax.Precision.HIGHEST
SCALE = math.sqrt(math.log2(math.e))
NT = (((1,), (1,)), ((), ()))
TN = (((0,), (0,)), ((), ()))
BLOCK = 256
UNROLL = 4
GROUP = 16
PLAN_SOURCE, PLAN_ORDER, PLAN_COUNT = 32, 62, 63
SOURCES = 32


def dot(left, right):
    return jnp.dot(left, right, preferred_element_type=F32)


def dot_nt(left, right):
    return lax.dot_general(left, right, NT, preferred_element_type=F32)


def dot_tn(left, right):
    return lax.dot_general(left, right, TN, preferred_element_type=F32)


def halves(value):
    high = value.astype(BF16)
    low = (value - high.astype(F32)).astype(BF16)
    return high, low


def dot3(left, right):
    left_high, left_low = halves(left)
    right_high, right_low = halves(right)
    return dot(left_high, right_high) + dot(left_high, right_low) + dot(left_low, right_high)


def grant(mebibytes):
    return pltpu.CompilerParams(vmem_limit_bytes=mebibytes * 1024 * 1024)


def iota(shape, dim):
    return lax.broadcasted_iota(jnp.int32, shape, dim)


def coords_of(ref, leaf):
    width = ref.shape[2]
    row = iota((8, width), 0)
    value = jnp.zeros((8, width), F32)
    for dim in range(3):
        line = jnp.broadcast_to(ref[dim, pl.ds(leaf, 1), :], (8, width))
        value = jnp.where(row == dim, line, value)
    return value


def pieces(coords):
    row = iota(coords.shape, 0)
    used = row < 3
    scaled = jnp.where(used, coords, 0.0) * SCALE
    high = scaled.astype(BF16).astype(F32)
    rest = scaled - high
    mid = rest.astype(BF16).astype(F32)
    low = (rest - mid).astype(BF16).astype(F32)
    norm = -0.5 * jnp.sum(scaled * scaled, axis=0, keepdims=True)
    norm_high = norm.astype(BF16).astype(F32)
    norm_rest = norm - norm_high
    norm_mid = norm_rest.astype(BF16).astype(F32)
    norm_low = norm_rest - norm_mid
    norms = jnp.where(row == 0, norm_high, jnp.where(row == 1, norm_mid, jnp.where(row == 2, norm_low, 0.0)))
    ones = jnp.where(used, 1.0, 0.0)
    return high, mid, low, norms, ones


def left_rows(parts):
    high, mid, low, norms, ones = parts
    return jnp.concatenate([high, high, mid, mid, high, low, ones, norms], axis=0)


def right_rows(parts):
    high, mid, low, norms, ones = parts
    return jnp.concatenate([high, mid, high, mid, low, high, norms, ones], axis=0)


def padded_left(parts):
    rows = left_rows(parts)
    return jnp.concatenate([jnp.zeros_like(rows), rows], axis=0).astype(BF16)


def packed_rows(weights, parts):
    weights_high = weights.astype(BF16).astype(F32)
    return jnp.concatenate([weights_high, weights - weights_high, right_rows(parts)], axis=0).astype(BF16)


def upward_kernel(
    points_ref, dens_ref, surface_ref, counts_ref, up_ref, shift_ref, pack_ref, target_ref, message_ref, send_ref,
    slab_ref, check_ref
):
    leaf_count, q_width, p_width = dens_ref.shape
    eq_width = surface_ref.shape[2]
    node_count = leaf_count // 8
    lane = iota((q_width, p_width), 1)
    row = iota((8, p_width), 0)

    def node_step(node, carry):
        for child in range(8):
            leaf = node * 8 + child
            count = counts_ref[leaf]
            weights = jnp.where(lane < count, dens_ref[leaf], 0.0)
            coords = coords_of(points_ref, leaf)
            message_ref[leaf, :q_width, :] = weights
            message_ref[leaf, q_width:, :] = jnp.where(row == 3, count.astype(F32), coords)
            parts = pieces(coords)
            rows = packed_rows(weights, parts)
            pack = rows.T
            pack_ref[leaf] = pack
            target_ref[leaf] = padded_left(parts).T
            values = jnp.exp2(dot(pack, padded_left(pieces(coords_of(surface_ref, leaf)))))
            values_high, values_low = halves(values)
            both = dot(rows[: 2 * q_width], values_high)
            check = both[:q_width] + both[q_width:] + dot(rows[:q_width], values_low)
            check_ref[child, pl.ds(pl.multiple_of(node * q_width, q_width), q_width), :] = check
        return carry

    lax.fori_loop(0, node_count, node_step, 0)

    def child_step(child, total):
        leaf_eq = dot3(check_ref[child], up_ref[...])
        return total + dot3(leaf_eq, shift_ref[child])

    node_eq = lax.fori_loop(0, 8, child_step, jnp.zeros((node_count * q_width, eq_width), F32))
    send_ref[: node_count * q_width, :] = node_eq.astype(BF16)
    slab_eq = jnp.zeros((q_width, eq_width), F32)
    for child in range(8):
        slab_eq = slab_eq + dot3(node_eq[child * q_width : (child + 1) * q_width], shift_ref[child])
    index = lax.axis_index("oct")
    slab = dot3(slab_eq, shift_ref[index & 7])
    slab_ref[...] = slab
    high, rest = halves(slab)
    low = (slab - high.astype(F32) - rest.astype(F32)).astype(BF16)
    for place, part in enumerate((high, rest, low)):
        start = node_count * q_width + place * q_width
        send_ref[start : start + q_width, :] = part


def far_kernel(
    lower_ref, own_ref, upper_ref, vlist_ref, table_hbm, out_ref, table_ref, tail_ref, wide_ref, total_ref, sems
):
    node_count, type_count = vlist_ref.shape
    eq_width = own_ref.shape[1]
    q_width = out_ref.shape[0] // node_count
    lanes = node_count * q_width
    tile = 128 // q_width
    chunk = 8
    chunk_rows = chunk * eq_width
    chunk_count = eq_width // chunk
    full = type_count // 128

    def copies_of(number):
        span = pl.ds(number * chunk_rows, chunk_rows)
        copies = []
        for part in range(full):
            source = table_hbm.at[span, pl.ds(part * 128, 128)]
            copies.append(pltpu.make_async_copy(source, table_ref.at[part, span], sems.at[number, part]))
        source = table_hbm.at[span, pl.ds(full * 128, type_count - full * 128)]
        copies.append(pltpu.make_async_copy(source, tail_ref.at[span], sems.at[number, full]))
        return copies

    for number in range(chunk_count):
        for copy in copies_of(number):
            copy.start()

    index = lax.axis_index("oct")
    repeat = (iota((q_width, 128), 1) % q_width == iota((q_width, 128), 0)).astype(BF16)
    for part, source in enumerate((lower_ref, own_ref, upper_ref)):
        for node in range(node_count):
            spread = dot_tn(source[node * q_width : (node + 1) * q_width, :], repeat)
            wide_ref[pl.ds(part * node_count + node, eq_width, stride=SOURCES), :] = spread
    for place in range(3 * node_count, SOURCES):
        wide_ref[pl.ds(place, eq_width, stride=SOURCES), :] = jnp.zeros((eq_width, 128), F32)

    ids = vlist_ref[...]
    places = jnp.where(ids >= 0, ids - (index - 1) * node_count, -1).astype(F32).astype(BF16)
    spread = (iota((node_count, lanes), 1) // SOURCES == iota((node_count, lanes), 0)).astype(BF16)
    wanted = dot_tn(places, spread)
    chosen = (wanted == (iota((type_count, lanes), 1) % SOURCES).astype(F32)).astype(F32)
    chosen_full = chosen[: full * 128].astype(BF16)
    chosen_tail = chosen[full * 128 :].astype(BF16)
    lane_node = iota((SOURCES, 128), 1) // q_width
    nothing = jnp.zeros((SOURCES, 128), F32)
    total_ref[...] = jnp.zeros_like(total_ref)

    def chunk_step(number, carry):
        for copy in copies_of(number):
            copy.wait()
        span = pl.ds(pl.multiple_of(number * chunk_rows, chunk_rows), chunk_rows)
        left = jnp.concatenate([table_ref[part, span, :] for part in range(full)], axis=1)
        summed = dot(left, chosen_full) + dot(tail_ref[span, :], chosen_tail)
        lefts, rights = [], []
        for step in range(chunk):
            value = summed[step * eq_width : (step + 1) * eq_width]
            high = value.astype(BF16).astype(F32)
            lefts.append(jnp.concatenate([high, value - high], axis=0).astype(BF16))
            row = number * chunk + step
            sent = wide_ref[pl.ds(pl.multiple_of(row * SOURCES, SOURCES), SOURCES), :]
            parts = [jnp.where(lane_node == place, sent, 0.0) for place in range(tile)]
            for node in range(node_count):
                line = [parts[node % tile] if place == node // tile else nothing for place in range(node_count // tile)]
                rights.append(jnp.concatenate(line, axis=1))
        product = dot(jnp.concatenate(lefts, axis=1), jnp.concatenate(rights, axis=0).astype(BF16))
        total_ref[...] += product[:eq_width] + product[eq_width:]
        return carry

    lax.fori_loop(0, chunk_count, chunk_step, 0)
    out_ref[...] = total_ref[...].T


def near_kernel(
    plan_ref, own_pack_ref, side_pack_ref, target_ref, out_ref, gather_ref, value_ref, total_ref, owner_ref
):
    leaf_count, q_width, p_width = out_ref.shape
    slot_count = 27
    member_blocks = -(-slot_count * p_width // BLOCK)
    total_ref[...] = jnp.zeros_like(total_ref)
    for number in range(UNROLL):
        owner_ref[number] = leaf_count

    def group_step(group, carry):
        def gather(member, inner):
            leaf = plan_ref[PLAN_ORDER, group * GROUP + member]
            for slot in range(slot_count):
                pack_ref = own_pack_ref if slot == 0 or 9 <= slot < 18 else side_pack_ref
                source = pl.multiple_of(plan_ref[PLAN_SOURCE + slot, leaf], p_width)
                offset = pl.multiple_of(plan_ref[slot, leaf], 16)
                gather_ref[pl.ds(offset, p_width), :] = pack_ref[pl.ds(source, p_width), :]
            offset = pl.multiple_of(plan_ref[slot_count, leaf], 16)
            gather_ref[pl.ds(offset, BLOCK), :] = jnp.zeros((BLOCK, 128), BF16)
            first = lax.shift_right_logical(plan_ref[0, leaf], 8)
            for number in range(member_blocks):
                owner_ref[UNROLL + first + number] = leaf
            return inner

        lax.fori_loop(0, GROUP, gather, 0)
        last = plan_ref[PLAN_ORDER, group * GROUP + GROUP - 1]
        block_count = lax.shift_right_logical(plan_ref[slot_count, last] + (BLOCK - 1), 8)
        for number in range(2 * UNROLL):
            owner_ref[UNROLL + block_count + number] = leaf_count

        def sources_of(block):
            return gather_ref[pl.ds(pl.multiple_of(block * BLOCK, BLOCK), BLOCK), :]

        def run(rows):
            def blocks_step(step, inner):
                slot = jnp.bitwise_and(step, 1) * UNROLL
                for part in range(UNROLL):
                    block = jnp.maximum(step - 1, 0) * UNROLL + part
                    leaf = owner_ref[step * UNROLL + part]
                    values = [value_ref[UNROLL - slot + part, side, :rows] for side in range(2)]
                    total_ref[leaf, :rows] += dot(jnp.concatenate(values, axis=1), sources_of(block))
                for part in range(UNROLL):
                    block = step * UNROLL + part
                    leaf = jnp.minimum(owner_ref[UNROLL + block], leaf_count - 1)
                    values = jnp.exp2(dot_nt(target_ref[leaf, :rows], sources_of(block))).astype(BF16)
                    for side in range(2):
                        value_ref[slot + part, side, :rows] = values[:, side * 128 : (side + 1) * 128]
                return inner

            lax.fori_loop(0, lax.div(block_count + (2 * UNROLL - 1), UNROLL), blocks_step, 0)

        largest = plan_ref[PLAN_COUNT, last]
        for low, rows in ((0, 32), (32, 64), (64, 96), (96, 128)):
            pl.when((largest > low) & (largest <= rows))(lambda rows=rows: run(rows))
        return carry

    lax.fori_loop(0, leaf_count // GROUP, group_step, 0)

    def turn_step(step, carry):
        for part in range(8):
            turned = total_ref[step * 8 + part, :, : 2 * q_width].T
            out_ref[step * 8 + part] = turned[:q_width] + turned[q_width:]
        return carry

    lax.fori_loop(0, leaf_count // 8, turn_step, 0)


def as_column(line):
    width = line.shape[1]
    wide = jnp.concatenate([line, jnp.zeros((1, 128 - width), F32)], axis=1) if width < 128 else line
    return jnp.broadcast_to(wide, (128, 128)).T[:width, :width]


def plan_of(ulist_ref, counts, plan_ref):
    slot_count, leaf_count = ulist_ref.shape
    index = lax.axis_index("oct")
    shape = (leaf_count, leaf_count)
    row, column = iota(shape, 0), iota(shape, 1)
    tables = [as_column(line) for line in counts]
    own = jnp.broadcast_to(counts[1], shape)
    before = (tables[1] < own) | ((tables[1] == own) & (row < column))
    rank = jnp.sum(jnp.where(before, 1.0, 0.0), axis=0, keepdims=True)
    rank_column = as_column(rank).astype(jnp.int32)
    rank_wide = jnp.broadcast_to(rank, shape).astype(jnp.int32)

    offset = jnp.zeros((1, leaf_count), jnp.int32)
    offsets = []
    for slot in range(slot_count):
        side = 1 if slot == 0 else (0 if slot < 9 else (1 if slot < 18 else 2))
        ids = ulist_ref[slot : slot + 1, :]
        place = jnp.where(ids >= 0, ids - (index + (side - 1)) * leaf_count, 0)
        found = jnp.sum(jnp.where(row == place, tables[side], 0.0), axis=0, keepdims=True).astype(jnp.int32)
        length = jnp.where(ids >= 0, jnp.bitwise_and(found + 15, -16), 0)
        start = place + (leaf_count if side == 2 else 0)
        plan_ref[PLAN_SOURCE + slot : PLAN_SOURCE + slot + 1, :] = start * 128
        offsets.append(offset)
        offset = offset + length
    offsets.append(offset)
    blocks = lax.shift_right_logical(offset + (BLOCK - 1), 8)
    blocks_column = as_column(blocks.astype(F32))
    group_shift = GROUP.bit_length() - 1
    same = lax.shift_right_logical(rank_column, group_shift) == lax.shift_right_logical(rank_wide, group_shift)
    first = jnp.sum(jnp.where(same & (rank_column < rank_wide), blocks_column, 0.0), axis=0, keepdims=True)
    first = first.astype(jnp.int32) * BLOCK
    for number, value in enumerate(offsets):
        plan_ref[number : number + 1, :] = first + value
    order = jnp.sum(jnp.where(rank_column == column, row.astype(F32), 0.0), axis=0, keepdims=True)
    plan_ref[PLAN_ORDER : PLAN_ORDER + 1, :] = order.astype(jnp.int32)
    plan_ref[PLAN_COUNT : PLAN_COUNT + 1, :] = counts[1].astype(jnp.int32)


def pack_kernel(
    lower_ref, upper_ref, ulist_ref, own_counts_ref, sum_ref, pair_ref, shift_ref, pack_ref, plan_ref, top_ref, next_ref
):
    leaf_count, rows, p_width = lower_ref.shape
    q_width = rows - 8
    index = lax.axis_index("oct")
    top = sum_ref[...] + pair_ref[...]
    top_ref[...] = top
    next_ref[...] = dot3(top, shift_ref[jnp.right_shift(index, 3) & 7])
    lane = iota((1, leaf_count), 1)

    def pack_step(step, counts):
        side_counts = list(counts)
        for part in range(4):
            leaf = step * 4 + part
            for side, source in enumerate((lower_ref, upper_ref)):
                tail = source[leaf, q_width:, :]
                packed = packed_rows(source[leaf, :q_width, :], pieces(tail)).T
                start = pl.multiple_of((side * leaf_count + leaf) * p_width, p_width)
                pack_ref[pl.ds(start, p_width), :] = packed
                side_counts[side] = jnp.where(lane == leaf, tail[3:4, :leaf_count], side_counts[side])
        return tuple(side_counts)

    nothing = jnp.zeros((1, leaf_count), F32)
    lower_counts, upper_counts = lax.fori_loop(0, leaf_count // 4, pack_step, (nothing, nothing))
    plan_of(ulist_ref, (lower_counts, own_counts_ref[...].astype(F32), upper_counts), plan_ref)


def final_kernel(
    level_count, plan_ref, pack_ref, surface_ref, near_ref, far_ref, coarse_ref, shift_ref, down_ref, *rest
):
    top_refs, (out_ref, node_ref, down_leaf_ref) = rest[:level_count], rest[level_count:]
    leaf_count, q_width, p_width = out_ref.shape
    eq_width = far_ref.shape[1]
    node_count = leaf_count // 8
    index = lax.axis_index("oct")
    slab_local = jnp.zeros((q_width, eq_width), F32)
    for level, top_ref in enumerate(top_refs):
        slab_local = slab_local + dot3(top_ref[...], coarse_ref[jnp.right_shift(index, 3 * level) & 7])
    for node in range(node_count):
        rows = slice(node * q_width, (node + 1) * q_width)
        node_ref[rows, :] = far_ref[rows, :] + dot3(slab_local, shift_ref[node])

    def child_step(child, carry):
        down_leaf_ref[child] = dot3(dot3(node_ref[...], shift_ref[child]), down_ref[...])
        return carry

    lax.fori_loop(0, 8, child_step, 0)
    lane = iota((q_width, p_width), 1)

    def leaves_step(step, carry):
        def run(rows):
            for part in range(8):
                leaf = plan_ref[PLAN_ORDER, step * 8 + part]
                child = jnp.bitwise_and(leaf, 7)
                node_row = pl.multiple_of(lax.shift_right_logical(leaf, 3) * q_width, q_width)
                own = pack_ref[pl.ds(pl.multiple_of(leaf * p_width, p_width), rows), :]
                values = jnp.exp2(dot(own, padded_left(pieces(coords_of(surface_ref, leaf)))))
                values_high, values_low = halves(values)
                down = down_leaf_ref[child, pl.ds(node_row, q_width), :]
                down_high = down.astype(BF16).astype(F32)
                down_rows = jnp.concatenate([down_high, down - down_high], axis=0).astype(BF16)
                down_first = jnp.concatenate([down_high, jnp.zeros_like(down_high)], axis=0).astype(BF16)
                far = dot_nt(values_high, down_rows) + dot_nt(values_low, down_first)
                if rows < p_width:
                    far = jnp.concatenate([far, jnp.zeros((p_width - rows, 2 * q_width), F32)], axis=0)
                turned = far.T
                summed = turned[:q_width] + turned[q_width:] + near_ref[leaf]
                out_ref[leaf] = jnp.where(lane < plan_ref[PLAN_COUNT, leaf], summed, 0.0)

        largest = plan_ref[PLAN_COUNT, plan_ref[PLAN_ORDER, step * 8 + 7]]
        for low, rows in ((0, 32), (32, 64), (64, 96), (96, 128)):
            pl.when((largest > low) & (largest <= rows))(lambda rows=rows: run(rows))
        return carry

    lax.fori_loop(0, node_count, leaves_step, 0)


def shifted(value, size):
    up = [(i, i + 1) for i in range(size - 1)]
    down = [(j, i) for i, j in up]
    return lax.ppermute(value, "oct", up), lax.ppermute(value, "oct", down)


def swapped(value, size, bit):
    return lax.ppermute(value, "oct", [(source, source ^ (1 << bit)) for source in range(size)])


def local(
    points,
    dens,
    surface,
    counts,
    ulist,
    vlist,
    up_inverse,
    down_inverse,
    shift_up,
    shift_down,
    coarse,
    translate,
):
    leaf_count, q_width, p_width = dens.shape
    eq_width = surface.shape[2]
    node_count, type_count = vlist.shape
    node_rows = node_count * q_width
    size = lax.axis_size("oct")
    bits = size.bit_length() - 1
    index = lax.axis_index("oct")
    vmem = pl.BlockSpec(memory_space=pltpu.VMEM)
    smem = pl.BlockSpec(memory_space=pltpu.SMEM)
    hbm = pl.BlockSpec(memory_space=pl.ANY)
    params = grant(56)
    points = jnp.transpose(points, (1, 0, 2))
    surface = jnp.transpose(surface, (1, 0, 2))
    ulist = ulist.T
    table = jnp.transpose(translate, (1, 2, 0))

    pack, targets, message, send, slab = pl.pallas_call(
        upward_kernel,
        out_shape=(
            jax.ShapeDtypeStruct((leaf_count, p_width, 128), BF16),
            jax.ShapeDtypeStruct((leaf_count, p_width, 128), BF16),
            jax.ShapeDtypeStruct((leaf_count, q_width + 8, p_width), F32),
            jax.ShapeDtypeStruct((node_rows + 3 * q_width, eq_width), BF16),
            jax.ShapeDtypeStruct((q_width, eq_width), F32),
        ),
        in_specs=[vmem, vmem, vmem, smem, vmem, vmem],
        out_specs=(vmem,) * 5,
        scratch_shapes=[pltpu.VMEM((8, node_rows, eq_width), F32)],
        compiler_params=params,
        name="upward",
    )(points, dens, surface, counts, up_inverse, shift_up)

    send_lower, send_upper = shifted(send, size)
    partner = jnp.where(index & 1 == 1, send_lower[node_rows:], send_upper[node_rows:]).astype(F32)
    total = slab + (partner[:q_width] + partner[q_width : 2 * q_width] + partner[2 * q_width :])
    message, total = lax.optimization_barrier((message, total))
    lower, upper = shifted(message, size)
    total = total + swapped(total, size, 1)
    pair = swapped(total, size, 2)
    send_lower, total = lax.optimization_barrier((send_lower, total))

    table = table.reshape(eq_width * eq_width, type_count)
    far_node = pl.pallas_call(
        far_kernel,
        out_shape=jax.ShapeDtypeStruct((node_rows, eq_width), F32),
        in_specs=[vmem, vmem, vmem, vmem, hbm],
        out_specs=vmem,
        scratch_shapes=[
            pltpu.VMEM((type_count // 128, eq_width * eq_width, 128), BF16),
            pltpu.VMEM((eq_width * eq_width, type_count % 128), BF16),
            pltpu.VMEM((eq_width * SOURCES, 128), F32),
            pltpu.VMEM((eq_width, node_rows), F32),
            pltpu.SemaphoreType.DMA((eq_width // 8, type_count // 128 + 1)),
        ],
        compiler_params=params,
        cost_estimate=pl.CostEstimate(flops=2 * 10**10, bytes_accessed=18 * 10**6, transcendentals=0),
        name="far",
    )(send_lower, send, send_upper, vlist, table)
    far_node, lower, upper = lax.optimization_barrier((far_node, lower, upper))

    side_pack, plan, top, current = pl.pallas_call(
        pack_kernel,
        out_shape=(
            jax.ShapeDtypeStruct((2 * leaf_count * p_width, 128), BF16),
            jax.ShapeDtypeStruct((64, leaf_count), jnp.int32),
            jax.ShapeDtypeStruct((q_width, eq_width), F32),
            jax.ShapeDtypeStruct((q_width, eq_width), F32),
        ),
        in_specs=[vmem] * 7,
        out_specs=(vmem,) * 4,
        compiler_params=params,
        name="pack",
    )(lower, upper, ulist, counts.reshape(1, leaf_count), total, pair, shift_up)

    tops = [top]
    for level in range(3, bits, 3):
        if level > 3:
            current = jnp.dot(current, shift_up[jnp.right_shift(index, level) & 7], precision=HIGHEST)
        for bit in range(level, min(level + 3, bits)):
            current = current + swapped(current, size, bit)
        tops.append(current)

    pack = pack.reshape(leaf_count * p_width, 128)
    group_blocks = GROUP * -(-ulist.shape[0] * p_width // BLOCK)
    near = pl.pallas_call(
        near_kernel,
        out_shape=jax.ShapeDtypeStruct((leaf_count, q_width, p_width), F32),
        in_specs=[smem, vmem, vmem, vmem],
        out_specs=vmem,
        scratch_shapes=[
            pltpu.VMEM(((group_blocks + 2 * UNROLL + 2) * BLOCK, 128), BF16),
            pltpu.VMEM((2 * UNROLL, 2, p_width, 128), BF16),
            pltpu.VMEM((leaf_count + 1, p_width, 128), F32),
            pltpu.SMEM((group_blocks + 4 * UNROLL,), jnp.int32),
        ],
        compiler_params=params,
        cost_estimate=pl.CostEstimate(flops=3 * 10**10, bytes_accessed=10**7, transcendentals=0),
        name="near",
    )(plan, pack, side_pack, targets)

    return pl.pallas_call(
        lambda *refs: final_kernel(len(tops), *refs),
        out_shape=jax.ShapeDtypeStruct((leaf_count, q_width, p_width), F32),
        in_specs=[smem] + [vmem] * (7 + len(tops)),
        out_specs=vmem,
        scratch_shapes=[
            pltpu.VMEM((node_rows, eq_width), F32),
            pltpu.VMEM((8, node_rows, eq_width), F32),
        ],
        compiler_params=params,
        name="final",
    )(plan, pack, surface, near, far_node, coarse, shift_down, down_inverse, *tops)


def solution(mesh):
    placed = (
        P("oct", None, None),
        P("oct", None, None),
        P("oct", None, None),
        P("oct"),
        P("oct", None),
        P("oct", None),
        P(),
        P(),
        P(),
        P(),
        P(),
        P(),
    )
    return jax.shard_map(
        local, mesh=mesh, in_specs=placed, out_specs=P("oct", None, None), check_vma=False
    )
```

```python
import math

import jax
import jax.numpy as jnp
from jax import lax
from jax.experimental import pallas as pl
from jax.experimental.pallas import tpu as pltpu
from jax.sharding import PartitionSpec as P

F32 = jnp.float32
BF16 = jnp.bfloat16
HIGHEST = lax.Precision.HIGHEST
SCALE = math.sqrt(math.log2(math.e))
NT = (((1,), (1,)), ((), ()))
TN = (((0,), (0,)), ((), ()))
BLOCK = 256
UNROLL = 4
PIECE = 64
CLASS_ROWS = (32, 64, 96, 128)
PLAN_PLACES, PLAN_CLASS, PLAN_ORDER, PLAN_COUNT = 56, 60, 61, 62
SOURCES = 32


def dot(left, right):
    return jnp.dot(left, right, preferred_element_type=F32)


def dot_nt(left, right):
    return lax.dot_general(left, right, NT, preferred_element_type=F32)


def dot_tn(left, right):
    return lax.dot_general(left, right, TN, preferred_element_type=F32)


def halves(value):
    high = value.astype(BF16)
    low = (value - high.astype(F32)).astype(BF16)
    return high, low


def dot3(left, right):
    left_high, left_low = halves(left)
    right_high, right_low = halves(right)
    return dot(left_high, right_high) + dot(left_high, right_low) + dot(left_low, right_high)


def grant(mebibytes):
    return pltpu.CompilerParams(vmem_limit_bytes=mebibytes * 1024 * 1024)


def iota(shape, dim):
    return lax.broadcasted_iota(jnp.int32, shape, dim)


def coords_of(ref, leaf):
    width = ref.shape[2]
    row = iota((8, width), 0)
    value = jnp.zeros((8, width), F32)
    for dim in range(3):
        line = jnp.broadcast_to(ref[dim, pl.ds(leaf, 1), :], (8, width))
        value = jnp.where(row == dim, line, value)
    return value


def pieces(coords):
    row = iota(coords.shape, 0)
    used = row < 3
    scaled = jnp.where(used, coords, 0.0) * SCALE
    high = scaled.astype(BF16).astype(F32)
    rest = scaled - high
    mid = rest.astype(BF16).astype(F32)
    low = (rest - mid).astype(BF16).astype(F32)
    norm = -0.5 * jnp.sum(scaled * scaled, axis=0, keepdims=True)
    norm_high = norm.astype(BF16).astype(F32)
    norm_rest = norm - norm_high
    norm_mid = norm_rest.astype(BF16).astype(F32)
    norm_low = norm_rest - norm_mid
    norms = jnp.where(row == 0, norm_high, jnp.where(row == 1, norm_mid, jnp.where(row == 2, norm_low, 0.0)))
    ones = jnp.where(used, 1.0, 0.0)
    return high, mid, low, norms, ones


def paired(first, second):
    return first + pltpu.roll(second, 4, 0)


def left_rows(parts):
    high, mid, low, norms, ones = parts
    return jnp.concatenate([paired(high, high), paired(mid, mid), paired(high, low), paired(ones, norms)], axis=0)


def right_rows(parts):
    high, mid, low, norms, ones = parts
    both = paired(high, mid)
    return jnp.concatenate([both, both, paired(low, high), paired(norms, ones)], axis=0)


def weight_rows(weights):
    high = weights.astype(BF16).astype(F32)
    return [high, weights - high]


def put_features(feature_ref, leaf, rows):
    lower = iota(rows.shape, 1) < PIECE
    for half in range(2):
        alone = jnp.where(lower == (half == 0), rows, 0.0)
        span = pl.ds(pl.multiple_of((2 * leaf + half) * 32, 32), 32)
        feature_ref[half, span, :] = alone.astype(BF16)
        feature_ref[1 - half, span, :] = pltpu.roll(alone, PIECE, 1).astype(BF16)


def upward_kernel(
    points_ref, dens_ref, surface_ref, counts_ref, up_ref, shift_ref, pack_ref, feature_ref, turned_ref,
    message_ref, send_ref, slab_ref, check_ref
):
    leaf_count, q_width, p_width = dens_ref.shape
    eq_width = surface_ref.shape[2]
    node_count = leaf_count // 8
    lane = iota((q_width, p_width), 1)
    row = iota((8, p_width), 0)

    def node_step(node, carry):
        for child in range(8):
            leaf = node * 8 + child
            count = counts_ref[leaf]
            weights = jnp.where(lane < count, dens_ref[leaf], 0.0)
            coords = coords_of(points_ref, leaf)
            message_ref[leaf, :q_width, :] = weights
            message_ref[leaf, q_width:, :] = jnp.where(row == 3, count.astype(F32), coords)
            parts = pieces(coords)
            weight_parts = weight_rows(weights)
            right = right_rows(parts)
            pack = jnp.concatenate([left_rows(parts)] + weight_parts + [right], axis=0).astype(BF16).T
            pack_ref[pl.ds(pl.multiple_of(leaf * p_width, p_width), p_width), :] = pack
            put_features(feature_ref, leaf, right)
            surface = left_rows(pieces(coords_of(surface_ref, leaf)))
            turned_ref[leaf] = surface.astype(BF16).T
            wide = jnp.concatenate([jnp.zeros((96, eq_width), F32), surface], axis=0).astype(BF16)
            values_high, values_low = halves(jnp.exp2(dot(pack, wide)))
            rows = jnp.concatenate(weight_parts, axis=0).astype(BF16)
            both = dot(rows, values_high)
            check = both[:q_width] + both[q_width:] + dot(rows[:q_width], values_low)
            check_ref[child, pl.ds(pl.multiple_of(node * q_width, q_width), q_width), :] = check
        return carry

    lax.fori_loop(0, node_count, node_step, 0)

    node_eq = jnp.zeros((node_count * q_width, eq_width), F32)
    for child in range(8):
        node_eq = node_eq + dot3(dot3(check_ref[child], up_ref[...]), shift_ref[child])
    send_ref[: node_count * q_width, :] = node_eq.astype(BF16)
    slab_eq = jnp.zeros((q_width, eq_width), F32)
    for child in range(8):
        slab_eq = slab_eq + dot3(node_eq[child * q_width : (child + 1) * q_width], shift_ref[child])
    index = lax.axis_index("oct")
    slab = dot3(slab_eq, shift_ref[index & 7])
    slab_ref[...] = slab
    high, rest = halves(slab)
    low = (slab - high.astype(F32) - rest.astype(F32)).astype(BF16)
    for place, part in enumerate((high, rest, low)):
        start = node_count * q_width + place * q_width
        send_ref[start : start + q_width, :] = part


def far_kernel(
    lower_ref, own_ref, upper_ref, vlist_ref, table_hbm, out_ref, table_ref, tail_ref, wide_ref, total_ref, sems
):
    node_count, type_count = vlist_ref.shape
    eq_width = own_ref.shape[1]
    q_width = out_ref.shape[0] // node_count
    lanes = node_count * q_width
    tile = 128 // q_width
    chunk = 8
    chunk_rows = chunk * eq_width
    chunk_count = eq_width // chunk
    full = type_count // 128

    def copies_of(number):
        span = pl.ds(number * chunk_rows, chunk_rows)
        copies = []
        for part in range(full):
            source = table_hbm.at[span, pl.ds(part * 128, 128)]
            copies.append(pltpu.make_async_copy(source, table_ref.at[part, span], sems.at[number, part]))
        source = table_hbm.at[span, pl.ds(full * 128, type_count - full * 128)]
        copies.append(pltpu.make_async_copy(source, tail_ref.at[span], sems.at[number, full]))
        return copies

    for number in range(chunk_count):
        for copy in copies_of(number):
            copy.start()

    index = lax.axis_index("oct")
    repeat = (iota((q_width, 128), 1) % q_width == iota((q_width, 128), 0)).astype(BF16)
    for part, source in enumerate((lower_ref, own_ref, upper_ref)):
        for node in range(node_count):
            spread = dot_tn(source[node * q_width : (node + 1) * q_width, :], repeat)
            wide_ref[pl.ds(part * node_count + node, eq_width, stride=SOURCES), :] = spread
    for place in range(3 * node_count, SOURCES):
        wide_ref[pl.ds(place, eq_width, stride=SOURCES), :] = jnp.zeros((eq_width, 128), F32)

    ids = vlist_ref[...]
    places = jnp.where(ids >= 0, ids - (index - 1) * node_count, -1).astype(F32).astype(BF16)
    spread = (iota((node_count, lanes), 1) // SOURCES == iota((node_count, lanes), 0)).astype(BF16)
    wanted = dot_tn(places, spread)
    chosen = (wanted == (iota((type_count, lanes), 1) % SOURCES).astype(F32)).astype(F32)
    chosen_full = chosen[: full * 128].astype(BF16)
    chosen_tail = chosen[full * 128 :].astype(BF16)
    lane_node = iota((SOURCES, 128), 1) // q_width
    nothing = jnp.zeros((SOURCES, 128), F32)
    total_ref[...] = jnp.zeros_like(total_ref)

    def chunk_step(number, carry):
        for copy in copies_of(number):
            copy.wait()
        span = pl.ds(pl.multiple_of(number * chunk_rows, chunk_rows), chunk_rows)
        left = jnp.concatenate([table_ref[part, span, :] for part in range(full)], axis=1)
        summed = dot(left, chosen_full) + dot(tail_ref[span, :], chosen_tail)
        lefts, rights = [], []
        for step in range(chunk):
            value = summed[step * eq_width : (step + 1) * eq_width]
            high = value.astype(BF16).astype(F32)
            lefts.append(jnp.concatenate([high, value - high], axis=0).astype(BF16))
            row = number * chunk + step
            sent = wide_ref[pl.ds(pl.multiple_of(row * SOURCES, SOURCES), SOURCES), :]
            parts = [jnp.where(lane_node == place, sent, 0.0) for place in range(tile)]
            for node in range(node_count):
                line = [parts[node % tile] if place == node // tile else nothing for place in range(node_count // tile)]
                rights.append(jnp.concatenate(line, axis=1))
        product = dot(jnp.concatenate(lefts, axis=1), jnp.concatenate(rights, axis=0).astype(BF16))
        total_ref[...] += product[:eq_width] + product[eq_width:]
        return carry

    lax.fori_loop(0, chunk_count, chunk_step, 0)
    out_ref[...] = total_ref[...].T


def near_kernel(
    plan_ref, item_ref, own_hbm, side_hbm, own_feature_hbm, side_feature_hbm, out_ref, pack_ref, feature_ref,
    value_ref, total_ref, sems
):
    leaf_count, q_width, p_width = out_ref.shape
    own_rows, side_rows = own_hbm.shape[0], side_hbm.shape[0]
    own_lines, side_lines = own_feature_hbm.shape[1], side_feature_hbm.shape[1]
    copies = [
        (own_hbm, pack_ref.at[pl.ds(0, own_rows)]),
        (side_hbm, pack_ref.at[pl.ds(own_rows, side_rows)]),
        (own_feature_hbm, feature_ref.at[:, pl.ds(0, own_lines)]),
        (side_feature_hbm, feature_ref.at[:, pl.ds(own_lines, side_lines)]),
    ]
    copies = [pltpu.make_async_copy(source, target, sems.at[n]) for n, (source, target) in enumerate(copies)]
    for copy in copies:
        copy.start()
    pack_ref[own_rows + side_rows :, :] = jnp.zeros((PIECE, 128), BF16)
    feature_ref[:, own_lines + side_lines :, :] = jnp.zeros((2, 32, 128), BF16)
    total_ref[...] = jnp.zeros_like(total_ref)
    for copy in copies:
        copy.wait()
    step_lanes = 128 // UNROLL
    shift = step_lanes.bit_length() - 1

    def item_of(step, part):
        line = lax.shift_right_logical(step, shift)
        lane = jnp.bitwise_and(step, step_lanes - 1) * UNROLL + part
        return item_ref[line, lane], item_ref[8 + line, lane]

    def sources_of(leaf, place):
        rows = []
        for number in range(BLOCK // PIECE):
            start = pl.multiple_of(plan_ref[place + number, leaf] * 2, PIECE)
            rows.append(pack_ref[pl.ds(start, PIECE), :])
        return jnp.concatenate(rows, axis=0)

    def features_of(leaf, place):
        tiles = []
        for tile in range(BLOCK // 128):
            starts = [pl.multiple_of(plan_ref[place + 2 * tile + half, leaf], 32) for half in range(2)]
            halves_of = [feature_ref[half, pl.ds(start, 32), :] for half, start in enumerate(starts)]
            tiles.append(halves_of[0] + halves_of[1])
        return jnp.concatenate(tiles, axis=1)

    def run(rows, first, count):
        def blocks_step(step, carry):
            slot = jnp.bitwise_and(step, 1) * UNROLL
            for part in range(UNROLL):
                leaf, place = item_of(step - 1, part)
                values = [value_ref[UNROLL - slot + part, side, :rows] for side in range(2)]
                total_ref[leaf, :rows] += dot(jnp.concatenate(values, axis=1), sources_of(leaf, place))
            for part in range(UNROLL):
                leaf, place = item_of(step, part)
                start = pl.multiple_of(jnp.minimum(leaf, leaf_count - 1) * p_width, p_width)
                targets = pack_ref[pl.ds(start, rows), :][:, :32]
                values = jnp.exp2(dot(targets, features_of(leaf, place))).astype(BF16)
                for side in range(2):
                    value_ref[slot + part, side, :rows] = values[:, side * 128 : (side + 1) * 128]
            return carry

        lax.fori_loop(first, first + count, blocks_step, 0)

    for number, rows in enumerate(CLASS_ROWS):
        run(rows, plan_ref[PLAN_CLASS, 2 * number], plan_ref[PLAN_CLASS, 2 * number + 1])

    def turn_step(step, carry):
        for part in range(8):
            turned = total_ref[step * 8 + part].T
            out_ref[step * 8 + part] = turned[32 : 32 + q_width] + turned[32 + q_width : 32 + 2 * q_width]
        return carry

    lax.fori_loop(0, leaf_count // 8, turn_step, 0)


def as_column(line):
    width = line.shape[1]
    wide = jnp.concatenate([line, jnp.zeros((1, 128 - width), F32)], axis=1) if width < 128 else line
    return jnp.broadcast_to(wide, (128, 128)).T[:width, :width]


def plan_of(ulist_ref, counts, plan_ref, item_ref):
    slot_count, leaf_count = ulist_ref.shape
    index = lax.axis_index("oct")
    shape = (leaf_count, leaf_count)
    row, column = iota(shape, 0), iota(shape, 1)
    tables = [as_column(line) for line in counts]
    own = jnp.broadcast_to(counts[1], shape)
    before = (tables[1] < own) | ((tables[1] == own) & (row < column))
    rank = jnp.sum(jnp.where(before, 1.0, 0.0), axis=0, keepdims=True)
    rank_column = as_column(rank).astype(jnp.int32)
    rank_wide = jnp.broadcast_to(rank, shape).astype(jnp.int32)

    block_pieces = BLOCK // PIECE
    zero_row = 3 * leaf_count * 64
    place_shape = (PLAN_PLACES, leaf_count)
    place_row = iota(place_shape, 0)
    listed = jnp.full(place_shape, zero_row, jnp.int32)
    offset = jnp.zeros((1, leaf_count), jnp.int32)
    for slot in range(slot_count):
        side = 1 if slot == 0 else (0 if slot < 9 else (1 if slot < 18 else 2))
        ids = ulist_ref[slot : slot + 1, :]
        place = jnp.where(ids >= 0, ids - (index + (side - 1)) * leaf_count, 0)
        found = jnp.sum(jnp.where(row == place, tables[side], 0.0), axis=0, keepdims=True).astype(jnp.int32)
        length = lax.shift_right_logical(found + (PIECE - 1), PIECE.bit_length() - 1)
        length = jnp.where(ids >= 0, length, 0)
        start = (place + (1, 0, 2)[side] * leaf_count) * 64
        inside = (place_row >= offset) & (place_row < offset + length)
        listed = jnp.where(inside, start + (place_row - offset) * 32, listed)
        offset = offset + length
    plan_ref[:PLAN_PLACES, :leaf_count] = listed
    plan_ref[:PLAN_PLACES, leaf_count:] = jnp.full((PLAN_PLACES, 128 - leaf_count), zero_row, jnp.int32)

    blocks = lax.shift_right_logical(offset + (block_pieces - 1), block_pieces.bit_length() - 1)
    blocks_column = as_column(blocks.astype(F32))
    own_class = lax.shift_right_logical(counts[1].astype(jnp.int32) - 1, 5)
    class_column = as_column(own_class.astype(F32)).astype(jnp.int32)
    earlier = (class_column == jnp.broadcast_to(own_class, shape)) & (rank_column < rank_wide)
    first = jnp.sum(jnp.where(earlier, blocks_column, 0.0), axis=0, keepdims=True).astype(jnp.int32)
    lane = iota((1, 128), 1)
    steps_line = jnp.zeros((1, 128), jnp.int32)
    start = jnp.ones((1, 1), jnp.int32)
    for number in range(len(CLASS_ROWS)):
        inside = jnp.where(own_class == number, blocks.astype(F32), 0.0)
        items = jnp.sum(inside, axis=1, keepdims=True).astype(jnp.int32)
        steps = lax.shift_right_logical(items + (2 * UNROLL - 1), UNROLL.bit_length() - 1)
        steps = jnp.where(items > 0, steps, 0)
        first = first + jnp.where(own_class == number, start * UNROLL, 0)
        steps_line = jnp.where(lane == 2 * number, start, jnp.where(lane == 2 * number + 1, steps, steps_line))
        start = start + steps
    plan_ref[PLAN_CLASS : PLAN_CLASS + 1, :] = steps_line

    first_column = as_column(first.astype(F32))
    wide = (leaf_count, 128)
    first_wide = jnp.concatenate([first_column] * (128 // leaf_count), axis=1).astype(jnp.int32)
    blocks_wide = jnp.concatenate([blocks_column] * (128 // leaf_count), axis=1).astype(jnp.int32)
    leaf_row = iota(wide, 0).astype(F32)
    for line in range(8):
        after = iota(wide, 1) + 128 * line - first_wide
        inside = (after >= 0) & (after < blocks_wide)
        leaf = jnp.sum(jnp.where(inside, leaf_row - leaf_count, 0.0), axis=0, keepdims=True)
        place = jnp.sum(jnp.where(inside, (after * block_pieces).astype(F32), 0.0), axis=0, keepdims=True)
        item_ref[line : line + 1, :] = leaf.astype(jnp.int32) + leaf_count
        item_ref[8 + line : 9 + line, :] = place.astype(jnp.int32)

    order = jnp.sum(jnp.where(rank_column == column, row.astype(F32), 0.0), axis=0, keepdims=True)
    plan_ref[PLAN_ORDER : PLAN_ORDER + 1, :leaf_count] = order.astype(jnp.int32)
    plan_ref[PLAN_COUNT : PLAN_COUNT + 1, :leaf_count] = counts[1].astype(jnp.int32)


def pack_kernel(
    lower_ref, upper_ref, ulist_ref, own_counts_ref, sum_ref, pair_ref, shift_ref, pack_ref, feature_ref, plan_ref,
    item_ref, top_ref, next_ref
):
    leaf_count, rows, p_width = lower_ref.shape
    q_width = rows - 8
    index = lax.axis_index("oct")
    top = sum_ref[...] + pair_ref[...]
    top_ref[...] = top
    next_ref[...] = dot3(top, shift_ref[jnp.right_shift(index, 3) & 7])
    lane = iota((1, leaf_count), 1)
    blank = jnp.zeros((32, p_width), F32)

    def pack_step(step, counts):
        side_counts = list(counts)
        for part in range(4):
            leaf = step * 4 + part
            for side, source in enumerate((lower_ref, upper_ref)):
                tail = source[leaf, q_width:, :]
                place = side * leaf_count + leaf
                weights = weight_rows(source[leaf, :q_width, :])
                packed = jnp.concatenate([blank] + weights + [blank], axis=0).astype(BF16).T
                pack_ref[pl.ds(pl.multiple_of(place * p_width, p_width), p_width), :] = packed
                put_features(feature_ref, place, right_rows(pieces(tail)))
                side_counts[side] = jnp.where(lane == leaf, tail[3:4, :leaf_count], side_counts[side])
        return tuple(side_counts)

    nothing = jnp.zeros((1, leaf_count), F32)
    lower_counts, upper_counts = lax.fori_loop(0, leaf_count // 4, pack_step, (nothing, nothing))
    plan_of(ulist_ref, (lower_counts, own_counts_ref[...].astype(F32), upper_counts), plan_ref, item_ref)


def final_kernel(
    level_count, counts_ref, feature_ref, turned_ref, near_ref, far_ref, coarse_ref, shift_ref, down_ref, *rest
):
    top_refs, (out_ref, node_ref, down_leaf_ref) = rest[:level_count], rest[level_count:]
    leaf_count, q_width, p_width = out_ref.shape
    eq_width = far_ref.shape[1]
    node_count = leaf_count // 8
    index = lax.axis_index("oct")
    slab_local = jnp.zeros((q_width, eq_width), F32)
    for level, top_ref in enumerate(top_refs):
        slab_local = slab_local + dot3(top_ref[...], coarse_ref[jnp.right_shift(index, 3 * level) & 7])
    for node in range(node_count):
        rows = slice(node * q_width, (node + 1) * q_width)
        node_ref[rows, :] = far_ref[rows, :] + dot3(slab_local, shift_ref[node])

    for child in range(8):
        down_leaf_ref[child] = dot3(dot3(node_ref[...], shift_ref[child]), down_ref[...])
    lane = iota((q_width, p_width), 1)

    def node_step(node, carry):
        for child in range(8):
            leaf = node * 8 + child
            starts = [pl.multiple_of((2 * leaf + half) * 32, 32) for half in range(2)]
            features = feature_ref[0, pl.ds(starts[0], 32), :] + feature_ref[1, pl.ds(starts[1], 32), :]
            values_high, values_low = halves(jnp.exp2(dot(turned_ref[leaf], features)))
            down = weight_rows(down_leaf_ref[child, pl.ds(pl.multiple_of(node * q_width, q_width), q_width), :])
            both = dot(jnp.concatenate(down, axis=0).astype(BF16), values_high)
            far = both[:q_width] + both[q_width:] + dot(down[0].astype(BF16), values_low)
            out_ref[leaf] = jnp.where(lane < counts_ref[leaf], far + near_ref[leaf], 0.0)
        return carry

    lax.fori_loop(0, node_count, node_step, 0)


def shifted(value, size):
    up = [(i, i + 1) for i in range(size - 1)]
    down = [(j, i) for i, j in up]
    return lax.ppermute(value, "oct", up), lax.ppermute(value, "oct", down)


def swapped(value, size, bit):
    return lax.ppermute(value, "oct", [(source, source ^ (1 << bit)) for source in range(size)])


def local(
    points,
    dens,
    surface,
    counts,
    ulist,
    vlist,
    up_inverse,
    down_inverse,
    shift_up,
    shift_down,
    coarse,
    translate,
):
    leaf_count, q_width, p_width = dens.shape
    eq_width = surface.shape[2]
    node_count, type_count = vlist.shape
    node_rows = node_count * q_width
    size = lax.axis_size("oct")
    bits = size.bit_length() - 1
    index = lax.axis_index("oct")
    vmem = pl.BlockSpec(memory_space=pltpu.VMEM)
    smem = pl.BlockSpec(memory_space=pltpu.SMEM)
    hbm = pl.BlockSpec(memory_space=pl.ANY)
    params = grant(56)
    points = jnp.transpose(points, (1, 0, 2))
    surface = jnp.transpose(surface, (1, 0, 2))
    ulist = ulist.T
    table = jnp.transpose(translate, (1, 2, 0))

    pack, features, turned, message, send, slab = pl.pallas_call(
        upward_kernel,
        out_shape=(
            jax.ShapeDtypeStruct((leaf_count * p_width, 128), BF16),
            jax.ShapeDtypeStruct((2, leaf_count * 64, p_width), BF16),
            jax.ShapeDtypeStruct((leaf_count, eq_width, 32), BF16),
            jax.ShapeDtypeStruct((leaf_count, q_width + 8, p_width), F32),
            jax.ShapeDtypeStruct((node_rows + 3 * q_width, eq_width), BF16),
            jax.ShapeDtypeStruct((q_width, eq_width), F32),
        ),
        in_specs=[vmem, vmem, vmem, smem, vmem, vmem],
        out_specs=(vmem,) * 6,
        scratch_shapes=[pltpu.VMEM((8, node_rows, eq_width), F32)],
        compiler_params=params,
        name="upward",
    )(points, dens, surface, counts, up_inverse, shift_up)

    send_lower, send_upper = shifted(send, size)
    partner = jnp.where(index & 1 == 1, send_lower[node_rows:], send_upper[node_rows:]).astype(F32)
    total = slab + (partner[:q_width] + partner[q_width : 2 * q_width] + partner[2 * q_width :])
    message, total = lax.optimization_barrier((message, total))
    lower, upper = shifted(message, size)
    total = total + swapped(total, size, 1)
    pair = swapped(total, size, 2)
    send_lower, total = lax.optimization_barrier((send_lower, total))

    table = table.reshape(eq_width * eq_width, type_count)
    far_node = pl.pallas_call(
        far_kernel,
        out_shape=jax.ShapeDtypeStruct((node_rows, eq_width), F32),
        in_specs=[vmem, vmem, vmem, vmem, hbm],
        out_specs=vmem,
        scratch_shapes=[
            pltpu.VMEM((type_count // 128, eq_width * eq_width, 128), BF16),
            pltpu.VMEM((eq_width * eq_width, type_count % 128), BF16),
            pltpu.VMEM((eq_width * SOURCES, 128), F32),
            pltpu.VMEM((eq_width, node_rows), F32),
            pltpu.SemaphoreType.DMA((eq_width // 8, type_count // 128 + 1)),
        ],
        compiler_params=params,
        cost_estimate=pl.CostEstimate(flops=2 * 10**10, bytes_accessed=18 * 10**6, transcendentals=0),
        name="far",
    )(send_lower, send, send_upper, vlist, table)
    far_node, lower, upper = lax.optimization_barrier((far_node, lower, upper))

    side_pack, side_features, plan, items, top, current = pl.pallas_call(
        pack_kernel,
        out_shape=(
            jax.ShapeDtypeStruct((2 * leaf_count * p_width, 128), BF16),
            jax.ShapeDtypeStruct((2, 2 * leaf_count * 64, p_width), BF16),
            jax.ShapeDtypeStruct((64, 128), jnp.int32),
            jax.ShapeDtypeStruct((16, 128), jnp.int32),
            jax.ShapeDtypeStruct((q_width, eq_width), F32),
            jax.ShapeDtypeStruct((q_width, eq_width), F32),
        ),
        in_specs=[vmem] * 7,
        out_specs=(vmem,) * 6,
        compiler_params=params,
        name="pack",
    )(lower, upper, ulist, counts.reshape(1, leaf_count), total, pair, shift_up)

    tops = [top]
    for level in range(3, bits, 3):
        if level > 3:
            current = jnp.dot(current, shift_up[jnp.right_shift(index, level) & 7], precision=HIGHEST)
        for bit in range(level, min(level + 3, bits)):
            current = current + swapped(current, size, bit)
        tops.append(current)

    near = pl.pallas_call(
        near_kernel,
        out_shape=jax.ShapeDtypeStruct((leaf_count, q_width, p_width), F32),
        in_specs=[smem, smem, hbm, hbm, hbm, hbm],
        out_specs=vmem,
        scratch_shapes=[
            pltpu.VMEM((3 * leaf_count * p_width + PIECE, 128), BF16),
            pltpu.VMEM((2, 3 * leaf_count * 64 + 32, 128), BF16),
            pltpu.VMEM((2 * UNROLL, 2, p_width, 128), BF16),
            pltpu.VMEM((leaf_count + 1, p_width, 128), F32),
            pltpu.SemaphoreType.DMA((4,)),
        ],
        compiler_params=params,
        cost_estimate=pl.CostEstimate(flops=3 * 10**10, bytes_accessed=10**7, transcendentals=0),
        name="near",
    )(plan, items, pack, side_pack, features, side_features)

    return pl.pallas_call(
        lambda *refs: final_kernel(len(tops), *refs),
        out_shape=jax.ShapeDtypeStruct((leaf_count, q_width, p_width), F32),
        in_specs=[smem] + [vmem] * (7 + len(tops)),
        out_specs=vmem,
        scratch_shapes=[
            pltpu.VMEM((node_rows, eq_width), F32),
            pltpu.VMEM((8, node_rows, eq_width), F32),
        ],
        compiler_params=params,
        name="final",
    )(counts, features, turned, near, far_node, coarse, shift_down, down_inverse, *tops)


def solution(mesh):
    placed = (
        P("oct", None, None),
        P("oct", None, None),
        P("oct", None, None),
        P("oct"),
        P("oct", None),
        P("oct", None),
        P(),
        P(),
        P(),
        P(),
        P(),
        P(),
    )
    return jax.shard_map(
        local, mesh=mesh, in_specs=placed, out_specs=P("oct", None, None), check_vma=False
    )
```

```python
import math

import jax
import jax.numpy as jnp
from jax import lax
from jax.experimental import pallas as pl
from jax.experimental.pallas import tpu as pltpu
from jax.sharding import PartitionSpec as P

F32 = jnp.float32
BF16 = jnp.bfloat16
HIGHEST = lax.Precision.HIGHEST
SCALE = math.sqrt(math.log2(math.e))
NT = (((1,), (1,)), ((), ()))
TN = (((0,), (0,)), ((), ()))
BLOCK = 256
UNROLL = 4
PIECE = 64
CLASS_ROWS = (32, 64, 96, 128)
PLAN_PLACES, PLAN_CLASS, PLAN_ORDER, PLAN_COUNT = 56, 60, 61, 62
SOURCES = 32
CHUNK = 4


def dot(left, right):
    return jnp.dot(left, right, preferred_element_type=F32)


def dot_nt(left, right):
    return lax.dot_general(left, right, NT, preferred_element_type=F32)


def dot_tn(left, right):
    return lax.dot_general(left, right, TN, preferred_element_type=F32)


def halves(value):
    high = value.astype(BF16)
    low = (value - high.astype(F32)).astype(BF16)
    return high, low


def dot3(left, right):
    left_high, left_low = halves(left)
    right_high, right_low = halves(right)
    return dot(left_high, right_high) + dot(left_high, right_low) + dot(left_low, right_high)


def grant(mebibytes):
    return pltpu.CompilerParams(vmem_limit_bytes=mebibytes * 1024 * 1024)


def iota(shape, dim):
    return lax.broadcasted_iota(jnp.int32, shape, dim)


def coords_of(ref, leaf):
    width = ref.shape[2]
    row = iota((8, width), 0)
    value = jnp.zeros((8, width), F32)
    for dim in range(3):
        line = jnp.broadcast_to(ref[dim, pl.ds(leaf, 1), :], (8, width))
        value = jnp.where(row == dim, line, value)
    return value


def pieces(coords):
    row = iota(coords.shape, 0)
    used = row < 3
    scaled = jnp.where(used, coords, 0.0) * SCALE
    high = scaled.astype(BF16).astype(F32)
    rest = scaled - high
    mid = rest.astype(BF16).astype(F32)
    low = (rest - mid).astype(BF16).astype(F32)
    norm = -0.5 * jnp.sum(scaled * scaled, axis=0, keepdims=True)
    norm_high = norm.astype(BF16).astype(F32)
    norm_rest = norm - norm_high
    norm_mid = norm_rest.astype(BF16).astype(F32)
    norm_low = norm_rest - norm_mid
    norms = jnp.where(row == 0, norm_high, jnp.where(row == 1, norm_mid, jnp.where(row == 2, norm_low, 0.0)))
    ones = jnp.where(used, 1.0, 0.0)
    return high, mid, low, norms, ones


def paired(first, second):
    return first + pltpu.roll(second, 4, 0)


def left_rows(parts):
    high, mid, low, norms, ones = parts
    return jnp.concatenate([paired(high, high), paired(mid, mid), paired(high, low), paired(ones, norms)], axis=0)


def right_rows(parts):
    high, mid, low, norms, ones = parts
    both = paired(high, mid)
    return jnp.concatenate([both, both, paired(low, high), paired(norms, ones)], axis=0)


def weight_rows(weights):
    high = weights.astype(BF16).astype(F32)
    return [high, weights - high]


def feature_versions(rows):
    lower = iota(rows.shape, 1) < PIECE
    versions = []
    for half in range(2):
        alone = jnp.where(lower == (half == 0), rows, 0.0)
        versions.append((half, half, alone.astype(BF16)))
        versions.append((half, 1 - half, pltpu.roll(alone, PIECE, 1).astype(BF16)))
    return versions


def put_features(feature_ref, leaf, versions):
    for half, place, value in versions:
        span = pl.ds(pl.multiple_of((2 * leaf + half) * 32, 32), 32)
        feature_ref[place, span, :] = value


def upward_kernel(
    points_ref, dens_ref, surface_ref, counts_ref, up_ref, shift_ref, pack_ref, feature_ref, turned_ref,
    message_ref, send_ref, slab_ref, check_ref
):
    leaf_count, q_width, p_width = dens_ref.shape
    eq_width = surface_ref.shape[2]
    node_count = leaf_count // 8
    lane = iota((q_width, p_width), 1)
    row = iota((8, p_width), 0)

    def node_step(node, carry):
        leaves = [node * 8 + child for child in range(8)]
        counts = [counts_ref[leaf] for leaf in leaves]
        weights = [jnp.where(lane < count, dens_ref[leaf], 0.0) for leaf, count in zip(leaves, counts)]
        coords = [coords_of(points_ref, leaf) for leaf in leaves]
        surfaces = [left_rows(pieces(coords_of(surface_ref, leaf))) for leaf in leaves]
        parts = [pieces(value) for value in coords]
        rights = [right_rows(value) for value in parts]
        lists = [weight_rows(value) for value in weights]
        packs = [
            jnp.concatenate([left_rows(part)] + split + [right], axis=0).astype(BF16).T
            for part, split, right in zip(parts, lists, rights)
        ]
        blank = jnp.zeros((96, eq_width), F32)
        wides = [jnp.concatenate([blank, value], axis=0).astype(BF16) for value in surfaces]
        exponents = [dot(pack, wide) for pack, wide in zip(packs, wides)]
        values = [halves(jnp.exp2(value)) for value in exponents]
        rows = [jnp.concatenate(split, axis=0).astype(BF16) for split in lists]
        firsts = [dot(row, value[0]) for row, value in zip(rows, values)]
        seconds = [dot(row[:q_width], value[1]) for row, value in zip(rows, values)]
        turned = [value.astype(BF16).T for value in surfaces]
        versions = [feature_versions(right) for right in rights]
        for child, leaf in enumerate(leaves):
            message_ref[leaf, :q_width, :] = weights[child]
            message_ref[leaf, q_width:, :] = jnp.where(row == 3, counts[child].astype(F32), coords[child])
            pack_ref[pl.ds(pl.multiple_of(leaf * p_width, p_width), p_width), :] = packs[child]
            turned_ref[leaf] = turned[child]
            put_features(feature_ref, leaf, versions[child])
            check = firsts[child][:q_width] + firsts[child][q_width:] + seconds[child]
            check_ref[child, pl.ds(pl.multiple_of(node * q_width, q_width), q_width), :] = check
        return carry

    lax.fori_loop(0, node_count, node_step, 0)

    node_eq = jnp.zeros((node_count * q_width, eq_width), F32)
    for child in range(8):
        node_eq = node_eq + dot3(dot3(check_ref[child], up_ref[...]), shift_ref[child])
    send_ref[: node_count * q_width, :] = node_eq.astype(BF16)
    slab_eq = jnp.zeros((q_width, eq_width), F32)
    for child in range(8):
        slab_eq = slab_eq + dot3(node_eq[child * q_width : (child + 1) * q_width], shift_ref[child])
    index = lax.axis_index("oct")
    slab = dot3(slab_eq, shift_ref[index & 7])
    slab_ref[...] = slab
    high, rest = halves(slab)
    low = (slab - high.astype(F32) - rest.astype(F32)).astype(BF16)
    for place, part in enumerate((high, rest, low)):
        start = node_count * q_width + place * q_width
        send_ref[start : start + q_width, :] = part


def far_kernel(
    lower_ref, own_ref, upper_ref, vlist_ref, table_hbm, out_ref, table_ref, tail_ref, wide_ref, total_ref, first_ref, sems
):
    node_count, type_count = vlist_ref.shape
    eq_width = own_ref.shape[1]
    q_width = out_ref.shape[0] // node_count
    lanes = node_count * q_width
    tile = 128 // q_width
    chunk = CHUNK
    chunk_rows = chunk * eq_width
    chunk_count = eq_width // chunk
    full = type_count // 128

    def copies_of(number):
        span = pl.ds(number * chunk_rows, chunk_rows)
        copies = []
        for part in range(full):
            source = table_hbm.at[span, pl.ds(part * 128, 128)]
            copies.append(pltpu.make_async_copy(source, table_ref.at[part, span], sems.at[number, part]))
        source = table_hbm.at[span, pl.ds(full * 128, type_count - full * 128)]
        copies.append(pltpu.make_async_copy(source, tail_ref.at[span], sems.at[number, full]))
        return copies

    for number in range(chunk_count):
        for copy in copies_of(number):
            copy.start()

    index = lax.axis_index("oct")
    repeat = (iota((q_width, 128), 1) % q_width == iota((q_width, 128), 0)).astype(BF16)
    for part, source in enumerate((lower_ref, own_ref, upper_ref)):
        for node in range(node_count):
            spread = dot_tn(source[node * q_width : (node + 1) * q_width, :], repeat)
            wide_ref[pl.ds(part * node_count + node, eq_width, stride=SOURCES), :] = spread
    for place in range(3 * node_count, SOURCES):
        wide_ref[pl.ds(place, eq_width, stride=SOURCES), :] = jnp.zeros((eq_width, 128), F32)

    ids = vlist_ref[...]
    places = jnp.where(ids >= 0, ids - (index - 1) * node_count, -1).astype(F32).astype(BF16)
    spread = (iota((node_count, lanes), 1) // SOURCES == iota((node_count, lanes), 0)).astype(BF16)
    wanted = dot_tn(places, spread)
    chosen = (wanted == (iota((type_count, lanes), 1) % SOURCES).astype(F32)).astype(F32)
    chosen_full = chosen[: full * 128].astype(BF16)
    chosen_tail = chosen[full * 128 :].astype(BF16)
    lane_node = iota((SOURCES, 128), 1) // q_width
    nothing = jnp.zeros((SOURCES, 128), F32)
    total_ref[...] = jnp.zeros_like(total_ref)

    def table_of(number):
        span = pl.ds(pl.multiple_of(number * chunk_rows, chunk_rows), chunk_rows)
        left = jnp.concatenate([table_ref[part, span, :] for part in range(full)], axis=1)
        return left, tail_ref[span, :]

    def first_product(left, tail):
        return dot(left, chosen_full) + dot(tail, chosen_tail)

    def second_product(number, summed):
        lefts, rights = [], []
        for step in range(chunk):
            value = summed[step * eq_width : (step + 1) * eq_width]
            high = value.astype(BF16).astype(F32)
            lefts.append(jnp.concatenate([high, value - high], axis=0).astype(BF16))
            row = number * chunk + step
            sent = wide_ref[pl.ds(pl.multiple_of(row * SOURCES, SOURCES), SOURCES), :]
            parts = [jnp.where(lane_node == place, sent, 0.0) for place in range(tile)]
            for node in range(node_count):
                line = [parts[node % tile] if place == node // tile else nothing for place in range(node_count // tile)]
                rights.append(jnp.concatenate(line, axis=1))
        product = dot(jnp.concatenate(lefts, axis=1), jnp.concatenate(rights, axis=0).astype(BF16))
        return product[:eq_width] + product[eq_width:]

    def wait_for(number):
        for copy in copies_of(number):
            copy.wait()

    wait_for(0)
    first_ref[...] = first_product(*table_of(0))

    def pair_step(pair, carry):
        number = 2 * pair
        wait_for(number + 1)
        pl.when(pair < chunk_count // 2 - 1)(lambda: wait_for(number + 2))
        ahead = table_of(number + 1)
        behind = table_of(jnp.minimum(number + 2, chunk_count - 1))
        summed = first_ref[...]
        middle = first_product(*ahead)
        total = second_product(number, summed)
        following = first_product(*behind)
        total = total + second_product(number + 1, middle)
        first_ref[...] = following
        total_ref[...] += total
        return carry

    lax.fori_loop(0, chunk_count // 2, pair_step, 0)
    out_ref[...] = total_ref[...].T


def near_kernel(
    plan_ref, item_ref, own_hbm, side_hbm, own_feature_hbm, side_feature_hbm, out_ref, pack_ref, feature_ref,
    value_ref, total_ref, sems
):
    leaf_count, q_width, p_width = out_ref.shape
    own_rows, side_rows = own_hbm.shape[0], side_hbm.shape[0]
    own_lines, side_lines = own_feature_hbm.shape[1], side_feature_hbm.shape[1]
    copies = [
        (own_hbm, pack_ref.at[pl.ds(0, own_rows)]),
        (side_hbm, pack_ref.at[pl.ds(own_rows, side_rows)]),
        (own_feature_hbm, feature_ref.at[:, pl.ds(0, own_lines)]),
        (side_feature_hbm, feature_ref.at[:, pl.ds(own_lines, side_lines)]),
    ]
    copies = [pltpu.make_async_copy(source, target, sems.at[n]) for n, (source, target) in enumerate(copies)]
    for copy in copies:
        copy.start()
    pack_ref[own_rows + side_rows :, :] = jnp.zeros((PIECE, 128), BF16)
    feature_ref[:, own_lines + side_lines :, :] = jnp.zeros((2, 32, 128), BF16)
    total_ref[...] = jnp.zeros_like(total_ref)
    for copy in copies:
        copy.wait()
    step_lanes = 128 // UNROLL
    shift = step_lanes.bit_length() - 1

    def item_of(step, part):
        line = lax.shift_right_logical(step, shift)
        lane = jnp.bitwise_and(step, step_lanes - 1) * UNROLL + part
        return item_ref[line, lane], item_ref[8 + line, lane]

    def sources_of(leaf, place):
        rows = []
        for number in range(BLOCK // PIECE):
            start = pl.multiple_of(plan_ref[place + number, leaf] * 2, PIECE)
            rows.append(pack_ref[pl.ds(start, PIECE), :])
        return jnp.concatenate(rows, axis=0)

    def features_of(leaf, place):
        tiles = []
        for tile in range(BLOCK // 128):
            starts = [pl.multiple_of(plan_ref[place + 2 * tile + half, leaf], 32) for half in range(2)]
            halves_of = [feature_ref[half, pl.ds(start, 32), :] for half, start in enumerate(starts)]
            tiles.append(halves_of[0] + halves_of[1])
        return jnp.concatenate(tiles, axis=1)

    def run(rows, first, count):
        def blocks_step(step, carry):
            slot = jnp.bitwise_and(step, 1) * UNROLL
            done = [item_of(step - 1, part) for part in range(UNROLL)]
            items = [item_of(step, part) for part in range(UNROLL)]
            features = [features_of(leaf, place) for leaf, place in items]
            targets = []
            for leaf, _ in items:
                start = pl.multiple_of(jnp.minimum(leaf, leaf_count - 1) * p_width, p_width)
                targets.append(pack_ref[pl.ds(start, rows), :][:, :32])
            sources = [sources_of(leaf, place) for leaf, place in done]
            values = [
                jnp.concatenate([value_ref[UNROLL - slot + part, side, :rows] for side in range(2)], axis=1)
                for part in range(UNROLL)
            ]
            exponents = [dot(target, feature) for target, feature in zip(targets, features)]
            products = [dot(value, source) for value, source in zip(values, sources)]
            following = [jnp.exp2(value).astype(BF16) for value in exponents]
            for part, value in enumerate(following):
                for side in range(2):
                    value_ref[slot + part, side, :rows] = value[:, side * 128 : (side + 1) * 128]
            for (leaf, _), product in zip(done, products):
                total_ref[leaf, :rows] += product
            return carry

        lax.fori_loop(first, first + count, blocks_step, 0)

    for number, rows in enumerate(CLASS_ROWS):
        run(rows, plan_ref[PLAN_CLASS, 2 * number], plan_ref[PLAN_CLASS, 2 * number + 1])

    def turn_step(step, carry):
        turned = [total_ref[step * 8 + part].T for part in range(8)]
        for part, value in enumerate(turned):
            out_ref[step * 8 + part] = value[32 : 32 + q_width] + value[32 + q_width : 32 + 2 * q_width]
        return carry

    lax.fori_loop(0, leaf_count // 8, turn_step, 0)


def as_column(line):
    width = line.shape[1]
    wide = jnp.concatenate([line, jnp.zeros((1, 128 - width), F32)], axis=1) if width < 128 else line
    return jnp.broadcast_to(wide, (128, 128)).T[:width, :width]


def plan_of(ulist_ref, counts, plan_ref, item_ref):
    slot_count, leaf_count = ulist_ref.shape
    index = lax.axis_index("oct")
    shape = (leaf_count, leaf_count)
    row, column = iota(shape, 0), iota(shape, 1)
    tables = [as_column(line) for line in counts]
    own = jnp.broadcast_to(counts[1], shape)
    before = (tables[1] < own) | ((tables[1] == own) & (row < column))
    rank = jnp.sum(jnp.where(before, 1.0, 0.0), axis=0, keepdims=True)
    rank_column = as_column(rank).astype(jnp.int32)
    rank_wide = jnp.broadcast_to(rank, shape).astype(jnp.int32)

    block_pieces = BLOCK // PIECE
    zero_row = 3 * leaf_count * 64
    place_shape = (PLAN_PLACES, leaf_count)
    place_row = iota(place_shape, 0)
    listed = jnp.full(place_shape, zero_row, jnp.int32)
    offset = jnp.zeros((1, leaf_count), jnp.int32)
    for slot in range(slot_count):
        side = 1 if slot == 0 else (0 if slot < 9 else (1 if slot < 18 else 2))
        ids = ulist_ref[slot : slot + 1, :]
        place = jnp.where(ids >= 0, ids - (index + (side - 1)) * leaf_count, 0)
        found = jnp.sum(jnp.where(row == place, tables[side], 0.0), axis=0, keepdims=True).astype(jnp.int32)
        length = lax.shift_right_logical(found + (PIECE - 1), PIECE.bit_length() - 1)
        length = jnp.where(ids >= 0, length, 0)
        start = (place + (1, 0, 2)[side] * leaf_count) * 64
        inside = (place_row >= offset) & (place_row < offset + length)
        listed = jnp.where(inside, start + (place_row - offset) * 32, listed)
        offset = offset + length
    plan_ref[:PLAN_PLACES, :leaf_count] = listed
    plan_ref[:PLAN_PLACES, leaf_count:] = jnp.full((PLAN_PLACES, 128 - leaf_count), zero_row, jnp.int32)

    blocks = lax.shift_right_logical(offset + (block_pieces - 1), block_pieces.bit_length() - 1)
    blocks_column = as_column(blocks.astype(F32))
    own_class = lax.shift_right_logical(counts[1].astype(jnp.int32) - 1, 5)
    class_column = as_column(own_class.astype(F32)).astype(jnp.int32)
    earlier = (class_column == jnp.broadcast_to(own_class, shape)) & (rank_column < rank_wide)
    first = jnp.sum(jnp.where(earlier, blocks_column, 0.0), axis=0, keepdims=True).astype(jnp.int32)
    lane = iota((1, 128), 1)
    steps_line = jnp.zeros((1, 128), jnp.int32)
    start = jnp.ones((1, 1), jnp.int32)
    for number in range(len(CLASS_ROWS)):
        inside = jnp.where(own_class == number, blocks.astype(F32), 0.0)
        items = jnp.sum(inside, axis=1, keepdims=True).astype(jnp.int32)
        steps = lax.shift_right_logical(items + (2 * UNROLL - 1), UNROLL.bit_length() - 1)
        steps = jnp.where(items > 0, steps, 0)
        first = first + jnp.where(own_class == number, start * UNROLL, 0)
        steps_line = jnp.where(lane == 2 * number, start, jnp.where(lane == 2 * number + 1, steps, steps_line))
        start = start + steps
    plan_ref[PLAN_CLASS : PLAN_CLASS + 1, :] = steps_line

    first_column = as_column(first.astype(F32))
    wide = (leaf_count, 128)
    first_wide = jnp.concatenate([first_column] * (128 // leaf_count), axis=1).astype(jnp.int32)
    blocks_wide = jnp.concatenate([blocks_column] * (128 // leaf_count), axis=1).astype(jnp.int32)
    leaf_row = iota(wide, 0).astype(F32)
    for line in range(8):
        after = iota(wide, 1) + 128 * line - first_wide
        inside = (after >= 0) & (after < blocks_wide)
        leaf = jnp.sum(jnp.where(inside, leaf_row - leaf_count, 0.0), axis=0, keepdims=True)
        place = jnp.sum(jnp.where(inside, (after * block_pieces).astype(F32), 0.0), axis=0, keepdims=True)
        item_ref[line : line + 1, :] = leaf.astype(jnp.int32) + leaf_count
        item_ref[8 + line : 9 + line, :] = place.astype(jnp.int32)

    order = jnp.sum(jnp.where(rank_column == column, row.astype(F32), 0.0), axis=0, keepdims=True)
    plan_ref[PLAN_ORDER : PLAN_ORDER + 1, :leaf_count] = order.astype(jnp.int32)
    plan_ref[PLAN_COUNT : PLAN_COUNT + 1, :leaf_count] = counts[1].astype(jnp.int32)


def pack_kernel(
    lower_ref, upper_ref, ulist_ref, own_counts_ref, sum_ref, pair_ref, shift_ref, pack_ref, feature_ref, plan_ref,
    item_ref, top_ref, next_ref
):
    leaf_count, rows, p_width = lower_ref.shape
    q_width = rows - 8
    index = lax.axis_index("oct")
    top = sum_ref[...] + pair_ref[...]
    top_ref[...] = top
    next_ref[...] = dot3(top, shift_ref[jnp.right_shift(index, 3) & 7])
    lane = iota((1, leaf_count), 1)
    blank = jnp.zeros((32, p_width), F32)

    def pack_step(step, counts):
        side_counts = list(counts)
        chosen = [(step * 4 + part, side) for part in range(4) for side in range(2)]
        sources = (lower_ref, upper_ref)
        tails = [sources[side][leaf, q_width:, :] for leaf, side in chosen]
        weights = [weight_rows(sources[side][leaf, :q_width, :]) for leaf, side in chosen]
        packs = [jnp.concatenate([blank] + value + [blank], axis=0).astype(BF16).T for value in weights]
        versions = [feature_versions(right_rows(pieces(tail))) for tail in tails]
        for (leaf, side), tail, pack, version in zip(chosen, tails, packs, versions):
            place = side * leaf_count + leaf
            pack_ref[pl.ds(pl.multiple_of(place * p_width, p_width), p_width), :] = pack
            put_features(feature_ref, place, version)
            side_counts[side] = jnp.where(lane == leaf, tail[3:4, :leaf_count], side_counts[side])
        return tuple(side_counts)

    nothing = jnp.zeros((1, leaf_count), F32)
    lower_counts, upper_counts = lax.fori_loop(0, leaf_count // 4, pack_step, (nothing, nothing))
    plan_of(ulist_ref, (lower_counts, own_counts_ref[...].astype(F32), upper_counts), plan_ref, item_ref)


def final_kernel(
    level_count, counts_ref, feature_ref, turned_ref, near_ref, far_ref, coarse_ref, shift_ref, down_ref, *rest
):
    top_refs, (out_ref, node_ref, down_leaf_ref) = rest[:level_count], rest[level_count:]
    leaf_count, q_width, p_width = out_ref.shape
    eq_width = far_ref.shape[1]
    node_count = leaf_count // 8
    index = lax.axis_index("oct")
    slab_local = jnp.zeros((q_width, eq_width), F32)
    for level, top_ref in enumerate(top_refs):
        slab_local = slab_local + dot3(top_ref[...], coarse_ref[jnp.right_shift(index, 3 * level) & 7])
    for node in range(node_count):
        rows = slice(node * q_width, (node + 1) * q_width)
        node_ref[rows, :] = far_ref[rows, :] + dot3(slab_local, shift_ref[node])

    for child in range(8):
        down_leaf_ref[child] = dot3(dot3(node_ref[...], shift_ref[child]), down_ref[...])
    lane = iota((q_width, p_width), 1)

    def node_step(node, carry):
        leaves = [node * 8 + child for child in range(8)]
        features = []
        for leaf in leaves:
            starts = [pl.multiple_of((2 * leaf + half) * 32, 32) for half in range(2)]
            features.append(feature_ref[0, pl.ds(starts[0], 32), :] + feature_ref[1, pl.ds(starts[1], 32), :])
        turned = [turned_ref[leaf] for leaf in leaves]
        node_rows = pl.ds(pl.multiple_of(node * q_width, q_width), q_width)
        downs = [weight_rows(down_leaf_ref[child, node_rows, :]) for child in range(8)]
        nears = [near_ref[leaf] for leaf in leaves]
        exponents = [dot(left, right) for left, right in zip(turned, features)]
        values = [halves(jnp.exp2(value)) for value in exponents]
        firsts = [dot(jnp.concatenate(down, axis=0).astype(BF16), value[0]) for down, value in zip(downs, values)]
        seconds = [dot(down[0].astype(BF16), value[1]) for down, value in zip(downs, values)]
        for child, leaf in enumerate(leaves):
            far = firsts[child][:q_width] + firsts[child][q_width:] + seconds[child]
            out_ref[leaf] = jnp.where(lane < counts_ref[leaf], far + nears[child], 0.0)
        return carry

    lax.fori_loop(0, node_count, node_step, 0)


def shifted(value, size):
    up = [(i, i + 1) for i in range(size - 1)]
    down = [(j, i) for i, j in up]
    return lax.ppermute(value, "oct", up), lax.ppermute(value, "oct", down)


def swapped(value, size, bit):
    return lax.ppermute(value, "oct", [(source, source ^ (1 << bit)) for source in range(size)])


def local(
    points,
    dens,
    surface,
    counts,
    ulist,
    vlist,
    up_inverse,
    down_inverse,
    shift_up,
    shift_down,
    coarse,
    translate,
):
    leaf_count, q_width, p_width = dens.shape
    eq_width = surface.shape[2]
    node_count, type_count = vlist.shape
    node_rows = node_count * q_width
    size = lax.axis_size("oct")
    bits = size.bit_length() - 1
    index = lax.axis_index("oct")
    vmem = pl.BlockSpec(memory_space=pltpu.VMEM)
    smem = pl.BlockSpec(memory_space=pltpu.SMEM)
    hbm = pl.BlockSpec(memory_space=pl.ANY)
    params = grant(56)
    points = jnp.transpose(points, (1, 0, 2))
    surface = jnp.transpose(surface, (1, 0, 2))
    ulist = ulist.T
    table = jnp.transpose(translate, (1, 2, 0))

    pack, features, turned, message, send, slab = pl.pallas_call(
        upward_kernel,
        out_shape=(
            jax.ShapeDtypeStruct((leaf_count * p_width, 128), BF16),
            jax.ShapeDtypeStruct((2, leaf_count * 64, p_width), BF16),
            jax.ShapeDtypeStruct((leaf_count, eq_width, 32), BF16),
            jax.ShapeDtypeStruct((leaf_count, q_width + 8, p_width), F32),
            jax.ShapeDtypeStruct((node_rows + 3 * q_width, eq_width), BF16),
            jax.ShapeDtypeStruct((q_width, eq_width), F32),
        ),
        in_specs=[vmem, vmem, vmem, smem, vmem, vmem],
        out_specs=(vmem,) * 6,
        scratch_shapes=[pltpu.VMEM((8, node_rows, eq_width), F32)],
        compiler_params=params,
        name="upward",
    )(points, dens, surface, counts, up_inverse, shift_up)

    send_lower, send_upper = shifted(send, size)
    partner = jnp.where(index & 1 == 1, send_lower[node_rows:], send_upper[node_rows:]).astype(F32)
    total = slab + (partner[:q_width] + partner[q_width : 2 * q_width] + partner[2 * q_width :])
    message, total = lax.optimization_barrier((message, total))
    lower, upper = shifted(message, size)
    total = total + swapped(total, size, 1)
    pair = swapped(total, size, 2)
    send_lower, total = lax.optimization_barrier((send_lower, total))

    table = table.reshape(eq_width * eq_width, type_count)
    far_node = pl.pallas_call(
        far_kernel,
        out_shape=jax.ShapeDtypeStruct((node_rows, eq_width), F32),
        in_specs=[vmem, vmem, vmem, vmem, hbm],
        out_specs=vmem,
        scratch_shapes=[
            pltpu.VMEM((type_count // 128, eq_width * eq_width, 128), BF16),
            pltpu.VMEM((eq_width * eq_width, type_count % 128), BF16),
            pltpu.VMEM((eq_width * SOURCES, 128), F32),
            pltpu.VMEM((eq_width, node_rows), F32),
            pltpu.VMEM((CHUNK * eq_width, node_rows), F32),
            pltpu.SemaphoreType.DMA((eq_width // CHUNK, type_count // 128 + 1)),
        ],
        compiler_params=params,
        cost_estimate=pl.CostEstimate(flops=2 * 10**10, bytes_accessed=18 * 10**6, transcendentals=0),
        name="far",
    )(send_lower, send, send_upper, vlist, table)
    far_node, lower, upper = lax.optimization_barrier((far_node, lower, upper))

    side_pack, side_features, plan, items, top, current = pl.pallas_call(
        pack_kernel,
        out_shape=(
            jax.ShapeDtypeStruct((2 * leaf_count * p_width, 128), BF16),
            jax.ShapeDtypeStruct((2, 2 * leaf_count * 64, p_width), BF16),
            jax.ShapeDtypeStruct((64, 128), jnp.int32),
            jax.ShapeDtypeStruct((16, 128), jnp.int32),
            jax.ShapeDtypeStruct((q_width, eq_width), F32),
            jax.ShapeDtypeStruct((q_width, eq_width), F32),
        ),
        in_specs=[vmem] * 7,
        out_specs=(vmem,) * 6,
        compiler_params=params,
        name="pack",
    )(lower, upper, ulist, counts.reshape(1, leaf_count), total, pair, shift_up)

    tops = [top]
    for level in range(3, bits, 3):
        if level > 3:
            current = jnp.dot(current, shift_up[jnp.right_shift(index, level) & 7], precision=HIGHEST)
        for bit in range(level, min(level + 3, bits)):
            current = current + swapped(current, size, bit)
        tops.append(current)

    near = pl.pallas_call(
        near_kernel,
        out_shape=jax.ShapeDtypeStruct((leaf_count, q_width, p_width), F32),
        in_specs=[smem, smem, hbm, hbm, hbm, hbm],
        out_specs=vmem,
        scratch_shapes=[
            pltpu.VMEM((3 * leaf_count * p_width + PIECE, 128), BF16),
            pltpu.VMEM((2, 3 * leaf_count * 64 + 32, 128), BF16),
            pltpu.VMEM((2 * UNROLL, 2, p_width, 128), BF16),
            pltpu.VMEM((leaf_count + 1, p_width, 128), F32),
            pltpu.SemaphoreType.DMA((4,)),
        ],
        compiler_params=params,
        cost_estimate=pl.CostEstimate(flops=3 * 10**10, bytes_accessed=10**7, transcendentals=0),
        name="near",
    )(plan, items, pack, side_pack, features, side_features)

    return pl.pallas_call(
        lambda *refs: final_kernel(len(tops), *refs),
        out_shape=jax.ShapeDtypeStruct((leaf_count, q_width, p_width), F32),
        in_specs=[smem] + [vmem] * (7 + len(tops)),
        out_specs=vmem,
        scratch_shapes=[
            pltpu.VMEM((node_rows, eq_width), F32),
            pltpu.VMEM((8, node_rows, eq_width), F32),
        ],
        compiler_params=params,
        name="final",
    )(counts, features, turned, near, far_node, coarse, shift_down, down_inverse, *tops)


def solution(mesh):
    placed = (
        P("oct", None, None),
        P("oct", None, None),
        P("oct", None, None),
        P("oct"),
        P("oct", None),
        P("oct", None),
        P(),
        P(),
        P(),
        P(),
        P(),
        P(),
    )
    return jax.shard_map(
        local, mesh=mesh, in_specs=placed, out_specs=P("oct", None, None), check_vma=False
    )
```

```python
import math

import jax
import jax.numpy as jnp
from jax import lax
from jax.experimental import pallas as pl
from jax.experimental.pallas import tpu as pltpu
from jax.sharding import PartitionSpec as P

F32 = jnp.float32
BF16 = jnp.bfloat16
HIGHEST = lax.Precision.HIGHEST
SCALE = math.sqrt(math.log2(math.e))
NT = (((1,), (1,)), ((), ()))
TN = (((0,), (0,)), ((), ()))
BLOCK = 256
UNROLL = 4
PIECE = 64
CLASS_ROWS = (32, 64, 96, 128)
PLAN_PLACES, PLAN_CLASS, PLAN_ORDER, PLAN_COUNT = 56, 60, 61, 62
SOURCES = 32
CHUNK = 4


def dot(left, right):
    return jnp.dot(left, right, preferred_element_type=F32)


def dot_nt(left, right):
    return lax.dot_general(left, right, NT, preferred_element_type=F32)


def dot_tn(left, right):
    return lax.dot_general(left, right, TN, preferred_element_type=F32)


def halves(value):
    high = value.astype(BF16)
    low = (value - high.astype(F32)).astype(BF16)
    return high, low


def dot3(left, right):
    left_high, left_low = halves(left)
    right_high, right_low = halves(right)
    return dot(left_high, right_high) + dot(left_high, right_low) + dot(left_low, right_high)


def grant(mebibytes):
    return pltpu.CompilerParams(vmem_limit_bytes=mebibytes * 1024 * 1024)


def iota(shape, dim):
    return lax.broadcasted_iota(jnp.int32, shape, dim)


def coords_of(ref, leaf):
    width = ref.shape[2]
    row = iota((8, width), 0)
    value = jnp.zeros((8, width), F32)
    for dim in range(3):
        line = jnp.broadcast_to(ref[dim, pl.ds(leaf, 1), :], (8, width))
        value = jnp.where(row == dim, line, value)
    return value


def pieces(coords):
    row = iota(coords.shape, 0)
    used = row < 3
    scaled = jnp.where(used, coords, 0.0) * SCALE
    high = scaled.astype(BF16).astype(F32)
    rest = scaled - high
    mid = rest.astype(BF16).astype(F32)
    low = (rest - mid).astype(BF16).astype(F32)
    norm = -0.5 * jnp.sum(scaled * scaled, axis=0, keepdims=True)
    norm_high = norm.astype(BF16).astype(F32)
    norm_rest = norm - norm_high
    norm_mid = norm_rest.astype(BF16).astype(F32)
    norm_low = norm_rest - norm_mid
    norms = jnp.where(row == 0, norm_high, jnp.where(row == 1, norm_mid, jnp.where(row == 2, norm_low, 0.0)))
    ones = jnp.where(used, 1.0, 0.0)
    return high, mid, low, norms, ones


def paired(first, second):
    return first + pltpu.roll(second, 4, 0)


def left_rows(parts):
    high, mid, low, norms, ones = parts
    return jnp.concatenate([paired(high, high), paired(mid, mid), paired(high, low), paired(ones, norms)], axis=0)


def right_rows(parts):
    high, mid, low, norms, ones = parts
    both = paired(high, mid)
    return jnp.concatenate([both, both, paired(low, high), paired(norms, ones)], axis=0)


def weight_rows(weights):
    high = weights.astype(BF16).astype(F32)
    return [high, weights - high]


def feature_versions(rows):
    lower = iota(rows.shape, 1) < PIECE
    versions = []
    for half in range(2):
        alone = jnp.where(lower == (half == 0), rows, 0.0)
        versions.append((half, half, alone.astype(BF16)))
        versions.append((half, 1 - half, pltpu.roll(alone, PIECE, 1).astype(BF16)))
    return versions


def put_features(feature_ref, leaf, versions):
    for half, place, value in versions:
        span = pl.ds(pl.multiple_of((2 * leaf + half) * 32, 32), 32)
        feature_ref[place, span, :] = value


def upward_kernel(
    level_count, points_ref, dens_ref, surface_ref, counts_ref, count_line_ref, up_ref, shift_ref, pack_ref, feature_ref, turned_ref,
    message_ref, send_ref, slab_ref, check_ref
):
    leaf_count, q_width, p_width = dens_ref.shape
    eq_width = surface_ref.shape[2]
    node_count = leaf_count // 8
    lane = iota((q_width, p_width), 1)
    row = iota((8, p_width), 0)

    def node_step(node, carry):
        leaves = [node * 8 + child for child in range(8)]
        counts = [counts_ref[leaf] for leaf in leaves]
        weights = [jnp.where(lane < count, dens_ref[leaf], 0.0) for leaf, count in zip(leaves, counts)]
        coords = [coords_of(points_ref, leaf) for leaf in leaves]
        surfaces = [left_rows(pieces(coords_of(surface_ref, leaf))) for leaf in leaves]
        parts = [pieces(value) for value in coords]
        rights = [right_rows(value) for value in parts]
        lists = [weight_rows(value) for value in weights]
        packs = [
            jnp.concatenate([left_rows(part)] + split + [right], axis=0).astype(BF16).T
            for part, split, right in zip(parts, lists, rights)
        ]
        blank = jnp.zeros((96, eq_width), F32)
        wides = [jnp.concatenate([blank, value], axis=0).astype(BF16) for value in surfaces]
        exponents = [dot(pack, wide) for pack, wide in zip(packs, wides)]
        values = [halves(jnp.exp2(value)) for value in exponents]
        rows = [jnp.concatenate(split, axis=0).astype(BF16) for split in lists]
        firsts = [dot(row, value[0]) for row, value in zip(rows, values)]
        seconds = [dot(row[:q_width], value[1]) for row, value in zip(rows, values)]
        turned = [value.astype(BF16).T for value in surfaces]
        versions = [feature_versions(right) for right in rights]
        for child, leaf in enumerate(leaves):
            message_ref[leaf, :q_width, :] = weights[child]
            message_ref[leaf, q_width:, :] = jnp.where(row == 3, counts[child].astype(F32), coords[child])
            pack_ref[pl.ds(pl.multiple_of(leaf * p_width, p_width), p_width), :] = packs[child]
            turned_ref[leaf] = turned[child]
            put_features(feature_ref, leaf, versions[child])
            check = firsts[child][:q_width] + firsts[child][q_width:] + seconds[child]
            check_ref[child, pl.ds(pl.multiple_of(node * q_width, q_width), q_width), :] = check
        return carry

    lax.fori_loop(0, node_count, node_step, 0)

    node_eq = jnp.zeros((node_count * q_width, eq_width), F32)
    for child in range(8):
        node_eq = node_eq + dot3(dot3(check_ref[child], up_ref[...]), shift_ref[child])
    send_ref[: node_count * q_width, :] = node_eq.astype(BF16)
    slab_eq = jnp.zeros((q_width, eq_width), F32)
    for child in range(8):
        slab_eq = slab_eq + dot3(node_eq[child * q_width : (child + 1) * q_width], shift_ref[child])
    index = lax.axis_index("oct")
    slab = slab_eq
    start = node_count * q_width
    for level in range(level_count):
        slab = dot3(slab, shift_ref[jnp.right_shift(index, 3 * level) & 7])
        slab_ref[level * q_width : (level + 1) * q_width, :] = slab
        high, rest = halves(slab)
        low = (slab - high.astype(F32) - rest.astype(F32)).astype(BF16)
        for place, part in enumerate((high, rest, low)):
            first = start + (place * level_count + level) * q_width
            send_ref[first : first + q_width, :] = part
    line = jnp.concatenate([count_line_ref[...].astype(F32), jnp.zeros((1, eq_width - leaf_count), F32)], axis=1)
    start = start + 3 * level_count * q_width
    send_ref[start : start + 16, :] = jnp.broadcast_to(line, (16, eq_width)).astype(BF16)


def far_kernel(
    lower_ref, own_ref, upper_ref, vlist_ref, ulist_ref, table_hbm, out_ref, plan_ref, item_ref, table_ref, tail_ref,
    wide_ref, total_ref, first_ref, sems
):
    node_count, type_count = vlist_ref.shape
    eq_width = own_ref.shape[1]
    q_width = out_ref.shape[0] // node_count
    lanes = node_count * q_width
    tile = 128 // q_width
    chunk = CHUNK
    chunk_rows = chunk * eq_width
    chunk_count = eq_width // chunk
    full = type_count // 128

    def copies_of(number):
        span = pl.ds(number * chunk_rows, chunk_rows)
        copies = []
        for part in range(full):
            source = table_hbm.at[span, pl.ds(part * 128, 128)]
            copies.append(pltpu.make_async_copy(source, table_ref.at[part, span], sems.at[number, part]))
        source = table_hbm.at[span, pl.ds(full * 128, type_count - full * 128)]
        copies.append(pltpu.make_async_copy(source, tail_ref.at[span], sems.at[number, full]))
        return copies

    for number in range(chunk_count):
        for copy in copies_of(number):
            copy.start()

    index = lax.axis_index("oct")
    repeat = (iota((q_width, 128), 1) % q_width == iota((q_width, 128), 0)).astype(BF16)
    for part, source in enumerate((lower_ref, own_ref, upper_ref)):
        for node in range(node_count):
            spread = dot_tn(source[node * q_width : (node + 1) * q_width, :], repeat)
            wide_ref[pl.ds(part * node_count + node, eq_width, stride=SOURCES), :] = spread
    for place in range(3 * node_count, SOURCES):
        wide_ref[pl.ds(place, eq_width, stride=SOURCES), :] = jnp.zeros((eq_width, 128), F32)

    ids = vlist_ref[...]
    places = jnp.where(ids >= 0, ids - (index - 1) * node_count, -1).astype(F32).astype(BF16)
    spread = (iota((node_count, lanes), 1) // SOURCES == iota((node_count, lanes), 0)).astype(BF16)
    wanted = dot_tn(places, spread)
    chosen = (wanted == (iota((type_count, lanes), 1) % SOURCES).astype(F32)).astype(F32)
    chosen_full = chosen[: full * 128].astype(BF16)
    chosen_tail = chosen[full * 128 :].astype(BF16)
    lane_node = iota((SOURCES, 128), 1) // q_width
    nothing = jnp.zeros((SOURCES, 128), F32)
    total_ref[...] = jnp.zeros_like(total_ref)

    leaf_count = ulist_ref.shape[1]
    start = own_ref.shape[0] - 16
    lines = [ref[start:, :].astype(F32)[:1, :leaf_count] for ref in (lower_ref, own_ref, upper_ref)]
    plan_of(ulist_ref, lines, plan_ref, item_ref)

    def table_of(number):
        span = pl.ds(pl.multiple_of(number * chunk_rows, chunk_rows), chunk_rows)
        left = jnp.concatenate([table_ref[part, span, :] for part in range(full)], axis=1)
        return left, tail_ref[span, :]

    def first_product(left, tail):
        return dot(left, chosen_full) + dot(tail, chosen_tail)

    def second_product(number, summed):
        lefts, rights = [], []
        for step in range(chunk):
            value = summed[step * eq_width : (step + 1) * eq_width]
            high = value.astype(BF16).astype(F32)
            lefts.append(jnp.concatenate([high, value - high], axis=0).astype(BF16))
            row = number * chunk + step
            sent = wide_ref[pl.ds(pl.multiple_of(row * SOURCES, SOURCES), SOURCES), :]
            parts = [jnp.where(lane_node == place, sent, 0.0) for place in range(tile)]
            for node in range(node_count):
                line = [parts[node % tile] if place == node // tile else nothing for place in range(node_count // tile)]
                rights.append(jnp.concatenate(line, axis=1))
        product = dot(jnp.concatenate(lefts, axis=1), jnp.concatenate(rights, axis=0).astype(BF16))
        return product[:eq_width] + product[eq_width:]

    def wait_for(number):
        for copy in copies_of(number):
            copy.wait()

    wait_for(0)
    first_ref[...] = first_product(*table_of(0))

    def pair_step(pair, carry):
        number = 2 * pair
        wait_for(number + 1)
        pl.when(pair < chunk_count // 2 - 1)(lambda: wait_for(number + 2))
        ahead = table_of(number + 1)
        behind = table_of(jnp.minimum(number + 2, chunk_count - 1))
        summed = first_ref[...]
        middle = first_product(*ahead)
        total = second_product(number, summed)
        following = first_product(*behind)
        total = total + second_product(number + 1, middle)
        first_ref[...] = following
        total_ref[...] += total
        return carry

    lax.fori_loop(0, chunk_count // 2, pair_step, 0)
    out_ref[...] = total_ref[...].T


def near_kernel(
    plan_ref, item_ref, own_hbm, own_feature_hbm, lower_ref, upper_ref, out_ref, pack_ref, feature_ref, value_ref,
    total_ref, sems
):
    leaf_count, q_width, p_width = out_ref.shape
    own_rows, own_lines = own_hbm.shape[0], own_feature_hbm.shape[1]
    own_copy = pltpu.make_async_copy(own_hbm, pack_ref.at[pl.ds(0, own_rows)], sems.at[0])
    feature_copy = pltpu.make_async_copy(own_feature_hbm, feature_ref.at[:, pl.ds(0, own_lines)], sems.at[1])
    own_copy.start()
    feature_copy.start()
    pack_ref[3 * own_rows :, :] = jnp.zeros((PIECE, 128), BF16)
    feature_ref[:, 3 * own_lines :, :] = jnp.zeros((2, 32, 128), BF16)
    total_ref[...] = jnp.zeros_like(total_ref)
    blank = jnp.zeros((32, p_width), F32)

    def pack_step(step, carry):
        chosen = [(step * 4 + part, side) for part in range(4) for side in range(2)]
        sources = (lower_ref, upper_ref)
        weights = [weight_rows(sources[side][leaf, :q_width, :]) for leaf, side in chosen]
        versions = [feature_versions(right_rows(pieces(sources[side][leaf, q_width:, :]))) for leaf, side in chosen]
        packs = [jnp.concatenate([blank] + value + [blank], axis=0).astype(BF16).T for value in weights]
        for (leaf, side), pack, version in zip(chosen, packs, versions):
            place = (1 + side) * leaf_count + leaf
            pack_ref[pl.ds(pl.multiple_of(place * p_width, p_width), p_width), :] = pack
            put_features(feature_ref, place, version)
        return carry

    lax.fori_loop(0, leaf_count // 4, pack_step, 0)
    own_copy.wait()
    feature_copy.wait()
    step_lanes = 128 // UNROLL
    shift = step_lanes.bit_length() - 1

    def item_of(step, part):
        line = lax.shift_right_logical(step, shift)
        lane = jnp.bitwise_and(step, step_lanes - 1) * UNROLL + part
        return item_ref[line, lane], item_ref[8 + line, lane]

    def sources_of(leaf, place):
        rows = []
        for number in range(BLOCK // PIECE):
            start = pl.multiple_of(plan_ref[place + number, leaf] * 2, PIECE)
            rows.append(pack_ref[pl.ds(start, PIECE), :])
        return jnp.concatenate(rows, axis=0)

    def features_of(leaf, place):
        tiles = []
        for tile in range(BLOCK // 128):
            starts = [pl.multiple_of(plan_ref[place + 2 * tile + half, leaf], 32) for half in range(2)]
            halves_of = [feature_ref[half, pl.ds(start, 32), :] for half, start in enumerate(starts)]
            tiles.append(halves_of[0] + halves_of[1])
        return jnp.concatenate(tiles, axis=1)

    def run(rows, first, count):
        def blocks_step(step, carry):
            slot = jnp.bitwise_and(step, 1) * UNROLL
            done = [item_of(step - 1, part) for part in range(UNROLL)]
            items = [item_of(step, part) for part in range(UNROLL)]
            features = [features_of(leaf, place) for leaf, place in items]
            targets = []
            for leaf, _ in items:
                start = pl.multiple_of(jnp.minimum(leaf, leaf_count - 1) * p_width, p_width)
                targets.append(pack_ref[pl.ds(start, rows), :][:, :32])
            sources = [sources_of(leaf, place) for leaf, place in done]
            values = [
                jnp.concatenate([value_ref[UNROLL - slot + part, side, :rows] for side in range(2)], axis=1)
                for part in range(UNROLL)
            ]
            exponents = [dot(target, feature) for target, feature in zip(targets, features)]
            products = []
            for part in range(0, UNROLL, 2):
                left = jnp.concatenate(values[part : part + 2], axis=0)
                both = dot(left, jnp.concatenate(sources[part : part + 2], axis=1))
                products += [both[:rows, :128], both[rows:, 128:]]
            following = [jnp.exp2(value).astype(BF16) for value in exponents]
            for part, value in enumerate(following):
                for side in range(2):
                    value_ref[slot + part, side, :rows] = value[:, side * 128 : (side + 1) * 128]
            for (leaf, _), product in zip(done, products):
                total_ref[leaf, :rows] += product
            return carry

        lax.fori_loop(first, first + count, blocks_step, 0)

    for number, rows in enumerate(CLASS_ROWS):
        run(rows, plan_ref[PLAN_CLASS, 2 * number], plan_ref[PLAN_CLASS, 2 * number + 1])

    def turn_step(step, carry):
        turned = [total_ref[step * 8 + part].T for part in range(8)]
        for part, value in enumerate(turned):
            out_ref[step * 8 + part] = value[32 : 32 + q_width] + value[32 + q_width : 32 + 2 * q_width]
        return carry

    lax.fori_loop(0, leaf_count // 8, turn_step, 0)


def as_column(line):
    width = line.shape[1]
    wide = jnp.concatenate([line, jnp.zeros((1, 128 - width), F32)], axis=1) if width < 128 else line
    return jnp.broadcast_to(wide, (128, 128)).T[:width, :width]


def plan_of(ulist_ref, counts, plan_ref, item_ref):
    slot_count, leaf_count = ulist_ref.shape
    index = lax.axis_index("oct")
    shape = (leaf_count, leaf_count)
    row, column = iota(shape, 0), iota(shape, 1)
    tables = [as_column(line) for line in counts]
    own = jnp.broadcast_to(counts[1], shape)
    before = (tables[1] < own) | ((tables[1] == own) & (row < column))
    rank = jnp.sum(jnp.where(before, 1.0, 0.0), axis=0, keepdims=True)
    rank_column = as_column(rank).astype(jnp.int32)
    rank_wide = jnp.broadcast_to(rank, shape).astype(jnp.int32)

    block_pieces = BLOCK // PIECE
    zero_row = 3 * leaf_count * 64
    place_shape = (PLAN_PLACES, leaf_count)
    place_row = iota(place_shape, 0)
    listed = jnp.full(place_shape, zero_row, jnp.int32)
    offset = jnp.zeros((1, leaf_count), jnp.int32)
    for slot in range(slot_count):
        side = 1 if slot == 0 else (0 if slot < 9 else (1 if slot < 18 else 2))
        ids = ulist_ref[slot : slot + 1, :]
        place = jnp.where(ids >= 0, ids - (index + (side - 1)) * leaf_count, 0)
        found = jnp.sum(jnp.where(row == place, tables[side], 0.0), axis=0, keepdims=True).astype(jnp.int32)
        length = lax.shift_right_logical(found + (PIECE - 1), PIECE.bit_length() - 1)
        length = jnp.where(ids >= 0, length, 0)
        start = (place + (1, 0, 2)[side] * leaf_count) * 64
        inside = (place_row >= offset) & (place_row < offset + length)
        listed = jnp.where(inside, start + (place_row - offset) * 32, listed)
        offset = offset + length
    plan_ref[:PLAN_PLACES, :leaf_count] = listed
    plan_ref[:PLAN_PLACES, leaf_count:] = jnp.full((PLAN_PLACES, 128 - leaf_count), zero_row, jnp.int32)

    blocks = lax.shift_right_logical(offset + (block_pieces - 1), block_pieces.bit_length() - 1)
    blocks_column = as_column(blocks.astype(F32))
    own_class = lax.shift_right_logical(counts[1].astype(jnp.int32) - 1, 5)
    class_column = as_column(own_class.astype(F32)).astype(jnp.int32)
    earlier = (class_column == jnp.broadcast_to(own_class, shape)) & (rank_column < rank_wide)
    first = jnp.sum(jnp.where(earlier, blocks_column, 0.0), axis=0, keepdims=True).astype(jnp.int32)
    lane = iota((1, 128), 1)
    steps_line = jnp.zeros((1, 128), jnp.int32)
    start = jnp.ones((1, 1), jnp.int32)
    for number in range(len(CLASS_ROWS)):
        inside = jnp.where(own_class == number, blocks.astype(F32), 0.0)
        items = jnp.sum(inside, axis=1, keepdims=True).astype(jnp.int32)
        steps = lax.shift_right_logical(items + (2 * UNROLL - 1), UNROLL.bit_length() - 1)
        steps = jnp.where(items > 0, steps, 0)
        first = first + jnp.where(own_class == number, start * UNROLL, 0)
        steps_line = jnp.where(lane == 2 * number, start, jnp.where(lane == 2 * number + 1, steps, steps_line))
        start = start + steps
    plan_ref[PLAN_CLASS : PLAN_CLASS + 1, :] = steps_line

    first_column = as_column(first.astype(F32))
    wide = (leaf_count, 128)
    first_wide = jnp.concatenate([first_column] * (128 // leaf_count), axis=1).astype(jnp.int32)
    blocks_wide = jnp.concatenate([blocks_column] * (128 // leaf_count), axis=1).astype(jnp.int32)
    leaf_row = iota(wide, 0).astype(F32)
    for line in range(8):
        after = iota(wide, 1) + 128 * line - first_wide
        inside = (after >= 0) & (after < blocks_wide)
        leaf = jnp.sum(jnp.where(inside, leaf_row - leaf_count, 0.0), axis=0, keepdims=True)
        place = jnp.sum(jnp.where(inside, (after * block_pieces).astype(F32), 0.0), axis=0, keepdims=True)
        item_ref[line : line + 1, :] = leaf.astype(jnp.int32) + leaf_count
        item_ref[8 + line : 9 + line, :] = place.astype(jnp.int32)

    order = jnp.sum(jnp.where(rank_column == column, row.astype(F32), 0.0), axis=0, keepdims=True)
    plan_ref[PLAN_ORDER : PLAN_ORDER + 1, :leaf_count] = order.astype(jnp.int32)
    plan_ref[PLAN_COUNT : PLAN_COUNT + 1, :leaf_count] = counts[1].astype(jnp.int32)


def final_kernel(
    level_count, counts_ref, feature_ref, turned_ref, near_ref, far_ref, coarse_ref, shift_ref, down_ref, *rest
):
    top_refs, (out_ref, node_ref, down_leaf_ref) = rest[:level_count], rest[level_count:]
    leaf_count, q_width, p_width = out_ref.shape
    eq_width = far_ref.shape[1]
    node_count = leaf_count // 8
    index = lax.axis_index("oct")
    slab_local = jnp.zeros((q_width, eq_width), F32)
    for level, top_ref in enumerate(top_refs):
        slab_local = slab_local + dot3(top_ref[:q_width, :], coarse_ref[jnp.right_shift(index, 3 * level) & 7])
    for node in range(node_count):
        rows = slice(node * q_width, (node + 1) * q_width)
        node_ref[rows, :] = far_ref[rows, :] + dot3(slab_local, shift_ref[node])

    for child in range(8):
        down_leaf_ref[child] = dot3(dot3(node_ref[...], shift_ref[child]), down_ref[...])
    lane = iota((q_width, p_width), 1)

    def node_step(node, carry):
        leaves = [node * 8 + child for child in range(8)]
        features = []
        for leaf in leaves:
            starts = [pl.multiple_of((2 * leaf + half) * 32, 32) for half in range(2)]
            features.append(feature_ref[0, pl.ds(starts[0], 32), :] + feature_ref[1, pl.ds(starts[1], 32), :])
        turned = [turned_ref[leaf] for leaf in leaves]
        node_rows = pl.ds(pl.multiple_of(node * q_width, q_width), q_width)
        downs = [weight_rows(down_leaf_ref[child, node_rows, :]) for child in range(8)]
        nears = [near_ref[leaf] for leaf in leaves]
        exponents = [dot(left, right) for left, right in zip(turned, features)]
        values = [halves(jnp.exp2(value)) for value in exponents]
        lefts = [jnp.concatenate(down, axis=0).astype(BF16) for down in downs]
        products = [dot(left, jnp.concatenate(value, axis=1)) for left, value in zip(lefts, values)]
        for child, leaf in enumerate(leaves):
            product = products[child]
            far = product[:q_width, :p_width] + product[q_width:, :p_width] + product[:q_width, p_width:]
            out_ref[leaf] = jnp.where(lane < counts_ref[leaf], far + nears[child], 0.0)
        return carry

    lax.fori_loop(0, node_count, node_step, 0)


def shifted(value, size):
    up = [(i, i + 1) for i in range(size - 1)]
    down = [(j, i) for i, j in up]
    return lax.ppermute(value, "oct", up), lax.ppermute(value, "oct", down)


def swapped(value, size, bit):
    return lax.ppermute(value, "oct", [(source, source ^ (1 << bit)) for source in range(size)])


def local(
    points,
    dens,
    surface,
    counts,
    ulist,
    vlist,
    up_inverse,
    down_inverse,
    shift_up,
    shift_down,
    coarse,
    translate,
):
    leaf_count, q_width, p_width = dens.shape
    eq_width = surface.shape[2]
    node_count, type_count = vlist.shape
    node_rows = node_count * q_width
    size = lax.axis_size("oct")
    bits = size.bit_length() - 1
    level_count = -(-bits // 3)
    level_rows = level_count * q_width
    index = lax.axis_index("oct")
    vmem = pl.BlockSpec(memory_space=pltpu.VMEM)
    smem = pl.BlockSpec(memory_space=pltpu.SMEM)
    hbm = pl.BlockSpec(memory_space=pl.ANY)
    params = grant(56)
    points = jnp.transpose(points, (1, 0, 2))
    surface = jnp.transpose(surface, (1, 0, 2))
    ulist = ulist.T
    table = jnp.transpose(translate, (1, 2, 0))

    pack, features, turned, message, send, slab = pl.pallas_call(
        lambda *refs: upward_kernel(level_count, *refs),
        out_shape=(
            jax.ShapeDtypeStruct((leaf_count * p_width, 128), BF16),
            jax.ShapeDtypeStruct((2, leaf_count * 64, p_width), BF16),
            jax.ShapeDtypeStruct((leaf_count, eq_width, 32), BF16),
            jax.ShapeDtypeStruct((leaf_count, q_width + 8, p_width), F32),
            jax.ShapeDtypeStruct((node_rows + 3 * level_count * q_width + 16, eq_width), BF16),
            jax.ShapeDtypeStruct((level_count * q_width, eq_width), F32),
        ),
        in_specs=[vmem, vmem, vmem, smem, vmem, vmem, vmem],
        out_specs=(vmem,) * 6,
        scratch_shapes=[pltpu.VMEM((8, node_rows, eq_width), F32)],
        compiler_params=params,
        name="upward",
    )(points, dens, surface, counts, counts.reshape(1, leaf_count), up_inverse, shift_up)

    send_lower, send_upper = shifted(send, size)
    ends = slice(node_rows, node_rows + 3 * level_rows)
    partner = jnp.where(index & 1 == 1, send_lower[ends], send_upper[ends]).astype(F32)
    total = slab + (partner[:level_rows] + partner[level_rows : 2 * level_rows] + partner[2 * level_rows :])
    message, total = lax.optimization_barrier((message, total))
    lower, upper = shifted(message, size)
    tops = []
    for level in range(level_count):
        if level:
            tops.append(total)
            total = total[q_width:]
        for bit in range(max(1, 3 * level), min(3 * level + 3, bits)):
            total = total + swapped(total, size, bit)
    tops.append(total)

    table = table.reshape(eq_width * eq_width, type_count)
    far_node, plan, items = pl.pallas_call(
        far_kernel,
        out_shape=(
            jax.ShapeDtypeStruct((node_rows, eq_width), F32),
            jax.ShapeDtypeStruct((64, 128), jnp.int32),
            jax.ShapeDtypeStruct((16, 128), jnp.int32),
        ),
        in_specs=[vmem, vmem, vmem, vmem, vmem, hbm],
        out_specs=(vmem,) * 3,
        scratch_shapes=[
            pltpu.VMEM((type_count // 128, eq_width * eq_width, 128), BF16),
            pltpu.VMEM((eq_width * eq_width, type_count % 128), BF16),
            pltpu.VMEM((eq_width * SOURCES, 128), F32),
            pltpu.VMEM((eq_width, node_rows), F32),
            pltpu.VMEM((CHUNK * eq_width, node_rows), F32),
            pltpu.SemaphoreType.DMA((eq_width // CHUNK, type_count // 128 + 1)),
        ],
        compiler_params=params,
        cost_estimate=pl.CostEstimate(flops=2 * 10**10, bytes_accessed=18 * 10**6, transcendentals=0),
        name="far",
    )(send_lower, send, send_upper, vlist, ulist, table)
    far_node, lower, upper = lax.optimization_barrier((far_node, lower, upper))

    near = pl.pallas_call(
        near_kernel,
        out_shape=jax.ShapeDtypeStruct((leaf_count, q_width, p_width), F32),
        in_specs=[smem, smem, hbm, hbm, vmem, vmem],
        out_specs=vmem,
        scratch_shapes=[
            pltpu.VMEM((3 * leaf_count * p_width + PIECE, 128), BF16),
            pltpu.VMEM((2, 3 * leaf_count * 64 + 32, 128), BF16),
            pltpu.VMEM((2 * UNROLL, 2, p_width, 128), BF16),
            pltpu.VMEM((leaf_count + 1, p_width, 128), F32),
            pltpu.SemaphoreType.DMA((2,)),
        ],
        compiler_params=params,
        cost_estimate=pl.CostEstimate(flops=3 * 10**10, bytes_accessed=10**7, transcendentals=0),
        name="near",
    )(plan, items, pack, features, lower, upper)

    return pl.pallas_call(
        lambda *refs: final_kernel(len(tops), *refs),
        out_shape=jax.ShapeDtypeStruct((leaf_count, q_width, p_width), F32),
        in_specs=[smem] + [vmem] * (7 + len(tops)),
        out_specs=vmem,
        scratch_shapes=[
            pltpu.VMEM((node_rows, eq_width), F32),
            pltpu.VMEM((8, node_rows, eq_width), F32),
        ],
        compiler_params=params,
        name="final",
    )(counts, features, turned, near, far_node, coarse, shift_down, down_inverse, *tops)


def solution(mesh):
    placed = (
        P("oct", None, None),
        P("oct", None, None),
        P("oct", None, None),
        P("oct"),
        P("oct", None),
        P("oct", None),
        P(),
        P(),
        P(),
        P(),
        P(),
        P(),
    )
    return jax.shard_map(
        local, mesh=mesh, in_specs=placed, out_specs=P("oct", None, None), check_vma=False
    )
```

```python
import math

import jax
import jax.numpy as jnp
from jax import lax
from jax.experimental import pallas as pl
from jax.experimental.pallas import tpu as pltpu
from jax.sharding import PartitionSpec as P

F32 = jnp.float32
BF16 = jnp.bfloat16
HIGHEST = lax.Precision.HIGHEST
SCALE = math.sqrt(math.log2(math.e))
NT = (((1,), (1,)), ((), ()))
TN = (((0,), (0,)), ((), ()))
BLOCK = 256
UNROLL = 8
TOTALS = 4
PIECE = 64
CLASS_ROWS = (32, 64, 96, 128)
PLACES = 56
SOURCES = 32
CHUNK = 4


def dot(left, right):
    return jnp.dot(left, right, preferred_element_type=F32)


def dot_nt(left, right):
    return lax.dot_general(left, right, NT, preferred_element_type=F32)


def dot_tn(left, right):
    return lax.dot_general(left, right, TN, preferred_element_type=F32)


def halves(value):
    high = value.astype(BF16)
    low = (value - high.astype(F32)).astype(BF16)
    return high, low


def dot3(left, right):
    left_high, left_low = halves(left)
    right_high, right_low = halves(right)
    return dot(left_high, right_high) + dot(left_high, right_low) + dot(left_low, right_high)


def grant(mebibytes):
    return pltpu.CompilerParams(vmem_limit_bytes=mebibytes * 1024 * 1024)


def iota(shape, dim):
    return lax.broadcasted_iota(jnp.int32, shape, dim)


def coords_of(ref, leaf):
    width = ref.shape[2]
    row = iota((8, width), 0)
    value = jnp.zeros((8, width), F32)
    for dim in range(3):
        line = jnp.broadcast_to(ref[dim, pl.ds(leaf, 1), :], (8, width))
        value = jnp.where(row == dim, line, value)
    return value


def pieces(coords):
    row = iota(coords.shape, 0)
    used = row < 3
    scaled = jnp.where(used, coords, 0.0) * SCALE
    high = scaled.astype(BF16).astype(F32)
    rest = scaled - high
    mid = rest.astype(BF16).astype(F32)
    low = (rest - mid).astype(BF16).astype(F32)
    norm = -0.5 * jnp.sum(scaled * scaled, axis=0, keepdims=True)
    norm_high = norm.astype(BF16).astype(F32)
    norm_rest = norm - norm_high
    norm_mid = norm_rest.astype(BF16).astype(F32)
    norm_low = norm_rest - norm_mid
    norms = jnp.where(row == 0, norm_high, jnp.where(row == 1, norm_mid, jnp.where(row == 2, norm_low, 0.0)))
    ones = jnp.where(used, 1.0, 0.0)
    return high, mid, low, norms, ones


def paired(first, second):
    return first + pltpu.roll(second, 4, 0)


def left_rows(parts):
    high, mid, low, norms, ones = parts
    return jnp.concatenate([paired(high, high), paired(mid, mid), paired(high, low), paired(ones, norms)], axis=0)


def right_rows(parts):
    high, mid, low, norms, ones = parts
    both = paired(high, mid)
    return jnp.concatenate([both, both, paired(low, high), paired(norms, ones)], axis=0)


def weight_rows(weights):
    high = weights.astype(BF16).astype(F32)
    return [high, weights - high]


def feature_versions(rows):
    lower = iota(rows.shape, 1) < PIECE
    versions = []
    for half in range(2):
        alone = jnp.where(lower == (half == 0), rows, 0.0)
        versions.append((half, half, alone.astype(BF16)))
        versions.append((half, 1 - half, pltpu.roll(alone, PIECE, 1).astype(BF16)))
    return versions


def put_features(feature_ref, leaf, versions):
    for half, place, value in versions:
        feature_ref[place, 2 * leaf + half] = value


def put_pack(pack_ref, leaf, value):
    pack_ref[pl.ds(2 * leaf, 2)] = value.reshape(2, PIECE, 128)


def upward_kernel(
    level_count, points_ref, dens_ref, surface_ref, counts_ref, count_line_ref, up_ref, shift_ref, pack_ref, feature_ref, turned_ref,
    message_ref, send_ref, slab_ref, check_ref
):
    leaf_count, q_width, p_width = dens_ref.shape
    eq_width = surface_ref.shape[2]
    node_count = leaf_count // 8
    lane = iota((q_width, p_width), 1)
    row = iota((8, p_width), 0)

    def node_step(node, carry):
        leaves = [node * 8 + child for child in range(8)]
        counts = [counts_ref[leaf] for leaf in leaves]
        weights = [jnp.where(lane < count, dens_ref[leaf], 0.0) for leaf, count in zip(leaves, counts)]
        coords = [coords_of(points_ref, leaf) for leaf in leaves]
        surfaces = [left_rows(pieces(coords_of(surface_ref, leaf))) for leaf in leaves]
        parts = [pieces(value) for value in coords]
        rights = [right_rows(value) for value in parts]
        lists = [weight_rows(value) for value in weights]
        packs = [
            jnp.concatenate([left_rows(part)] + split + [right], axis=0).astype(BF16).T
            for part, split, right in zip(parts, lists, rights)
        ]
        blank = jnp.zeros((96, eq_width), F32)
        wides = [jnp.concatenate([blank, value], axis=0).astype(BF16) for value in surfaces]
        exponents = [dot(pack, wide) for pack, wide in zip(packs, wides)]
        values = [halves(jnp.exp2(value)) for value in exponents]
        rows = [jnp.concatenate(split, axis=0).astype(BF16) for split in lists]
        firsts = [dot(row, value[0]) for row, value in zip(rows, values)]
        seconds = [dot(row[:q_width], value[1]) for row, value in zip(rows, values)]
        fours = [jnp.concatenate(surfaces[first : first + 4], axis=0).astype(BF16).T for first in range(0, 8, 4)]
        versions = [feature_versions(right) for right in rights]
        for number, four in enumerate(fours):
            turned_ref[2 * node + number] = four
        for child, leaf in enumerate(leaves):
            message_ref[leaf, :q_width, :] = weights[child]
            message_ref[leaf, q_width:, :] = jnp.where(row == 3, counts[child].astype(F32), coords[child])
            put_pack(pack_ref, leaf, packs[child])
            put_features(feature_ref, leaf, versions[child])
            check = firsts[child][:q_width] + firsts[child][q_width:] + seconds[child]
            check_ref[child, pl.ds(pl.multiple_of(node * q_width, q_width), q_width), :] = check
        return carry

    lax.fori_loop(0, node_count, node_step, 0)

    node_eq = jnp.zeros((node_count * q_width, eq_width), F32)
    for child in range(8):
        node_eq = node_eq + dot3(dot3(check_ref[child], up_ref[...]), shift_ref[child])
    send_ref[: node_count * q_width, :] = node_eq.astype(BF16)
    slab_eq = jnp.zeros((q_width, eq_width), F32)
    for child in range(8):
        slab_eq = slab_eq + dot3(node_eq[child * q_width : (child + 1) * q_width], shift_ref[child])
    index = lax.axis_index("oct")
    slab = slab_eq
    start = node_count * q_width
    for level in range(level_count):
        slab = dot3(slab, shift_ref[jnp.right_shift(index, 3 * level) & 7])
        slab_ref[level * q_width : (level + 1) * q_width, :] = slab
        high, rest = halves(slab)
        low = (slab - high.astype(F32) - rest.astype(F32)).astype(BF16)
        for place, part in enumerate((high, rest, low)):
            first = start + (place * level_count + level) * q_width
            send_ref[first : first + q_width, :] = part
    start = start + 3 * level_count * q_width
    line = jnp.concatenate([count_line_ref[...].astype(F32), jnp.zeros((1, eq_width - leaf_count), F32)], axis=1)
    send_ref[start : start + 16, :] = jnp.broadcast_to(line, (16, eq_width)).astype(BF16)


def far_kernel(
    lower_ref, own_ref, upper_ref, vlist_ref, ulist_ref, table_hbm, out_ref, step_ref, piece_ref, item_ref, table_ref,
    tail_ref, wide_ref, total_ref, first_ref, sems
):
    node_count, type_count = vlist_ref.shape
    eq_width = own_ref.shape[1]
    q_width = out_ref.shape[0] // node_count
    lanes = node_count * q_width
    tile = 128 // q_width
    chunk = CHUNK
    chunk_rows = chunk * eq_width
    chunk_count = eq_width // chunk
    full = type_count // 128

    def copies_of(number):
        span = pl.ds(number * chunk_rows, chunk_rows)
        copies = []
        for part in range(full):
            source = table_hbm.at[span, pl.ds(part * 128, 128)]
            copies.append(pltpu.make_async_copy(source, table_ref.at[part, span], sems.at[number, part]))
        source = table_hbm.at[span, pl.ds(full * 128, type_count - full * 128)]
        copies.append(pltpu.make_async_copy(source, tail_ref.at[span], sems.at[number, full]))
        return copies

    for number in range(chunk_count):
        for copy in copies_of(number):
            copy.start()

    index = lax.axis_index("oct")
    repeat = (iota((q_width, 128), 1) % q_width == iota((q_width, 128), 0)).astype(BF16)
    for part, source in enumerate((lower_ref, own_ref, upper_ref)):
        for node in range(node_count):
            spread = dot_tn(source[node * q_width : (node + 1) * q_width, :], repeat)
            wide_ref[pl.ds(part * node_count + node, eq_width, stride=SOURCES), :] = spread
    for place in range(3 * node_count, SOURCES):
        wide_ref[pl.ds(place, eq_width, stride=SOURCES), :] = jnp.zeros((eq_width, 128), F32)

    ids = vlist_ref[...]
    places = jnp.where(ids >= 0, ids - (index - 1) * node_count, -1).astype(F32).astype(BF16)
    spread = (iota((node_count, lanes), 1) // SOURCES == iota((node_count, lanes), 0)).astype(BF16)
    wanted = dot_tn(places, spread)
    chosen = (wanted == (iota((type_count, lanes), 1) % SOURCES).astype(F32)).astype(F32)
    chosen_full = chosen[: full * 128].astype(BF16)
    chosen_tail = chosen[full * 128 :].astype(BF16)
    lane_node = iota((SOURCES, 128), 1) // q_width
    nothing = jnp.zeros((SOURCES, 128), F32)
    total_ref[...] = jnp.zeros_like(total_ref)

    leaf_count = ulist_ref.shape[1]
    start = own_ref.shape[0] - 16
    lines = [ref[start:, :].astype(F32)[:1, :leaf_count] for ref in (lower_ref, own_ref, upper_ref)]
    plan_of(ulist_ref, lines, step_ref, piece_ref, item_ref)

    def table_of(number):
        span = pl.ds(pl.multiple_of(number * chunk_rows, chunk_rows), chunk_rows)
        left = jnp.concatenate([table_ref[part, span, :] for part in range(full)], axis=1)
        return left, tail_ref[span, :]

    def first_product(left, tail):
        return dot(left, chosen_full) + dot(tail, chosen_tail)

    def second_product(number, summed):
        lefts, rights = [], []
        for step in range(chunk):
            value = summed[step * eq_width : (step + 1) * eq_width]
            high = value.astype(BF16).astype(F32)
            lefts.append(jnp.concatenate([high, value - high], axis=0).astype(BF16))
            row = number * chunk + step
            sent = wide_ref[pl.ds(pl.multiple_of(row * SOURCES, SOURCES), SOURCES), :]
            parts = [jnp.where(lane_node == place, sent, 0.0) for place in range(tile)]
            for node in range(node_count):
                line = [parts[node % tile] if place == node // tile else nothing for place in range(node_count // tile)]
                rights.append(jnp.concatenate(line, axis=1))
        product = dot(jnp.concatenate(lefts, axis=1), jnp.concatenate(rights, axis=0).astype(BF16))
        return product[:eq_width] + product[eq_width:]

    def wait_for(number):
        for copy in copies_of(number):
            copy.wait()

    wait_for(0)
    first_ref[...] = first_product(*table_of(0))

    def pair_step(pair, carry):
        number = 2 * pair
        wait_for(number + 1)
        pl.when(pair < chunk_count // 2 - 1)(lambda: wait_for(number + 2))
        ahead = table_of(number + 1)
        behind = table_of(jnp.minimum(number + 2, chunk_count - 1))
        summed = first_ref[...]
        middle = first_product(*ahead)
        total = second_product(number, summed)
        following = first_product(*behind)
        total = total + second_product(number + 1, middle)
        first_ref[...] = following
        total_ref[...] += total
        return carry

    lax.fori_loop(0, chunk_count // 2, pair_step, 0)
    out_ref[...] = total_ref[...].T


def near_kernel(
    step_ref, piece_ref, item_ref, own_hbm, own_feature_hbm, lower_ref, upper_ref, out_ref, pack_ref, feature_ref, value_ref,
    *rest
):
    total_refs, sems = rest[:TOTALS], rest[TOTALS]
    leaf_count, q_width, p_width = out_ref.shape
    own = pl.ds(0, 2 * leaf_count)
    own_copy = pltpu.make_async_copy(own_hbm, pack_ref.at[own], sems.at[0])
    feature_copy = pltpu.make_async_copy(own_feature_hbm, feature_ref.at[:, own], sems.at[1])
    own_copy.start()
    feature_copy.start()
    pack_ref[6 * leaf_count] = jnp.zeros((PIECE, 128), BF16)
    for half in range(2):
        feature_ref[half, 6 * leaf_count] = jnp.zeros((32, 128), BF16)
    for total_ref in total_refs:
        total_ref[...] = jnp.zeros_like(total_ref)
    blank = jnp.zeros((32, p_width), F32)

    def pack_step(step, carry):
        chosen = [(step * 4 + part, side) for part in range(4) for side in range(2)]
        sources = (lower_ref, upper_ref)
        weights = [weight_rows(sources[side][leaf, :q_width, :]) for leaf, side in chosen]
        versions = [feature_versions(right_rows(pieces(sources[side][leaf, q_width:, :]))) for leaf, side in chosen]
        packs = [jnp.concatenate([blank] + value + [blank], axis=0).astype(BF16).T for value in weights]
        for (leaf, side), pack, version in zip(chosen, packs, versions):
            place = (1 + side) * leaf_count + leaf
            put_pack(pack_ref, place, pack)
            put_features(feature_ref, place, version)
        return carry

    lax.fori_loop(0, leaf_count // 4, pack_step, 0)
    own_copy.wait()
    feature_copy.wait()
    block_pieces = BLOCK // PIECE

    def items_of(step):
        first = step * UNROLL
        leaves = [item_ref[first + part] for part in range(UNROLL)]
        first = first * block_pieces
        pieces_of = [
            [piece_ref[first + part * block_pieces + number] for number in range(block_pieces)] for part in range(UNROLL)
        ]
        return list(zip(leaves, pieces_of))

    def sources_of(numbers):
        return jnp.concatenate([pack_ref[number] for number in numbers], axis=0)

    def features_of(numbers):
        tiles = []
        for tile in range(BLOCK // 128):
            tiles.append(feature_ref[0, numbers[2 * tile]] + feature_ref[1, numbers[2 * tile + 1]])
        return jnp.concatenate(tiles, axis=1)

    def targets_of(leaf, rows):
        first = 2 * jnp.minimum(leaf, leaf_count - 1)
        if rows <= PIECE:
            return pack_ref[first, :rows][:, :32]
        return jnp.concatenate([pack_ref[first][:, :32], pack_ref[first + 1, : rows - PIECE][:, :32]], axis=0)

    def run(rows, first, count):
        def blocks_step(step, carry):
            slot = jnp.bitwise_and(step, 1) * UNROLL
            done, items = items_of(step - 1), items_of(step)
            features = [features_of(numbers) for _, numbers in items]
            targets = [targets_of(leaf, rows) for leaf, _ in items]
            sources = [sources_of(numbers) for _, numbers in done]
            values = [
                jnp.concatenate([value_ref[UNROLL - slot + part, side, :rows] for side in range(2)], axis=1)
                for part in range(UNROLL)
            ]
            exponents = [dot(target, feature) for target, feature in zip(targets, features)]
            products = []
            for part in range(0, UNROLL, 2):
                left = jnp.concatenate(values[part : part + 2], axis=0)
                both = dot(left, jnp.concatenate(sources[part : part + 2], axis=1))
                products += [both[:rows, :128], both[rows:, 128:]]
            following = [jnp.exp2(value).astype(BF16) for value in exponents]
            for part, value in enumerate(following):
                for side in range(2):
                    value_ref[slot + part, side, :rows] = value[:, side * 128 : (side + 1) * 128]
            for first in range(0, UNROLL, TOTALS):
                sums = [
                    total_refs[part][done[first + part][0], :rows] + products[first + part] for part in range(TOTALS)
                ]
                for part, value in enumerate(sums):
                    total_refs[part][done[first + part][0], :rows] = value
            return carry

        lax.fori_loop(first, first + count, blocks_step, 0)

    for number, rows in enumerate(CLASS_ROWS):
        run(rows, step_ref[0, 2 * number], step_ref[0, 2 * number + 1])

    def turn_step(step, carry):
        sums = [[total_ref[step * 8 + part] for total_ref in total_refs] for part in range(8)]
        turned = [(a + b + (c + d)).T for a, b, c, d in sums]
        for part, value in enumerate(turned):
            out_ref[step * 8 + part] = value[32 : 32 + q_width] + value[32 + q_width : 32 + 2 * q_width]
        return carry

    lax.fori_loop(0, leaf_count // 8, turn_step, 0)


def as_column(line):
    width = line.shape[1]
    wide = jnp.concatenate([line, jnp.zeros((1, 128 - width), F32)], axis=1) if width < 128 else line
    return jnp.broadcast_to(wide, (128, 128)).T[:width, :width]


def plan_of(ulist_ref, counts, step_ref, piece_ref, item_ref):
    slot_count, leaf_count = ulist_ref.shape
    index = lax.axis_index("oct")
    shape = (leaf_count, leaf_count)
    row, column = iota(shape, 0), iota(shape, 1)
    tables = [as_column(line) for line in counts]
    own = jnp.broadcast_to(counts[1], shape)
    before = (tables[1] < own) | ((tables[1] == own) & (row < column))
    rank = jnp.sum(jnp.where(before, 1.0, 0.0), axis=0, keepdims=True)
    rank_column = as_column(rank).astype(jnp.int32)
    rank_wide = jnp.broadcast_to(rank, shape).astype(jnp.int32)

    block_pieces = BLOCK // PIECE
    empty = 6 * leaf_count
    place_shape = (PLACES, leaf_count)
    place_row = iota(place_shape, 0)
    listed = jnp.full(place_shape, empty, jnp.int32)
    offset = jnp.zeros((1, leaf_count), jnp.int32)
    for slot in range(slot_count):
        side = 1 if slot == 0 else (0 if slot < 9 else (1 if slot < 18 else 2))
        ids = ulist_ref[slot : slot + 1, :]
        place = jnp.where(ids >= 0, ids - (index + (side - 1)) * leaf_count, 0)
        found = jnp.sum(jnp.where(row == place, tables[side], 0.0), axis=0, keepdims=True).astype(jnp.int32)
        length = lax.shift_right_logical(found + (PIECE - 1), PIECE.bit_length() - 1)
        length = jnp.where(ids >= 0, length, 0)
        start = (place + (1, 0, 2)[side] * leaf_count) * 2
        inside = (place_row >= offset) & (place_row < offset + length)
        listed = jnp.where(inside, start + place_row - offset, listed)
        offset = offset + length

    blocks = lax.shift_right_logical(offset + (block_pieces - 1), block_pieces.bit_length() - 1)
    blocks_column = as_column(blocks.astype(F32))
    own_class = lax.shift_right_logical(counts[1].astype(jnp.int32) - 1, 5)
    class_column = as_column(own_class.astype(F32)).astype(jnp.int32)
    earlier = (class_column == jnp.broadcast_to(own_class, shape)) & (rank_column < rank_wide)
    first = jnp.sum(jnp.where(earlier, blocks_column, 0.0), axis=0, keepdims=True).astype(jnp.int32)
    lane = iota((1, 128), 1)
    steps_line = jnp.zeros((1, 128), jnp.int32)
    start = jnp.ones((1, 1), jnp.int32)
    for number in range(len(CLASS_ROWS)):
        inside = jnp.where(own_class == number, blocks.astype(F32), 0.0)
        items = jnp.sum(inside, axis=1, keepdims=True).astype(jnp.int32)
        steps = lax.shift_right_logical(items + (2 * UNROLL - 1), UNROLL.bit_length() - 1)
        steps = jnp.where(items > 0, steps, 0)
        first = first + jnp.where(own_class == number, start * UNROLL, 0)
        steps_line = jnp.where(lane == 2 * number, start, jnp.where(lane == 2 * number + 1, steps, steps_line))
        start = start + steps
    step_ref[...] = steps_line

    first_column = as_column(first.astype(F32))[:, :1].astype(jnp.int32)
    blocks_column = blocks_column[:, :1].astype(jnp.int32)
    high = lax.shift_right_logical(listed, 8).astype(F32)
    low = jnp.bitwise_and(listed, 255).astype(F32)
    parts = jnp.concatenate([high, low], axis=0).astype(BF16)
    chunk = 1024
    wide = (leaf_count, chunk)
    column = iota(wide, 1)
    leaf_row = iota(wide, 0).astype(F32)
    for number in range(block_pieces):
        entry = column + chunk * number
        after = lax.shift_right_logical(entry, block_pieces.bit_length() - 1) - first_column
        inside = (after >= 0) & (after < blocks_column)
        place = after * block_pieces + jnp.bitwise_and(entry, block_pieces - 1)
        place = jnp.sum(jnp.where(inside, place.astype(F32), 0.0), axis=0, keepdims=True).astype(jnp.int32)
        found = jnp.sum(jnp.where(inside, 1.0, 0.0), axis=0, keepdims=True)
        both = dot(parts, jnp.where(inside, 1.0, 0.0).astype(BF16))
        value = both[:PLACES] * 256.0 + both[PLACES:]
        value = jnp.sum(jnp.where(iota((PLACES, chunk), 0) == place, value, 0.0), axis=0, keepdims=True)
        value = jnp.where(found > 0.0, value, float(empty)).astype(jnp.int32)
        for line in range(8):
            piece_ref[8 * number + line : 8 * number + line + 1, :] = value[:, line * 128 : (line + 1) * 128]
    after = column - first_column
    inside = (after >= 0) & (after < blocks_column)
    leaf = jnp.sum(jnp.where(inside, leaf_row - leaf_count, 0.0), axis=0, keepdims=True).astype(jnp.int32) + leaf_count
    for line in range(8):
        item_ref[line : line + 1, :] = leaf[:, line * 128 : (line + 1) * 128]


def final_kernel(
    level_count, counts_ref, feature_ref, turned_ref, near_ref, far_ref, coarse_ref, shift_ref, down_ref, *rest
):
    top_refs, (out_ref, node_ref, down_leaf_ref) = rest[:level_count], rest[level_count:]
    leaf_count, q_width, p_width = out_ref.shape
    eq_width = far_ref.shape[1]
    node_count = leaf_count // 8
    index = lax.axis_index("oct")
    slab_local = jnp.zeros((q_width, eq_width), F32)
    for level, top_ref in enumerate(top_refs):
        slab_local = slab_local + dot3(top_ref[:q_width, :], coarse_ref[jnp.right_shift(index, 3 * level) & 7])
    for node in range(node_count):
        rows = slice(node * q_width, (node + 1) * q_width)
        node_ref[rows, :] = far_ref[rows, :] + dot3(slab_local, shift_ref[node])

    for child in range(8):
        down_leaf_ref[child] = dot3(dot3(node_ref[...], shift_ref[child]), down_ref[...])
    lane = iota((q_width, p_width), 1)

    def node_step(node, carry):
        leaves = [node * 8 + child for child in range(8)]
        features = []
        for leaf in leaves:
            features.append(feature_ref[0, 2 * leaf] + feature_ref[1, 2 * leaf + 1])
        turned = [turned_ref[2 * node + number] for number in range(2)]
        node_rows = pl.ds(pl.multiple_of(node * q_width, q_width), q_width)
        downs = [weight_rows(down_leaf_ref[child, node_rows, :]) for child in range(8)]
        nears = [near_ref[leaf] for leaf in leaves]
        blank = jnp.zeros((32, p_width), BF16)
        exponents = []
        for first in range(0, 8, 2):
            sides = []
            for child in (first, first + 1):
                lines = [features[child] if place == child % 4 else blank for place in range(4)]
                sides.append(jnp.concatenate(lines, axis=0))
            both = dot(turned[first // 4], jnp.concatenate(sides, axis=1))
            exponents += [both[:, :p_width], both[:, p_width:]]
        values = [halves(jnp.exp2(value)) for value in exponents]
        lefts = [jnp.concatenate(down, axis=0).astype(BF16) for down in downs]
        products = [dot(left, jnp.concatenate(value, axis=1)) for left, value in zip(lefts, values)]
        for child, leaf in enumerate(leaves):
            product = products[child]
            far = product[:q_width, :p_width] + product[q_width:, :p_width] + product[:q_width, p_width:]
            out_ref[leaf] = jnp.where(lane < counts_ref[leaf], far + nears[child], 0.0)
        return carry

    lax.fori_loop(0, node_count, node_step, 0)


def shifted(value, size):
    up = [(i, i + 1) for i in range(size - 1)]
    down = [(j, i) for i, j in up]
    return lax.ppermute(value, "oct", up), lax.ppermute(value, "oct", down)


def swapped(value, size, bit):
    return lax.ppermute(value, "oct", [(source, source ^ (1 << bit)) for source in range(size)])


def local(
    points,
    dens,
    surface,
    counts,
    ulist,
    vlist,
    up_inverse,
    down_inverse,
    shift_up,
    shift_down,
    coarse,
    translate,
):
    leaf_count, q_width, p_width = dens.shape
    eq_width = surface.shape[2]
    node_count, type_count = vlist.shape
    node_rows = node_count * q_width
    size = lax.axis_size("oct")
    bits = size.bit_length() - 1
    level_count = -(-bits // 3)
    level_rows = level_count * q_width
    index = lax.axis_index("oct")
    vmem = pl.BlockSpec(memory_space=pltpu.VMEM)
    smem = pl.BlockSpec(memory_space=pltpu.SMEM)
    hbm = pl.BlockSpec(memory_space=pl.ANY)
    params = grant(56)
    points = jnp.transpose(points, (1, 0, 2))
    surface = jnp.transpose(surface, (1, 0, 2))
    ulist = ulist.T
    table = jnp.transpose(translate, (1, 2, 0))

    pack, features, turned, message, send, slab = pl.pallas_call(
        lambda *refs: upward_kernel(level_count, *refs),
        out_shape=(
            jax.ShapeDtypeStruct((2 * leaf_count, PIECE, 128), BF16),
            jax.ShapeDtypeStruct((2, 2 * leaf_count, 32, p_width), BF16),
            jax.ShapeDtypeStruct((leaf_count // 4, eq_width, 128), BF16),
            jax.ShapeDtypeStruct((leaf_count, q_width + 8, p_width), F32),
            jax.ShapeDtypeStruct((node_rows + 3 * level_rows + 16, eq_width), BF16),
            jax.ShapeDtypeStruct((level_rows, eq_width), F32),
        ),
        in_specs=[vmem, vmem, vmem, smem, vmem, vmem, vmem],
        out_specs=(vmem,) * 6,
        scratch_shapes=[pltpu.VMEM((8, node_rows, eq_width), F32)],
        compiler_params=params,
        name="upward",
    )(points, dens, surface, counts, counts.reshape(1, leaf_count), up_inverse, shift_up)

    send_lower, send_upper = shifted(send, size)
    ends = slice(node_rows, node_rows + 3 * level_rows)
    partner = jnp.where(index & 1 == 1, send_lower[ends], send_upper[ends]).astype(F32)
    total = slab + (partner[:level_rows] + partner[level_rows : 2 * level_rows] + partner[2 * level_rows :])
    message, total = lax.optimization_barrier((message, total))
    lower, upper = shifted(message, size)
    exchanges = [(level, bit) for level in range(level_count) for bit in range(max(1, 3 * level), min(3 * level + 3, bits))]
    tops = []

    def exchange(total, wanted):
        level, bit = wanted
        if level and bit == 3 * level:
            tops.append(total)
            total = total[q_width:]
        return total, swapped(total, size, bit)

    early, late = exchanges[:2], exchanges[2:]
    total, arrived = exchange(total, early[0])
    total = total + arrived
    total, arrived = exchange(total, early[1])
    send_lower, total = lax.optimization_barrier((send_lower, total))

    table = table.reshape(eq_width * eq_width, type_count)
    far_node, steps, piece_table, items = pl.pallas_call(
        far_kernel,
        out_shape=(
            jax.ShapeDtypeStruct((node_rows, eq_width), F32),
            jax.ShapeDtypeStruct((1, 128), jnp.int32),
            jax.ShapeDtypeStruct((32, 128), jnp.int32),
            jax.ShapeDtypeStruct((8, 128), jnp.int32),
        ),
        in_specs=[vmem, vmem, vmem, vmem, vmem, hbm],
        out_specs=(vmem,) * 4,
        scratch_shapes=[
            pltpu.VMEM((type_count // 128, eq_width * eq_width, 128), BF16),
            pltpu.VMEM((eq_width * eq_width, type_count % 128), BF16),
            pltpu.VMEM((eq_width * SOURCES, 128), F32),
            pltpu.VMEM((eq_width, node_rows), F32),
            pltpu.VMEM((CHUNK * eq_width, node_rows), F32),
            pltpu.SemaphoreType.DMA((eq_width // CHUNK, type_count // 128 + 1)),
        ],
        compiler_params=params,
        cost_estimate=pl.CostEstimate(flops=2 * 10**10, bytes_accessed=18 * 10**6, transcendentals=0),
        name="far",
    )(send_lower, send, send_upper, vlist, ulist, table)
    far_node, lower, upper = lax.optimization_barrier((far_node, lower, upper))

    far_node, total, arrived = lax.optimization_barrier((far_node, total, arrived))
    for wanted in late:
        total = total + arrived
        total, arrived = exchange(total, wanted)
    steps, total = lax.optimization_barrier((steps, total))
    near = pl.pallas_call(
        near_kernel,
        out_shape=jax.ShapeDtypeStruct((leaf_count, q_width, p_width), F32),
        in_specs=[smem, smem, smem, hbm, hbm, vmem, vmem],
        out_specs=vmem,
        scratch_shapes=[
            pltpu.VMEM((6 * leaf_count + 1, PIECE, 128), BF16),
            pltpu.VMEM((2, 6 * leaf_count + 1, 32, 128), BF16),
            pltpu.VMEM((2 * UNROLL, 2, p_width, 128), BF16),
            *[pltpu.VMEM((leaf_count + 1, p_width, 128), F32)] * TOTALS,
            pltpu.SemaphoreType.DMA((2,)),
        ],
        compiler_params=params,
        cost_estimate=pl.CostEstimate(flops=3 * 10**10, bytes_accessed=10**7, transcendentals=0),
        name="near",
    )(steps, piece_table.reshape(-1), items.reshape(-1), pack, features, lower, upper)

    tops.append(total + arrived)
    return pl.pallas_call(
        lambda *refs: final_kernel(level_count, *refs),
        out_shape=jax.ShapeDtypeStruct((leaf_count, q_width, p_width), F32),
        in_specs=[smem] + [vmem] * (7 + len(tops)),
        out_specs=vmem,
        scratch_shapes=[
            pltpu.VMEM((node_rows, eq_width), F32),
            pltpu.VMEM((8, node_rows, eq_width), F32),
        ],
        compiler_params=params,
        name="final",
    )(counts, features, turned, near, far_node, coarse, shift_down, down_inverse, *tops)


def solution(mesh):
    placed = (
        P("oct", None, None),
        P("oct", None, None),
        P("oct", None, None),
        P("oct"),
        P("oct", None),
        P("oct", None),
        P(),
        P(),
        P(),
        P(),
        P(),
        P(),
    )
    return jax.shard_map(
        local, mesh=mesh, in_specs=placed, out_specs=P("oct", None, None), check_vma=False
    )
```

```python
import math

import jax
import jax.numpy as jnp
from jax import lax
from jax.experimental import pallas as pl
from jax.experimental.pallas import tpu as pltpu
from jax.sharding import PartitionSpec as P

F32 = jnp.float32
BF16 = jnp.bfloat16
HIGHEST = lax.Precision.HIGHEST
SCALE = math.sqrt(math.log2(math.e))
NT = (((1,), (1,)), ((), ()))
TN = (((0,), (0,)), ((), ()))
BLOCK = 256
UNROLL = 8
TOTALS = 2
PIECE = 64
CLASS_ROWS = (32, 64, 96, 128)
PLACES = 56
SOURCES = 32
CHUNK = 4


def dot(left, right):
    return jnp.dot(left, right, preferred_element_type=F32)


def dot_nt(left, right):
    return lax.dot_general(left, right, NT, preferred_element_type=F32)


def dot_tn(left, right):
    return lax.dot_general(left, right, TN, preferred_element_type=F32)


def halves(value):
    high = value.astype(BF16)
    low = (value - high.astype(F32)).astype(BF16)
    return high, low


def dot3(left, right):
    left_high, left_low = halves(left)
    right_high, right_low = halves(right)
    return dot(left_high, right_high) + dot(left_high, right_low) + dot(left_low, right_high)


def grant(mebibytes):
    return pltpu.CompilerParams(vmem_limit_bytes=mebibytes * 1024 * 1024)


def iota(shape, dim):
    return lax.broadcasted_iota(jnp.int32, shape, dim)


def coords_of(ref, leaf):
    width = ref.shape[2]
    row = iota((8, width), 0)
    value = jnp.zeros((8, width), F32)
    for dim in range(3):
        line = jnp.broadcast_to(ref[dim, pl.ds(leaf, 1), :], (8, width))
        value = jnp.where(row == dim, line, value)
    return value


def pieces(coords):
    row = iota(coords.shape, 0)
    used = row < 3
    scaled = jnp.where(used, coords, 0.0) * SCALE
    high = scaled.astype(BF16).astype(F32)
    rest = scaled - high
    mid = rest.astype(BF16).astype(F32)
    low = (rest - mid).astype(BF16).astype(F32)
    norm = -0.5 * jnp.sum(scaled * scaled, axis=0, keepdims=True)
    norm_high = norm.astype(BF16).astype(F32)
    norm_rest = norm - norm_high
    norm_mid = norm_rest.astype(BF16).astype(F32)
    norm_low = norm_rest - norm_mid
    norms = jnp.where(row == 0, norm_high, jnp.where(row == 1, norm_mid, jnp.where(row == 2, norm_low, 0.0)))
    ones = jnp.where(used, 1.0, 0.0)
    return high, mid, low, norms, ones


def paired(first, second):
    return first + pltpu.roll(second, 4, 0)


def left_rows(parts):
    high, mid, low, norms, ones = parts
    return jnp.concatenate([paired(high, high), paired(mid, mid), paired(high, low), paired(ones, norms)], axis=0)


def right_rows(parts):
    high, mid, low, norms, ones = parts
    both = paired(high, mid)
    return jnp.concatenate([both, both, paired(low, high), paired(norms, ones)], axis=0)


def weight_rows(weights):
    high = weights.astype(BF16).astype(F32)
    return [high, weights - high]


def feature_versions(rows):
    lower = iota(rows.shape, 1) < PIECE
    versions = []
    for half in range(2):
        alone = jnp.where(lower == (half == 0), rows, 0.0)
        versions.append((half, half, alone.astype(BF16)))
        versions.append((half, 1 - half, pltpu.roll(alone, PIECE, 1).astype(BF16)))
    return versions


def put_features(feature_ref, leaf, versions):
    for half, place, value in versions:
        feature_ref[place, 2 * leaf + half] = value


def put_pack(pack_ref, leaf, value):
    pack_ref[pl.ds(2 * leaf, 2)] = value.reshape(2, PIECE, 128)


def upward_kernel(
    level_count, points_ref, dens_ref, surface_ref, counts_ref, count_line_ref, up_ref, shift_ref, pack_ref, feature_ref, turned_ref,
    message_ref, send_ref, slab_ref, check_ref
):
    leaf_count, q_width, p_width = dens_ref.shape
    eq_width = surface_ref.shape[2]
    node_count = leaf_count // 8
    lane = iota((q_width, p_width), 1)
    row = iota((8, p_width), 0)

    def node_step(node, carry):
        leaves = [node * 8 + child for child in range(8)]
        counts = [counts_ref[leaf] for leaf in leaves]
        weights = [jnp.where(lane < count, dens_ref[leaf], 0.0) for leaf, count in zip(leaves, counts)]
        coords = [coords_of(points_ref, leaf) for leaf in leaves]
        surfaces = [left_rows(pieces(coords_of(surface_ref, leaf))) for leaf in leaves]
        parts = [pieces(value) for value in coords]
        rights = [right_rows(value) for value in parts]
        lists = [weight_rows(value) for value in weights]
        packs = [
            jnp.concatenate([left_rows(part)] + split + [right], axis=0).astype(BF16).T
            for part, split, right in zip(parts, lists, rights)
        ]
        blank = jnp.zeros((96, eq_width), F32)
        wides = [jnp.concatenate([blank, value], axis=0).astype(BF16) for value in surfaces]
        exponents = [dot(pack, wide) for pack, wide in zip(packs, wides)]
        values = [halves(jnp.exp2(value)) for value in exponents]
        rows = [jnp.concatenate(split, axis=0).astype(BF16) for split in lists]
        firsts = [dot(row, value[0]) for row, value in zip(rows, values)]
        seconds = [dot(row[:q_width], value[1]) for row, value in zip(rows, values)]
        fours = [jnp.concatenate(surfaces[first : first + 4], axis=0).astype(BF16).T for first in range(0, 8, 4)]
        versions = [feature_versions(right) for right in rights]
        for number, four in enumerate(fours):
            turned_ref[2 * node + number] = four
        for child, leaf in enumerate(leaves):
            message_ref[leaf, :q_width, :] = weights[child]
            message_ref[leaf, q_width:, :] = jnp.where(row == 3, counts[child].astype(F32), coords[child])
            put_pack(pack_ref, leaf, packs[child])
            put_features(feature_ref, leaf, versions[child])
            check = firsts[child][:q_width] + firsts[child][q_width:] + seconds[child]
            check_ref[child, pl.ds(pl.multiple_of(node * q_width, q_width), q_width), :] = check
        return carry

    lax.fori_loop(0, node_count, node_step, 0)

    node_eq = jnp.zeros((node_count * q_width, eq_width), F32)
    for child in range(8):
        node_eq = node_eq + dot3(dot3(check_ref[child], up_ref[...]), shift_ref[child])
    send_ref[: node_count * q_width, :] = node_eq.astype(BF16)
    slab_eq = jnp.zeros((q_width, eq_width), F32)
    for child in range(8):
        slab_eq = slab_eq + dot3(node_eq[child * q_width : (child + 1) * q_width], shift_ref[child])
    index = lax.axis_index("oct")
    slab = slab_eq
    start = node_count * q_width
    for level in range(level_count):
        slab = dot3(slab, shift_ref[jnp.right_shift(index, 3 * level) & 7])
        slab_ref[level * q_width : (level + 1) * q_width, :] = slab
        high, rest = halves(slab)
        for place, part in enumerate((high, rest)):
            first = start + (place * level_count + level) * q_width
            send_ref[first : first + q_width, :] = part
    start = start + 2 * level_count * q_width
    line = jnp.concatenate([count_line_ref[...].astype(F32), jnp.zeros((1, eq_width - leaf_count), F32)], axis=1)
    send_ref[start : start + 16, :] = jnp.broadcast_to(line, (16, eq_width)).astype(BF16)


def far_kernel(
    lower_ref, own_ref, upper_ref, vlist_ref, ulist_ref, table_hbm, out_ref, step_ref, piece_ref, item_ref, table_ref,
    tail_ref, wide_ref, total_ref, first_ref, sems
):
    node_count, type_count = vlist_ref.shape
    eq_width = own_ref.shape[1]
    q_width = out_ref.shape[0] // node_count
    lanes = node_count * q_width
    tile = 128 // q_width
    chunk = CHUNK
    chunk_rows = chunk * eq_width
    chunk_count = eq_width // chunk
    full = type_count // 128

    def copies_of(number):
        span = pl.ds(number * chunk_rows, chunk_rows)
        copies = []
        for part in range(full):
            source = table_hbm.at[span, pl.ds(part * 128, 128)]
            copies.append(pltpu.make_async_copy(source, table_ref.at[part, span], sems.at[number, part]))
        source = table_hbm.at[span, pl.ds(full * 128, type_count - full * 128)]
        copies.append(pltpu.make_async_copy(source, tail_ref.at[span], sems.at[number, full]))
        return copies

    for number in range(chunk_count):
        for copy in copies_of(number):
            copy.start()

    index = lax.axis_index("oct")
    repeat = (iota((q_width, 128), 1) % q_width == iota((q_width, 128), 0)).astype(BF16)
    for part, source in enumerate((lower_ref, own_ref, upper_ref)):
        for node in range(node_count):
            spread = dot_tn(source[node * q_width : (node + 1) * q_width, :], repeat)
            wide_ref[pl.ds(part * node_count + node, eq_width, stride=SOURCES), :] = spread
    for place in range(3 * node_count, SOURCES):
        wide_ref[pl.ds(place, eq_width, stride=SOURCES), :] = jnp.zeros((eq_width, 128), F32)

    ids = vlist_ref[...]
    places = jnp.where(ids >= 0, ids - (index - 1) * node_count, -1).astype(F32).astype(BF16)
    spread = (iota((node_count, lanes), 1) // SOURCES == iota((node_count, lanes), 0)).astype(BF16)
    wanted = dot_tn(places, spread)
    chosen = (wanted == (iota((type_count, lanes), 1) % SOURCES).astype(F32)).astype(F32)
    chosen_full = chosen[: full * 128].astype(BF16)
    chosen_tail = chosen[full * 128 :].astype(BF16)
    lane_node = iota((SOURCES, 128), 1) // q_width
    nothing = jnp.zeros((SOURCES, 128), F32)
    total_ref[...] = jnp.zeros_like(total_ref)

    leaf_count = ulist_ref.shape[1]
    start = own_ref.shape[0] - 16
    lines = [ref[start:, :].astype(F32)[:1, :leaf_count] for ref in (lower_ref, own_ref, upper_ref)]
    plan_of(ulist_ref, lines, step_ref, piece_ref, item_ref)

    def table_of(number):
        span = pl.ds(pl.multiple_of(number * chunk_rows, chunk_rows), chunk_rows)
        left = jnp.concatenate([table_ref[part, span, :] for part in range(full)], axis=1)
        return left, tail_ref[span, :]

    def first_product(left, tail):
        return dot(left, chosen_full) + dot(tail, chosen_tail)

    def second_product(number, summed):
        lefts, rights = [], []
        for step in range(chunk):
            value = summed[step * eq_width : (step + 1) * eq_width]
            high = value.astype(BF16).astype(F32)
            lefts.append(jnp.concatenate([high, value - high], axis=0).astype(BF16))
            row = number * chunk + step
            sent = wide_ref[pl.ds(pl.multiple_of(row * SOURCES, SOURCES), SOURCES), :]
            parts = [jnp.where(lane_node == place, sent, 0.0) for place in range(tile)]
            for node in range(node_count):
                line = [parts[node % tile] if place == node // tile else nothing for place in range(node_count // tile)]
                rights.append(jnp.concatenate(line, axis=1))
        product = dot(jnp.concatenate(lefts, axis=1), jnp.concatenate(rights, axis=0).astype(BF16))
        return product[:eq_width] + product[eq_width:]

    def wait_for(number):
        for copy in copies_of(number):
            copy.wait()

    wait_for(0)
    first_ref[...] = first_product(*table_of(0))

    def pair_step(pair, carry):
        number = 2 * pair
        wait_for(number + 1)
        pl.when(pair < chunk_count // 2 - 1)(lambda: wait_for(number + 2))
        ahead = table_of(number + 1)
        behind = table_of(jnp.minimum(number + 2, chunk_count - 1))
        summed = first_ref[...]
        middle = first_product(*ahead)
        total = second_product(number, summed)
        following = first_product(*behind)
        total = total + second_product(number + 1, middle)
        first_ref[...] = following
        total_ref[...] += total
        return carry

    lax.fori_loop(0, chunk_count // 2, pair_step, 0)
    out_ref[...] = total_ref[...].T


def near_kernel(
    step_ref, piece_ref, item_ref, own_hbm, own_feature_hbm, lower_ref, upper_ref, out_ref, pack_ref, feature_ref,
    *rest
):
    total_refs, sems = rest[:TOTALS], rest[TOTALS]
    leaf_count, q_width, p_width = out_ref.shape
    own = pl.ds(0, 2 * leaf_count)
    own_copy = pltpu.make_async_copy(own_hbm, pack_ref.at[own], sems.at[0])
    feature_copy = pltpu.make_async_copy(own_feature_hbm, feature_ref.at[:, own], sems.at[1])
    own_copy.start()
    feature_copy.start()
    pack_ref[6 * leaf_count] = jnp.zeros((PIECE, 128), BF16)
    for half in range(2):
        feature_ref[half, 6 * leaf_count] = jnp.zeros((32, 128), BF16)
    for total_ref in total_refs:
        total_ref[...] = jnp.zeros_like(total_ref)
    blank = jnp.zeros((32, p_width), F32)

    def pack_step(step, carry):
        chosen = [(step * 4 + part, side) for part in range(4) for side in range(2)]
        sources = (lower_ref, upper_ref)
        weights = [weight_rows(sources[side][leaf, :q_width, :]) for leaf, side in chosen]
        versions = [feature_versions(right_rows(pieces(sources[side][leaf, q_width:, :]))) for leaf, side in chosen]
        packs = [jnp.concatenate([blank] + value + [blank], axis=0).astype(BF16).T for value in weights]
        for (leaf, side), pack, version in zip(chosen, packs, versions):
            place = (1 + side) * leaf_count + leaf
            put_pack(pack_ref, place, pack)
            put_features(feature_ref, place, version)
        return carry

    lax.fori_loop(0, leaf_count // 4, pack_step, 0)
    own_copy.wait()
    feature_copy.wait()
    block_pieces = BLOCK // PIECE

    def items_of(step):
        first = step * UNROLL
        leaves = [item_ref[first + part] for part in range(UNROLL)]
        first = first * block_pieces
        pieces_of = [
            [piece_ref[first + part * block_pieces + number] for number in range(block_pieces)] for part in range(UNROLL)
        ]
        return list(zip(leaves, pieces_of))

    def sources_of(numbers):
        return jnp.concatenate([pack_ref[number] for number in numbers], axis=0)

    def features_of(numbers):
        tiles = []
        for tile in range(BLOCK // 128):
            tiles.append(feature_ref[0, numbers[2 * tile]] + feature_ref[1, numbers[2 * tile + 1]])
        return jnp.concatenate(tiles, axis=1)

    def targets_of(leaf, rows):
        first = 2 * jnp.minimum(leaf, leaf_count - 1)
        if rows <= PIECE:
            return pack_ref[first, :rows][:, :32]
        return jnp.concatenate([pack_ref[first][:, :32], pack_ref[first + 1, : rows - PIECE][:, :32]], axis=0)

    def run(rows, first, count):
        def blocks_step(step, carry):
            items = items_of(step)
            features = [features_of(numbers) for _, numbers in items]
            targets = [targets_of(leaf, rows) for leaf, _ in items]
            sources = [sources_of(numbers) for _, numbers in items]
            exponents = [dot(target, feature) for target, feature in zip(targets, features)]
            values = [jnp.exp2(value).astype(BF16) for value in exponents]
            products = []
            for part in range(0, UNROLL, 2):
                left = jnp.concatenate(values[part : part + 2], axis=0)
                both = dot(left, jnp.concatenate(sources[part : part + 2], axis=1))
                products += [both[:rows, :128], both[rows:, 128:]]
            for first in range(0, UNROLL, TOTALS):
                sums = [
                    total_refs[part][items[first + part][0], :rows] + products[first + part] for part in range(TOTALS)
                ]
                for part, value in enumerate(sums):
                    total_refs[part][items[first + part][0], :rows] = value
            return carry

        lax.fori_loop(first, first + count, blocks_step, 0)

    for number, rows in enumerate(CLASS_ROWS):
        run(rows, step_ref[0, 2 * number], step_ref[0, 2 * number + 1])

    def turn_step(step, carry):
        sums = [[total_ref[step * 8 + part] for total_ref in total_refs] for part in range(8)]
        turned = [sum(values[1:], values[0]).T for values in sums]
        for part, value in enumerate(turned):
            out_ref[step * 8 + part] = value[32 : 32 + q_width] + value[32 + q_width : 32 + 2 * q_width]
        return carry

    lax.fori_loop(0, leaf_count // 8, turn_step, 0)


def as_column(line):
    width = line.shape[1]
    wide = jnp.concatenate([line, jnp.zeros((1, 128 - width), F32)], axis=1) if width < 128 else line
    return jnp.broadcast_to(wide, (128, 128)).T[:width, :width]


def plan_of(ulist_ref, counts, step_ref, piece_ref, item_ref):
    slot_count, leaf_count = ulist_ref.shape
    index = lax.axis_index("oct")
    shape = (leaf_count, leaf_count)
    row, column = iota(shape, 0), iota(shape, 1)
    tables = [as_column(line) for line in counts]
    own = jnp.broadcast_to(counts[1], shape)
    before = (tables[1] < own) | ((tables[1] == own) & (row < column))
    rank = jnp.sum(jnp.where(before, 1.0, 0.0), axis=0, keepdims=True)
    rank_column = as_column(rank).astype(jnp.int32)
    rank_wide = jnp.broadcast_to(rank, shape).astype(jnp.int32)

    block_pieces = BLOCK // PIECE
    empty = 6 * leaf_count
    place_shape = (PLACES, leaf_count)
    place_row = iota(place_shape, 0)
    listed = jnp.full(place_shape, empty, jnp.int32)
    offset = jnp.zeros((1, leaf_count), jnp.int32)
    for slot in range(slot_count):
        side = 1 if slot == 0 else (0 if slot < 9 else (1 if slot < 18 else 2))
        ids = ulist_ref[slot : slot + 1, :]
        place = jnp.where(ids >= 0, ids - (index + (side - 1)) * leaf_count, 0)
        found = jnp.sum(jnp.where(row == place, tables[side], 0.0), axis=0, keepdims=True).astype(jnp.int32)
        length = lax.shift_right_logical(found + (PIECE - 1), PIECE.bit_length() - 1)
        length = jnp.where(ids >= 0, length, 0)
        start = (place + (1, 0, 2)[side] * leaf_count) * 2
        inside = (place_row >= offset) & (place_row < offset + length)
        listed = jnp.where(inside, start + place_row - offset, listed)
        offset = offset + length

    blocks = lax.shift_right_logical(offset + (block_pieces - 1), block_pieces.bit_length() - 1)
    blocks_column = as_column(blocks.astype(F32))
    own_class = lax.shift_right_logical(counts[1].astype(jnp.int32) - 1, 5)
    class_column = as_column(own_class.astype(F32)).astype(jnp.int32)
    earlier = (class_column == jnp.broadcast_to(own_class, shape)) & (rank_column < rank_wide)
    first = jnp.sum(jnp.where(earlier, blocks_column, 0.0), axis=0, keepdims=True).astype(jnp.int32)
    lane = iota((1, 128), 1)
    steps_line = jnp.zeros((1, 128), jnp.int32)
    start = jnp.ones((1, 1), jnp.int32)
    for number in range(len(CLASS_ROWS)):
        inside = jnp.where(own_class == number, blocks.astype(F32), 0.0)
        items = jnp.sum(inside, axis=1, keepdims=True).astype(jnp.int32)
        steps = lax.shift_right_logical(items + (UNROLL - 1), UNROLL.bit_length() - 1)
        first = first + jnp.where(own_class == number, start * UNROLL, 0)
        steps_line = jnp.where(lane == 2 * number, start, jnp.where(lane == 2 * number + 1, steps, steps_line))
        start = start + steps
    step_ref[...] = steps_line

    first_column = as_column(first.astype(F32))[:, :1].astype(jnp.int32)
    blocks_column = blocks_column[:, :1].astype(jnp.int32)
    high = lax.shift_right_logical(listed, 8).astype(F32)
    low = jnp.bitwise_and(listed, 255).astype(F32)
    parts = jnp.concatenate([high, low], axis=0).astype(BF16)
    chunk = 1024
    wide = (leaf_count, chunk)
    column = iota(wide, 1)
    leaf_row = iota(wide, 0).astype(F32)
    for number in range(block_pieces):
        entry = column + chunk * number
        after = lax.shift_right_logical(entry, block_pieces.bit_length() - 1) - first_column
        inside = (after >= 0) & (after < blocks_column)
        place = after * block_pieces + jnp.bitwise_and(entry, block_pieces - 1)
        place = jnp.sum(jnp.where(inside, place.astype(F32), 0.0), axis=0, keepdims=True).astype(jnp.int32)
        found = jnp.sum(jnp.where(inside, 1.0, 0.0), axis=0, keepdims=True)
        both = dot(parts, jnp.where(inside, 1.0, 0.0).astype(BF16))
        value = both[:PLACES] * 256.0 + both[PLACES:]
        value = jnp.sum(jnp.where(iota((PLACES, chunk), 0) == place, value, 0.0), axis=0, keepdims=True)
        value = jnp.where(found > 0.0, value, float(empty)).astype(jnp.int32)
        for line in range(8):
            piece_ref[8 * number + line : 8 * number + line + 1, :] = value[:, line * 128 : (line + 1) * 128]
    after = column - first_column
    inside = (after >= 0) & (after < blocks_column)
    leaf = jnp.sum(jnp.where(inside, leaf_row - leaf_count, 0.0), axis=0, keepdims=True).astype(jnp.int32) + leaf_count
    for line in range(8):
        item_ref[line : line + 1, :] = leaf[:, line * 128 : (line + 1) * 128]


def final_kernel(
    level_count, counts_ref, feature_ref, turned_ref, near_ref, far_ref, coarse_ref, shift_ref, down_ref, *rest
):
    top_refs, (out_ref, node_ref, down_leaf_ref) = rest[:level_count], rest[level_count:]
    leaf_count, q_width, p_width = out_ref.shape
    eq_width = far_ref.shape[1]
    node_count = leaf_count // 8
    index = lax.axis_index("oct")
    slab_local = jnp.zeros((q_width, eq_width), F32)
    for level, top_ref in enumerate(top_refs):
        slab_local = slab_local + dot3(top_ref[:q_width, :], coarse_ref[jnp.right_shift(index, 3 * level) & 7])
    for node in range(node_count):
        rows = slice(node * q_width, (node + 1) * q_width)
        node_ref[rows, :] = far_ref[rows, :] + dot3(slab_local, shift_ref[node])

    for child in range(8):
        down_leaf_ref[child] = dot3(dot3(node_ref[...], shift_ref[child]), down_ref[...])
    lane = iota((q_width, p_width), 1)

    def node_step(node, carry):
        leaves = [node * 8 + child for child in range(8)]
        features = []
        for leaf in leaves:
            features.append(feature_ref[0, 2 * leaf] + feature_ref[1, 2 * leaf + 1])
        turned = [turned_ref[2 * node + number] for number in range(2)]
        node_rows = pl.ds(pl.multiple_of(node * q_width, q_width), q_width)
        downs = [weight_rows(down_leaf_ref[child, node_rows, :]) for child in range(8)]
        nears = [near_ref[leaf] for leaf in leaves]
        blank = jnp.zeros((32, p_width), BF16)
        exponents = []
        for first in range(0, 8, 2):
            sides = []
            for child in (first, first + 1):
                lines = [features[child] if place == child % 4 else blank for place in range(4)]
                sides.append(jnp.concatenate(lines, axis=0))
            both = dot(turned[first // 4], jnp.concatenate(sides, axis=1))
            exponents += [both[:, :p_width], both[:, p_width:]]
        values = [halves(jnp.exp2(value)) for value in exponents]
        lefts = [jnp.concatenate(down, axis=0).astype(BF16) for down in downs]
        products = [dot(left, jnp.concatenate(value, axis=1)) for left, value in zip(lefts, values)]
        for child, leaf in enumerate(leaves):
            product = products[child]
            far = product[:q_width, :p_width] + product[q_width:, :p_width] + product[:q_width, p_width:]
            out_ref[leaf] = jnp.where(lane < counts_ref[leaf], far + nears[child], 0.0)
        return carry

    lax.fori_loop(0, node_count, node_step, 0)


def shifted(value, size):
    up = [(i, i + 1) for i in range(size - 1)]
    down = [(j, i) for i, j in up]
    return lax.ppermute(value, "oct", up), lax.ppermute(value, "oct", down)


def swapped(value, size, bit):
    return lax.ppermute(value, "oct", [(source, source ^ (1 << bit)) for source in range(size)])


def local(
    points,
    dens,
    surface,
    counts,
    ulist,
    vlist,
    up_inverse,
    down_inverse,
    shift_up,
    shift_down,
    coarse,
    translate,
):
    leaf_count, q_width, p_width = dens.shape
    eq_width = surface.shape[2]
    node_count, type_count = vlist.shape
    node_rows = node_count * q_width
    size = lax.axis_size("oct")
    bits = size.bit_length() - 1
    level_count = -(-bits // 3)
    level_rows = level_count * q_width
    index = lax.axis_index("oct")
    vmem = pl.BlockSpec(memory_space=pltpu.VMEM)
    smem = pl.BlockSpec(memory_space=pltpu.SMEM)
    hbm = pl.BlockSpec(memory_space=pl.ANY)
    params = grant(56)
    points = jnp.transpose(points, (1, 0, 2))
    surface = jnp.transpose(surface, (1, 0, 2))
    ulist = ulist.T
    table = jnp.transpose(translate, (1, 2, 0))

    pack, features, turned, message, send, slab = pl.pallas_call(
        lambda *refs: upward_kernel(level_count, *refs),
        out_shape=(
            jax.ShapeDtypeStruct((2 * leaf_count, PIECE, 128), BF16),
            jax.ShapeDtypeStruct((2, 2 * leaf_count, 32, p_width), BF16),
            jax.ShapeDtypeStruct((leaf_count // 4, eq_width, 128), BF16),
            jax.ShapeDtypeStruct((leaf_count, q_width + 8, p_width), F32),
            jax.ShapeDtypeStruct((node_rows + 2 * level_rows + 16, eq_width), BF16),
            jax.ShapeDtypeStruct((level_rows, eq_width), F32),
        ),
        in_specs=[vmem, vmem, vmem, smem, vmem, vmem, vmem],
        out_specs=(vmem,) * 6,
        scratch_shapes=[pltpu.VMEM((8, node_rows, eq_width), F32)],
        compiler_params=params,
        name="upward",
    )(points, dens, surface, counts, counts.reshape(1, leaf_count), up_inverse, shift_up)

    send_lower, send_upper = shifted(send, size)
    ends = slice(node_rows, node_rows + 2 * level_rows)
    partner = jnp.where(index & 1 == 1, send_lower[ends], send_upper[ends]).astype(F32)
    total = slab + (partner[:level_rows] + partner[level_rows:])
    message, total = lax.optimization_barrier((message, total))
    lower, upper = shifted(message, size)
    exchanges = [(level, bit) for level in range(level_count) for bit in range(max(1, 3 * level), min(3 * level + 3, bits))]
    tops = []

    def exchange(total, wanted):
        level, bit = wanted
        if level and bit == 3 * level:
            tops.append(total)
            total = total[q_width:]
        return total, swapped(total, size, bit)

    early, late = exchanges[:2], exchanges[2:]
    total, arrived = exchange(total, early[0])
    total = total + arrived
    total, arrived = exchange(total, early[1])
    send_lower, total = lax.optimization_barrier((send_lower, total))

    table = table.reshape(eq_width * eq_width, type_count)
    far_node, steps, piece_table, items = pl.pallas_call(
        far_kernel,
        out_shape=(
            jax.ShapeDtypeStruct((node_rows, eq_width), F32),
            jax.ShapeDtypeStruct((1, 128), jnp.int32),
            jax.ShapeDtypeStruct((32, 128), jnp.int32),
            jax.ShapeDtypeStruct((8, 128), jnp.int32),
        ),
        in_specs=[vmem, vmem, vmem, vmem, vmem, hbm],
        out_specs=(vmem,) * 4,
        scratch_shapes=[
            pltpu.VMEM((type_count // 128, eq_width * eq_width, 128), BF16),
            pltpu.VMEM((eq_width * eq_width, type_count % 128), BF16),
            pltpu.VMEM((eq_width * SOURCES, 128), F32),
            pltpu.VMEM((eq_width, node_rows), F32),
            pltpu.VMEM((CHUNK * eq_width, node_rows), F32),
            pltpu.SemaphoreType.DMA((eq_width // CHUNK, type_count // 128 + 1)),
        ],
        compiler_params=params,
        cost_estimate=pl.CostEstimate(flops=2 * 10**10, bytes_accessed=18 * 10**6, transcendentals=0),
        name="far",
    )(send_lower, send, send_upper, vlist, ulist, table)
    far_node, lower, upper = lax.optimization_barrier((far_node, lower, upper))

    far_node, total, arrived = lax.optimization_barrier((far_node, total, arrived))
    for wanted in late:
        total = total + arrived
        total, arrived = exchange(total, wanted)
    steps, total = lax.optimization_barrier((steps, total))
    near = pl.pallas_call(
        near_kernel,
        out_shape=jax.ShapeDtypeStruct((leaf_count, q_width, p_width), F32),
        in_specs=[smem, smem, smem, hbm, hbm, vmem, vmem],
        out_specs=vmem,
        scratch_shapes=[
            pltpu.VMEM((6 * leaf_count + 1, PIECE, 128), BF16),
            pltpu.VMEM((2, 6 * leaf_count + 1, 32, 128), BF16),
            *[pltpu.VMEM((leaf_count + 1, p_width, 128), F32)] * TOTALS,
            pltpu.SemaphoreType.DMA((2,)),
        ],
        compiler_params=params,
        cost_estimate=pl.CostEstimate(flops=3 * 10**10, bytes_accessed=10**7, transcendentals=0),
        name="near",
    )(steps, piece_table.reshape(-1), items.reshape(-1), pack, features, lower, upper)

    tops.append(total + arrived)
    return pl.pallas_call(
        lambda *refs: final_kernel(level_count, *refs),
        out_shape=jax.ShapeDtypeStruct((leaf_count, q_width, p_width), F32),
        in_specs=[smem] + [vmem] * (7 + len(tops)),
        out_specs=vmem,
        scratch_shapes=[
            pltpu.VMEM((node_rows, eq_width), F32),
            pltpu.VMEM((8, node_rows, eq_width), F32),
        ],
        compiler_params=params,
        name="final",
    )(counts, features, turned, near, far_node, coarse, shift_down, down_inverse, *tops)


def solution(mesh):
    placed = (
        P("oct", None, None),
        P("oct", None, None),
        P("oct", None, None),
        P("oct"),
        P("oct", None),
        P("oct", None),
        P(),
        P(),
        P(),
        P(),
        P(),
        P(),
    )
    return jax.shard_map(
        local, mesh=mesh, in_specs=placed, out_specs=P("oct", None, None), check_vma=False
    )
```

```python
import math

import jax
import jax.numpy as jnp
from jax import lax
from jax.experimental import pallas as pl
from jax.experimental.pallas import tpu as pltpu
from jax.sharding import PartitionSpec as P

F32 = jnp.float32
BF16 = jnp.bfloat16
HIGHEST = lax.Precision.HIGHEST
SCALE = math.sqrt(math.log2(math.e))
NT = (((1,), (1,)), ((), ()))
TN = (((0,), (0,)), ((), ()))
BLOCK = 256
UNROLL = 8
TOTALS = 2
PIECE = 64
CLASS_ROWS = (32, 64, 96, 128)
PLACES = 56
SOURCES = 32
CHUNK = 4
FIRST, SECOND = 16, 8


def dot(left, right):
    return jnp.dot(left, right, preferred_element_type=F32)


def dot_nt(left, right):
    return lax.dot_general(left, right, NT, preferred_element_type=F32)


def dot_tn(left, right):
    return lax.dot_general(left, right, TN, preferred_element_type=F32)


def halves(value):
    high = value.astype(BF16)
    low = (value - high.astype(F32)).astype(BF16)
    return high, low


def dot3(left, right):
    left_high, left_low = halves(left)
    right_high, right_low = halves(right)
    return dot(left_high, right_high) + dot(left_high, right_low) + dot(left_low, right_high)


def grant(mebibytes):
    return pltpu.CompilerParams(vmem_limit_bytes=mebibytes * 1024 * 1024)


def iota(shape, dim):
    return lax.broadcasted_iota(jnp.int32, shape, dim)


def coords_of(ref, leaf):
    width = ref.shape[2]
    row = iota((8, width), 0)
    value = jnp.zeros((8, width), F32)
    for dim in range(3):
        line = jnp.broadcast_to(ref[dim, pl.ds(leaf, 1), :], (8, width))
        value = jnp.where(row == dim, line, value)
    return value


def pieces(coords):
    row = iota(coords.shape, 0)
    used = row < 3
    scaled = jnp.where(used, coords, 0.0) * SCALE
    high = scaled.astype(BF16).astype(F32)
    rest = scaled - high
    mid = rest.astype(BF16).astype(F32)
    low = (rest - mid).astype(BF16).astype(F32)
    norm = -0.5 * jnp.sum(scaled * scaled, axis=0, keepdims=True)
    norm_high = norm.astype(BF16).astype(F32)
    norm_rest = norm - norm_high
    norm_mid = norm_rest.astype(BF16).astype(F32)
    norm_low = norm_rest - norm_mid
    norms = jnp.where(row == 0, norm_high, jnp.where(row == 1, norm_mid, jnp.where(row == 2, norm_low, 0.0)))
    ones = jnp.where(used, 1.0, 0.0)
    return high, mid, low, norms, ones


def paired(first, second):
    return first + pltpu.roll(second, 4, 0)


def left_rows(parts):
    high, mid, low, norms, ones = parts
    return jnp.concatenate([paired(high, high), paired(mid, mid), paired(high, low), paired(ones, norms)], axis=0)


def right_rows(parts):
    high, mid, low, norms, ones = parts
    both = paired(high, mid)
    return jnp.concatenate([both, both, paired(low, high), paired(norms, ones)], axis=0)


def weight_rows(weights):
    high = weights.astype(BF16).astype(F32)
    return [high, weights - high]


def feature_versions(rows):
    lower = iota(rows.shape, 1) < PIECE
    versions = []
    for half in range(2):
        alone = jnp.where(lower == (half == 0), rows, 0.0)
        versions.append((half, half, alone.astype(BF16)))
        versions.append((half, 1 - half, pltpu.roll(alone, PIECE, 1).astype(BF16)))
    return versions


def put_features(feature_ref, leaf, versions):
    for half, place, value in versions:
        feature_ref[place, 2 * leaf + half] = value


def put_pack(pack_ref, leaf, value):
    pack_ref[pl.ds(2 * leaf, 2)] = value.reshape(2, PIECE, 128)


def upward_kernel(
    level_count, points_ref, dens_ref, surface_ref, counts_ref, count_line_ref, up_ref, shift_ref, pack_hbm, feature_hbm, turned_hbm,
    message_hbm, send_ref, slab_ref, check_ref, pack_ref, feature_ref, turned_ref, message_ref, sems
):
    leaf_count, q_width, p_width = dens_ref.shape
    eq_width = surface_ref.shape[2]
    node_count = leaf_count // 8
    lane = iota((q_width, p_width), 1)
    row = iota((8, p_width), 0)

    def copies_of(node):
        leaves, pairs, fours = pl.ds(8 * node, 8), pl.ds(16 * node, 16), pl.ds(2 * node, 2)
        ends = [
            (pack_ref.at[pairs], pack_hbm.at[pairs]),
            (feature_ref.at[:, pairs], feature_hbm.at[:, pairs]),
            (turned_ref.at[fours], turned_hbm.at[fours]),
            (message_ref.at[leaves], message_hbm.at[leaves]),
        ]
        return [pltpu.make_async_copy(*end, sems.at[node, number]) for number, end in enumerate(ends)]

    def node_step(node, carry):
        leaves = [node * 8 + child for child in range(8)]
        counts = [counts_ref[leaf] for leaf in leaves]
        weights = [jnp.where(lane < count, dens_ref[leaf], 0.0) for leaf, count in zip(leaves, counts)]
        coords = [coords_of(points_ref, leaf) for leaf in leaves]
        surfaces = [left_rows(pieces(coords_of(surface_ref, leaf))) for leaf in leaves]
        parts = [pieces(value) for value in coords]
        rights = [right_rows(value) for value in parts]
        lists = [weight_rows(value) for value in weights]
        packs = [
            jnp.concatenate([left_rows(part)] + split + [right], axis=0).astype(BF16).T
            for part, split, right in zip(parts, lists, rights)
        ]
        blank = jnp.zeros((96, eq_width), F32)
        wides = [jnp.concatenate([blank, value], axis=0).astype(BF16) for value in surfaces]
        exponents = [dot(pack, wide) for pack, wide in zip(packs, wides)]
        values = [halves(jnp.exp2(value)) for value in exponents]
        rows = [jnp.concatenate(split, axis=0).astype(BF16) for split in lists]
        firsts = [dot(row, value[0]) for row, value in zip(rows, values)]
        seconds = [dot(row[:q_width], value[1]) for row, value in zip(rows, values)]
        fours = [jnp.concatenate(surfaces[first : first + 4], axis=0).astype(BF16).T for first in range(0, 8, 4)]
        versions = [feature_versions(right) for right in rights]
        for number, four in enumerate(fours):
            turned_ref[2 * node + number] = four
        for child, leaf in enumerate(leaves):
            message_ref[leaf, :q_width, :] = weights[child]
            message_ref[leaf, q_width:, :] = jnp.where(row == 3, counts[child].astype(F32), coords[child])
            put_pack(pack_ref, leaf, packs[child])
            put_features(feature_ref, leaf, versions[child])
            check = firsts[child][:q_width] + firsts[child][q_width:] + seconds[child]
            check_ref[child, pl.ds(pl.multiple_of(node * q_width, q_width), q_width), :] = check
        for copy in copies_of(node):
            copy.start()
        return carry

    lax.fori_loop(0, node_count, node_step, 0)

    node_eq = jnp.zeros((node_count * q_width, eq_width), F32)
    for child in range(8):
        node_eq = node_eq + dot3(dot3(check_ref[child], up_ref[...]), shift_ref[child])
    send_ref[: node_count * q_width, :] = node_eq.astype(BF16)
    slab_eq = jnp.zeros((q_width, eq_width), F32)
    for child in range(8):
        slab_eq = slab_eq + dot3(node_eq[child * q_width : (child + 1) * q_width], shift_ref[child])
    index = lax.axis_index("oct")
    slab = slab_eq
    start = node_count * q_width
    for level in range(level_count):
        slab = dot3(slab, shift_ref[jnp.right_shift(index, 3 * level) & 7])
        slab_ref[level * q_width : (level + 1) * q_width, :] = slab
        high, rest = halves(slab)
        for place, part in enumerate((high, rest)):
            first = start + (place * level_count + level) * q_width
            send_ref[first : first + q_width, :] = part
    start = start + 2 * level_count * q_width
    line = jnp.concatenate([count_line_ref[...].astype(F32), jnp.zeros((1, eq_width - leaf_count), F32)], axis=1)
    send_ref[start : start + 16, :] = jnp.broadcast_to(line, (16, eq_width)).astype(BF16)

    def wait_step(node, carry):
        for copy in copies_of(node):
            copy.wait()
        return carry

    lax.fori_loop(0, node_count, wait_step, 0)


def far_kernel(
    lower_ref, own_ref, upper_ref, vlist_ref, ulist_ref, table_hbm, out_ref, step_ref, piece_ref, item_ref, table_ref,
    tail_ref, wide_ref, total_ref, first_ref, sems
):
    node_count, type_count = vlist_ref.shape
    eq_width = own_ref.shape[1]
    q_width = out_ref.shape[0] // node_count
    lanes = node_count * q_width
    tile = 128 // q_width
    chunk = CHUNK
    chunk_rows = chunk * eq_width
    chunk_count = eq_width // chunk
    full = type_count // 128

    def copies_of(number):
        span = pl.ds(number * chunk_rows, chunk_rows)
        copies = []
        for part in range(full):
            source = table_hbm.at[span, pl.ds(part * 128, 128)]
            copies.append(pltpu.make_async_copy(source, table_ref.at[part, span], sems.at[number, part]))
        source = table_hbm.at[span, pl.ds(full * 128, type_count - full * 128)]
        copies.append(pltpu.make_async_copy(source, tail_ref.at[span], sems.at[number, full]))
        return copies

    for number in range(chunk_count):
        for copy in copies_of(number):
            copy.start()

    index = lax.axis_index("oct")
    repeat = (iota((q_width, 128), 1) % q_width == iota((q_width, 128), 0)).astype(BF16)
    for part, source in enumerate((lower_ref, own_ref, upper_ref)):
        for node in range(node_count):
            spread = dot_tn(source[node * q_width : (node + 1) * q_width, :], repeat)
            wide_ref[pl.ds(part * node_count + node, eq_width, stride=SOURCES), :] = spread
    for place in range(3 * node_count, SOURCES):
        wide_ref[pl.ds(place, eq_width, stride=SOURCES), :] = jnp.zeros((eq_width, 128), F32)

    ids = vlist_ref[...]
    places = jnp.where(ids >= 0, ids - (index - 1) * node_count, -1).astype(F32).astype(BF16)
    lane = iota((1, lanes), 1)
    second_half = jnp.bitwise_and(lane, 63)
    node_of = jnp.where(lane < 128, lane // FIRST, second_half // SECOND)
    source_of = jnp.where(lane < 128, lane % FIRST, FIRST + second_half % SECOND)
    spread = (jnp.broadcast_to(node_of, (node_count, lanes)) == iota((node_count, lanes), 0)).astype(BF16)
    wanted = dot_tn(places, spread)
    chosen = (wanted == source_of.astype(F32)).astype(F32)
    chosen_full = chosen[: full * 128].astype(BF16)
    chosen_tail = chosen[full * 128 :].astype(BF16)
    lane_node = iota((SOURCES, 128), 1) // q_width
    lower_lanes = iota((eq_width, 128), 1) < 64
    total_ref[...] = jnp.zeros_like(total_ref)

    leaf_count = ulist_ref.shape[1]
    start = own_ref.shape[0] - 16
    lines = [ref[start:, :].astype(F32)[:1, :leaf_count] for ref in (lower_ref, own_ref, upper_ref)]
    plan_of(ulist_ref, lines, step_ref, piece_ref, item_ref)

    def table_of(number):
        span = pl.ds(pl.multiple_of(number * chunk_rows, chunk_rows), chunk_rows)
        left = jnp.concatenate([table_ref[part, span, :] for part in range(full)], axis=1)
        return left, tail_ref[span, :]

    def first_product(left, tail):
        return dot(left, chosen_full) + dot(tail, chosen_tail)

    def block_rows(sents, first, count):
        lines = []
        for sent in sents:
            blank = jnp.zeros((count, 128), F32)
            for node in range(node_count):
                own = sent[node % tile][first : first + count]
                line = [own if place == node // tile else blank for place in range(node_count // tile)]
                lines.append(jnp.concatenate(line, axis=1))
        return lines

    def second_product(number, summed):
        lefts, rights = [], []
        for step in range(0, chunk, 2):
            sents = []
            for place in (step, step + 1):
                row = number * chunk + place
                sent = wide_ref[pl.ds(pl.multiple_of(row * SOURCES, SOURCES), SOURCES), :]
                sents.append([jnp.where(lane_node == part, sent, 0.0) for part in range(tile)])
            pair = [summed[place * eq_width : (place + 1) * eq_width] for place in (step, step + 1)]
            tiles = [pair[0][:, :128], pair[1][:, :128], jnp.where(lower_lanes, pair[0][:, 128:], pair[1][:, 128:])]
            for value in tiles:
                high = value.astype(BF16).astype(F32)
                lefts.append(jnp.concatenate([high, value - high], axis=0).astype(BF16))
            rights += block_rows(sents, 0, FIRST) + block_rows(sents, FIRST, SECOND)
        product = dot(jnp.concatenate(lefts, axis=1), jnp.concatenate(rights, axis=0).astype(BF16))
        return product[:eq_width] + product[eq_width:]

    def wait_for(number):
        for copy in copies_of(number):
            copy.wait()

    wait_for(0)
    first_ref[...] = first_product(*table_of(0))

    def pair_step(pair, carry):
        number = 2 * pair
        wait_for(number + 1)
        pl.when(pair < chunk_count // 2 - 1)(lambda: wait_for(number + 2))
        ahead = table_of(number + 1)
        behind = table_of(jnp.minimum(number + 2, chunk_count - 1))
        summed = first_ref[...]
        middle = first_product(*ahead)
        total = second_product(number, summed)
        following = first_product(*behind)
        total = total + second_product(number + 1, middle)
        first_ref[...] = following
        total_ref[...] += total
        return carry

    lax.fori_loop(0, chunk_count // 2, pair_step, 0)
    out_ref[...] = total_ref[...].T


def near_kernel(
    step_ref, piece_ref, item_ref, own_hbm, own_feature_hbm, lower_ref, upper_ref, out_ref, pack_ref, feature_ref,
    *rest
):
    total_refs, sems = rest[:TOTALS], rest[TOTALS]
    leaf_count, q_width, p_width = out_ref.shape
    own = pl.ds(0, 2 * leaf_count)
    own_copy = pltpu.make_async_copy(own_hbm, pack_ref.at[own], sems.at[0])
    feature_copy = pltpu.make_async_copy(own_feature_hbm, feature_ref.at[:, own], sems.at[1])
    own_copy.start()
    feature_copy.start()
    pack_ref[6 * leaf_count] = jnp.zeros((PIECE, 128), BF16)
    for half in range(2):
        feature_ref[half, 6 * leaf_count] = jnp.zeros((32, 128), BF16)
    for total_ref in total_refs:
        total_ref[...] = jnp.zeros_like(total_ref)
    blank = jnp.zeros((32, p_width), F32)

    def pack_step(step, carry):
        chosen = [(step * 4 + part, side) for part in range(4) for side in range(2)]
        sources = (lower_ref, upper_ref)
        weights = [weight_rows(sources[side][leaf, :q_width, :]) for leaf, side in chosen]
        versions = [feature_versions(right_rows(pieces(sources[side][leaf, q_width:, :]))) for leaf, side in chosen]
        packs = [jnp.concatenate([blank] + value + [blank], axis=0).astype(BF16).T for value in weights]
        for (leaf, side), pack, version in zip(chosen, packs, versions):
            place = (1 + side) * leaf_count + leaf
            put_pack(pack_ref, place, pack)
            put_features(feature_ref, place, version)
        return carry

    lax.fori_loop(0, leaf_count // 4, pack_step, 0)
    own_copy.wait()
    feature_copy.wait()
    block_pieces = BLOCK // PIECE

    def items_of(step):
        first = step * UNROLL
        leaves = [item_ref[first + part] for part in range(UNROLL)]
        first = first * block_pieces
        pieces_of = [
            [piece_ref[first + part * block_pieces + number] for number in range(block_pieces)] for part in range(UNROLL)
        ]
        return list(zip(leaves, pieces_of))

    def sources_of(numbers):
        return jnp.concatenate([pack_ref[number] for number in numbers], axis=0)

    def features_of(numbers):
        tiles = []
        for tile in range(BLOCK // 128):
            tiles.append(feature_ref[0, numbers[2 * tile]] + feature_ref[1, numbers[2 * tile + 1]])
        return jnp.concatenate(tiles, axis=1)

    def targets_of(leaf, rows):
        first = 2 * jnp.minimum(leaf, leaf_count - 1)
        if rows <= PIECE:
            return pack_ref[first, :rows][:, :32]
        return jnp.concatenate([pack_ref[first][:, :32], pack_ref[first + 1, : rows - PIECE][:, :32]], axis=0)

    def run(rows, first, count):
        def blocks_step(step, carry):
            items = items_of(step)
            features = [features_of(numbers) for _, numbers in items]
            targets = [targets_of(leaf, rows) for leaf, _ in items]
            sources = [sources_of(numbers) for _, numbers in items]
            exponents = [dot(target, feature) for target, feature in zip(targets, features)]
            values = [jnp.exp2(value).astype(BF16) for value in exponents]
            products = []
            for part in range(0, UNROLL, 2):
                left = jnp.concatenate(values[part : part + 2], axis=0)
                both = dot(left, jnp.concatenate(sources[part : part + 2], axis=1))
                products += [both[:rows, :128], both[rows:, 128:]]
            for first in range(0, UNROLL, TOTALS):
                sums = [
                    total_refs[part][items[first + part][0], :rows] + products[first + part] for part in range(TOTALS)
                ]
                for part, value in enumerate(sums):
                    total_refs[part][items[first + part][0], :rows] = value
            return carry

        lax.fori_loop(first, first + count, blocks_step, 0)

    for number, rows in enumerate(CLASS_ROWS):
        run(rows, step_ref[0, 2 * number], step_ref[0, 2 * number + 1])

    def turn_step(step, carry):
        sums = [[total_ref[step * 8 + part] for total_ref in total_refs] for part in range(8)]
        turned = [sum(values[1:], values[0]).T for values in sums]
        for part, value in enumerate(turned):
            out_ref[step * 8 + part] = value[32 : 32 + q_width] + value[32 + q_width : 32 + 2 * q_width]
        return carry

    lax.fori_loop(0, leaf_count // 8, turn_step, 0)


def as_column(line):
    width = line.shape[1]
    wide = jnp.concatenate([line, jnp.zeros((1, 128 - width), F32)], axis=1) if width < 128 else line
    return jnp.broadcast_to(wide, (128, 128)).T[:width, :width]


def plan_of(ulist_ref, counts, step_ref, piece_ref, item_ref):
    slot_count, leaf_count = ulist_ref.shape
    index = lax.axis_index("oct")
    shape = (leaf_count, leaf_count)
    row, column = iota(shape, 0), iota(shape, 1)
    tables = [as_column(line) for line in counts]
    own = jnp.broadcast_to(counts[1], shape)
    before = (tables[1] < own) | ((tables[1] == own) & (row < column))
    rank = jnp.sum(jnp.where(before, 1.0, 0.0), axis=0, keepdims=True)
    rank_column = as_column(rank).astype(jnp.int32)
    rank_wide = jnp.broadcast_to(rank, shape).astype(jnp.int32)

    block_pieces = BLOCK // PIECE
    empty = 6 * leaf_count
    place_shape = (PLACES, leaf_count)
    place_row = iota(place_shape, 0)
    listed = jnp.full(place_shape, empty, jnp.int32)
    offset = jnp.zeros((1, leaf_count), jnp.int32)
    for slot in range(slot_count):
        side = 1 if slot == 0 else (0 if slot < 9 else (1 if slot < 18 else 2))
        ids = ulist_ref[slot : slot + 1, :]
        place = jnp.where(ids >= 0, ids - (index + (side - 1)) * leaf_count, 0)
        found = jnp.sum(jnp.where(row == place, tables[side], 0.0), axis=0, keepdims=True).astype(jnp.int32)
        length = lax.shift_right_logical(found + (PIECE - 1), PIECE.bit_length() - 1)
        length = jnp.where(ids >= 0, length, 0)
        start = (place + (1, 0, 2)[side] * leaf_count) * 2
        inside = (place_row >= offset) & (place_row < offset + length)
        listed = jnp.where(inside, start + place_row - offset, listed)
        offset = offset + length

    blocks = lax.shift_right_logical(offset + (block_pieces - 1), block_pieces.bit_length() - 1)
    blocks_column = as_column(blocks.astype(F32))
    own_class = lax.shift_right_logical(counts[1].astype(jnp.int32) - 1, 5)
    class_column = as_column(own_class.astype(F32)).astype(jnp.int32)
    earlier = (class_column == jnp.broadcast_to(own_class, shape)) & (rank_column < rank_wide)
    first = jnp.sum(jnp.where(earlier, blocks_column, 0.0), axis=0, keepdims=True).astype(jnp.int32)
    lane = iota((1, 128), 1)
    steps_line = jnp.zeros((1, 128), jnp.int32)
    start = jnp.ones((1, 1), jnp.int32)
    for number in range(len(CLASS_ROWS)):
        inside = jnp.where(own_class == number, blocks.astype(F32), 0.0)
        items = jnp.sum(inside, axis=1, keepdims=True).astype(jnp.int32)
        steps = lax.shift_right_logical(items + (UNROLL - 1), UNROLL.bit_length() - 1)
        first = first + jnp.where(own_class == number, start * UNROLL, 0)
        steps_line = jnp.where(lane == 2 * number, start, jnp.where(lane == 2 * number + 1, steps, steps_line))
        start = start + steps
    step_ref[...] = steps_line

    first_column = as_column(first.astype(F32))[:, :1].astype(jnp.int32)
    blocks_column = blocks_column[:, :1].astype(jnp.int32)
    high = lax.shift_right_logical(listed, 8).astype(F32)
    low = jnp.bitwise_and(listed, 255).astype(F32)
    parts = jnp.concatenate([high, low], axis=0).astype(BF16)
    chunk = 1024
    wide = (leaf_count, chunk)
    column = iota(wide, 1)
    leaf_row = iota(wide, 0).astype(F32)
    for number in range(block_pieces):
        entry = column + chunk * number
        after = lax.shift_right_logical(entry, block_pieces.bit_length() - 1) - first_column
        inside = (after >= 0) & (after < blocks_column)
        place = after * block_pieces + jnp.bitwise_and(entry, block_pieces - 1)
        place = jnp.sum(jnp.where(inside, place.astype(F32), 0.0), axis=0, keepdims=True).astype(jnp.int32)
        found = jnp.sum(jnp.where(inside, 1.0, 0.0), axis=0, keepdims=True)
        both = dot(parts, jnp.where(inside, 1.0, 0.0).astype(BF16))
        value = both[:PLACES] * 256.0 + both[PLACES:]
        value = jnp.sum(jnp.where(iota((PLACES, chunk), 0) == place, value, 0.0), axis=0, keepdims=True)
        value = jnp.where(found > 0.0, value, float(empty)).astype(jnp.int32)
        for line in range(8):
            piece_ref[8 * number + line : 8 * number + line + 1, :] = value[:, line * 128 : (line + 1) * 128]
    after = column - first_column
    inside = (after >= 0) & (after < blocks_column)
    leaf = jnp.sum(jnp.where(inside, leaf_row - leaf_count, 0.0), axis=0, keepdims=True).astype(jnp.int32) + leaf_count
    for line in range(8):
        item_ref[line : line + 1, :] = leaf[:, line * 128 : (line + 1) * 128]


def final_kernel(
    level_count, counts_ref, feature_ref, turned_ref, near_ref, far_ref, coarse_ref, shift_ref, down_ref, *rest
):
    top_refs, (out_ref, node_ref, down_leaf_ref) = rest[:level_count], rest[level_count:]
    leaf_count, q_width, p_width = out_ref.shape
    eq_width = far_ref.shape[1]
    node_count = leaf_count // 8
    index = lax.axis_index("oct")
    slab_local = jnp.zeros((q_width, eq_width), F32)
    for level, top_ref in enumerate(top_refs):
        slab_local = slab_local + dot3(top_ref[:q_width, :], coarse_ref[jnp.right_shift(index, 3 * level) & 7])
    for node in range(node_count):
        rows = slice(node * q_width, (node + 1) * q_width)
        node_ref[rows, :] = far_ref[rows, :] + dot3(slab_local, shift_ref[node])

    for child in range(8):
        down_leaf_ref[child] = dot3(dot3(node_ref[...], shift_ref[child]), down_ref[...])
    lane = iota((q_width, p_width), 1)

    def node_step(node, carry):
        leaves = [node * 8 + child for child in range(8)]
        features = []
        for leaf in leaves:
            features.append(feature_ref[0, 2 * leaf] + feature_ref[1, 2 * leaf + 1])
        turned = [turned_ref[2 * node + number] for number in range(2)]
        node_rows = pl.ds(pl.multiple_of(node * q_width, q_width), q_width)
        downs = [weight_rows(down_leaf_ref[child, node_rows, :]) for child in range(8)]
        nears = [near_ref[leaf] for leaf in leaves]
        blank = jnp.zeros((32, p_width), BF16)
        exponents = []
        for first in range(0, 8, 2):
            sides = []
            for child in (first, first + 1):
                lines = [features[child] if place == child % 4 else blank for place in range(4)]
                sides.append(jnp.concatenate(lines, axis=0))
            both = dot(turned[first // 4], jnp.concatenate(sides, axis=1))
            exponents += [both[:, :p_width], both[:, p_width:]]
        values = [halves(jnp.exp2(value)) for value in exponents]
        lefts = [jnp.concatenate(down, axis=0).astype(BF16) for down in downs]
        products = [dot(left, jnp.concatenate(value, axis=1)) for left, value in zip(lefts, values)]
        for child, leaf in enumerate(leaves):
            product = products[child]
            far = product[:q_width, :p_width] + product[q_width:, :p_width] + product[:q_width, p_width:]
            out_ref[leaf] = jnp.where(lane < counts_ref[leaf], far + nears[child], 0.0)
        return carry

    lax.fori_loop(0, node_count, node_step, 0)


def shifted(value, size):
    up = [(i, i + 1) for i in range(size - 1)]
    down = [(j, i) for i, j in up]
    return lax.ppermute(value, "oct", up), lax.ppermute(value, "oct", down)


def swapped(value, size, bit):
    return lax.ppermute(value, "oct", [(source, source ^ (1 << bit)) for source in range(size)])


def local(
    points,
    dens,
    surface,
    counts,
    ulist,
    vlist,
    up_inverse,
    down_inverse,
    shift_up,
    shift_down,
    coarse,
    translate,
):
    leaf_count, q_width, p_width = dens.shape
    eq_width = surface.shape[2]
    node_count, type_count = vlist.shape
    node_rows = node_count * q_width
    size = lax.axis_size("oct")
    bits = size.bit_length() - 1
    level_count = -(-bits // 3)
    level_rows = level_count * q_width
    index = lax.axis_index("oct")
    vmem = pl.BlockSpec(memory_space=pltpu.VMEM)
    smem = pl.BlockSpec(memory_space=pltpu.SMEM)
    hbm = pl.BlockSpec(memory_space=pl.ANY)
    params = grant(56)
    points = jnp.transpose(points, (1, 0, 2))
    surface = jnp.transpose(surface, (1, 0, 2))
    ulist = ulist.T
    table = jnp.transpose(translate, (1, 2, 0))

    pack, features, turned, message, send, slab = pl.pallas_call(
        lambda *refs: upward_kernel(level_count, *refs),
        out_shape=(
            jax.ShapeDtypeStruct((2 * leaf_count, PIECE, 128), BF16),
            jax.ShapeDtypeStruct((2, 2 * leaf_count, 32, p_width), BF16),
            jax.ShapeDtypeStruct((leaf_count // 4, eq_width, 128), BF16),
            jax.ShapeDtypeStruct((leaf_count, q_width + 8, p_width), F32),
            jax.ShapeDtypeStruct((node_rows + 2 * level_rows + 16, eq_width), BF16),
            jax.ShapeDtypeStruct((level_rows, eq_width), F32),
        ),
        in_specs=[vmem, vmem, vmem, smem, vmem, vmem, vmem],
        out_specs=(hbm,) * 4 + (vmem,) * 2,
        scratch_shapes=[
            pltpu.VMEM((8, node_rows, eq_width), F32),
            pltpu.VMEM((2 * leaf_count, PIECE, 128), BF16),
            pltpu.VMEM((2, 2 * leaf_count, 32, p_width), BF16),
            pltpu.VMEM((leaf_count // 4, eq_width, 128), BF16),
            pltpu.VMEM((leaf_count, q_width + 8, p_width), F32),
            pltpu.SemaphoreType.DMA((node_count, 4)),
        ],
        compiler_params=params,
        name="upward",
    )(points, dens, surface, counts, counts.reshape(1, leaf_count), up_inverse, shift_up)

    send_lower, send_upper = shifted(send, size)
    ends = slice(node_rows, node_rows + 2 * level_rows)
    partner = jnp.where(index & 1 == 1, send_lower[ends], send_upper[ends]).astype(F32)
    total = slab + (partner[:level_rows] + partner[level_rows:])
    message, total = lax.optimization_barrier((message, total))
    lower, upper = shifted(message, size)
    exchanges = [(level, bit) for level in range(level_count) for bit in range(max(1, 3 * level), min(3 * level + 3, bits))]
    tops = []

    def exchange(total, wanted):
        level, bit = wanted
        if level and bit == 3 * level:
            tops.append(total)
            total = total[q_width:]
        return total, swapped(total, size, bit)

    early, late = exchanges[:2], exchanges[2:]
    total, arrived = exchange(total, early[0])
    total = total + arrived
    total, arrived = exchange(total, early[1])
    send_lower, total = lax.optimization_barrier((send_lower, total))

    table = table.reshape(eq_width * eq_width, type_count)
    far_node, steps, piece_table, items = pl.pallas_call(
        far_kernel,
        out_shape=(
            jax.ShapeDtypeStruct((node_rows, eq_width), F32),
            jax.ShapeDtypeStruct((1, 128), jnp.int32),
            jax.ShapeDtypeStruct((32, 128), jnp.int32),
            jax.ShapeDtypeStruct((8, 128), jnp.int32),
        ),
        in_specs=[vmem, vmem, vmem, vmem, vmem, hbm],
        out_specs=(vmem,) * 4,
        scratch_shapes=[
            pltpu.VMEM((type_count // 128, eq_width * eq_width, 128), BF16),
            pltpu.VMEM((eq_width * eq_width, type_count % 128), BF16),
            pltpu.VMEM((eq_width * SOURCES, 128), F32),
            pltpu.VMEM((eq_width, node_rows), F32),
            pltpu.VMEM((CHUNK * eq_width, node_rows), F32),
            pltpu.SemaphoreType.DMA((eq_width // CHUNK, type_count // 128 + 1)),
        ],
        compiler_params=params,
        cost_estimate=pl.CostEstimate(flops=2 * 10**10, bytes_accessed=18 * 10**6, transcendentals=0),
        name="far",
    )(send_lower, send, send_upper, vlist, ulist, table)
    far_node, lower, upper = lax.optimization_barrier((far_node, lower, upper))

    far_node, total, arrived = lax.optimization_barrier((far_node, total, arrived))
    for wanted in late:
        total = total + arrived
        total, arrived = exchange(total, wanted)
    steps, total = lax.optimization_barrier((steps, total))
    near = pl.pallas_call(
        near_kernel,
        out_shape=jax.ShapeDtypeStruct((leaf_count, q_width, p_width), F32),
        in_specs=[smem, smem, smem, hbm, hbm, vmem, vmem],
        out_specs=vmem,
        scratch_shapes=[
            pltpu.VMEM((6 * leaf_count + 1, PIECE, 128), BF16),
            pltpu.VMEM((2, 6 * leaf_count + 1, 32, 128), BF16),
            *[pltpu.VMEM((leaf_count + 1, p_width, 128), F32)] * TOTALS,
            pltpu.SemaphoreType.DMA((2,)),
        ],
        compiler_params=params,
        cost_estimate=pl.CostEstimate(flops=3 * 10**10, bytes_accessed=10**7, transcendentals=0),
        name="near",
    )(steps, piece_table.reshape(-1), items.reshape(-1), pack, features, lower, upper)

    tops.append(total + arrived)
    return pl.pallas_call(
        lambda *refs: final_kernel(level_count, *refs),
        out_shape=jax.ShapeDtypeStruct((leaf_count, q_width, p_width), F32),
        in_specs=[smem] + [vmem] * (7 + len(tops)),
        out_specs=vmem,
        scratch_shapes=[
            pltpu.VMEM((node_rows, eq_width), F32),
            pltpu.VMEM((8, node_rows, eq_width), F32),
        ],
        compiler_params=params,
        name="final",
    )(counts, features, turned, near, far_node, coarse, shift_down, down_inverse, *tops)


def solution(mesh):
    placed = (
        P("oct", None, None),
        P("oct", None, None),
        P("oct", None, None),
        P("oct"),
        P("oct", None),
        P("oct", None),
        P(),
        P(),
        P(),
        P(),
        P(),
        P(),
    )
    return jax.shard_map(
        local, mesh=mesh, in_specs=placed, out_specs=P("oct", None, None), check_vma=False
    )
```

```python
import math

import jax
import jax.numpy as jnp
from jax import lax
from jax.experimental import pallas as pl
from jax.experimental.pallas import tpu as pltpu
from jax.sharding import PartitionSpec as P

F32 = jnp.float32
BF16 = jnp.bfloat16
HIGHEST = lax.Precision.HIGHEST
SCALE = math.sqrt(math.log2(math.e))
NT = (((1,), (1,)), ((), ()))
TN = (((0,), (0,)), ((), ()))
BLOCK = 256
UNROLL = 8
TOTALS = 2
PIECE = 64
CLASS_ROWS = (32, 64, 96, 128)
PLACES = 56
SOURCES = 32
CHUNK = 4
FIRST, SECOND = 16, 8


def dot(left, right):
    return jnp.dot(left, right, preferred_element_type=F32)


def dot_nt(left, right):
    return lax.dot_general(left, right, NT, preferred_element_type=F32)


def dot_tn(left, right):
    return lax.dot_general(left, right, TN, preferred_element_type=F32)


def halves(value):
    high = value.astype(BF16)
    low = (value - high.astype(F32)).astype(BF16)
    return high, low


def dot3(left, right):
    left_high, left_low = halves(left)
    right_high, right_low = halves(right)
    return dot(left_high, right_high) + dot(left_high, right_low) + dot(left_low, right_high)


def grant(mebibytes):
    return pltpu.CompilerParams(vmem_limit_bytes=mebibytes * 1024 * 1024)


def iota(shape, dim):
    return lax.broadcasted_iota(jnp.int32, shape, dim)


def coords_of(ref, leaf):
    width = ref.shape[2]
    row = iota((8, width), 0)
    value = jnp.zeros((8, width), F32)
    for dim in range(3):
        line = jnp.broadcast_to(ref[dim, pl.ds(leaf, 1), :], (8, width))
        value = jnp.where(row == dim, line, value)
    return value


def pieces(coords):
    row = iota(coords.shape, 0)
    used = row < 3
    scaled = jnp.where(used, coords, 0.0) * SCALE
    high = scaled.astype(BF16).astype(F32)
    rest = scaled - high
    mid = rest.astype(BF16).astype(F32)
    low = (rest - mid).astype(BF16).astype(F32)
    norm = -0.5 * jnp.sum(scaled * scaled, axis=0, keepdims=True)
    norm_high = norm.astype(BF16).astype(F32)
    norm_rest = norm - norm_high
    norm_mid = norm_rest.astype(BF16).astype(F32)
    norm_low = norm_rest - norm_mid
    norms = jnp.where(row == 0, norm_high, jnp.where(row == 1, norm_mid, jnp.where(row == 2, norm_low, 0.0)))
    ones = jnp.where(used, 1.0, 0.0)
    return high, mid, low, norms, ones


def paired(first, second):
    return first + pltpu.roll(second, 4, 0)


def left_rows(parts):
    high, mid, low, norms, ones = parts
    return jnp.concatenate([paired(high, high), paired(mid, mid), paired(high, low), paired(ones, norms)], axis=0)


def right_rows(parts):
    high, mid, low, norms, ones = parts
    both = paired(high, mid)
    return jnp.concatenate([both, both, paired(low, high), paired(norms, ones)], axis=0)


def weight_rows(weights):
    high = weights.astype(BF16).astype(F32)
    return [high, weights - high]


def feature_versions(rows):
    lower = iota(rows.shape, 1) < PIECE
    versions = []
    for half in range(2):
        alone = jnp.where(lower == (half == 0), rows, 0.0)
        versions.append((half, half, alone.astype(BF16)))
        versions.append((half, 1 - half, pltpu.roll(alone, PIECE, 1).astype(BF16)))
    return versions


def put_features(feature_ref, leaf, versions):
    for half, place, value in versions:
        feature_ref[place, 2 * leaf + half] = value


def put_pack(pack_ref, leaf, value):
    pack_ref[pl.ds(2 * leaf, 2)] = value.reshape(2, PIECE, 128)


def upward_kernel(
    level_count, points_ref, dens_ref, surface_ref, counts_ref, count_line_ref, up_ref, shift_ref, pack_ref, send_ref,
    slab_ref, check_ref
):
    leaf_count, q_width, p_width = dens_ref.shape
    eq_width = surface_ref.shape[2]
    node_count = leaf_count // 8
    lane = iota((q_width, p_width), 1)

    def node_step(node, carry):
        leaves = [node * 8 + child for child in range(8)]
        counts = [counts_ref[leaf] for leaf in leaves]
        weights = [jnp.where(lane < count, dens_ref[leaf], 0.0) for leaf, count in zip(leaves, counts)]
        coords = [coords_of(points_ref, leaf) for leaf in leaves]
        surfaces = [left_rows(pieces(coords_of(surface_ref, leaf))) for leaf in leaves]
        parts = [pieces(value) for value in coords]
        rights = [right_rows(value) for value in parts]
        lists = [weight_rows(value) for value in weights]
        packs = [
            jnp.concatenate([left_rows(part)] + split + [right], axis=0).astype(BF16).T
            for part, split, right in zip(parts, lists, rights)
        ]
        blank = jnp.zeros((96, eq_width), F32)
        wides = [jnp.concatenate([blank, value], axis=0).astype(BF16) for value in surfaces]
        exponents = [dot(pack, wide) for pack, wide in zip(packs, wides)]
        values = [halves(jnp.exp2(value)) for value in exponents]
        rows = [jnp.concatenate(split, axis=0).astype(BF16) for split in lists]
        firsts = [dot(row, value[0]) for row, value in zip(rows, values)]
        seconds = [dot(row[:q_width], value[1]) for row, value in zip(rows, values)]
        for child, leaf in enumerate(leaves):
            put_pack(pack_ref, leaf, packs[child])
            check = firsts[child][:q_width] + firsts[child][q_width:] + seconds[child]
            check_ref[child, pl.ds(pl.multiple_of(node * q_width, q_width), q_width), :] = check
        return carry

    lax.fori_loop(0, node_count, node_step, 0)

    node_eq = jnp.zeros((node_count * q_width, eq_width), F32)
    for child in range(8):
        node_eq = node_eq + dot3(dot3(check_ref[child], up_ref[...]), shift_ref[child])
    send_ref[: node_count * q_width, :] = node_eq.astype(BF16)
    slab_eq = jnp.zeros((q_width, eq_width), F32)
    for child in range(8):
        slab_eq = slab_eq + dot3(node_eq[child * q_width : (child + 1) * q_width], shift_ref[child])
    index = lax.axis_index("oct")
    slab = slab_eq
    start = node_count * q_width
    for level in range(level_count):
        slab = dot3(slab, shift_ref[jnp.right_shift(index, 3 * level) & 7])
        slab_ref[level * q_width : (level + 1) * q_width, :] = slab
        high, rest = halves(slab)
        for place, part in enumerate((high, rest)):
            first = start + (place * level_count + level) * q_width
            send_ref[first : first + q_width, :] = part
    start = start + 2 * level_count * q_width
    line = jnp.concatenate([count_line_ref[...].astype(F32), jnp.zeros((1, eq_width - leaf_count), F32)], axis=1)
    send_ref[start : start + 16, :] = jnp.broadcast_to(line, (16, eq_width)).astype(BF16)


def outline_kernel(
    points_ref, dens_ref, surface_ref, counts_ref, order_ref, feature_ref, turned_ref, message_ref
):
    leaf_count, q_width, p_width = dens_ref.shape
    lane = iota((q_width, p_width), 1)
    row = iota((8, p_width), 0)

    def node_step(node, carry):
        leaves = [node * 8 + child for child in range(8)]
        counts = [counts_ref[leaf] for leaf in leaves]
        weights = [jnp.where(lane < count, dens_ref[leaf], 0.0) for leaf, count in zip(leaves, counts)]
        coords = [coords_of(points_ref, leaf) for leaf in leaves]
        surfaces = [left_rows(pieces(coords_of(surface_ref, leaf))) for leaf in leaves]
        versions = [feature_versions(right_rows(pieces(value))) for value in coords]
        fours = [jnp.concatenate(surfaces[first : first + 4], axis=0).astype(BF16).T for first in range(0, 8, 4)]
        for number, four in enumerate(fours):
            turned_ref[2 * node + number] = four
        for child, leaf in enumerate(leaves):
            message_ref[leaf, :q_width, :] = weights[child]
            message_ref[leaf, q_width:, :] = jnp.where(row == 3, counts[child].astype(F32), coords[child])
            put_features(feature_ref, leaf, versions[child])
        return carry

    lax.fori_loop(0, leaf_count // 8, node_step, 0)


def far_kernel(
    lower_ref, own_ref, upper_ref, vlist_ref, ulist_ref, table_hbm, out_ref, step_ref, piece_ref, item_ref, table_ref,
    tail_ref, wide_ref, total_ref, first_ref, sems
):
    node_count, type_count = vlist_ref.shape
    eq_width = own_ref.shape[1]
    q_width = out_ref.shape[0] // node_count
    lanes = node_count * q_width
    tile = 128 // q_width
    chunk = CHUNK
    chunk_rows = chunk * eq_width
    chunk_count = eq_width // chunk
    full = type_count // 128

    def copies_of(number):
        span = pl.ds(number * chunk_rows, chunk_rows)
        copies = []
        for part in range(full):
            source = table_hbm.at[span, pl.ds(part * 128, 128)]
            copies.append(pltpu.make_async_copy(source, table_ref.at[part, span], sems.at[number, part]))
        source = table_hbm.at[span, pl.ds(full * 128, type_count - full * 128)]
        copies.append(pltpu.make_async_copy(source, tail_ref.at[span], sems.at[number, full]))
        return copies

    for number in range(chunk_count):
        for copy in copies_of(number):
            copy.start()

    index = lax.axis_index("oct")
    repeat = (iota((q_width, 128), 1) % q_width == iota((q_width, 128), 0)).astype(BF16)
    for part, source in enumerate((lower_ref, own_ref, upper_ref)):
        for node in range(node_count):
            spread = dot_tn(source[node * q_width : (node + 1) * q_width, :], repeat)
            wide_ref[pl.ds(part * node_count + node, eq_width, stride=SOURCES), :] = spread
    for place in range(3 * node_count, SOURCES):
        wide_ref[pl.ds(place, eq_width, stride=SOURCES), :] = jnp.zeros((eq_width, 128), F32)

    ids = vlist_ref[...]
    places = jnp.where(ids >= 0, ids - (index - 1) * node_count, -1).astype(F32).astype(BF16)
    lane = iota((1, lanes), 1)
    second_half = jnp.bitwise_and(lane, 63)
    node_of = jnp.where(lane < 128, lane // FIRST, second_half // SECOND)
    source_of = jnp.where(lane < 128, lane % FIRST, FIRST + second_half % SECOND)
    spread = (jnp.broadcast_to(node_of, (node_count, lanes)) == iota((node_count, lanes), 0)).astype(BF16)
    wanted = dot_tn(places, spread)
    chosen = (wanted == source_of.astype(F32)).astype(F32)
    chosen_full = chosen[: full * 128].astype(BF16)
    chosen_tail = chosen[full * 128 :].astype(BF16)
    lane_node = iota((SOURCES, 128), 1) // q_width
    lower_lanes = iota((eq_width, 128), 1) < 64
    total_ref[...] = jnp.zeros_like(total_ref)

    leaf_count = ulist_ref.shape[1]
    start = own_ref.shape[0] - 16
    lines = [ref[start:, :].astype(F32)[:1, :leaf_count] for ref in (lower_ref, own_ref, upper_ref)]
    plan_of(ulist_ref, lines, step_ref, piece_ref, item_ref)

    def table_of(number):
        span = pl.ds(pl.multiple_of(number * chunk_rows, chunk_rows), chunk_rows)
        left = jnp.concatenate([table_ref[part, span, :] for part in range(full)], axis=1)
        return left, tail_ref[span, :]

    def first_product(left, tail):
        return dot(left, chosen_full) + dot(tail, chosen_tail)

    def block_rows(sents, first, count):
        lines = []
        for sent in sents:
            blank = jnp.zeros((count, 128), F32)
            for node in range(node_count):
                own = sent[node % tile][first : first + count]
                line = [own if place == node // tile else blank for place in range(node_count // tile)]
                lines.append(jnp.concatenate(line, axis=1))
        return lines

    def second_product(number, summed):
        lefts, rights = [], []
        for step in range(0, chunk, 2):
            sents = []
            for place in (step, step + 1):
                row = number * chunk + place
                sent = wide_ref[pl.ds(pl.multiple_of(row * SOURCES, SOURCES), SOURCES), :]
                sents.append([jnp.where(lane_node == part, sent, 0.0) for part in range(tile)])
            pair = [summed[place * eq_width : (place + 1) * eq_width] for place in (step, step + 1)]
            tiles = [pair[0][:, :128], pair[1][:, :128], jnp.where(lower_lanes, pair[0][:, 128:], pair[1][:, 128:])]
            for value in tiles:
                high = value.astype(BF16).astype(F32)
                lefts.append(jnp.concatenate([high, value - high], axis=0).astype(BF16))
            rights += block_rows(sents, 0, FIRST) + block_rows(sents, FIRST, SECOND)
        product = dot(jnp.concatenate(lefts, axis=1), jnp.concatenate(rights, axis=0).astype(BF16))
        return product[:eq_width] + product[eq_width:]

    def wait_for(number):
        for copy in copies_of(number):
            copy.wait()

    wait_for(0)
    first_ref[...] = first_product(*table_of(0))

    def pair_step(pair, carry):
        number = 2 * pair
        wait_for(number + 1)
        pl.when(pair < chunk_count // 2 - 1)(lambda: wait_for(number + 2))
        ahead = table_of(number + 1)
        behind = table_of(jnp.minimum(number + 2, chunk_count - 1))
        summed = first_ref[...]
        middle = first_product(*ahead)
        total = second_product(number, summed)
        following = first_product(*behind)
        total = total + second_product(number + 1, middle)
        first_ref[...] = following
        total_ref[...] += total
        return carry

    lax.fori_loop(0, chunk_count // 2, pair_step, 0)
    out_ref[...] = total_ref[...].T


def near_kernel(
    step_ref, piece_ref, item_ref, own_hbm, own_feature_hbm, lower_ref, upper_ref, out_ref, pack_ref, feature_ref,
    *rest
):
    total_refs, sems = rest[:TOTALS], rest[TOTALS]
    leaf_count, q_width, p_width = out_ref.shape
    own = pl.ds(0, 2 * leaf_count)
    own_copy = pltpu.make_async_copy(own_hbm, pack_ref.at[own], sems.at[0])
    feature_copy = pltpu.make_async_copy(own_feature_hbm, feature_ref.at[:, own], sems.at[1])
    own_copy.start()
    feature_copy.start()
    pack_ref[6 * leaf_count] = jnp.zeros((PIECE, 128), BF16)
    for half in range(2):
        feature_ref[half, 6 * leaf_count] = jnp.zeros((32, 128), BF16)
    for total_ref in total_refs:
        total_ref[...] = jnp.zeros_like(total_ref)
    def pack_step(step, carry):
        chosen = [(step * 4 + part, side) for side in range(2) for part in range(4)]
        sources = (lower_ref, upper_ref)
        weights = [weight_rows(sources[side][leaf, :q_width, :]) for leaf, side in chosen]
        versions = [feature_versions(right_rows(pieces(sources[side][leaf, q_width:, :]))) for leaf, side in chosen]
        packs = []
        for part in range(0, len(chosen), 2):
            (high, low), (next_high, next_low) = weights[part : part + 2]
            both = jnp.concatenate([next_low, high, low, next_high], axis=0).astype(BF16).T
            packs += [both, pltpu.roll(both.astype(F32), 64, 1).astype(BF16)]
        for (leaf, side), pack, version in zip(chosen, packs, versions):
            place = (1 + side) * leaf_count + leaf
            put_pack(pack_ref, place, pack)
            put_features(feature_ref, place, version)
        return carry

    lax.fori_loop(0, leaf_count // 4, pack_step, 0)
    own_copy.wait()
    feature_copy.wait()
    block_pieces = BLOCK // PIECE

    def items_of(step):
        first = step * UNROLL
        leaves = [item_ref[first + part] for part in range(UNROLL)]
        first = first * block_pieces
        pieces_of = [
            [piece_ref[first + part * block_pieces + number] for number in range(block_pieces)] for part in range(UNROLL)
        ]
        return list(zip(leaves, pieces_of))

    def sources_of(numbers):
        return jnp.concatenate([pack_ref[number] for number in numbers], axis=0)

    def features_of(numbers):
        tiles = []
        for tile in range(BLOCK // 128):
            tiles.append(feature_ref[0, numbers[2 * tile]] + feature_ref[1, numbers[2 * tile + 1]])
        return jnp.concatenate(tiles, axis=1)

    def targets_of(leaf, rows):
        first = 2 * jnp.minimum(leaf, leaf_count - 1)
        if rows <= PIECE:
            return pack_ref[first, :rows][:, :32]
        return jnp.concatenate([pack_ref[first][:, :32], pack_ref[first + 1, : rows - PIECE][:, :32]], axis=0)

    def run(rows, first, count):
        def blocks_step(step, carry):
            items = items_of(step)
            features = [features_of(numbers) for _, numbers in items]
            targets = [targets_of(leaf, rows) for leaf, _ in items]
            sources = [sources_of(numbers) for _, numbers in items]
            exponents = [dot(target, feature) for target, feature in zip(targets, features)]
            values = [jnp.exp2(value).astype(BF16) for value in exponents]
            products = []
            for part in range(0, UNROLL, 2):
                left = jnp.concatenate(values[part : part + 2], axis=0)
                both = dot(left, jnp.concatenate(sources[part : part + 2], axis=1))
                products += [both[:rows, :128], both[rows:, 128:]]
            for first in range(0, UNROLL, TOTALS):
                sums = [
                    total_refs[part][items[first + part][0], :rows] + products[first + part] for part in range(TOTALS)
                ]
                for part, value in enumerate(sums):
                    total_refs[part][items[first + part][0], :rows] = value
            return carry

        lax.fori_loop(first, first + count, blocks_step, 0)

    for number, rows in enumerate(CLASS_ROWS):
        run(rows, step_ref[0, 2 * number], step_ref[0, 2 * number + 1])

    def turn_step(step, carry):
        sums = [[total_ref[step * 8 + part] for total_ref in total_refs] for part in range(8)]
        sums = [sum(values[1:], values[0]) for values in sums]
        inner = (iota((p_width, 128), 1) >= 32) & (iota((p_width, 128), 1) < 96)
        for part in range(0, 8, 2):
            turned = jnp.where(inner, sums[part], pltpu.roll(sums[part + 1], 64, 1)).T
            out_ref[step * 8 + part] = turned[32 : 32 + q_width] + turned[32 + q_width : 32 + 2 * q_width]
            out_ref[step * 8 + part + 1] = turned[96 : 96 + q_width] + turned[:q_width]
        return carry

    lax.fori_loop(0, leaf_count // 8, turn_step, 0)


def as_column(line):
    width = line.shape[1]
    wide = jnp.concatenate([line, jnp.zeros((1, 128 - width), F32)], axis=1) if width < 128 else line
    return jnp.broadcast_to(wide, (128, 128)).T[:width, :width]


def plan_of(ulist_ref, counts, step_ref, piece_ref, item_ref):
    slot_count, leaf_count = ulist_ref.shape
    index = lax.axis_index("oct")
    shape = (leaf_count, leaf_count)
    row, column = iota(shape, 0), iota(shape, 1)
    tables = [as_column(line) for line in counts]
    own = jnp.broadcast_to(counts[1], shape)
    before = (tables[1] < own) | ((tables[1] == own) & (row < column))
    rank = jnp.sum(jnp.where(before, 1.0, 0.0), axis=0, keepdims=True)
    rank_column = as_column(rank).astype(jnp.int32)
    rank_wide = jnp.broadcast_to(rank, shape).astype(jnp.int32)

    block_pieces = BLOCK // PIECE
    empty = 6 * leaf_count
    place_shape = (PLACES, leaf_count)
    place_row = iota(place_shape, 0)
    listed = jnp.full(place_shape, empty, jnp.int32)
    offset = jnp.zeros((1, leaf_count), jnp.int32)
    for slot in range(slot_count):
        side = 1 if slot == 0 else (0 if slot < 9 else (1 if slot < 18 else 2))
        ids = ulist_ref[slot : slot + 1, :]
        place = jnp.where(ids >= 0, ids - (index + (side - 1)) * leaf_count, 0)
        found = jnp.sum(jnp.where(row == place, tables[side], 0.0), axis=0, keepdims=True).astype(jnp.int32)
        length = lax.shift_right_logical(found + (PIECE - 1), PIECE.bit_length() - 1)
        length = jnp.where(ids >= 0, length, 0)
        start = (place + (1, 0, 2)[side] * leaf_count) * 2
        inside = (place_row >= offset) & (place_row < offset + length)
        listed = jnp.where(inside, start + place_row - offset, listed)
        offset = offset + length

    blocks = lax.shift_right_logical(offset + (block_pieces - 1), block_pieces.bit_length() - 1)
    blocks_column = as_column(blocks.astype(F32))
    own_class = lax.shift_right_logical(counts[1].astype(jnp.int32) - 1, 5)
    class_column = as_column(own_class.astype(F32)).astype(jnp.int32)
    earlier = (class_column == jnp.broadcast_to(own_class, shape)) & (rank_column < rank_wide)
    first = jnp.sum(jnp.where(earlier, blocks_column, 0.0), axis=0, keepdims=True).astype(jnp.int32)
    lane = iota((1, 128), 1)
    steps_line = jnp.zeros((1, 128), jnp.int32)
    start = jnp.ones((1, 1), jnp.int32)
    for number in range(len(CLASS_ROWS)):
        inside = jnp.where(own_class == number, blocks.astype(F32), 0.0)
        items = jnp.sum(inside, axis=1, keepdims=True).astype(jnp.int32)
        steps = lax.shift_right_logical(items + (UNROLL - 1), UNROLL.bit_length() - 1)
        first = first + jnp.where(own_class == number, start * UNROLL, 0)
        steps_line = jnp.where(lane == 2 * number, start, jnp.where(lane == 2 * number + 1, steps, steps_line))
        start = start + steps
    step_ref[...] = steps_line

    first_column = as_column(first.astype(F32))[:, :1].astype(jnp.int32)
    blocks_column = blocks_column[:, :1].astype(jnp.int32)
    high = lax.shift_right_logical(listed, 8).astype(F32)
    low = jnp.bitwise_and(listed, 255).astype(F32)
    parts = jnp.concatenate([high, low], axis=0).astype(BF16)
    chunk = 1024
    wide = (leaf_count, chunk)
    column = iota(wide, 1)
    leaf_row = iota(wide, 0).astype(F32)
    for number in range(block_pieces):
        entry = column + chunk * number
        after = lax.shift_right_logical(entry, block_pieces.bit_length() - 1) - first_column
        inside = (after >= 0) & (after < blocks_column)
        place = after * block_pieces + jnp.bitwise_and(entry, block_pieces - 1)
        place = jnp.sum(jnp.where(inside, place.astype(F32), 0.0), axis=0, keepdims=True).astype(jnp.int32)
        found = jnp.sum(jnp.where(inside, 1.0, 0.0), axis=0, keepdims=True)
        both = dot(parts, jnp.where(inside, 1.0, 0.0).astype(BF16))
        value = both[:PLACES] * 256.0 + both[PLACES:]
        value = jnp.sum(jnp.where(iota((PLACES, chunk), 0) == place, value, 0.0), axis=0, keepdims=True)
        value = jnp.where(found > 0.0, value, float(empty)).astype(jnp.int32)
        for line in range(8):
            piece_ref[8 * number + line : 8 * number + line + 1, :] = value[:, line * 128 : (line + 1) * 128]
    after = column - first_column
    inside = (after >= 0) & (after < blocks_column)
    leaf = jnp.sum(jnp.where(inside, leaf_row - leaf_count, 0.0), axis=0, keepdims=True).astype(jnp.int32) + leaf_count
    for line in range(8):
        item_ref[line : line + 1, :] = leaf[:, line * 128 : (line + 1) * 128]


def final_kernel(
    level_count, counts_ref, feature_ref, turned_ref, near_ref, far_ref, coarse_ref, shift_ref, down_ref, *rest
):
    top_refs, (out_ref, node_ref, down_leaf_ref) = rest[:level_count], rest[level_count:]
    leaf_count, q_width, p_width = out_ref.shape
    eq_width = far_ref.shape[1]
    node_count = leaf_count // 8
    index = lax.axis_index("oct")
    slab_local = jnp.zeros((q_width, eq_width), F32)
    for level, top_ref in enumerate(top_refs):
        slab_local = slab_local + dot3(top_ref[:q_width, :], coarse_ref[jnp.right_shift(index, 3 * level) & 7])
    for node in range(node_count):
        rows = slice(node * q_width, (node + 1) * q_width)
        node_ref[rows, :] = far_ref[rows, :] + dot3(slab_local, shift_ref[node])

    for child in range(8):
        down_leaf_ref[child] = dot3(dot3(node_ref[...], shift_ref[child]), down_ref[...])
    lane = iota((q_width, p_width), 1)

    def node_step(node, carry):
        leaves = [node * 8 + child for child in range(8)]
        features = []
        for leaf in leaves:
            features.append(feature_ref[0, 2 * leaf] + feature_ref[1, 2 * leaf + 1])
        turned = [turned_ref[2 * node + number] for number in range(2)]
        node_rows = pl.ds(pl.multiple_of(node * q_width, q_width), q_width)
        downs = [weight_rows(down_leaf_ref[child, node_rows, :]) for child in range(8)]
        nears = [near_ref[leaf] for leaf in leaves]
        blank = jnp.zeros((32, p_width), BF16)
        exponents = []
        for first in range(0, 8, 2):
            sides = []
            for child in (first, first + 1):
                lines = [features[child] if place == child % 4 else blank for place in range(4)]
                sides.append(jnp.concatenate(lines, axis=0))
            both = dot(turned[first // 4], jnp.concatenate(sides, axis=1))
            exponents += [both[:, :p_width], both[:, p_width:]]
        values = [halves(jnp.exp2(value)) for value in exponents]
        lefts = [jnp.concatenate(down, axis=0).astype(BF16) for down in downs]
        products = [dot(left, jnp.concatenate(value, axis=1)) for left, value in zip(lefts, values)]
        for child, leaf in enumerate(leaves):
            product = products[child]
            far = product[:q_width, :p_width] + product[q_width:, :p_width] + product[:q_width, p_width:]
            out_ref[leaf] = jnp.where(lane < counts_ref[leaf], far + nears[child], 0.0)
        return carry

    lax.fori_loop(0, node_count, node_step, 0)


def shifted(value, size):
    up = [(i, i + 1) for i in range(size - 1)]
    down = [(j, i) for i, j in up]
    return lax.ppermute(value, "oct", up), lax.ppermute(value, "oct", down)


def swapped(value, size, bit):
    return lax.ppermute(value, "oct", [(source, source ^ (1 << bit)) for source in range(size)])


def local(
    points,
    dens,
    surface,
    counts,
    ulist,
    vlist,
    up_inverse,
    down_inverse,
    shift_up,
    shift_down,
    coarse,
    translate,
):
    leaf_count, q_width, p_width = dens.shape
    eq_width = surface.shape[2]
    node_count, type_count = vlist.shape
    node_rows = node_count * q_width
    size = lax.axis_size("oct")
    bits = size.bit_length() - 1
    level_count = -(-bits // 3)
    level_rows = level_count * q_width
    index = lax.axis_index("oct")
    vmem = pl.BlockSpec(memory_space=pltpu.VMEM)
    smem = pl.BlockSpec(memory_space=pltpu.SMEM)
    hbm = pl.BlockSpec(memory_space=pl.ANY)
    params = grant(56)
    points = jnp.transpose(points, (1, 0, 2))
    surface = jnp.transpose(surface, (1, 0, 2))
    ulist = ulist.T
    table = jnp.transpose(translate, (1, 2, 0))

    pack, send, slab = pl.pallas_call(
        lambda *refs: upward_kernel(level_count, *refs),
        out_shape=(
            jax.ShapeDtypeStruct((2 * leaf_count, PIECE, 128), BF16),
            jax.ShapeDtypeStruct((node_rows + 2 * level_rows + 16, eq_width), BF16),
            jax.ShapeDtypeStruct((level_rows, eq_width), F32),
        ),
        in_specs=[vmem, vmem, vmem, smem, vmem, vmem, vmem],
        out_specs=(vmem,) * 3,
        scratch_shapes=[pltpu.VMEM((8, node_rows, eq_width), F32)],
        compiler_params=params,
        name="upward",
    )(points, dens, surface, counts, counts.reshape(1, leaf_count), up_inverse, shift_up)

    send_lower, send_upper = shifted(send, size)
    features, turned, message = pl.pallas_call(
        outline_kernel,
        out_shape=(
            jax.ShapeDtypeStruct((2, 2 * leaf_count, 32, p_width), BF16),
            jax.ShapeDtypeStruct((leaf_count // 4, eq_width, 128), BF16),
            jax.ShapeDtypeStruct((leaf_count, q_width + 8, p_width), F32),
        ),
        in_specs=[vmem, vmem, vmem, smem, hbm],
        out_specs=(vmem,) * 3,
        compiler_params=params,
        cost_estimate=pl.CostEstimate(flops=4 * 10**9, bytes_accessed=10**7, transcendentals=0),
        name="outline",
    )(points, dens, surface, counts, slab)
    ends = slice(node_rows, node_rows + 2 * level_rows)
    partner = jnp.where(index & 1 == 1, send_lower[ends], send_upper[ends]).astype(F32)
    total = slab + (partner[:level_rows] + partner[level_rows:])
    message, total = lax.optimization_barrier((message, total))
    lower, upper = shifted(message, size)
    exchanges = [(level, bit) for level in range(level_count) for bit in range(max(1, 3 * level), min(3 * level + 3, bits))]
    tops = []

    def exchange(total, wanted):
        level, bit = wanted
        if level and bit == 3 * level:
            tops.append(total)
            total = total[q_width:]
        return total, swapped(total, size, bit)

    early, late = exchanges[:2], exchanges[2:]
    total, arrived = exchange(total, early[0])
    total = total + arrived
    total, arrived = exchange(total, early[1])
    send_lower, total = lax.optimization_barrier((send_lower, total))

    table = table.reshape(eq_width * eq_width, type_count)
    far_node, steps, piece_table, items = pl.pallas_call(
        far_kernel,
        out_shape=(
            jax.ShapeDtypeStruct((node_rows, eq_width), F32),
            jax.ShapeDtypeStruct((1, 128), jnp.int32),
            jax.ShapeDtypeStruct((32, 128), jnp.int32),
            jax.ShapeDtypeStruct((8, 128), jnp.int32),
        ),
        in_specs=[vmem, vmem, vmem, vmem, vmem, hbm],
        out_specs=(vmem,) * 4,
        scratch_shapes=[
            pltpu.VMEM((type_count // 128, eq_width * eq_width, 128), BF16),
            pltpu.VMEM((eq_width * eq_width, type_count % 128), BF16),
            pltpu.VMEM((eq_width * SOURCES, 128), F32),
            pltpu.VMEM((eq_width, node_rows), F32),
            pltpu.VMEM((CHUNK * eq_width, node_rows), F32),
            pltpu.SemaphoreType.DMA((eq_width // CHUNK, type_count // 128 + 1)),
        ],
        compiler_params=params,
        cost_estimate=pl.CostEstimate(flops=2 * 10**10, bytes_accessed=18 * 10**6, transcendentals=0),
        name="far",
    )(send_lower, send, send_upper, vlist, ulist, table)
    far_node, lower, upper = lax.optimization_barrier((far_node, lower, upper))

    far_node, total, arrived = lax.optimization_barrier((far_node, total, arrived))
    for wanted in late:
        total = total + arrived
        total, arrived = exchange(total, wanted)
    steps, total = lax.optimization_barrier((steps, total))
    near = pl.pallas_call(
        near_kernel,
        out_shape=jax.ShapeDtypeStruct((leaf_count, q_width, p_width), F32),
        in_specs=[smem, smem, smem, hbm, hbm, vmem, vmem],
        out_specs=vmem,
        scratch_shapes=[
            pltpu.VMEM((6 * leaf_count + 1, PIECE, 128), BF16),
            pltpu.VMEM((2, 6 * leaf_count + 1, 32, 128), BF16),
            *[pltpu.VMEM((leaf_count + 1, p_width, 128), F32)] * TOTALS,
            pltpu.SemaphoreType.DMA((2,)),
        ],
        compiler_params=params,
        cost_estimate=pl.CostEstimate(flops=3 * 10**10, bytes_accessed=10**7, transcendentals=0),
        name="near",
    )(steps, piece_table.reshape(-1), items.reshape(-1), pack, features, lower, upper)

    tops.append(total + arrived)
    return pl.pallas_call(
        lambda *refs: final_kernel(level_count, *refs),
        out_shape=jax.ShapeDtypeStruct((leaf_count, q_width, p_width), F32),
        in_specs=[smem] + [vmem] * (7 + len(tops)),
        out_specs=vmem,
        scratch_shapes=[
            pltpu.VMEM((node_rows, eq_width), F32),
            pltpu.VMEM((8, node_rows, eq_width), F32),
        ],
        compiler_params=params,
        name="final",
    )(counts, features, turned, near, far_node, coarse, shift_down, down_inverse, *tops)


def solution(mesh):
    placed = (
        P("oct", None, None),
        P("oct", None, None),
        P("oct", None, None),
        P("oct"),
        P("oct", None),
        P("oct", None),
        P(),
        P(),
        P(),
        P(),
        P(),
        P(),
    )
    return jax.shard_map(
        local, mesh=mesh, in_specs=placed, out_specs=P("oct", None, None), check_vma=False
    )
```

```python
import math

import jax
import jax.numpy as jnp
from jax import lax
from jax.experimental import pallas as pl
from jax.experimental.pallas import tpu as pltpu
from jax.sharding import PartitionSpec as P

F32 = jnp.float32
BF16 = jnp.bfloat16
HIGHEST = lax.Precision.HIGHEST
SCALE = math.sqrt(math.log2(math.e))
NT = (((1,), (1,)), ((), ()))
TN = (((0,), (0,)), ((), ()))
BLOCK = 256
UNROLL = 8
TOTALS = 2
PIECE = 64
CLASS_ROWS = (32, 64, 96, 128)
PLACES = 56
SOURCES = 32
CHUNK = 4
FIRST, SECOND = 16, 8


def dot(left, right):
    return jnp.dot(left, right, preferred_element_type=F32)


def dot_nt(left, right):
    return lax.dot_general(left, right, NT, preferred_element_type=F32)


def dot_tn(left, right):
    return lax.dot_general(left, right, TN, preferred_element_type=F32)


def halves(value):
    high = value.astype(BF16)
    low = (value - high.astype(F32)).astype(BF16)
    return high, low


def dot3(left, right):
    left_high, left_low = halves(left)
    right_high, right_low = halves(right)
    return dot(left_high, right_high) + dot(left_high, right_low) + dot(left_low, right_high)


def grant(mebibytes):
    return pltpu.CompilerParams(vmem_limit_bytes=mebibytes * 1024 * 1024)


def iota(shape, dim):
    return lax.broadcasted_iota(jnp.int32, shape, dim)


def coords_of(ref, leaf):
    width = ref.shape[2]
    row = iota((8, width), 0)
    value = jnp.zeros((8, width), F32)
    for dim in range(3):
        line = jnp.broadcast_to(ref[dim, pl.ds(leaf, 1), :], (8, width))
        value = jnp.where(row == dim, line, value)
    return value


def pieces(coords):
    row = iota(coords.shape, 0)
    used = row < 3
    scaled = jnp.where(used, coords, 0.0) * SCALE
    high = scaled.astype(BF16).astype(F32)
    rest = scaled - high
    mid = rest.astype(BF16).astype(F32)
    low = (rest - mid).astype(BF16).astype(F32)
    norm = -0.5 * jnp.sum(scaled * scaled, axis=0, keepdims=True)
    norm_high = norm.astype(BF16).astype(F32)
    norm_rest = norm - norm_high
    norm_mid = norm_rest.astype(BF16).astype(F32)
    norm_low = norm_rest - norm_mid
    norms = jnp.where(row == 0, norm_high, jnp.where(row == 1, norm_mid, jnp.where(row == 2, norm_low, 0.0)))
    ones = jnp.where(used, 1.0, 0.0)
    return high, mid, low, norms, ones


def paired(first, second):
    return first + pltpu.roll(second, 4, 0)


def left_rows(parts):
    high, mid, low, norms, ones = parts
    return jnp.concatenate([paired(high, high), paired(mid, mid), paired(high, low), paired(ones, norms)], axis=0)


def right_rows(parts):
    high, mid, low, norms, ones = parts
    both = paired(high, mid)
    return jnp.concatenate([both, both, paired(low, high), paired(norms, ones)], axis=0)


def weight_rows(weights):
    high = weights.astype(BF16).astype(F32)
    return [high, weights - high]


def feature_versions(rows):
    lower = iota(rows.shape, 1) < PIECE
    versions = []
    for half in range(2):
        alone = jnp.where(lower == (half == 0), rows, 0.0)
        versions.append((half, half, alone.astype(BF16)))
        versions.append((half, 1 - half, pltpu.roll(alone, PIECE, 1).astype(BF16)))
    return versions


def put_features(feature_ref, leaf, versions):
    for half, place, value in versions:
        feature_ref[place, 2 * leaf + half] = value


def put_pack(pack_ref, leaf, value):
    pack_ref[pl.ds(2 * leaf, 2)] = value.reshape(2, PIECE, 128)


def upward_kernel(
    level_count, points_ref, dens_ref, surface_ref, counts_ref, count_line_ref, up_ref, shift_ref, pack_ref, send_ref,
    slab_ref, check_ref
):
    leaf_count, q_width, p_width = dens_ref.shape
    eq_width = surface_ref.shape[2]
    node_count = leaf_count // 8
    lane = iota((q_width, p_width), 1)

    def node_step(node, carry):
        leaves = [node * 8 + child for child in range(8)]
        counts = [counts_ref[leaf] for leaf in leaves]
        weights = [jnp.where(lane < count, dens_ref[leaf], 0.0) for leaf, count in zip(leaves, counts)]
        coords = [coords_of(points_ref, leaf) for leaf in leaves]
        surfaces = [left_rows(pieces(coords_of(surface_ref, leaf))) for leaf in leaves]
        parts = [pieces(value) for value in coords]
        rights = [right_rows(value) for value in parts]
        lists = [weight_rows(value) for value in weights]
        packs = [
            jnp.concatenate([left_rows(part)] + split + [right], axis=0).astype(BF16).T
            for part, split, right in zip(parts, lists, rights)
        ]
        blank = jnp.zeros((96, eq_width), F32)
        wides = [jnp.concatenate([blank, value], axis=0).astype(BF16) for value in surfaces]
        exponents = [dot(pack, wide) for pack, wide in zip(packs, wides)]
        values = [halves(jnp.exp2(value)) for value in exponents]
        rows = [jnp.concatenate(split, axis=0).astype(BF16) for split in lists]
        firsts = [dot(row, value[0]) for row, value in zip(rows, values)]
        seconds = [dot(row[:q_width], value[1]) for row, value in zip(rows, values)]
        for child, leaf in enumerate(leaves):
            put_pack(pack_ref, leaf, packs[child])
            check = firsts[child][:q_width] + firsts[child][q_width:] + seconds[child]
            check_ref[child, pl.ds(pl.multiple_of(node * q_width, q_width), q_width), :] = check
        return carry

    lax.fori_loop(0, node_count, node_step, 0)

    node_eq = jnp.zeros((node_count * q_width, eq_width), F32)
    for child in range(8):
        node_eq = node_eq + dot3(dot3(check_ref[child], up_ref[...]), shift_ref[child])
    send_ref[: node_count * q_width, :] = node_eq.astype(BF16)
    slab_eq = jnp.zeros((q_width, eq_width), F32)
    for child in range(8):
        slab_eq = slab_eq + dot3(node_eq[child * q_width : (child + 1) * q_width], shift_ref[child])
    index = lax.axis_index("oct")
    slab = slab_eq
    start = node_count * q_width
    for level in range(level_count):
        slab = dot3(slab, shift_ref[jnp.right_shift(index, 3 * level) & 7])
        slab_ref[level * q_width : (level + 1) * q_width, :] = slab
        high, rest = halves(slab)
        for place, part in enumerate((high, rest)):
            first = start + (place * level_count + level) * q_width
            send_ref[first : first + q_width, :] = part
    start = start + 2 * level_count * q_width
    line = jnp.concatenate([count_line_ref[...].astype(F32), jnp.zeros((1, eq_width - leaf_count), F32)], axis=1)
    send_ref[start : start + 16, :] = jnp.broadcast_to(line, (16, eq_width)).astype(BF16)


def outline_kernel(
    points_ref, dens_ref, surface_ref, counts_ref, order_ref, feature_ref, turned_ref, message_ref
):
    leaf_count, q_width, p_width = dens_ref.shape
    lane = iota((q_width, p_width), 1)

    def node_step(node, carry):
        leaves = [node * 8 + child for child in range(8)]
        counts = [counts_ref[leaf] for leaf in leaves]
        weights = [jnp.where(lane < count, dens_ref[leaf], 0.0) for leaf, count in zip(leaves, counts)]
        coords = [coords_of(points_ref, leaf) for leaf in leaves]
        surfaces = [left_rows(pieces(coords_of(surface_ref, leaf))) for leaf in leaves]
        versions = [feature_versions(right_rows(pieces(value))) for value in coords]
        fours = [jnp.concatenate(surfaces[first : first + 4], axis=0).astype(BF16).T for first in range(0, 8, 4)]
        for number, four in enumerate(fours):
            turned_ref[2 * node + number] = four
        for child, leaf in enumerate(leaves):
            pair, side = node * 4 + child // 2, child % 2
            message_ref[pair, side * q_width : (side + 1) * q_width, :] = weights[child]
            put_features(feature_ref, leaf, versions[child])
        for number in range(4):
            message_ref[node * 4 + number, 2 * q_width :, :] = paired(coords[2 * number], coords[2 * number + 1])
        return carry

    lax.fori_loop(0, leaf_count // 8, node_step, 0)


def far_kernel(
    lower_ref, own_ref, upper_ref, vlist_ref, ulist_ref, table_hbm, out_ref, step_ref, piece_ref, item_ref, table_ref,
    tail_ref, wide_ref, total_ref, first_ref, sems
):
    node_count, type_count = vlist_ref.shape
    eq_width = own_ref.shape[1]
    q_width = out_ref.shape[0] // node_count
    lanes = node_count * q_width
    tile = 128 // q_width
    chunk = CHUNK
    chunk_rows = chunk * eq_width
    chunk_count = eq_width // chunk
    full = type_count // 128

    def copies_of(number):
        span = pl.ds(number * chunk_rows, chunk_rows)
        copies = []
        for part in range(full):
            source = table_hbm.at[span, pl.ds(part * 128, 128)]
            copies.append(pltpu.make_async_copy(source, table_ref.at[part, span], sems.at[number, part]))
        source = table_hbm.at[span, pl.ds(full * 128, type_count - full * 128)]
        copies.append(pltpu.make_async_copy(source, tail_ref.at[span], sems.at[number, full]))
        return copies

    for number in range(chunk_count):
        for copy in copies_of(number):
            copy.start()

    index = lax.axis_index("oct")
    repeat = (iota((q_width, 128), 1) % q_width == iota((q_width, 128), 0)).astype(BF16)
    for part, source in enumerate((lower_ref, own_ref, upper_ref)):
        for node in range(node_count):
            spread = dot_tn(source[node * q_width : (node + 1) * q_width, :], repeat)
            wide_ref[pl.ds(part * node_count + node, eq_width, stride=SOURCES), :] = spread
    for place in range(3 * node_count, SOURCES):
        wide_ref[pl.ds(place, eq_width, stride=SOURCES), :] = jnp.zeros((eq_width, 128), F32)

    ids = vlist_ref[...]
    places = jnp.where(ids >= 0, ids - (index - 1) * node_count, -1).astype(F32).astype(BF16)
    lane = iota((1, lanes), 1)
    second_half = jnp.bitwise_and(lane, 63)
    node_of = jnp.where(lane < 128, lane // FIRST, second_half // SECOND)
    source_of = jnp.where(lane < 128, lane % FIRST, FIRST + second_half % SECOND)
    spread = (jnp.broadcast_to(node_of, (node_count, lanes)) == iota((node_count, lanes), 0)).astype(BF16)
    wanted = dot_tn(places, spread)
    chosen = (wanted == source_of.astype(F32)).astype(F32)
    chosen_full = chosen[: full * 128].astype(BF16)
    chosen_tail = chosen[full * 128 :].astype(BF16)
    lane_node = iota((SOURCES, 128), 1) // q_width
    lower_lanes = iota((eq_width, 128), 1) < 64
    total_ref[...] = jnp.zeros_like(total_ref)

    leaf_count = ulist_ref.shape[1]
    start = own_ref.shape[0] - 16
    lines = [ref[start:, :].astype(F32)[:1, :leaf_count] for ref in (lower_ref, own_ref, upper_ref)]
    plan_of(ulist_ref, lines, step_ref, piece_ref, item_ref)

    def table_of(number):
        span = pl.ds(pl.multiple_of(number * chunk_rows, chunk_rows), chunk_rows)
        left = jnp.concatenate([table_ref[part, span, :] for part in range(full)], axis=1)
        return left, tail_ref[span, :]

    def first_product(left, tail):
        return dot(left, chosen_full) + dot(tail, chosen_tail)

    def block_rows(sents, first, count):
        lines = []
        for sent in sents:
            blank = jnp.zeros((count, 128), F32)
            for node in range(node_count):
                own = sent[node % tile][first : first + count]
                line = [own if place == node // tile else blank for place in range(node_count // tile)]
                lines.append(jnp.concatenate(line, axis=1))
        return lines

    def second_product(number, summed):
        lefts, rights = [], []
        for step in range(0, chunk, 2):
            sents = []
            for place in (step, step + 1):
                row = number * chunk + place
                sent = wide_ref[pl.ds(pl.multiple_of(row * SOURCES, SOURCES), SOURCES), :]
                sents.append([jnp.where(lane_node == part, sent, 0.0) for part in range(tile)])
            pair = [summed[place * eq_width : (place + 1) * eq_width] for place in (step, step + 1)]
            tiles = [pair[0][:, :128], pair[1][:, :128], jnp.where(lower_lanes, pair[0][:, 128:], pair[1][:, 128:])]
            for value in tiles:
                high = value.astype(BF16).astype(F32)
                lefts.append(jnp.concatenate([high, value - high], axis=0).astype(BF16))
            rights += block_rows(sents, 0, FIRST) + block_rows(sents, FIRST, SECOND)
        product = dot(jnp.concatenate(lefts, axis=1), jnp.concatenate(rights, axis=0).astype(BF16))
        return product[:eq_width] + product[eq_width:]

    def wait_for(number):
        for copy in copies_of(number):
            copy.wait()

    wait_for(0)
    first_ref[...] = first_product(*table_of(0))

    def pair_step(pair, carry):
        number = 2 * pair
        wait_for(number + 1)
        pl.when(pair < chunk_count // 2 - 1)(lambda: wait_for(number + 2))
        ahead = table_of(number + 1)
        behind = table_of(jnp.minimum(number + 2, chunk_count - 1))
        summed = first_ref[...]
        middle = first_product(*ahead)
        total = second_product(number, summed)
        following = first_product(*behind)
        total = total + second_product(number + 1, middle)
        first_ref[...] = following
        total_ref[...] += total
        return carry

    lax.fori_loop(0, chunk_count // 2, pair_step, 0)
    out_ref[...] = total_ref[...].T


def near_kernel(
    step_ref, piece_ref, item_ref, own_hbm, own_feature_hbm, lower_ref, upper_ref, out_ref, pack_ref, feature_ref,
    *rest
):
    total_refs, sems = rest[:TOTALS], rest[TOTALS]
    leaf_count, q_width, p_width = out_ref.shape
    own = pl.ds(0, 2 * leaf_count)
    own_copy = pltpu.make_async_copy(own_hbm, pack_ref.at[own], sems.at[0])
    feature_copy = pltpu.make_async_copy(own_feature_hbm, feature_ref.at[:, own], sems.at[1])
    own_copy.start()
    feature_copy.start()
    pack_ref[6 * leaf_count] = jnp.zeros((PIECE, 128), BF16)
    for half in range(2):
        feature_ref[half, 6 * leaf_count] = jnp.zeros((32, 128), BF16)
    for total_ref in total_refs:
        total_ref[...] = jnp.zeros_like(total_ref)
    def pack_step(step, carry):
        chosen = [(part, side) for side in range(2) for part in range(4)]
        sources = (lower_ref, upper_ref)
        weights, versions = [], []
        for part, side in chosen:
            place, half = step * 2 + part // 2, part % 2
            weights.append(weight_rows(sources[side][place, half * q_width : (half + 1) * q_width, :]))
            tail = sources[side][place, 2 * q_width :, :]
            tail = pltpu.roll(tail, 4, 0) if half else tail
            versions.append(feature_versions(right_rows(pieces(tail))))
        packs = []
        for part in range(0, len(chosen), 2):
            (high, low), (next_high, next_low) = weights[part : part + 2]
            both = jnp.concatenate([next_low, high, low, next_high], axis=0).astype(BF16).T
            packs += [both, pltpu.roll(both.astype(F32), 64, 1).astype(BF16)]
        for (part, side), pack, version in zip(chosen, packs, versions):
            place = (1 + side) * leaf_count + step * 4 + part
            put_pack(pack_ref, place, pack)
            put_features(feature_ref, place, version)
        return carry

    lax.fori_loop(0, leaf_count // 4, pack_step, 0)
    own_copy.wait()
    feature_copy.wait()
    block_pieces = BLOCK // PIECE

    def items_of(step):
        first = step * UNROLL
        leaves = [item_ref[first + part] for part in range(UNROLL)]
        first = first * block_pieces
        pieces_of = [
            [piece_ref[first + part * block_pieces + number] for number in range(block_pieces)] for part in range(UNROLL)
        ]
        return list(zip(leaves, pieces_of))

    def sources_of(numbers):
        return jnp.concatenate([pack_ref[number] for number in numbers], axis=0)

    def features_of(numbers):
        tiles = []
        for tile in range(BLOCK // 128):
            tiles.append(feature_ref[0, numbers[2 * tile]] + feature_ref[1, numbers[2 * tile + 1]])
        return jnp.concatenate(tiles, axis=1)

    def targets_of(leaf, rows):
        first = 2 * jnp.minimum(leaf, leaf_count - 1)
        if rows <= PIECE:
            return pack_ref[first, :rows][:, :32]
        return jnp.concatenate([pack_ref[first][:, :32], pack_ref[first + 1, : rows - PIECE][:, :32]], axis=0)

    def run(rows, first, count):
        def blocks_step(step, carry):
            items = items_of(step)
            features = [features_of(numbers) for _, numbers in items]
            targets = [targets_of(leaf, rows) for leaf, _ in items]
            sources = [sources_of(numbers) for _, numbers in items]
            exponents = [dot(target, feature) for target, feature in zip(targets, features)]
            values = [jnp.exp2(value).astype(BF16) for value in exponents]
            products = []
            for part in range(0, UNROLL, 2):
                left = jnp.concatenate(values[part : part + 2], axis=0)
                both = dot(left, jnp.concatenate(sources[part : part + 2], axis=1))
                products += [both[:rows, :128], both[rows:, 128:]]
            for first in range(0, UNROLL, TOTALS):
                sums = [
                    total_refs[part][items[first + part][0], :rows] + products[first + part] for part in range(TOTALS)
                ]
                for part, value in enumerate(sums):
                    total_refs[part][items[first + part][0], :rows] = value
            return carry

        lax.fori_loop(first, first + count, blocks_step, 0)

    for number, rows in enumerate(CLASS_ROWS):
        run(rows, step_ref[0, 2 * number], step_ref[0, 2 * number + 1])

    def turn_step(step, carry):
        sums = [[total_ref[step * 8 + part] for total_ref in total_refs] for part in range(8)]
        sums = [sum(values[1:], values[0]) for values in sums]
        inner = (iota((p_width, 128), 1) >= 32) & (iota((p_width, 128), 1) < 96)
        for part in range(0, 8, 2):
            turned = jnp.where(inner, sums[part], pltpu.roll(sums[part + 1], 64, 1)).T
            out_ref[step * 8 + part] = turned[32 : 32 + q_width] + turned[32 + q_width : 32 + 2 * q_width]
            out_ref[step * 8 + part + 1] = turned[96 : 96 + q_width] + turned[:q_width]
        return carry

    lax.fori_loop(0, leaf_count // 8, turn_step, 0)


def as_column(line):
    width = line.shape[1]
    wide = jnp.concatenate([line, jnp.zeros((1, 128 - width), F32)], axis=1) if width < 128 else line
    return jnp.broadcast_to(wide, (128, 128)).T[:width, :width]


def plan_of(ulist_ref, counts, step_ref, piece_ref, item_ref):
    slot_count, leaf_count = ulist_ref.shape
    index = lax.axis_index("oct")
    shape = (leaf_count, leaf_count)
    row, column = iota(shape, 0), iota(shape, 1)
    tables = [as_column(line) for line in counts]
    own = jnp.broadcast_to(counts[1], shape)
    before = (tables[1] < own) | ((tables[1] == own) & (row < column))
    rank = jnp.sum(jnp.where(before, 1.0, 0.0), axis=0, keepdims=True)
    rank_column = as_column(rank).astype(jnp.int32)
    rank_wide = jnp.broadcast_to(rank, shape).astype(jnp.int32)

    block_pieces = BLOCK // PIECE
    empty = 6 * leaf_count
    place_shape = (PLACES, leaf_count)
    place_row = iota(place_shape, 0)
    listed = jnp.full(place_shape, empty, jnp.int32)
    offset = jnp.zeros((1, leaf_count), jnp.int32)
    for slot in range(slot_count):
        side = 1 if slot == 0 else (0 if slot < 9 else (1 if slot < 18 else 2))
        ids = ulist_ref[slot : slot + 1, :]
        place = jnp.where(ids >= 0, ids - (index + (side - 1)) * leaf_count, 0)
        found = jnp.sum(jnp.where(row == place, tables[side], 0.0), axis=0, keepdims=True).astype(jnp.int32)
        length = lax.shift_right_logical(found + (PIECE - 1), PIECE.bit_length() - 1)
        length = jnp.where(ids >= 0, length, 0)
        start = (place + (1, 0, 2)[side] * leaf_count) * 2
        inside = (place_row >= offset) & (place_row < offset + length)
        listed = jnp.where(inside, start + place_row - offset, listed)
        offset = offset + length

    blocks = lax.shift_right_logical(offset + (block_pieces - 1), block_pieces.bit_length() - 1)
    blocks_column = as_column(blocks.astype(F32))
    own_class = lax.shift_right_logical(counts[1].astype(jnp.int32) - 1, 5)
    class_column = as_column(own_class.astype(F32)).astype(jnp.int32)
    earlier = (class_column == jnp.broadcast_to(own_class, shape)) & (rank_column < rank_wide)
    first = jnp.sum(jnp.where(earlier, blocks_column, 0.0), axis=0, keepdims=True).astype(jnp.int32)
    lane = iota((1, 128), 1)
    steps_line = jnp.zeros((1, 128), jnp.int32)
    start = jnp.ones((1, 1), jnp.int32)
    for number in range(len(CLASS_ROWS)):
        inside = jnp.where(own_class == number, blocks.astype(F32), 0.0)
        items = jnp.sum(inside, axis=1, keepdims=True).astype(jnp.int32)
        steps = lax.shift_right_logical(items + (UNROLL - 1), UNROLL.bit_length() - 1)
        first = first + jnp.where(own_class == number, start * UNROLL, 0)
        steps_line = jnp.where(lane == 2 * number, start, jnp.where(lane == 2 * number + 1, steps, steps_line))
        start = start + steps
    step_ref[...] = steps_line

    first_column = as_column(first.astype(F32))[:, :1].astype(jnp.int32)
    blocks_column = blocks_column[:, :1].astype(jnp.int32)
    high = lax.shift_right_logical(listed, 8).astype(F32)
    low = jnp.bitwise_and(listed, 255).astype(F32)
    parts = jnp.concatenate([high, low], axis=0).astype(BF16)
    chunk = 1024
    wide = (leaf_count, chunk)
    column = iota(wide, 1)
    leaf_row = iota(wide, 0).astype(F32)
    for number in range(block_pieces):
        entry = column + chunk * number
        after = lax.shift_right_logical(entry, block_pieces.bit_length() - 1) - first_column
        inside = (after >= 0) & (after < blocks_column)
        place = after * block_pieces + jnp.bitwise_and(entry, block_pieces - 1)
        place = jnp.sum(jnp.where(inside, place.astype(F32), 0.0), axis=0, keepdims=True).astype(jnp.int32)
        found = jnp.sum(jnp.where(inside, 1.0, 0.0), axis=0, keepdims=True)
        both = dot(parts, jnp.where(inside, 1.0, 0.0).astype(BF16))
        value = both[:PLACES] * 256.0 + both[PLACES:]
        value = jnp.sum(jnp.where(iota((PLACES, chunk), 0) == place, value, 0.0), axis=0, keepdims=True)
        value = jnp.where(found > 0.0, value, float(empty)).astype(jnp.int32)
        for line in range(8):
            piece_ref[8 * number + line : 8 * number + line + 1, :] = value[:, line * 128 : (line + 1) * 128]
    after = column - first_column
    inside = (after >= 0) & (after < blocks_column)
    leaf = jnp.sum(jnp.where(inside, leaf_row - leaf_count, 0.0), axis=0, keepdims=True).astype(jnp.int32) + leaf_count
    for line in range(8):
        item_ref[line : line + 1, :] = leaf[:, line * 128 : (line + 1) * 128]


def final_kernel(
    level_count, counts_ref, feature_ref, turned_ref, near_ref, far_ref, coarse_ref, shift_ref, down_ref, *rest
):
    top_refs, (out_ref, node_ref, down_leaf_ref) = rest[:level_count], rest[level_count:]
    leaf_count, q_width, p_width = out_ref.shape
    eq_width = far_ref.shape[1]
    node_count = leaf_count // 8
    index = lax.axis_index("oct")
    slab_local = jnp.zeros((q_width, eq_width), F32)
    for level, top_ref in enumerate(top_refs):
        slab_local = slab_local + dot3(top_ref[:q_width, :], coarse_ref[jnp.right_shift(index, 3 * level) & 7])
    for node in range(node_count):
        rows = slice(node * q_width, (node + 1) * q_width)
        node_ref[rows, :] = far_ref[rows, :] + dot3(slab_local, shift_ref[node])

    for child in range(8):
        down_leaf_ref[child] = dot3(dot3(node_ref[...], shift_ref[child]), down_ref[...])
    lane = iota((q_width, p_width), 1)

    def node_step(node, carry):
        leaves = [node * 8 + child for child in range(8)]
        features = []
        for leaf in leaves:
            features.append(feature_ref[0, 2 * leaf] + feature_ref[1, 2 * leaf + 1])
        turned = [turned_ref[2 * node + number] for number in range(2)]
        node_rows = pl.ds(pl.multiple_of(node * q_width, q_width), q_width)
        downs = [weight_rows(down_leaf_ref[child, node_rows, :]) for child in range(8)]
        nears = [near_ref[leaf] for leaf in leaves]
        blank = jnp.zeros((32, p_width), BF16)
        exponents = []
        for first in range(0, 8, 2):
            sides = []
            for child in (first, first + 1):
                lines = [features[child] if place == child % 4 else blank for place in range(4)]
                sides.append(jnp.concatenate(lines, axis=0))
            both = dot(turned[first // 4], jnp.concatenate(sides, axis=1))
            exponents += [both[:, :p_width], both[:, p_width:]]
        values = [halves(jnp.exp2(value)) for value in exponents]
        lefts = [jnp.concatenate(down, axis=0).astype(BF16) for down in downs]
        products = [dot(left, jnp.concatenate(value, axis=1)) for left, value in zip(lefts, values)]
        for child, leaf in enumerate(leaves):
            product = products[child]
            far = product[:q_width, :p_width] + product[q_width:, :p_width] + product[:q_width, p_width:]
            out_ref[leaf] = jnp.where(lane < counts_ref[leaf], far + nears[child], 0.0)
        return carry

    lax.fori_loop(0, node_count, node_step, 0)


def shifted(value, size):
    up = [(i, i + 1) for i in range(size - 1)]
    down = [(j, i) for i, j in up]
    return lax.ppermute(value, "oct", up), lax.ppermute(value, "oct", down)


def swapped(value, size, mask):
    return lax.ppermute(value, "oct", [(source, source ^ mask) for source in range(size)])


def local(
    points,
    dens,
    surface,
    counts,
    ulist,
    vlist,
    up_inverse,
    down_inverse,
    shift_up,
    shift_down,
    coarse,
    translate,
):
    leaf_count, q_width, p_width = dens.shape
    eq_width = surface.shape[2]
    node_count, type_count = vlist.shape
    node_rows = node_count * q_width
    size = lax.axis_size("oct")
    bits = size.bit_length() - 1
    level_count = -(-bits // 3)
    level_rows = level_count * q_width
    index = lax.axis_index("oct")
    vmem = pl.BlockSpec(memory_space=pltpu.VMEM)
    smem = pl.BlockSpec(memory_space=pltpu.SMEM)
    hbm = pl.BlockSpec(memory_space=pl.ANY)
    params = grant(56)
    points = jnp.transpose(points, (1, 0, 2))
    surface = jnp.transpose(surface, (1, 0, 2))
    ulist = ulist.T
    table = jnp.transpose(translate, (1, 2, 0))

    pack, send, slab = pl.pallas_call(
        lambda *refs: upward_kernel(level_count, *refs),
        out_shape=(
            jax.ShapeDtypeStruct((2 * leaf_count, PIECE, 128), BF16),
            jax.ShapeDtypeStruct((node_rows + 2 * level_rows + 16, eq_width), BF16),
            jax.ShapeDtypeStruct((level_rows, eq_width), F32),
        ),
        in_specs=[vmem, vmem, vmem, smem, vmem, vmem, vmem],
        out_specs=(vmem,) * 3,
        scratch_shapes=[pltpu.VMEM((8, node_rows, eq_width), F32)],
        compiler_params=params,
        name="upward",
    )(points, dens, surface, counts, counts.reshape(1, leaf_count), up_inverse, shift_up)

    send_lower, send_upper = shifted(send, size)
    features, turned, message = pl.pallas_call(
        outline_kernel,
        out_shape=(
            jax.ShapeDtypeStruct((2, 2 * leaf_count, 32, p_width), BF16),
            jax.ShapeDtypeStruct((leaf_count // 4, eq_width, 128), BF16),
            jax.ShapeDtypeStruct((leaf_count // 2, 2 * q_width + 8, p_width), F32),
        ),
        in_specs=[vmem, vmem, vmem, smem, hbm],
        out_specs=(vmem,) * 3,
        compiler_params=params,
        cost_estimate=pl.CostEstimate(flops=4 * 10**9, bytes_accessed=10**7, transcendentals=0),
        name="outline",
    )(points, dens, surface, counts, slab)
    lower, upper = shifted(message, size)
    send_lower, send_upper, features = lax.optimization_barrier((send_lower, send_upper, features))
    ends = slice(node_rows, node_rows + 2 * level_rows)
    partner = jnp.where(index & 1 == 1, send_lower[ends], send_upper[ends]).astype(F32)
    total = slab + (partner[:level_rows] + partner[level_rows:])
    total = total + swapped(total, size, 2)
    arrived = swapped(total, size, 4)
    send_lower, total = lax.optimization_barrier((send_lower, total))

    table = table.reshape(eq_width * eq_width, type_count)
    far_node, steps, piece_table, items = pl.pallas_call(
        far_kernel,
        out_shape=(
            jax.ShapeDtypeStruct((node_rows, eq_width), F32),
            jax.ShapeDtypeStruct((1, 128), jnp.int32),
            jax.ShapeDtypeStruct((32, 128), jnp.int32),
            jax.ShapeDtypeStruct((8, 128), jnp.int32),
        ),
        in_specs=[vmem, vmem, vmem, vmem, vmem, hbm],
        out_specs=(vmem,) * 4,
        scratch_shapes=[
            pltpu.VMEM((type_count // 128, eq_width * eq_width, 128), BF16),
            pltpu.VMEM((eq_width * eq_width, type_count % 128), BF16),
            pltpu.VMEM((eq_width * SOURCES, 128), F32),
            pltpu.VMEM((eq_width, node_rows), F32),
            pltpu.VMEM((CHUNK * eq_width, node_rows), F32),
            pltpu.SemaphoreType.DMA((eq_width // CHUNK, type_count // 128 + 1)),
        ],
        compiler_params=params,
        cost_estimate=pl.CostEstimate(flops=2 * 10**10, bytes_accessed=18 * 10**6, transcendentals=0),
        name="far",
    )(send_lower, send, send_upper, vlist, ulist, table)
    far_node, lower, upper = lax.optimization_barrier((far_node, lower, upper))

    far_node, total, arrived = lax.optimization_barrier((far_node, total, arrived))
    total = total + arrived
    shares = total[q_width:]
    others = [swapped(shares, size, mask << 3) for mask in range(1, size >> 3)]
    steps, shares = lax.optimization_barrier((steps, shares))
    near = pl.pallas_call(
        near_kernel,
        out_shape=jax.ShapeDtypeStruct((leaf_count, q_width, p_width), F32),
        in_specs=[smem, smem, smem, hbm, hbm, vmem, vmem],
        out_specs=vmem,
        scratch_shapes=[
            pltpu.VMEM((6 * leaf_count + 1, PIECE, 128), BF16),
            pltpu.VMEM((2, 6 * leaf_count + 1, 32, 128), BF16),
            *[pltpu.VMEM((leaf_count + 1, p_width, 128), F32)] * TOTALS,
            pltpu.SemaphoreType.DMA((2,)),
        ],
        compiler_params=params,
        cost_estimate=pl.CostEstimate(flops=3 * 10**10, bytes_accessed=10**7, transcendentals=0),
        name="near",
    )(steps, piece_table.reshape(-1), items.reshape(-1), pack, features, lower, upper)

    tops = [total]
    for level in range(1, level_count):
        rows = slice((level - 1) * q_width, level * q_width)
        group = 1 << (min(3 * level + 3, bits) - 3)
        tops.append(sum([other[rows] for other in others[: group - 1]], shares[rows]))
    return pl.pallas_call(
        lambda *refs: final_kernel(level_count, *refs),
        out_shape=jax.ShapeDtypeStruct((leaf_count, q_width, p_width), F32),
        in_specs=[smem] + [vmem] * (7 + len(tops)),
        out_specs=vmem,
        scratch_shapes=[
            pltpu.VMEM((node_rows, eq_width), F32),
            pltpu.VMEM((8, node_rows, eq_width), F32),
        ],
        compiler_params=params,
        name="final",
    )(counts, features, turned, near, far_node, coarse, shift_down, down_inverse, *tops)


def solution(mesh):
    placed = (
        P("oct", None, None),
        P("oct", None, None),
        P("oct", None, None),
        P("oct"),
        P("oct", None),
        P("oct", None),
        P(),
        P(),
        P(),
        P(),
        P(),
        P(),
    )
    return jax.shard_map(
        local, mesh=mesh, in_specs=placed, out_specs=P("oct", None, None), check_vma=False
    )
```

```python
import math

import jax
import jax.numpy as jnp
from jax import lax
from jax.experimental import pallas as pl
from jax.experimental.pallas import tpu as pltpu
from jax.sharding import PartitionSpec as P

F32 = jnp.float32
BF16 = jnp.bfloat16
HIGHEST = lax.Precision.HIGHEST
SCALE = math.sqrt(math.log2(math.e))
NT = (((1,), (1,)), ((), ()))
TN = (((0,), (0,)), ((), ()))
BLOCK = 256
UNROLL = 8
TOTALS = 2
PIECE = 64
CLASS_ROWS = tuple(range(16, 129, 16))
PLACES = 56
SOURCES = 32
CHUNK = 4
FIRST, SECOND = 16, 8


def dot(left, right):
    return jnp.dot(left, right, preferred_element_type=F32)


def dot_nt(left, right):
    return lax.dot_general(left, right, NT, preferred_element_type=F32)


def dot_tn(left, right):
    return lax.dot_general(left, right, TN, preferred_element_type=F32)


def halves(value):
    high = value.astype(BF16)
    low = (value - high.astype(F32)).astype(BF16)
    return high, low


def dot3(left, right):
    left_high, left_low = halves(left)
    right_high, right_low = halves(right)
    return dot(left_high, right_high) + dot(left_high, right_low) + dot(left_low, right_high)


def grant(mebibytes):
    return pltpu.CompilerParams(vmem_limit_bytes=mebibytes * 1024 * 1024)


def iota(shape, dim):
    return lax.broadcasted_iota(jnp.int32, shape, dim)


def coords_of(ref, leaf):
    width = ref.shape[2]
    row = iota((8, width), 0)
    value = jnp.zeros((8, width), F32)
    for dim in range(3):
        line = jnp.broadcast_to(ref[dim, pl.ds(leaf, 1), :], (8, width))
        value = jnp.where(row == dim, line, value)
    return value


def pieces(coords):
    row = iota(coords.shape, 0)
    used = row < 3
    scaled = jnp.where(used, coords, 0.0) * SCALE
    high = scaled.astype(BF16).astype(F32)
    rest = scaled - high
    mid = rest.astype(BF16).astype(F32)
    low = (rest - mid).astype(BF16).astype(F32)
    norm = -0.5 * jnp.sum(scaled * scaled, axis=0, keepdims=True)
    norm_high = norm.astype(BF16).astype(F32)
    norm_rest = norm - norm_high
    norm_mid = norm_rest.astype(BF16).astype(F32)
    norm_low = norm_rest - norm_mid
    norms = jnp.where(row == 0, norm_high, jnp.where(row == 1, norm_mid, jnp.where(row == 2, norm_low, 0.0)))
    ones = jnp.where(used, 1.0, 0.0)
    return high, mid, low, norms, ones


def paired(first, second):
    return first + pltpu.roll(second, 4, 0)


def left_rows(parts):
    high, mid, low, norms, ones = parts
    return jnp.concatenate([paired(high, high), paired(mid, mid), paired(high, low), paired(ones, norms)], axis=0)


def right_rows(parts):
    high, mid, low, norms, ones = parts
    both = paired(high, mid)
    return jnp.concatenate([both, both, paired(low, high), paired(norms, ones)], axis=0)


def weight_rows(weights):
    high = weights.astype(BF16).astype(F32)
    return [high, weights - high]


def feature_versions(rows):
    lower = iota(rows.shape, 1) < PIECE
    versions = []
    for half in range(2):
        alone = jnp.where(lower == (half == 0), rows, 0.0)
        versions.append((half, half, alone.astype(BF16)))
        versions.append((half, 1 - half, pltpu.roll(alone, PIECE, 1).astype(BF16)))
    return versions


def put_features(feature_ref, leaf, versions):
    for half, place, value in versions:
        feature_ref[place, 2 * leaf + half] = value


def put_pack(pack_ref, leaf, value):
    pack_ref[pl.ds(2 * leaf, 2)] = value.reshape(2, PIECE, 128)


def upward_kernel(
    level_count, points_ref, dens_ref, surface_ref, counts_ref, count_line_ref, up_ref, shift_ref, pack_ref, send_ref,
    slab_ref, check_ref
):
    leaf_count, q_width, p_width = dens_ref.shape
    eq_width = surface_ref.shape[2]
    node_count = leaf_count // 8
    lane = iota((q_width, p_width), 1)

    def node_step(node, carry):
        leaves = [node * 8 + child for child in range(8)]
        counts = [counts_ref[leaf] for leaf in leaves]
        weights = [jnp.where(lane < count, dens_ref[leaf], 0.0) for leaf, count in zip(leaves, counts)]
        coords = [coords_of(points_ref, leaf) for leaf in leaves]
        surfaces = [left_rows(pieces(coords_of(surface_ref, leaf))) for leaf in leaves]
        parts = [pieces(value) for value in coords]
        rights = [right_rows(value) for value in parts]
        lists = [weight_rows(value) for value in weights]
        packs = [
            jnp.concatenate([left_rows(part)] + split + [right], axis=0).astype(BF16).T
            for part, split, right in zip(parts, lists, rights)
        ]
        blank = jnp.zeros((96, eq_width), F32)
        wides = [jnp.concatenate([blank, value], axis=0).astype(BF16) for value in surfaces]
        exponents = [dot(pack, wide) for pack, wide in zip(packs, wides)]
        values = [halves(jnp.exp2(value)) for value in exponents]
        rows = [jnp.concatenate(split, axis=0).astype(BF16) for split in lists]
        firsts = [dot(row, value[0]) for row, value in zip(rows, values)]
        seconds = [dot(row[:q_width], value[1]) for row, value in zip(rows, values)]
        for child, leaf in enumerate(leaves):
            put_pack(pack_ref, leaf, packs[child])
            check = firsts[child][:q_width] + firsts[child][q_width:] + seconds[child]
            check_ref[child, pl.ds(pl.multiple_of(node * q_width, q_width), q_width), :] = check
        return carry

    lax.fori_loop(0, node_count, node_step, 0)

    node_eq = jnp.zeros((node_count * q_width, eq_width), F32)
    for child in range(8):
        node_eq = node_eq + dot3(dot3(check_ref[child], up_ref[...]), shift_ref[child])
    send_ref[: node_count * q_width, :] = node_eq.astype(BF16)
    slab_eq = jnp.zeros((q_width, eq_width), F32)
    for child in range(8):
        slab_eq = slab_eq + dot3(node_eq[child * q_width : (child + 1) * q_width], shift_ref[child])
    index = lax.axis_index("oct")
    slab = slab_eq
    start = node_count * q_width
    for level in range(level_count):
        slab = dot3(slab, shift_ref[jnp.right_shift(index, 3 * level) & 7])
        slab_ref[level * q_width : (level + 1) * q_width, :] = slab
        high, rest = halves(slab)
        for place, part in enumerate((high, rest)):
            first = start + (place * level_count + level) * q_width
            send_ref[first : first + q_width, :] = part
    start = start + 2 * level_count * q_width
    line = jnp.concatenate([count_line_ref[...].astype(F32), jnp.zeros((1, eq_width - leaf_count), F32)], axis=1)
    send_ref[start : start + 16, :] = jnp.broadcast_to(line, (16, eq_width)).astype(BF16)


def outline_kernel(
    points_ref, dens_ref, surface_ref, counts_ref, order_ref, feature_ref, turned_ref, message_ref
):
    leaf_count, q_width, p_width = dens_ref.shape
    lane = iota((q_width, p_width), 1)

    def node_step(node, carry):
        leaves = [node * 8 + child for child in range(8)]
        counts = [counts_ref[leaf] for leaf in leaves]
        weights = [jnp.where(lane < count, dens_ref[leaf], 0.0) for leaf, count in zip(leaves, counts)]
        coords = [coords_of(points_ref, leaf) for leaf in leaves]
        surfaces = [left_rows(pieces(coords_of(surface_ref, leaf))) for leaf in leaves]
        versions = [feature_versions(right_rows(pieces(value))) for value in coords]
        fours = [jnp.concatenate(surfaces[first : first + 4], axis=0).astype(BF16).T for first in range(0, 8, 4)]
        for number, four in enumerate(fours):
            turned_ref[2 * node + number] = four
        for child, leaf in enumerate(leaves):
            pair, side = node * 4 + child // 2, child % 2
            message_ref[pair, side * q_width : (side + 1) * q_width, :] = weights[child]
            put_features(feature_ref, leaf, versions[child])
        for number in range(4):
            message_ref[node * 4 + number, 2 * q_width :, :] = paired(coords[2 * number], coords[2 * number + 1])
        return carry

    lax.fori_loop(0, leaf_count // 8, node_step, 0)


def far_kernel(
    lower_ref, own_ref, upper_ref, vlist_ref, ulist_ref, table_hbm, out_ref, step_ref, piece_ref, item_ref, table_ref,
    tail_ref, wide_ref, total_ref, first_ref, sems
):
    node_count, type_count = vlist_ref.shape
    eq_width = own_ref.shape[1]
    q_width = out_ref.shape[0] // node_count
    lanes = node_count * q_width
    tile = 128 // q_width
    chunk = CHUNK
    chunk_rows = chunk * eq_width
    chunk_count = eq_width // chunk
    full = type_count // 128

    def copies_of(number):
        span = pl.ds(number * chunk_rows, chunk_rows)
        copies = []
        for part in range(full):
            source = table_hbm.at[span, pl.ds(part * 128, 128)]
            copies.append(pltpu.make_async_copy(source, table_ref.at[part, span], sems.at[number, part]))
        source = table_hbm.at[span, pl.ds(full * 128, type_count - full * 128)]
        copies.append(pltpu.make_async_copy(source, tail_ref.at[span], sems.at[number, full]))
        return copies

    for number in range(chunk_count):
        for copy in copies_of(number):
            copy.start()

    index = lax.axis_index("oct")
    repeat = (iota((q_width, 128), 1) % q_width == iota((q_width, 128), 0)).astype(BF16)
    for part, source in enumerate((lower_ref, own_ref, upper_ref)):
        for node in range(node_count):
            spread = dot_tn(source[node * q_width : (node + 1) * q_width, :], repeat)
            wide_ref[pl.ds(part * node_count + node, eq_width, stride=SOURCES), :] = spread
    for place in range(3 * node_count, SOURCES):
        wide_ref[pl.ds(place, eq_width, stride=SOURCES), :] = jnp.zeros((eq_width, 128), F32)

    ids = vlist_ref[...]
    places = jnp.where(ids >= 0, ids - (index - 1) * node_count, -1).astype(F32).astype(BF16)
    lane = iota((1, lanes), 1)
    second_half = jnp.bitwise_and(lane, 63)
    node_of = jnp.where(lane < 128, lane // FIRST, second_half // SECOND)
    source_of = jnp.where(lane < 128, lane % FIRST, FIRST + second_half % SECOND)
    spread = (jnp.broadcast_to(node_of, (node_count, lanes)) == iota((node_count, lanes), 0)).astype(BF16)
    wanted = dot_tn(places, spread)
    chosen = (wanted == source_of.astype(F32)).astype(F32)
    chosen_full = chosen[: full * 128].astype(BF16)
    chosen_tail = chosen[full * 128 :].astype(BF16)
    lane_node = iota((SOURCES, 128), 1) // q_width
    lower_lanes = iota((eq_width, 128), 1) < 64
    total_ref[...] = jnp.zeros_like(total_ref)

    leaf_count = ulist_ref.shape[1]
    start = own_ref.shape[0] - 16
    lines = [ref[start:, :].astype(F32)[:1, :leaf_count] for ref in (lower_ref, own_ref, upper_ref)]
    plan_of(ulist_ref, lines, step_ref, piece_ref, item_ref)

    def table_of(number):
        span = pl.ds(pl.multiple_of(number * chunk_rows, chunk_rows), chunk_rows)
        left = jnp.concatenate([table_ref[part, span, :] for part in range(full)], axis=1)
        return left, tail_ref[span, :]

    def first_product(left, tail):
        return dot(left, chosen_full) + dot(tail, chosen_tail)

    def block_rows(sents, first, count):
        lines = []
        for sent in sents:
            blank = jnp.zeros((count, 128), F32)
            for node in range(node_count):
                own = sent[node % tile][first : first + count]
                line = [own if place == node // tile else blank for place in range(node_count // tile)]
                lines.append(jnp.concatenate(line, axis=1))
        return lines

    def second_product(number, summed):
        lefts, rights = [], []
        for step in range(0, chunk, 2):
            sents = []
            for place in (step, step + 1):
                row = number * chunk + place
                sent = wide_ref[pl.ds(pl.multiple_of(row * SOURCES, SOURCES), SOURCES), :]
                sents.append([jnp.where(lane_node == part, sent, 0.0) for part in range(tile)])
            pair = [summed[place * eq_width : (place + 1) * eq_width] for place in (step, step + 1)]
            tiles = [pair[0][:, :128], pair[1][:, :128], jnp.where(lower_lanes, pair[0][:, 128:], pair[1][:, 128:])]
            for value in tiles:
                high = value.astype(BF16).astype(F32)
                lefts.append(jnp.concatenate([high, value - high], axis=0).astype(BF16))
            rights += block_rows(sents, 0, FIRST) + block_rows(sents, FIRST, SECOND)
        product = dot(jnp.concatenate(lefts, axis=1), jnp.concatenate(rights, axis=0).astype(BF16))
        return product[:eq_width] + product[eq_width:]

    def wait_for(number):
        for copy in copies_of(number):
            copy.wait()

    wait_for(0)
    first_ref[...] = first_product(*table_of(0))

    def pair_step(pair, carry):
        number = 2 * pair
        wait_for(number + 1)
        pl.when(pair < chunk_count // 2 - 1)(lambda: wait_for(number + 2))
        ahead = table_of(number + 1)
        behind = table_of(jnp.minimum(number + 2, chunk_count - 1))
        summed = first_ref[...]
        middle = first_product(*ahead)
        total = second_product(number, summed)
        following = first_product(*behind)
        total = total + second_product(number + 1, middle)
        first_ref[...] = following
        total_ref[...] += total
        return carry

    lax.fori_loop(0, chunk_count // 2, pair_step, 0)
    out_ref[...] = total_ref[...].T


def near_kernel(
    step_ref, piece_ref, item_ref, own_hbm, own_feature_hbm, lower_ref, upper_ref, out_ref, pack_ref, feature_ref,
    *rest
):
    total_refs, sems = rest[:TOTALS], rest[TOTALS]
    leaf_count, q_width, p_width = out_ref.shape
    own = pl.ds(0, 2 * leaf_count)
    own_copy = pltpu.make_async_copy(own_hbm, pack_ref.at[own], sems.at[0])
    feature_copy = pltpu.make_async_copy(own_feature_hbm, feature_ref.at[:, own], sems.at[1])
    own_copy.start()
    feature_copy.start()
    pack_ref[6 * leaf_count] = jnp.zeros((PIECE, 128), BF16)
    for half in range(2):
        feature_ref[half, 6 * leaf_count] = jnp.zeros((32, 128), BF16)
    for total_ref in total_refs:
        total_ref[...] = jnp.zeros_like(total_ref)
    def pack_step(step, carry):
        chosen = [(part, side) for side in range(2) for part in range(4)]
        sources = (lower_ref, upper_ref)
        weights, versions = [], []
        for part, side in chosen:
            place, half = step * 2 + part // 2, part % 2
            weights.append(weight_rows(sources[side][place, half * q_width : (half + 1) * q_width, :]))
            tail = sources[side][place, 2 * q_width :, :]
            tail = pltpu.roll(tail, 4, 0) if half else tail
            versions.append(feature_versions(right_rows(pieces(tail))))
        packs = []
        for part in range(0, len(chosen), 2):
            (high, low), (next_high, next_low) = weights[part : part + 2]
            both = jnp.concatenate([next_low, high, low, next_high], axis=0).astype(BF16).T
            packs += [both, pltpu.roll(both.astype(F32), 64, 1).astype(BF16)]
        for (part, side), pack, version in zip(chosen, packs, versions):
            place = (1 + side) * leaf_count + step * 4 + part
            put_pack(pack_ref, place, pack)
            put_features(feature_ref, place, version)
        return carry

    lax.fori_loop(0, leaf_count // 4, pack_step, 0)
    own_copy.wait()
    feature_copy.wait()
    block_pieces = BLOCK // PIECE

    def items_of(step):
        first = step * UNROLL
        leaves = [item_ref[first + part] for part in range(UNROLL)]
        first = first * block_pieces
        pieces_of = [
            [piece_ref[first + part * block_pieces + number] for number in range(block_pieces)] for part in range(UNROLL)
        ]
        return list(zip(leaves, pieces_of))

    def sources_of(numbers):
        return jnp.concatenate([pack_ref[number] for number in numbers], axis=0)

    def features_of(numbers):
        tiles = []
        for tile in range(BLOCK // 128):
            tiles.append(feature_ref[0, numbers[2 * tile]] + feature_ref[1, numbers[2 * tile + 1]])
        return jnp.concatenate(tiles, axis=1)

    def targets_of(leaf, rows):
        first = 2 * jnp.minimum(leaf, leaf_count - 1)
        if rows <= PIECE:
            return pack_ref[first, :rows][:, :32]
        return jnp.concatenate([pack_ref[first][:, :32], pack_ref[first + 1, : rows - PIECE][:, :32]], axis=0)

    def run(rows, first, count):
        def blocks_step(step, carry):
            items = items_of(step)
            features = [features_of(numbers) for _, numbers in items]
            targets = [targets_of(leaf, rows) for leaf, _ in items]
            sources = [sources_of(numbers) for _, numbers in items]
            exponents = [dot(target, feature) for target, feature in zip(targets, features)]
            values = [jnp.exp2(value).astype(BF16) for value in exponents]
            products = []
            for part in range(0, UNROLL, 2):
                left = jnp.concatenate(values[part : part + 2], axis=0)
                both = dot(left, jnp.concatenate(sources[part : part + 2], axis=1))
                products += [both[:rows, :128], both[rows:, 128:]]
            for first in range(0, UNROLL, TOTALS):
                sums = [
                    total_refs[part][items[first + part][0], :rows] + products[first + part] for part in range(TOTALS)
                ]
                for part, value in enumerate(sums):
                    total_refs[part][items[first + part][0], :rows] = value
            return carry

        lax.fori_loop(first, first + count, blocks_step, 0)

    for number, rows in enumerate(CLASS_ROWS):
        run(rows, step_ref[0, 2 * number], step_ref[0, 2 * number + 1])

    def turn_step(step, carry):
        sums = [[total_ref[step * 8 + part] for total_ref in total_refs] for part in range(8)]
        sums = [sum(values[1:], values[0]) for values in sums]
        inner = (iota((p_width, 128), 1) >= 32) & (iota((p_width, 128), 1) < 96)
        for part in range(0, 8, 2):
            turned = jnp.where(inner, sums[part], pltpu.roll(sums[part + 1], 64, 1)).T
            out_ref[step * 8 + part] = turned[32 : 32 + q_width] + turned[32 + q_width : 32 + 2 * q_width]
            out_ref[step * 8 + part + 1] = turned[96 : 96 + q_width] + turned[:q_width]
        return carry

    lax.fori_loop(0, leaf_count // 8, turn_step, 0)


def as_column(line):
    width = line.shape[1]
    wide = jnp.concatenate([line, jnp.zeros((1, 128 - width), F32)], axis=1) if width < 128 else line
    return jnp.broadcast_to(wide, (128, 128)).T[:width, :width]


def plan_of(ulist_ref, counts, step_ref, piece_ref, item_ref):
    slot_count, leaf_count = ulist_ref.shape
    index = lax.axis_index("oct")
    shape = (leaf_count, leaf_count)
    row, column = iota(shape, 0), iota(shape, 1)
    tables = [as_column(line) for line in counts]
    own = jnp.broadcast_to(counts[1], shape)
    before = (tables[1] < own) | ((tables[1] == own) & (row < column))
    rank = jnp.sum(jnp.where(before, 1.0, 0.0), axis=0, keepdims=True)
    rank_column = as_column(rank).astype(jnp.int32)
    rank_wide = jnp.broadcast_to(rank, shape).astype(jnp.int32)

    block_pieces = BLOCK // PIECE
    empty = 6 * leaf_count
    place_shape = (PLACES, leaf_count)
    place_row = iota(place_shape, 0)
    listed = jnp.full(place_shape, empty, jnp.int32)
    offset = jnp.zeros((1, leaf_count), jnp.int32)
    for slot in range(slot_count):
        side = 1 if slot == 0 else (0 if slot < 9 else (1 if slot < 18 else 2))
        ids = ulist_ref[slot : slot + 1, :]
        place = jnp.where(ids >= 0, ids - (index + (side - 1)) * leaf_count, 0)
        found = jnp.sum(jnp.where(row == place, tables[side], 0.0), axis=0, keepdims=True).astype(jnp.int32)
        length = lax.shift_right_logical(found + (PIECE - 1), PIECE.bit_length() - 1)
        length = jnp.where(ids >= 0, length, 0)
        start = (place + (1, 0, 2)[side] * leaf_count) * 2
        inside = (place_row >= offset) & (place_row < offset + length)
        listed = jnp.where(inside, start + place_row - offset, listed)
        offset = offset + length

    blocks = lax.shift_right_logical(offset + (block_pieces - 1), block_pieces.bit_length() - 1)
    blocks_column = as_column(blocks.astype(F32))
    own_class = lax.shift_right_logical(counts[1].astype(jnp.int32) - 1, 4)
    class_column = as_column(own_class.astype(F32)).astype(jnp.int32)
    earlier = (class_column == jnp.broadcast_to(own_class, shape)) & (rank_column < rank_wide)
    first = jnp.sum(jnp.where(earlier, blocks_column, 0.0), axis=0, keepdims=True).astype(jnp.int32)
    lane = iota((1, 128), 1)
    steps_line = jnp.zeros((1, 128), jnp.int32)
    start = jnp.ones((1, 1), jnp.int32)
    for number in range(len(CLASS_ROWS)):
        inside = jnp.where(own_class == number, blocks.astype(F32), 0.0)
        items = jnp.sum(inside, axis=1, keepdims=True).astype(jnp.int32)
        steps = lax.shift_right_logical(items + (UNROLL - 1), UNROLL.bit_length() - 1)
        first = first + jnp.where(own_class == number, start * UNROLL, 0)
        steps_line = jnp.where(lane == 2 * number, start, jnp.where(lane == 2 * number + 1, steps, steps_line))
        start = start + steps
    step_ref[...] = steps_line

    first_column = as_column(first.astype(F32))[:, :1].astype(jnp.int32)
    blocks_column = blocks_column[:, :1].astype(jnp.int32)
    high = lax.shift_right_logical(listed, 8).astype(F32)
    low = jnp.bitwise_and(listed, 255).astype(F32)
    parts = jnp.concatenate([high, low], axis=0).astype(BF16)
    chunk = 1024
    wide = (leaf_count, chunk)
    column = iota(wide, 1)
    leaf_row = iota(wide, 0).astype(F32)
    for number in range(block_pieces):
        entry = column + chunk * number
        after = lax.shift_right_logical(entry, block_pieces.bit_length() - 1) - first_column
        inside = (after >= 0) & (after < blocks_column)
        place = after * block_pieces + jnp.bitwise_and(entry, block_pieces - 1)
        place = jnp.sum(jnp.where(inside, place.astype(F32), 0.0), axis=0, keepdims=True).astype(jnp.int32)
        found = jnp.sum(jnp.where(inside, 1.0, 0.0), axis=0, keepdims=True)
        both = dot(parts, jnp.where(inside, 1.0, 0.0).astype(BF16))
        value = both[:PLACES] * 256.0 + both[PLACES:]
        value = jnp.sum(jnp.where(iota((PLACES, chunk), 0) == place, value, 0.0), axis=0, keepdims=True)
        value = jnp.where(found > 0.0, value, float(empty)).astype(jnp.int32)
        for line in range(8):
            piece_ref[8 * number + line : 8 * number + line + 1, :] = value[:, line * 128 : (line + 1) * 128]
    after = column - first_column
    inside = (after >= 0) & (after < blocks_column)
    leaf = jnp.sum(jnp.where(inside, leaf_row - leaf_count, 0.0), axis=0, keepdims=True).astype(jnp.int32) + leaf_count
    for line in range(8):
        item_ref[line : line + 1, :] = leaf[:, line * 128 : (line + 1) * 128]


def final_kernel(
    level_count, counts_ref, feature_hbm, turned_hbm, near_hbm, far_ref, coarse_hbm, shift_ref, down_ref, *rest
):
    top_refs, rest = rest[:level_count], rest[level_count:]
    out_ref, node_ref, down_leaf_ref, lower_ref, upper_ref, turned_ref, near_ref, coarse_ref, sems = rest
    leaf_count, q_width, p_width = out_ref.shape
    eq_width = far_ref.shape[1]
    node_count = leaf_count // 8
    index = lax.axis_index("oct")
    ends = [(coarse_hbm.at[jnp.right_shift(index, 3 * level) & 7], coarse_ref.at[level]) for level in range(level_count)]
    ends += [(feature_hbm.at[0, :, 0], lower_ref), (feature_hbm.at[1, :, 1], upper_ref)]
    ends += [(turned_hbm, turned_ref), (near_hbm, near_ref)]
    copies = [pltpu.make_async_copy(*end, sems.at[number]) for number, end in enumerate(ends)]
    for copy in copies:
        copy.start()
    for copy in copies[:level_count]:
        copy.wait()
    slab_local = jnp.zeros((q_width, eq_width), F32)
    for level, top_ref in enumerate(top_refs):
        slab_local = slab_local + dot3(top_ref[:q_width, :], coarse_ref[level])
    for node in range(node_count):
        rows = slice(node * q_width, (node + 1) * q_width)
        node_ref[rows, :] = far_ref[rows, :] + dot3(slab_local, shift_ref[node])

    for child in range(8):
        down_leaf_ref[child] = dot3(dot3(node_ref[...], shift_ref[child]), down_ref[...])
    for copy in copies[level_count:]:
        copy.wait()
    lane = iota((q_width, p_width), 1)

    def node_step(node, carry):
        leaves = [node * 8 + child for child in range(8)]
        features = []
        for leaf in leaves:
            features.append(lower_ref[leaf] + upper_ref[leaf])
        turned = [turned_ref[2 * node + number] for number in range(2)]
        node_rows = pl.ds(pl.multiple_of(node * q_width, q_width), q_width)
        downs = [weight_rows(down_leaf_ref[child, node_rows, :]) for child in range(8)]
        nears = [near_ref[leaf] for leaf in leaves]
        blank = jnp.zeros((32, p_width), BF16)
        exponents = []
        for first in range(0, 8, 2):
            sides = []
            for child in (first, first + 1):
                lines = [features[child] if place == child % 4 else blank for place in range(4)]
                sides.append(jnp.concatenate(lines, axis=0))
            both = dot(turned[first // 4], jnp.concatenate(sides, axis=1))
            exponents += [both[:, :p_width], both[:, p_width:]]
        values = [halves(jnp.exp2(value)) for value in exponents]
        lefts = [jnp.concatenate(down, axis=0).astype(BF16) for down in downs]
        products = [dot(left, jnp.concatenate(value, axis=1)) for left, value in zip(lefts, values)]
        for child, leaf in enumerate(leaves):
            product = products[child]
            far = product[:q_width, :p_width] + product[q_width:, :p_width] + product[:q_width, p_width:]
            out_ref[leaf] = jnp.where(lane < counts_ref[leaf], far + nears[child], 0.0)
        return carry

    lax.fori_loop(0, node_count, node_step, 0)


def shifted(value, size):
    up = [(i, i + 1) for i in range(size - 1)]
    down = [(j, i) for i, j in up]
    return lax.ppermute(value, "oct", up), lax.ppermute(value, "oct", down)


def swapped(value, size, mask):
    return lax.ppermute(value, "oct", [(source, source ^ mask) for source in range(size)])


def local(
    points,
    dens,
    surface,
    counts,
    ulist,
    vlist,
    up_inverse,
    down_inverse,
    shift_up,
    shift_down,
    coarse,
    translate,
):
    leaf_count, q_width, p_width = dens.shape
    eq_width = surface.shape[2]
    node_count, type_count = vlist.shape
    node_rows = node_count * q_width
    size = lax.axis_size("oct")
    bits = size.bit_length() - 1
    level_count = -(-bits // 3)
    level_rows = level_count * q_width
    index = lax.axis_index("oct")
    vmem = pl.BlockSpec(memory_space=pltpu.VMEM)
    smem = pl.BlockSpec(memory_space=pltpu.SMEM)
    hbm = pl.BlockSpec(memory_space=pl.ANY)
    params = grant(56)
    points = jnp.transpose(points, (1, 0, 2))
    surface = jnp.transpose(surface, (1, 0, 2))
    ulist = ulist.T
    table = jnp.transpose(translate, (1, 2, 0))

    pack, send, slab = pl.pallas_call(
        lambda *refs: upward_kernel(level_count, *refs),
        out_shape=(
            jax.ShapeDtypeStruct((2 * leaf_count, PIECE, 128), BF16),
            jax.ShapeDtypeStruct((node_rows + 2 * level_rows + 16, eq_width), BF16),
            jax.ShapeDtypeStruct((level_rows, eq_width), F32),
        ),
        in_specs=[vmem, vmem, vmem, smem, vmem, vmem, vmem],
        out_specs=(vmem,) * 3,
        scratch_shapes=[pltpu.VMEM((8, node_rows, eq_width), F32)],
        compiler_params=params,
        name="upward",
    )(points, dens, surface, counts, counts.reshape(1, leaf_count), up_inverse, shift_up)

    send_lower, send_upper = shifted(send, size)
    features, turned, message = pl.pallas_call(
        outline_kernel,
        out_shape=(
            jax.ShapeDtypeStruct((2, 2 * leaf_count, 32, p_width), BF16),
            jax.ShapeDtypeStruct((leaf_count // 4, eq_width, 128), BF16),
            jax.ShapeDtypeStruct((leaf_count // 2, 2 * q_width + 8, p_width), F32),
        ),
        in_specs=[vmem, vmem, vmem, smem, hbm],
        out_specs=(vmem,) * 3,
        compiler_params=params,
        cost_estimate=pl.CostEstimate(flops=4 * 10**9, bytes_accessed=10**7, transcendentals=0),
        name="outline",
    )(points, dens, surface, counts, slab)
    lower, upper = shifted(message, size)
    send_lower, send_upper, features = lax.optimization_barrier((send_lower, send_upper, features))
    ends = slice(node_rows, node_rows + 2 * level_rows)
    partner = jnp.where(index & 1 == 1, send_lower[ends], send_upper[ends]).astype(F32)
    total = slab + (partner[:level_rows] + partner[level_rows:])
    total = total + swapped(total, size, 2)
    arrived = swapped(total, size, 4)
    send_lower, total = lax.optimization_barrier((send_lower, total))

    table = table.reshape(eq_width * eq_width, type_count)
    far_node, steps, piece_table, items = pl.pallas_call(
        far_kernel,
        out_shape=(
            jax.ShapeDtypeStruct((node_rows, eq_width), F32),
            jax.ShapeDtypeStruct((1, 128), jnp.int32),
            jax.ShapeDtypeStruct((32, 128), jnp.int32),
            jax.ShapeDtypeStruct((8, 128), jnp.int32),
        ),
        in_specs=[vmem, vmem, vmem, vmem, vmem, hbm],
        out_specs=(vmem,) * 4,
        scratch_shapes=[
            pltpu.VMEM((type_count // 128, eq_width * eq_width, 128), BF16),
            pltpu.VMEM((eq_width * eq_width, type_count % 128), BF16),
            pltpu.VMEM((eq_width * SOURCES, 128), F32),
            pltpu.VMEM((eq_width, node_rows), F32),
            pltpu.VMEM((CHUNK * eq_width, node_rows), F32),
            pltpu.SemaphoreType.DMA((eq_width // CHUNK, type_count // 128 + 1)),
        ],
        compiler_params=params,
        cost_estimate=pl.CostEstimate(flops=2 * 10**10, bytes_accessed=18 * 10**6, transcendentals=0),
        name="far",
    )(send_lower, send, send_upper, vlist, ulist, table)
    far_node, lower, upper = lax.optimization_barrier((far_node, lower, upper))

    far_node, total, arrived = lax.optimization_barrier((far_node, total, arrived))
    total = total + arrived
    shares = total[q_width:]
    others = [swapped(shares, size, mask << 3) for mask in range(1, size >> 3)]
    steps, shares = lax.optimization_barrier((steps, shares))
    near = pl.pallas_call(
        near_kernel,
        out_shape=jax.ShapeDtypeStruct((leaf_count, q_width, p_width), F32),
        in_specs=[smem, smem, smem, hbm, hbm, vmem, vmem],
        out_specs=vmem,
        scratch_shapes=[
            pltpu.VMEM((6 * leaf_count + 1, PIECE, 128), BF16),
            pltpu.VMEM((2, 6 * leaf_count + 1, 32, 128), BF16),
            *[pltpu.VMEM((leaf_count + 1, p_width, 128), F32)] * TOTALS,
            pltpu.SemaphoreType.DMA((2,)),
        ],
        compiler_params=params,
        cost_estimate=pl.CostEstimate(flops=3 * 10**10, bytes_accessed=10**7, transcendentals=0),
        name="near",
    )(steps, piece_table.reshape(-1), items.reshape(-1), pack, features, lower, upper)

    tops = [total]
    for level in range(1, level_count):
        rows = slice((level - 1) * q_width, level * q_width)
        group = 1 << (min(3 * level + 3, bits) - 3)
        tops.append(sum([other[rows] for other in others[: group - 1]], shares[rows]))
    return pl.pallas_call(
        lambda *refs: final_kernel(level_count, *refs),
        out_shape=jax.ShapeDtypeStruct((leaf_count, q_width, p_width), F32),
        in_specs=[smem, hbm, hbm, hbm, vmem, hbm] + [vmem] * (2 + len(tops)),
        out_specs=vmem,
        scratch_shapes=[
            pltpu.VMEM((node_rows, eq_width), F32),
            pltpu.VMEM((8, node_rows, eq_width), F32),
            pltpu.VMEM((leaf_count, 32, p_width), BF16),
            pltpu.VMEM((leaf_count, 32, p_width), BF16),
            pltpu.VMEM((leaf_count // 4, eq_width, 128), BF16),
            pltpu.VMEM((leaf_count, q_width, p_width), F32),
            pltpu.VMEM((level_count, eq_width, eq_width), F32),
            pltpu.SemaphoreType.DMA((level_count + 4,)),
        ],
        compiler_params=params,
        name="final",
    )(counts, features.reshape(2, leaf_count, 2, 32, p_width), turned, near, far_node, coarse, shift_down, down_inverse, *tops)


def solution(mesh):
    placed = (
        P("oct", None, None),
        P("oct", None, None),
        P("oct", None, None),
        P("oct"),
        P("oct", None),
        P("oct", None),
        P(),
        P(),
        P(),
        P(),
        P(),
        P(),
    )
    return jax.shard_map(
        local, mesh=mesh, in_specs=placed, out_specs=P("oct", None, None), check_vma=False
    )
```

```python
import math

import jax
import jax.numpy as jnp
from jax import lax
from jax.experimental import pallas as pl
from jax.experimental.pallas import tpu as pltpu
from jax.sharding import PartitionSpec as P

F32 = jnp.float32
BF16 = jnp.bfloat16
HIGHEST = lax.Precision.HIGHEST
SCALE = math.sqrt(math.log2(math.e))
NT = (((1,), (1,)), ((), ()))
TN = (((0,), (0,)), ((), ()))
BLOCK = 256
UNROLL = 8
TOTALS = 2
PIECE = 64
CLASS_ROWS = tuple(range(16, 129, 16))
PLACES = 56
SOURCES = 32
CHUNK = 4
FIRST, SECOND = 16, 8


def dot(left, right):
    return jnp.dot(left, right, preferred_element_type=F32)


def dot_nt(left, right):
    return lax.dot_general(left, right, NT, preferred_element_type=F32)


def dot_tn(left, right):
    return lax.dot_general(left, right, TN, preferred_element_type=F32)


def halves(value):
    high = value.astype(BF16)
    low = (value - high.astype(F32)).astype(BF16)
    return high, low


def dot3(left, right):
    left_high, left_low = halves(left)
    right_high, right_low = halves(right)
    return dot(left_high, right_high) + dot(left_high, right_low) + dot(left_low, right_high)


def grant(mebibytes):
    return pltpu.CompilerParams(vmem_limit_bytes=mebibytes * 1024 * 1024)


def iota(shape, dim):
    return lax.broadcasted_iota(jnp.int32, shape, dim)


def coords_of(ref, leaf):
    width = ref.shape[2]
    row = iota((8, width), 0)
    value = jnp.zeros((8, width), F32)
    for dim in range(3):
        line = jnp.broadcast_to(ref[dim, pl.ds(leaf, 1), :], (8, width))
        value = jnp.where(row == dim, line, value)
    return value


def pieces(coords):
    row = iota(coords.shape, 0)
    used = row < 3
    scaled = jnp.where(used, coords, 0.0) * SCALE
    high = scaled.astype(BF16).astype(F32)
    rest = scaled - high
    mid = rest.astype(BF16).astype(F32)
    low = (rest - mid).astype(BF16).astype(F32)
    norm = -0.5 * jnp.sum(scaled * scaled, axis=0, keepdims=True)
    norm_high = norm.astype(BF16).astype(F32)
    norm_rest = norm - norm_high
    norm_mid = norm_rest.astype(BF16).astype(F32)
    norm_low = norm_rest - norm_mid
    norms = jnp.where(row == 0, norm_high, jnp.where(row == 1, norm_mid, jnp.where(row == 2, norm_low, 0.0)))
    ones = jnp.where(used, 1.0, 0.0)
    return high, mid, low, norms, ones


def paired(first, second):
    return first + pltpu.roll(second, 4, 0)


def left_rows(parts):
    high, mid, low, norms, ones = parts
    return jnp.concatenate([paired(high, high), paired(mid, mid), paired(high, low), paired(ones, norms)], axis=0)


def right_rows(parts):
    high, mid, low, norms, ones = parts
    both = paired(high, mid)
    return jnp.concatenate([both, both, paired(low, high), paired(norms, ones)], axis=0)


def weight_rows(weights):
    high = weights.astype(BF16).astype(F32)
    return [high, weights - high]


def feature_versions(rows):
    lower = iota(rows.shape, 1) < PIECE
    versions = []
    for half in range(2):
        alone = jnp.where(lower == (half == 0), rows, 0.0)
        versions.append((half, half, alone))
        versions.append((half, 1 - half, pltpu.roll(alone, PIECE, 1)))
    return versions


def put_features(feature_ref, leaf, versions):
    for half, place, value in versions:
        feature_ref[place, 2 * leaf + half] = value


def put_pack(pack_ref, leaf, value):
    pack_ref[pl.ds(2 * leaf, 2)] = value.reshape(2, PIECE, 128)


def upward_kernel(
    level_count, points_ref, dens_ref, surface_ref, counts_ref, count_line_ref, up_ref, shift_ref, pack_ref, send_ref,
    slab_ref, check_ref
):
    leaf_count, q_width, p_width = dens_ref.shape
    eq_width = surface_ref.shape[2]
    node_count = leaf_count // 8
    lane = iota((q_width, p_width), 1)

    def node_step(node, carry):
        leaves = [node * 8 + child for child in range(8)]
        counts = [counts_ref[leaf] for leaf in leaves]
        weights = [jnp.where(lane < count, dens_ref[leaf], 0.0) for leaf, count in zip(leaves, counts)]
        coords = [coords_of(points_ref, leaf) for leaf in leaves]
        surfaces = [left_rows(pieces(coords_of(surface_ref, leaf))) for leaf in leaves]
        parts = [pieces(value) for value in coords]
        rights = [right_rows(value) for value in parts]
        lists = [weight_rows(value) for value in weights]
        packs = [
            jnp.concatenate([left_rows(part)] + split + [right], axis=0).astype(BF16).T
            for part, split, right in zip(parts, lists, rights)
        ]
        blank = jnp.zeros((96, eq_width), F32)
        wides = [jnp.concatenate([blank, value], axis=0).astype(BF16) for value in surfaces]
        exponents = [dot(pack, wide) for pack, wide in zip(packs, wides)]
        values = [halves(jnp.exp2(value)) for value in exponents]
        rows = [jnp.concatenate(split, axis=0).astype(BF16) for split in lists]
        firsts = [dot(row, value[0]) for row, value in zip(rows, values)]
        seconds = [dot(row[:q_width], value[1]) for row, value in zip(rows, values)]
        for child, leaf in enumerate(leaves):
            put_pack(pack_ref, leaf, packs[child].astype(F32))
            check = firsts[child][:q_width] + firsts[child][q_width:] + seconds[child]
            check_ref[child, pl.ds(pl.multiple_of(node * q_width, q_width), q_width), :] = check
        return carry

    lax.fori_loop(0, node_count, node_step, 0)

    node_eq = jnp.zeros((node_count * q_width, eq_width), F32)
    for child in range(8):
        node_eq = node_eq + dot3(dot3(check_ref[child], up_ref[...]), shift_ref[child])
    send_ref[: node_count * q_width, :] = node_eq.astype(BF16)
    slab_eq = jnp.zeros((q_width, eq_width), F32)
    for child in range(8):
        slab_eq = slab_eq + dot3(node_eq[child * q_width : (child + 1) * q_width], shift_ref[child])
    index = lax.axis_index("oct")
    slab = slab_eq
    start = node_count * q_width
    for level in range(level_count):
        slab = dot3(slab, shift_ref[jnp.right_shift(index, 3 * level) & 7])
        slab_ref[level * q_width : (level + 1) * q_width, :] = slab
        high, rest = halves(slab)
        for place, part in enumerate((high, rest)):
            first = start + (place * level_count + level) * q_width
            send_ref[first : first + q_width, :] = part
    start = start + 2 * level_count * q_width
    line = jnp.concatenate([count_line_ref[...].astype(F32), jnp.zeros((1, eq_width - leaf_count), F32)], axis=1)
    send_ref[start : start + 16, :] = jnp.broadcast_to(line, (16, eq_width)).astype(BF16)


def outline_kernel(
    points_ref, dens_ref, surface_ref, counts_ref, order_ref, feature_ref, turned_ref, message_ref
):
    leaf_count, q_width, p_width = dens_ref.shape
    lane = iota((q_width, p_width), 1)

    def node_step(node, carry):
        leaves = [node * 8 + child for child in range(8)]
        counts = [counts_ref[leaf] for leaf in leaves]
        weights = [jnp.where(lane < count, dens_ref[leaf], 0.0) for leaf, count in zip(leaves, counts)]
        coords = [coords_of(points_ref, leaf) for leaf in leaves]
        surfaces = [left_rows(pieces(coords_of(surface_ref, leaf))) for leaf in leaves]
        versions = [feature_versions(right_rows(pieces(value))) for value in coords]
        fours = [jnp.concatenate(surfaces[first : first + 4], axis=0).astype(BF16).T for first in range(0, 8, 4)]
        for number, four in enumerate(fours):
            turned_ref[2 * node + number] = four
        for child, leaf in enumerate(leaves):
            pair, side = node * 4 + child // 2, child % 2
            message_ref[pair, side * q_width : (side + 1) * q_width, :] = weights[child]
            put_features(feature_ref, leaf, versions[child])
        for number in range(4):
            message_ref[node * 4 + number, 2 * q_width :, :] = paired(coords[2 * number], coords[2 * number + 1])
        return carry

    lax.fori_loop(0, leaf_count // 8, node_step, 0)


def far_kernel(
    lower_ref, own_ref, upper_ref, vlist_ref, ulist_ref, table_hbm, out_ref, step_ref, piece_ref, item_ref, table_ref,
    tail_ref, wide_ref, total_ref, first_ref, sems
):
    node_count, type_count = vlist_ref.shape
    eq_width = own_ref.shape[1]
    q_width = out_ref.shape[0] // node_count
    lanes = node_count * q_width
    tile = 128 // q_width
    chunk = CHUNK
    chunk_rows = chunk * eq_width
    chunk_count = eq_width // chunk
    full = type_count // 128

    def copies_of(number):
        span = pl.ds(number * chunk_rows, chunk_rows)
        copies = []
        for part in range(full):
            source = table_hbm.at[span, pl.ds(part * 128, 128)]
            copies.append(pltpu.make_async_copy(source, table_ref.at[part, span], sems.at[number, part]))
        source = table_hbm.at[span, pl.ds(full * 128, type_count - full * 128)]
        copies.append(pltpu.make_async_copy(source, tail_ref.at[span], sems.at[number, full]))
        return copies

    for number in range(chunk_count):
        for copy in copies_of(number):
            copy.start()

    index = lax.axis_index("oct")
    repeat = (iota((q_width, 128), 1) % q_width == iota((q_width, 128), 0)).astype(BF16)
    for part, source in enumerate((lower_ref, own_ref, upper_ref)):
        for node in range(node_count):
            spread = dot_tn(source[node * q_width : (node + 1) * q_width, :], repeat)
            wide_ref[pl.ds(part * node_count + node, eq_width, stride=SOURCES), :] = spread
    for place in range(3 * node_count, SOURCES):
        wide_ref[pl.ds(place, eq_width, stride=SOURCES), :] = jnp.zeros((eq_width, 128), F32)

    ids = vlist_ref[...]
    places = jnp.where(ids >= 0, ids - (index - 1) * node_count, -1).astype(F32).astype(BF16)
    lane = iota((1, lanes), 1)
    second_half = jnp.bitwise_and(lane, 63)
    node_of = jnp.where(lane < 128, lane // FIRST, second_half // SECOND)
    source_of = jnp.where(lane < 128, lane % FIRST, FIRST + second_half % SECOND)
    spread = (jnp.broadcast_to(node_of, (node_count, lanes)) == iota((node_count, lanes), 0)).astype(BF16)
    wanted = dot_tn(places, spread)
    chosen = (wanted == source_of.astype(F32)).astype(F32)
    chosen_full = chosen[: full * 128].astype(BF16)
    chosen_tail = chosen[full * 128 :].astype(BF16)
    lane_node = iota((SOURCES, 128), 1) // q_width
    lower_lanes = iota((eq_width, 128), 1) < 64
    total_ref[...] = jnp.zeros_like(total_ref)

    leaf_count = ulist_ref.shape[1]
    start = own_ref.shape[0] - 16
    lines = [ref[start:, :].astype(F32)[:1, :leaf_count] for ref in (lower_ref, own_ref, upper_ref)]
    plan_of(ulist_ref, lines, step_ref, piece_ref, item_ref)

    def table_of(number):
        span = pl.ds(pl.multiple_of(number * chunk_rows, chunk_rows), chunk_rows)
        left = jnp.concatenate([table_ref[part, span, :] for part in range(full)], axis=1)
        return left, tail_ref[span, :]

    def first_product(left, tail):
        return dot(left, chosen_full) + dot(tail, chosen_tail)

    def block_rows(sents, first, count):
        lines = []
        for sent in sents:
            blank = jnp.zeros((count, 128), F32)
            for node in range(node_count):
                own = sent[node % tile][first : first + count]
                line = [own if place == node // tile else blank for place in range(node_count // tile)]
                lines.append(jnp.concatenate(line, axis=1))
        return lines

    def second_product(number, summed):
        lefts, rights = [], []
        for step in range(0, chunk, 2):
            sents = []
            for place in (step, step + 1):
                row = number * chunk + place
                sent = wide_ref[pl.ds(pl.multiple_of(row * SOURCES, SOURCES), SOURCES), :]
                sents.append([jnp.where(lane_node == part, sent, 0.0) for part in range(tile)])
            pair = [summed[place * eq_width : (place + 1) * eq_width] for place in (step, step + 1)]
            tiles = [pair[0][:, :128], pair[1][:, :128], jnp.where(lower_lanes, pair[0][:, 128:], pair[1][:, 128:])]
            for value in tiles:
                high = value.astype(BF16).astype(F32)
                lefts.append(jnp.concatenate([high, value - high], axis=0).astype(BF16))
            rights += block_rows(sents, 0, FIRST) + block_rows(sents, FIRST, SECOND)
        product = dot(jnp.concatenate(lefts, axis=1), jnp.concatenate(rights, axis=0).astype(BF16))
        return product[:eq_width] + product[eq_width:]

    def wait_for(number):
        for copy in copies_of(number):
            copy.wait()

    wait_for(0)
    first_ref[...] = first_product(*table_of(0))

    def pair_step(pair, carry):
        number = 2 * pair
        wait_for(number + 1)
        pl.when(pair < chunk_count // 2 - 1)(lambda: wait_for(number + 2))
        ahead = table_of(number + 1)
        behind = table_of(jnp.minimum(number + 2, chunk_count - 1))
        summed = first_ref[...]
        middle = first_product(*ahead)
        total = second_product(number, summed)
        following = first_product(*behind)
        total = total + second_product(number + 1, middle)
        first_ref[...] = following
        total_ref[...] += total
        return carry

    lax.fori_loop(0, chunk_count // 2, pair_step, 0)
    out_ref[...] = total_ref[...].T


def near_kernel(
    step_ref, piece_ref, item_ref, own_hbm, own_feature_hbm, lower_ref, upper_ref, out_ref, pack_ref, feature_ref,
    *rest
):
    total_refs, sems = rest[:TOTALS], rest[TOTALS]
    leaf_count, q_width, p_width = out_ref.shape
    own = pl.ds(0, 2 * leaf_count)
    own_copy = pltpu.make_async_copy(own_hbm, pack_ref.at[own], sems.at[0])
    feature_copy = pltpu.make_async_copy(own_feature_hbm, feature_ref.at[:, own], sems.at[1])
    own_copy.start()
    feature_copy.start()
    pack_ref[6 * leaf_count] = jnp.zeros((PIECE, 128), F32)
    for half in range(2):
        feature_ref[half, 6 * leaf_count] = jnp.zeros((32, 128), F32)
    for total_ref in total_refs:
        total_ref[...] = jnp.zeros_like(total_ref)
    def pack_step(step, carry):
        chosen = [(part, side) for side in range(2) for part in range(4)]
        sources = (lower_ref, upper_ref)
        weights, versions = [], []
        for part, side in chosen:
            place, half = step * 2 + part // 2, part % 2
            weights.append(weight_rows(sources[side][place, half * q_width : (half + 1) * q_width, :]))
            tail = sources[side][place, 2 * q_width :, :]
            tail = pltpu.roll(tail, 4, 0) if half else tail
            versions.append(feature_versions(right_rows(pieces(tail))))
        packs = []
        for part in range(0, len(chosen), 2):
            (high, low), (next_high, next_low) = weights[part : part + 2]
            both = jnp.concatenate([next_low, high, low, next_high], axis=0).astype(BF16).T
            both = both.astype(F32)
            packs += [both, pltpu.roll(both, 64, 1)]
        for (part, side), pack, version in zip(chosen, packs, versions):
            place = (1 + side) * leaf_count + step * 4 + part
            put_pack(pack_ref, place, pack)
            put_features(feature_ref, place, version)
        return carry

    lax.fori_loop(0, leaf_count // 4, pack_step, 0)
    own_copy.wait()
    feature_copy.wait()
    block_pieces = BLOCK // PIECE

    def items_of(step):
        first = step * UNROLL
        leaves = [item_ref[first + part] for part in range(UNROLL)]
        first = first * block_pieces
        pieces_of = [
            [piece_ref[first + part * block_pieces + number] for number in range(block_pieces)] for part in range(UNROLL)
        ]
        return list(zip(leaves, pieces_of))

    def sources_of(numbers):
        return jnp.concatenate([pack_ref[number] for number in numbers], axis=0).astype(BF16)

    def features_of(numbers):
        tiles = []
        for tile in range(BLOCK // 128):
            tiles.append(feature_ref[0, numbers[2 * tile]] + feature_ref[1, numbers[2 * tile + 1]])
        return jnp.concatenate(tiles, axis=1).astype(BF16)

    def targets_of(leaf, rows):
        first = 2 * jnp.minimum(leaf, leaf_count - 1)
        value = pack_ref[first, : min(rows, PIECE)]
        if rows > PIECE:
            value = jnp.concatenate([value, pack_ref[first + 1, : rows - PIECE]], axis=0)
        return value.astype(BF16)[:, :32]

    def run(rows, first, count):
        def blocks_step(step, carry):
            items = items_of(step)
            features = [features_of(numbers) for _, numbers in items]
            targets = [targets_of(leaf, rows) for leaf, _ in items]
            sources = [sources_of(numbers) for _, numbers in items]
            exponents = [dot(target, feature) for target, feature in zip(targets, features)]
            values = [jnp.exp2(value).astype(BF16) for value in exponents]
            products = []
            for part in range(0, UNROLL, 2):
                left = jnp.concatenate(values[part : part + 2], axis=0)
                both = dot(left, jnp.concatenate(sources[part : part + 2], axis=1))
                products += [both[:rows, :128], both[rows:, 128:]]
            for first in range(0, UNROLL, TOTALS):
                sums = [
                    total_refs[part][items[first + part][0], :rows] + products[first + part] for part in range(TOTALS)
                ]
                for part, value in enumerate(sums):
                    total_refs[part][items[first + part][0], :rows] = value
            return carry

        lax.fori_loop(first, first + count, blocks_step, 0)

    for number, rows in enumerate(CLASS_ROWS):
        run(rows, step_ref[0, 2 * number], step_ref[0, 2 * number + 1])

    def turn_step(step, carry):
        sums = [[total_ref[step * 8 + part] for total_ref in total_refs] for part in range(8)]
        sums = [sum(values[1:], values[0]) for values in sums]
        inner = (iota((p_width, 128), 1) >= 32) & (iota((p_width, 128), 1) < 96)
        for part in range(0, 8, 2):
            turned = jnp.where(inner, sums[part], pltpu.roll(sums[part + 1], 64, 1)).T
            out_ref[step * 8 + part] = turned[32 : 32 + q_width] + turned[32 + q_width : 32 + 2 * q_width]
            out_ref[step * 8 + part + 1] = turned[96 : 96 + q_width] + turned[:q_width]
        return carry

    lax.fori_loop(0, leaf_count // 8, turn_step, 0)


def as_column(line):
    width = line.shape[1]
    wide = jnp.concatenate([line, jnp.zeros((1, 128 - width), F32)], axis=1) if width < 128 else line
    return jnp.broadcast_to(wide, (128, 128)).T[:width, :width]


def plan_of(ulist_ref, counts, step_ref, piece_ref, item_ref):
    slot_count, leaf_count = ulist_ref.shape
    index = lax.axis_index("oct")
    shape = (leaf_count, leaf_count)
    row, column = iota(shape, 0), iota(shape, 1)
    tables = [as_column(line) for line in counts]
    own = jnp.broadcast_to(counts[1], shape)
    before = (tables[1] < own) | ((tables[1] == own) & (row < column))
    rank = jnp.sum(jnp.where(before, 1.0, 0.0), axis=0, keepdims=True)
    rank_column = as_column(rank).astype(jnp.int32)
    rank_wide = jnp.broadcast_to(rank, shape).astype(jnp.int32)

    block_pieces = BLOCK // PIECE
    empty = 6 * leaf_count
    place_shape = (PLACES, leaf_count)
    place_row = iota(place_shape, 0)
    listed = jnp.full(place_shape, empty, jnp.int32)
    offset = jnp.zeros((1, leaf_count), jnp.int32)
    for slot in range(slot_count):
        side = 1 if slot == 0 else (0 if slot < 9 else (1 if slot < 18 else 2))
        ids = ulist_ref[slot : slot + 1, :]
        place = jnp.where(ids >= 0, ids - (index + (side - 1)) * leaf_count, 0)
        found = jnp.sum(jnp.where(row == place, tables[side], 0.0), axis=0, keepdims=True).astype(jnp.int32)
        length = lax.shift_right_logical(found + (PIECE - 1), PIECE.bit_length() - 1)
        length = jnp.where(ids >= 0, length, 0)
        start = (place + (1, 0, 2)[side] * leaf_count) * 2
        inside = (place_row >= offset) & (place_row < offset + length)
        listed = jnp.where(inside, start + place_row - offset, listed)
        offset = offset + length

    blocks = lax.shift_right_logical(offset + (block_pieces - 1), block_pieces.bit_length() - 1)
    blocks_column = as_column(blocks.astype(F32))
    own_class = lax.shift_right_logical(counts[1].astype(jnp.int32) - 1, 4)
    class_column = as_column(own_class.astype(F32)).astype(jnp.int32)
    earlier = (class_column == jnp.broadcast_to(own_class, shape)) & (rank_column < rank_wide)
    first = jnp.sum(jnp.where(earlier, blocks_column, 0.0), axis=0, keepdims=True).astype(jnp.int32)
    lane = iota((1, 128), 1)
    steps_line = jnp.zeros((1, 128), jnp.int32)
    start = jnp.ones((1, 1), jnp.int32)
    for number in range(len(CLASS_ROWS)):
        inside = jnp.where(own_class == number, blocks.astype(F32), 0.0)
        items = jnp.sum(inside, axis=1, keepdims=True).astype(jnp.int32)
        steps = lax.shift_right_logical(items + (UNROLL - 1), UNROLL.bit_length() - 1)
        first = first + jnp.where(own_class == number, start * UNROLL, 0)
        steps_line = jnp.where(lane == 2 * number, start, jnp.where(lane == 2 * number + 1, steps, steps_line))
        start = start + steps
    step_ref[...] = steps_line

    first_column = as_column(first.astype(F32))[:, :1].astype(jnp.int32)
    blocks_column = blocks_column[:, :1].astype(jnp.int32)
    high = lax.shift_right_logical(listed, 8).astype(F32)
    low = jnp.bitwise_and(listed, 255).astype(F32)
    parts = jnp.concatenate([high, low], axis=0).astype(BF16)
    chunk = 1024
    wide = (leaf_count, chunk)
    column = iota(wide, 1)
    leaf_row = iota(wide, 0).astype(F32)
    for number in range(block_pieces):
        entry = column + chunk * number
        after = lax.shift_right_logical(entry, block_pieces.bit_length() - 1) - first_column
        inside = (after >= 0) & (after < blocks_column)
        place = after * block_pieces + jnp.bitwise_and(entry, block_pieces - 1)
        place = jnp.sum(jnp.where(inside, place.astype(F32), 0.0), axis=0, keepdims=True).astype(jnp.int32)
        found = jnp.sum(jnp.where(inside, 1.0, 0.0), axis=0, keepdims=True)
        both = dot(parts, jnp.where(inside, 1.0, 0.0).astype(BF16))
        value = both[:PLACES] * 256.0 + both[PLACES:]
        value = jnp.sum(jnp.where(iota((PLACES, chunk), 0) == place, value, 0.0), axis=0, keepdims=True)
        value = jnp.where(found > 0.0, value, float(empty)).astype(jnp.int32)
        for line in range(8):
            piece_ref[8 * number + line : 8 * number + line + 1, :] = value[:, line * 128 : (line + 1) * 128]
    after = column - first_column
    inside = (after >= 0) & (after < blocks_column)
    leaf = jnp.sum(jnp.where(inside, leaf_row - leaf_count, 0.0), axis=0, keepdims=True).astype(jnp.int32) + leaf_count
    for line in range(8):
        item_ref[line : line + 1, :] = leaf[:, line * 128 : (line + 1) * 128]


def final_kernel(
    level_count, counts_ref, feature_hbm, turned_hbm, near_hbm, far_ref, coarse_hbm, shift_ref, down_ref, *rest
):
    top_refs, rest = rest[:level_count], rest[level_count:]
    out_ref, node_ref, down_leaf_ref, lower_ref, upper_ref, turned_ref, near_ref, coarse_ref, sems = rest
    leaf_count, q_width, p_width = out_ref.shape
    eq_width = far_ref.shape[1]
    node_count = leaf_count // 8
    index = lax.axis_index("oct")
    ends = [(coarse_hbm.at[jnp.right_shift(index, 3 * level) & 7], coarse_ref.at[level]) for level in range(level_count)]
    ends += [(feature_hbm.at[0, :, 0], lower_ref), (feature_hbm.at[1, :, 1], upper_ref)]
    ends += [(turned_hbm, turned_ref), (near_hbm, near_ref)]
    copies = [pltpu.make_async_copy(*end, sems.at[number]) for number, end in enumerate(ends)]
    for copy in copies:
        copy.start()
    for copy in copies[:level_count]:
        copy.wait()
    slab_local = jnp.zeros((q_width, eq_width), F32)
    for level, top_ref in enumerate(top_refs):
        slab_local = slab_local + dot3(top_ref[:q_width, :], coarse_ref[level])
    for node in range(node_count):
        rows = slice(node * q_width, (node + 1) * q_width)
        node_ref[rows, :] = far_ref[rows, :] + dot3(slab_local, shift_ref[node])

    for child in range(8):
        down_leaf_ref[child] = dot3(dot3(node_ref[...], shift_ref[child]), down_ref[...])
    for copy in copies[level_count:]:
        copy.wait()
    lane = iota((q_width, p_width), 1)

    def node_step(node, carry):
        leaves = [node * 8 + child for child in range(8)]
        features = []
        for leaf in leaves:
            features.append((lower_ref[leaf] + upper_ref[leaf]).astype(BF16))
        turned = [turned_ref[2 * node + number] for number in range(2)]
        node_rows = pl.ds(pl.multiple_of(node * q_width, q_width), q_width)
        downs = [weight_rows(down_leaf_ref[child, node_rows, :]) for child in range(8)]
        nears = [near_ref[leaf] for leaf in leaves]
        blank = jnp.zeros((32, p_width), BF16)
        exponents = []
        for first in range(0, 8, 2):
            sides = []
            for child in (first, first + 1):
                lines = [features[child] if place == child % 4 else blank for place in range(4)]
                sides.append(jnp.concatenate(lines, axis=0))
            both = dot(turned[first // 4], jnp.concatenate(sides, axis=1))
            exponents += [both[:, :p_width], both[:, p_width:]]
        values = [halves(jnp.exp2(value)) for value in exponents]
        lefts = [jnp.concatenate(down, axis=0).astype(BF16) for down in downs]
        products = [dot(left, jnp.concatenate(value, axis=1)) for left, value in zip(lefts, values)]
        for child, leaf in enumerate(leaves):
            product = products[child]
            far = product[:q_width, :p_width] + product[q_width:, :p_width] + product[:q_width, p_width:]
            out_ref[leaf] = jnp.where(lane < counts_ref[leaf], far + nears[child], 0.0)
        return carry

    lax.fori_loop(0, node_count, node_step, 0)


def shifted(value, size):
    up = [(i, i + 1) for i in range(size - 1)]
    down = [(j, i) for i, j in up]
    return lax.ppermute(value, "oct", up), lax.ppermute(value, "oct", down)


def swapped(value, size, mask):
    return lax.ppermute(value, "oct", [(source, source ^ mask) for source in range(size)])


def local(
    points,
    dens,
    surface,
    counts,
    ulist,
    vlist,
    up_inverse,
    down_inverse,
    shift_up,
    shift_down,
    coarse,
    translate,
):
    leaf_count, q_width, p_width = dens.shape
    eq_width = surface.shape[2]
    node_count, type_count = vlist.shape
    node_rows = node_count * q_width
    size = lax.axis_size("oct")
    bits = size.bit_length() - 1
    level_count = -(-bits // 3)
    level_rows = level_count * q_width
    index = lax.axis_index("oct")
    vmem = pl.BlockSpec(memory_space=pltpu.VMEM)
    smem = pl.BlockSpec(memory_space=pltpu.SMEM)
    hbm = pl.BlockSpec(memory_space=pl.ANY)
    params = grant(56)
    points = jnp.transpose(points, (1, 0, 2))
    surface = jnp.transpose(surface, (1, 0, 2))
    ulist = ulist.T
    table = jnp.transpose(translate, (1, 2, 0))

    pack, send, slab = pl.pallas_call(
        lambda *refs: upward_kernel(level_count, *refs),
        out_shape=(
            jax.ShapeDtypeStruct((2 * leaf_count, PIECE, 128), F32),
            jax.ShapeDtypeStruct((node_rows + 2 * level_rows + 16, eq_width), BF16),
            jax.ShapeDtypeStruct((level_rows, eq_width), F32),
        ),
        in_specs=[vmem, vmem, vmem, smem, vmem, vmem, vmem],
        out_specs=(vmem,) * 3,
        scratch_shapes=[pltpu.VMEM((8, node_rows, eq_width), F32)],
        compiler_params=params,
        name="upward",
    )(points, dens, surface, counts, counts.reshape(1, leaf_count), up_inverse, shift_up)

    send_lower, send_upper = shifted(send, size)
    features, turned, message = pl.pallas_call(
        outline_kernel,
        out_shape=(
            jax.ShapeDtypeStruct((2, 2 * leaf_count, 32, p_width), F32),
            jax.ShapeDtypeStruct((leaf_count // 4, eq_width, 128), BF16),
            jax.ShapeDtypeStruct((leaf_count // 2, 2 * q_width + 8, p_width), F32),
        ),
        in_specs=[vmem, vmem, vmem, smem, hbm],
        out_specs=(vmem,) * 3,
        compiler_params=params,
        cost_estimate=pl.CostEstimate(flops=4 * 10**9, bytes_accessed=10**7, transcendentals=0),
        name="outline",
    )(points, dens, surface, counts, slab)
    lower, upper = shifted(message, size)
    send_lower, send_upper, features = lax.optimization_barrier((send_lower, send_upper, features))
    ends = slice(node_rows, node_rows + 2 * level_rows)
    partner = jnp.where(index & 1 == 1, send_lower[ends], send_upper[ends]).astype(F32)
    total = slab + (partner[:level_rows] + partner[level_rows:])
    total = total + swapped(total, size, 2)
    arrived = swapped(total, size, 4)
    send_lower, total = lax.optimization_barrier((send_lower, total))

    table = table.reshape(eq_width * eq_width, type_count)
    far_node, steps, piece_table, items = pl.pallas_call(
        far_kernel,
        out_shape=(
            jax.ShapeDtypeStruct((node_rows, eq_width), F32),
            jax.ShapeDtypeStruct((1, 128), jnp.int32),
            jax.ShapeDtypeStruct((32, 128), jnp.int32),
            jax.ShapeDtypeStruct((8, 128), jnp.int32),
        ),
        in_specs=[vmem, vmem, vmem, vmem, vmem, hbm],
        out_specs=(vmem,) * 4,
        scratch_shapes=[
            pltpu.VMEM((type_count // 128, eq_width * eq_width, 128), BF16),
            pltpu.VMEM((eq_width * eq_width, type_count % 128), BF16),
            pltpu.VMEM((eq_width * SOURCES, 128), F32),
            pltpu.VMEM((eq_width, node_rows), F32),
            pltpu.VMEM((CHUNK * eq_width, node_rows), F32),
            pltpu.SemaphoreType.DMA((eq_width // CHUNK, type_count // 128 + 1)),
        ],
        compiler_params=params,
        cost_estimate=pl.CostEstimate(flops=2 * 10**10, bytes_accessed=18 * 10**6, transcendentals=0),
        name="far",
    )(send_lower, send, send_upper, vlist, ulist, table)
    far_node, lower, upper = lax.optimization_barrier((far_node, lower, upper))

    far_node, total, arrived = lax.optimization_barrier((far_node, total, arrived))
    total = total + arrived
    shares = total[q_width:]
    others = [swapped(shares, size, mask << 3) for mask in range(1, size >> 3)]
    steps, shares = lax.optimization_barrier((steps, shares))
    near = pl.pallas_call(
        near_kernel,
        out_shape=jax.ShapeDtypeStruct((leaf_count, q_width, p_width), F32),
        in_specs=[smem, smem, smem, hbm, hbm, vmem, vmem],
        out_specs=vmem,
        scratch_shapes=[
            pltpu.VMEM((6 * leaf_count + 1, PIECE, 128), F32),
            pltpu.VMEM((2, 6 * leaf_count + 1, 32, 128), F32),
            *[pltpu.VMEM((leaf_count + 1, p_width, 128), F32)] * TOTALS,
            pltpu.SemaphoreType.DMA((2,)),
        ],
        compiler_params=params,
        cost_estimate=pl.CostEstimate(flops=3 * 10**10, bytes_accessed=10**7, transcendentals=0),
        name="near",
    )(steps, piece_table.reshape(-1), items.reshape(-1), pack, features, lower, upper)

    tops = [total]
    for level in range(1, level_count):
        rows = slice((level - 1) * q_width, level * q_width)
        group = 1 << (min(3 * level + 3, bits) - 3)
        tops.append(sum([other[rows] for other in others[: group - 1]], shares[rows]))
    return pl.pallas_call(
        lambda *refs: final_kernel(level_count, *refs),
        out_shape=jax.ShapeDtypeStruct((leaf_count, q_width, p_width), F32),
        in_specs=[smem, hbm, hbm, hbm, vmem, hbm] + [vmem] * (2 + len(tops)),
        out_specs=vmem,
        scratch_shapes=[
            pltpu.VMEM((node_rows, eq_width), F32),
            pltpu.VMEM((8, node_rows, eq_width), F32),
            pltpu.VMEM((leaf_count, 32, p_width), F32),
            pltpu.VMEM((leaf_count, 32, p_width), F32),
            pltpu.VMEM((leaf_count // 4, eq_width, 128), BF16),
            pltpu.VMEM((leaf_count, q_width, p_width), F32),
            pltpu.VMEM((level_count, eq_width, eq_width), F32),
            pltpu.SemaphoreType.DMA((level_count + 4,)),
        ],
        compiler_params=params,
        name="final",
    )(counts, features.reshape(2, leaf_count, 2, 32, p_width), turned, near, far_node, coarse, shift_down, down_inverse, *tops)


def solution(mesh):
    placed = (
        P("oct", None, None),
        P("oct", None, None),
        P("oct", None, None),
        P("oct"),
        P("oct", None),
        P("oct", None),
        P(),
        P(),
        P(),
        P(),
        P(),
        P(),
    )
    return jax.shard_map(
        local, mesh=mesh, in_specs=placed, out_specs=P("oct", None, None), check_vma=False
    )
```

```python
import math

import jax
import jax.numpy as jnp
from jax import lax
from jax.experimental import pallas as pl
from jax.experimental.pallas import tpu as pltpu
from jax.sharding import PartitionSpec as P

F32 = jnp.float32
BF16 = jnp.bfloat16
HIGHEST = lax.Precision.HIGHEST
SCALE = math.sqrt(math.log2(math.e))
NT = (((1,), (1,)), ((), ()))
TN = (((0,), (0,)), ((), ()))
BLOCK = 256
UNROLL = 8
TOTALS = 2
PIECE = 64
CLASS_ROWS = tuple(range(16, 129, 16))
PLACES = 56
SOURCES = 32
CHUNK = 4
FIRST, SECOND = 16, 8


def dot(left, right):
    return jnp.dot(left, right, preferred_element_type=F32)


def dot_nt(left, right):
    return lax.dot_general(left, right, NT, preferred_element_type=F32)


def dot_tn(left, right):
    return lax.dot_general(left, right, TN, preferred_element_type=F32)


def halves(value):
    high = value.astype(BF16)
    low = (value - high.astype(F32)).astype(BF16)
    return high, low


def dot3(left, right):
    left_high, left_low = halves(left)
    right_high, right_low = halves(right)
    return dot(left_high, right_high) + dot(left_high, right_low) + dot(left_low, right_high)


def grant(mebibytes):
    return pltpu.CompilerParams(vmem_limit_bytes=mebibytes * 1024 * 1024)


def iota(shape, dim):
    return lax.broadcasted_iota(jnp.int32, shape, dim)


def coords_of(ref, leaf):
    width = ref.shape[2]
    row = iota((8, width), 0)
    value = jnp.zeros((8, width), F32)
    for dim in range(3):
        line = jnp.broadcast_to(ref[dim, pl.ds(leaf, 1), :], (8, width))
        value = jnp.where(row == dim, line, value)
    return value


def pieces(coords):
    row = iota(coords.shape, 0)
    used = row < 3
    scaled = jnp.where(used, coords, 0.0) * SCALE
    high = scaled.astype(BF16).astype(F32)
    rest = scaled - high
    mid = rest.astype(BF16).astype(F32)
    low = (rest - mid).astype(BF16).astype(F32)
    norm = -0.5 * jnp.sum(scaled * scaled, axis=0, keepdims=True)
    norm_high = norm.astype(BF16).astype(F32)
    norm_rest = norm - norm_high
    norm_mid = norm_rest.astype(BF16).astype(F32)
    norm_low = norm_rest - norm_mid
    norms = jnp.where(row == 0, norm_high, jnp.where(row == 1, norm_mid, jnp.where(row == 2, norm_low, 0.0)))
    ones = jnp.where(used, 1.0, 0.0)
    return high, mid, low, norms, ones


def paired(first, second):
    return first + pltpu.roll(second, 4, 0)


def left_rows(parts):
    high, mid, low, norms, ones = parts
    return jnp.concatenate([paired(high, high), paired(mid, mid), paired(high, low), paired(ones, norms)], axis=0)


def right_rows(parts):
    high, mid, low, norms, ones = parts
    both = paired(high, mid)
    return jnp.concatenate([both, both, paired(low, high), paired(norms, ones)], axis=0)


def weight_rows(weights):
    high = weights.astype(BF16).astype(F32)
    return [high, weights - high]


def feature_versions(rows):
    lower = iota(rows.shape, 1) < PIECE
    versions = []
    for half in range(2):
        alone = jnp.where(lower == (half == 0), rows, 0.0)
        versions.append((half, half, alone.astype(BF16)))
        versions.append((half, 1 - half, pltpu.roll(alone, PIECE, 1).astype(BF16)))
    return versions


def put_features(feature_ref, leaf, versions):
    for half, place, value in versions:
        feature_ref[place, 2 * leaf + half] = value


def put_pack(pack_ref, leaf, value):
    pack_ref[pl.ds(2 * leaf, 2)] = value.reshape(2, PIECE, 128)


def upward_kernel(
    level_count, points_ref, dens_ref, surface_ref, counts_ref, count_line_ref, up_ref, shift_ref, pack_ref, send_ref,
    slab_ref, check_ref
):
    leaf_count, q_width, p_width = dens_ref.shape
    eq_width = surface_ref.shape[2]
    node_count = leaf_count // 8
    lane = iota((q_width, p_width), 1)

    def node_step(node, carry):
        leaves = [node * 8 + child for child in range(8)]
        counts = [counts_ref[leaf] for leaf in leaves]
        weights = [jnp.where(lane < count, dens_ref[leaf], 0.0) for leaf, count in zip(leaves, counts)]
        coords = [coords_of(points_ref, leaf) for leaf in leaves]
        surfaces = [left_rows(pieces(coords_of(surface_ref, leaf))) for leaf in leaves]
        parts = [pieces(value) for value in coords]
        rights = [right_rows(value) for value in parts]
        lists = [weight_rows(value) for value in weights]
        packs = [
            jnp.concatenate([left_rows(part)] + split + [right], axis=0).astype(BF16).T
            for part, split, right in zip(parts, lists, rights)
        ]
        blank = jnp.zeros((96, eq_width), F32)
        wides = [jnp.concatenate([blank, value], axis=0).astype(BF16) for value in surfaces]
        exponents = [dot(pack, wide) for pack, wide in zip(packs, wides)]
        values = [halves(jnp.exp2(value)) for value in exponents]
        rows = [jnp.concatenate(split, axis=0).astype(BF16) for split in lists]
        firsts = [dot(row, value[0]) for row, value in zip(rows, values)]
        seconds = [dot(row[:q_width], value[1]) for row, value in zip(rows, values)]
        for child, leaf in enumerate(leaves):
            put_pack(pack_ref, leaf, packs[child])
            check = firsts[child][:q_width] + firsts[child][q_width:] + seconds[child]
            check_ref[child, pl.ds(pl.multiple_of(node * q_width, q_width), q_width), :] = check
        return carry

    lax.fori_loop(0, node_count, node_step, 0)

    node_eq = jnp.zeros((node_count * q_width, eq_width), F32)
    for child in range(8):
        node_eq = node_eq + dot3(dot3(check_ref[child], up_ref[...]), shift_ref[child])
    send_ref[: node_count * q_width, :] = node_eq.astype(BF16)
    slab_eq = jnp.zeros((q_width, eq_width), F32)
    for child in range(8):
        slab_eq = slab_eq + dot3(node_eq[child * q_width : (child + 1) * q_width], shift_ref[child])
    index = lax.axis_index("oct")
    slab = slab_eq
    start = node_count * q_width
    for level in range(level_count):
        slab = dot3(slab, shift_ref[jnp.right_shift(index, 3 * level) & 7])
        slab_ref[level * q_width : (level + 1) * q_width, :] = slab
        high, rest = halves(slab)
        for place, part in enumerate((high, rest)):
            first = start + (place * level_count + level) * q_width
            send_ref[first : first + q_width, :] = part
    start = start + 2 * level_count * q_width
    line = jnp.concatenate([count_line_ref[...].astype(F32), jnp.zeros((1, eq_width - leaf_count), F32)], axis=1)
    send_ref[start : start + 16, :] = jnp.broadcast_to(line, (16, eq_width)).astype(BF16)


def outline_kernel(
    points_ref, dens_ref, surface_ref, counts_ref, order_ref, feature_ref, turned_ref, message_ref
):
    leaf_count, q_width, p_width = dens_ref.shape
    lane = iota((q_width, p_width), 1)

    def node_step(node, carry):
        leaves = [node * 8 + child for child in range(8)]
        counts = [counts_ref[leaf] for leaf in leaves]
        weights = [jnp.where(lane < count, dens_ref[leaf], 0.0) for leaf, count in zip(leaves, counts)]
        coords = [coords_of(points_ref, leaf) for leaf in leaves]
        surfaces = [left_rows(pieces(coords_of(surface_ref, leaf))) for leaf in leaves]
        versions = [feature_versions(right_rows(pieces(value))) for value in coords]
        fours = [jnp.concatenate(surfaces[first : first + 4], axis=0).astype(BF16).T for first in range(0, 8, 4)]
        for number, four in enumerate(fours):
            turned_ref[2 * node + number] = four
        for child, leaf in enumerate(leaves):
            pair, side = node * 4 + child // 2, child % 2
            message_ref[pair, side * q_width : (side + 1) * q_width, :] = weights[child]
            put_features(feature_ref, leaf, versions[child])
        for number in range(4):
            message_ref[node * 4 + number, 2 * q_width :, :] = paired(coords[2 * number], coords[2 * number + 1])
        return carry

    lax.fori_loop(0, leaf_count // 8, node_step, 0)


def far_kernel(
    lower_ref, own_ref, upper_ref, vlist_ref, ulist_ref, table_hbm, out_ref, step_ref, piece_ref, item_ref, table_ref,
    tail_ref, wide_ref, total_ref, first_ref, sems
):
    node_count, type_count = vlist_ref.shape
    eq_width = own_ref.shape[1]
    q_width = out_ref.shape[0] // node_count
    lanes = node_count * q_width
    tile = 128 // q_width
    chunk = CHUNK
    chunk_rows = chunk * eq_width
    chunk_count = eq_width // chunk
    full = type_count // 128

    def copies_of(number):
        span = pl.ds(number * chunk_rows, chunk_rows)
        copies = []
        for part in range(full):
            source = table_hbm.at[span, pl.ds(part * 128, 128)]
            copies.append(pltpu.make_async_copy(source, table_ref.at[part, span], sems.at[number, part]))
        source = table_hbm.at[span, pl.ds(full * 128, type_count - full * 128)]
        copies.append(pltpu.make_async_copy(source, tail_ref.at[span], sems.at[number, full]))
        return copies

    for number in range(chunk_count):
        for copy in copies_of(number):
            copy.start()

    index = lax.axis_index("oct")
    repeat = (iota((q_width, 128), 1) % q_width == iota((q_width, 128), 0)).astype(BF16)
    for part, source in enumerate((lower_ref, own_ref, upper_ref)):
        for node in range(node_count):
            spread = dot_tn(source[node * q_width : (node + 1) * q_width, :], repeat)
            wide_ref[pl.ds(part * node_count + node, eq_width, stride=SOURCES), :] = spread
    for place in range(3 * node_count, SOURCES):
        wide_ref[pl.ds(place, eq_width, stride=SOURCES), :] = jnp.zeros((eq_width, 128), F32)

    ids = vlist_ref[...]
    places = jnp.where(ids >= 0, ids - (index - 1) * node_count, -1).astype(F32).astype(BF16)
    lane = iota((1, lanes), 1)
    second_half = jnp.bitwise_and(lane, 63)
    node_of = jnp.where(lane < 128, lane // FIRST, second_half // SECOND)
    source_of = jnp.where(lane < 128, lane % FIRST, FIRST + second_half % SECOND)
    spread = (jnp.broadcast_to(node_of, (node_count, lanes)) == iota((node_count, lanes), 0)).astype(BF16)
    wanted = dot_tn(places, spread)
    chosen = (wanted == source_of.astype(F32)).astype(F32)
    chosen_full = chosen[: full * 128].astype(BF16)
    chosen_tail = chosen[full * 128 :].astype(BF16)
    lane_node = iota((SOURCES, 128), 1) // q_width
    lower_lanes = iota((eq_width, 128), 1) < 64
    total_ref[...] = jnp.zeros_like(total_ref)

    leaf_count = ulist_ref.shape[1]
    start = own_ref.shape[0] - 16
    lines = [ref[start:, :].astype(F32)[:1, :leaf_count] for ref in (lower_ref, own_ref, upper_ref)]
    plan_of(ulist_ref, lines, step_ref, piece_ref, item_ref)

    def table_of(number):
        span = pl.ds(pl.multiple_of(number * chunk_rows, chunk_rows), chunk_rows)
        left = jnp.concatenate([table_ref[part, span, :] for part in range(full)], axis=1)
        return left, tail_ref[span, :]

    def first_product(left, tail):
        return dot(left, chosen_full) + dot(tail, chosen_tail)

    def block_rows(sents, first, count):
        lines = []
        for sent in sents:
            blank = jnp.zeros((count, 128), F32)
            for node in range(node_count):
                own = sent[node % tile][first : first + count]
                line = [own if place == node // tile else blank for place in range(node_count // tile)]
                lines.append(jnp.concatenate(line, axis=1))
        return lines

    def second_product(number, summed):
        lefts, rights = [], []
        for step in range(0, chunk, 2):
            sents = []
            for place in (step, step + 1):
                row = number * chunk + place
                sent = wide_ref[pl.ds(pl.multiple_of(row * SOURCES, SOURCES), SOURCES), :]
                sents.append([jnp.where(lane_node == part, sent, 0.0) for part in range(tile)])
            pair = [summed[place * eq_width : (place + 1) * eq_width] for place in (step, step + 1)]
            tiles = [pair[0][:, :128], pair[1][:, :128], jnp.where(lower_lanes, pair[0][:, 128:], pair[1][:, 128:])]
            for value in tiles:
                high = value.astype(BF16).astype(F32)
                lefts.append(jnp.concatenate([high, value - high], axis=0).astype(BF16))
            rights += block_rows(sents, 0, FIRST) + block_rows(sents, FIRST, SECOND)
        product = dot(jnp.concatenate(lefts, axis=1), jnp.concatenate(rights, axis=0).astype(BF16))
        return product[:eq_width] + product[eq_width:]

    def wait_for(number):
        for copy in copies_of(number):
            copy.wait()

    wait_for(0)
    first_ref[...] = first_product(*table_of(0))

    def pair_step(pair, carry):
        number = 2 * pair
        wait_for(number + 1)
        pl.when(pair < chunk_count // 2 - 1)(lambda: wait_for(number + 2))
        ahead = table_of(number + 1)
        behind = table_of(jnp.minimum(number + 2, chunk_count - 1))
        summed = first_ref[...]
        middle = first_product(*ahead)
        total = second_product(number, summed)
        following = first_product(*behind)
        total = total + second_product(number + 1, middle)
        first_ref[...] = following
        total_ref[...] += total
        return carry

    lax.fori_loop(0, chunk_count // 2, pair_step, 0)
    out_ref[...] = total_ref[...].T


def near_kernel(
    step_ref, piece_ref, item_ref, own_hbm, own_feature_hbm, lower_ref, upper_ref, out_ref, pack_ref, *rest
):
    total_refs, sems = rest[:TOTALS], rest[TOTALS]
    leaf_count, q_width, p_width = out_ref.shape
    own = pl.ds(0, 2 * leaf_count)
    ends = [(own_hbm, pack_ref.at[own, pl.ds(0, PIECE)])]
    ends += [(own_feature_hbm.at[half], pack_ref.at[own, pl.ds(PIECE + 32 * half, 32)]) for half in range(2)]
    copies = [pltpu.make_async_copy(*end, sems.at[number]) for number, end in enumerate(ends)]
    for copy in copies:
        copy.start()
    pack_ref[6 * leaf_count] = jnp.zeros((2 * PIECE, 128), BF16)
    for total_ref in total_refs:
        total_ref[...] = jnp.zeros_like(total_ref)
    def pack_step(step, carry):
        chosen = [(part, side) for side in range(2) for part in range(4)]
        sources = (lower_ref, upper_ref)
        weights, versions = [], []
        for part, side in chosen:
            place, half = step * 2 + part // 2, part % 2
            weights.append(weight_rows(sources[side][place, half * q_width : (half + 1) * q_width, :]))
            tail = sources[side][place, 2 * q_width :, :]
            tail = pltpu.roll(tail, 4, 0) if half else tail
            versions.append(feature_versions(right_rows(pieces(tail))))
        packs = []
        for part in range(0, len(chosen), 2):
            (high, low), (next_high, next_low) = weights[part : part + 2]
            both = jnp.concatenate([next_low, high, low, next_high], axis=0).astype(BF16).T
            packs += [both, pltpu.roll(both.astype(F32), 64, 1).astype(BF16)]
        for (part, side), pack, version in zip(chosen, packs, versions):
            place = (1 + side) * leaf_count + step * 4 + part
            pack_ref[pl.ds(2 * place, 2), :PIECE] = pack.reshape(2, PIECE, 128)
            for half, number, value in version:
                pack_ref[2 * place + half, PIECE + 32 * number : PIECE + 32 * (number + 1)] = value
        return carry

    lax.fori_loop(0, leaf_count // 4, pack_step, 0)
    for copy in copies:
        copy.wait()
    block_pieces = BLOCK // PIECE

    def items_of(step):
        first = step * UNROLL
        leaves = [item_ref[first + part] for part in range(UNROLL)]
        first = first * block_pieces
        pieces_of = [
            [piece_ref[first + part * block_pieces + number] for number in range(block_pieces)] for part in range(UNROLL)
        ]
        return list(zip(leaves, pieces_of))

    def sources_of(numbers):
        return jnp.concatenate([pack_ref[number, :PIECE] for number in numbers], axis=0)

    def features_of(numbers):
        tiles = []
        for tile in range(BLOCK // 128):
            lower = pack_ref[numbers[2 * tile], PIECE : PIECE + 32]
            tiles.append(lower + pack_ref[numbers[2 * tile + 1], PIECE + 32 :])
        return jnp.concatenate(tiles, axis=1)

    def targets_of(leaf, rows):
        first = 2 * leaf
        if rows <= PIECE:
            return pack_ref[first, :rows][:, :32]
        return jnp.concatenate([pack_ref[first, :PIECE][:, :32], pack_ref[first + 1, : rows - PIECE][:, :32]], axis=0)

    def run(rows, first, count):
        def blocks_step(step, carry):
            items = items_of(step)
            features = [features_of(numbers) for _, numbers in items]
            targets = [targets_of(leaf, rows) for leaf, _ in items]
            sources = [sources_of(numbers) for _, numbers in items]
            exponents = [dot(target, feature) for target, feature in zip(targets, features)]
            values = [jnp.exp2(value).astype(BF16) for value in exponents]
            products = []
            for part in range(0, UNROLL, 2):
                left = jnp.concatenate(values[part : part + 2], axis=0)
                both = dot(left, jnp.concatenate(sources[part : part + 2], axis=1))
                products += [both[:rows, :128], both[rows:, 128:]]
            for first in range(0, UNROLL, TOTALS):
                sums = [
                    total_refs[part][items[first + part][0], :rows] + products[first + part] for part in range(TOTALS)
                ]
                for part, value in enumerate(sums):
                    total_refs[part][items[first + part][0], :rows] = value
            return carry

        lax.fori_loop(first, first + count, blocks_step, 0)

    for number, rows in enumerate(CLASS_ROWS):
        run(rows, step_ref[0, 2 * number], step_ref[0, 2 * number + 1])

    def turn_step(step, carry):
        sums = [[total_ref[step * 8 + part] for total_ref in total_refs] for part in range(8)]
        sums = [sum(values[1:], values[0]) for values in sums]
        inner = (iota((p_width, 128), 1) >= 32) & (iota((p_width, 128), 1) < 96)
        for part in range(0, 8, 2):
            turned = jnp.where(inner, sums[part], pltpu.roll(sums[part + 1], 64, 1)).T
            out_ref[step * 8 + part] = turned[32 : 32 + q_width] + turned[32 + q_width : 32 + 2 * q_width]
            out_ref[step * 8 + part + 1] = turned[96 : 96 + q_width] + turned[:q_width]
        return carry

    lax.fori_loop(0, leaf_count // 8, turn_step, 0)


def as_column(line):
    width = line.shape[1]
    wide = jnp.concatenate([line, jnp.zeros((1, 128 - width), F32)], axis=1) if width < 128 else line
    return jnp.broadcast_to(wide, (128, 128)).T[:width, :width]


def plan_of(ulist_ref, counts, step_ref, piece_ref, item_ref):
    slot_count, leaf_count = ulist_ref.shape
    index = lax.axis_index("oct")
    shape = (leaf_count, leaf_count)
    row, column = iota(shape, 0), iota(shape, 1)
    tables = [as_column(line) for line in counts]
    own = jnp.broadcast_to(counts[1], shape)
    before = (tables[1] < own) | ((tables[1] == own) & (row < column))
    rank = jnp.sum(jnp.where(before, 1.0, 0.0), axis=0, keepdims=True)
    rank_column = as_column(rank).astype(jnp.int32)
    rank_wide = jnp.broadcast_to(rank, shape).astype(jnp.int32)

    block_pieces = BLOCK // PIECE
    empty = 6 * leaf_count
    place_shape = (PLACES, leaf_count)
    place_row = iota(place_shape, 0)
    listed = jnp.full(place_shape, empty, jnp.int32)
    offset = jnp.zeros((1, leaf_count), jnp.int32)
    for slot in range(slot_count):
        side = 1 if slot == 0 else (0 if slot < 9 else (1 if slot < 18 else 2))
        ids = ulist_ref[slot : slot + 1, :]
        place = jnp.where(ids >= 0, ids - (index + (side - 1)) * leaf_count, 0)
        found = jnp.sum(jnp.where(row == place, tables[side], 0.0), axis=0, keepdims=True).astype(jnp.int32)
        length = lax.shift_right_logical(found + (PIECE - 1), PIECE.bit_length() - 1)
        length = jnp.where(ids >= 0, length, 0)
        start = (place + (1, 0, 2)[side] * leaf_count) * 2
        inside = (place_row >= offset) & (place_row < offset + length)
        listed = jnp.where(inside, start + place_row - offset, listed)
        offset = offset + length

    blocks = lax.shift_right_logical(offset + (block_pieces - 1), block_pieces.bit_length() - 1)
    blocks_column = as_column(blocks.astype(F32))
    own_class = lax.shift_right_logical(counts[1].astype(jnp.int32) - 1, 4)
    class_column = as_column(own_class.astype(F32)).astype(jnp.int32)
    earlier = (class_column == jnp.broadcast_to(own_class, shape)) & (rank_column < rank_wide)
    first = jnp.sum(jnp.where(earlier, blocks_column, 0.0), axis=0, keepdims=True).astype(jnp.int32)
    lane = iota((1, 128), 1)
    steps_line = jnp.zeros((1, 128), jnp.int32)
    start = jnp.ones((1, 1), jnp.int32)
    for number in range(len(CLASS_ROWS)):
        inside = jnp.where(own_class == number, blocks.astype(F32), 0.0)
        items = jnp.sum(inside, axis=1, keepdims=True).astype(jnp.int32)
        steps = lax.shift_right_logical(items + (UNROLL - 1), UNROLL.bit_length() - 1)
        first = first + jnp.where(own_class == number, start * UNROLL, 0)
        steps_line = jnp.where(lane == 2 * number, start, jnp.where(lane == 2 * number + 1, steps, steps_line))
        start = start + steps
    step_ref[...] = steps_line

    first_column = as_column(first.astype(F32))[:, :1].astype(jnp.int32)
    blocks_column = blocks_column[:, :1].astype(jnp.int32)
    high = lax.shift_right_logical(listed, 8).astype(F32)
    low = jnp.bitwise_and(listed, 255).astype(F32)
    parts = jnp.concatenate([high, low], axis=0).astype(BF16)
    chunk = 1024
    wide = (leaf_count, chunk)
    column = iota(wide, 1)
    leaf_row = iota(wide, 0).astype(F32)
    for number in range(block_pieces):
        entry = column + chunk * number
        after = lax.shift_right_logical(entry, block_pieces.bit_length() - 1) - first_column
        inside = (after >= 0) & (after < blocks_column)
        place = after * block_pieces + jnp.bitwise_and(entry, block_pieces - 1)
        place = jnp.sum(jnp.where(inside, place.astype(F32), 0.0), axis=0, keepdims=True).astype(jnp.int32)
        found = jnp.sum(jnp.where(inside, 1.0, 0.0), axis=0, keepdims=True)
        both = dot(parts, jnp.where(inside, 1.0, 0.0).astype(BF16))
        value = both[:PLACES] * 256.0 + both[PLACES:]
        value = jnp.sum(jnp.where(iota((PLACES, chunk), 0) == place, value, 0.0), axis=0, keepdims=True)
        value = jnp.where(found > 0.0, value, float(empty)).astype(jnp.int32)
        for line in range(8):
            piece_ref[8 * number + line : 8 * number + line + 1, :] = value[:, line * 128 : (line + 1) * 128]
    after = column - first_column
    inside = (after >= 0) & (after < blocks_column)
    leaf = jnp.sum(jnp.where(inside, leaf_row - leaf_count, 0.0), axis=0, keepdims=True).astype(jnp.int32) + leaf_count
    for line in range(8):
        item_ref[line : line + 1, :] = leaf[:, line * 128 : (line + 1) * 128]


def final_kernel(
    level_count, counts_ref, feature_hbm, turned_hbm, near_hbm, far_ref, coarse_hbm, shift_ref, down_ref, *rest
):
    top_refs, rest = rest[:level_count], rest[level_count:]
    out_ref, node_ref, down_leaf_ref, lower_ref, upper_ref, turned_ref, near_ref, coarse_ref, sems = rest
    leaf_count, q_width, p_width = out_ref.shape
    eq_width = far_ref.shape[1]
    node_count = leaf_count // 8
    index = lax.axis_index("oct")
    ends = [(coarse_hbm.at[jnp.right_shift(index, 3 * level) & 7], coarse_ref.at[level]) for level in range(level_count)]
    ends += [(feature_hbm.at[0, :, 0], lower_ref), (feature_hbm.at[1, :, 1], upper_ref)]
    ends += [(turned_hbm, turned_ref), (near_hbm, near_ref)]
    copies = [pltpu.make_async_copy(*end, sems.at[number]) for number, end in enumerate(ends)]
    for copy in copies:
        copy.start()
    for copy in copies[:level_count]:
        copy.wait()
    slab_local = jnp.zeros((q_width, eq_width), F32)
    for level, top_ref in enumerate(top_refs):
        slab_local = slab_local + dot3(top_ref[:q_width, :], coarse_ref[level])
    for node in range(node_count):
        rows = slice(node * q_width, (node + 1) * q_width)
        node_ref[rows, :] = far_ref[rows, :] + dot3(slab_local, shift_ref[node])

    for child in range(8):
        down_leaf_ref[child] = dot3(dot3(node_ref[...], shift_ref[child]), down_ref[...])
    for copy in copies[level_count:]:
        copy.wait()
    lane = iota((q_width, p_width), 1)

    def node_step(node, carry):
        leaves = [node * 8 + child for child in range(8)]
        features = []
        for leaf in leaves:
            features.append(lower_ref[leaf] + upper_ref[leaf])
        turned = [turned_ref[2 * node + number] for number in range(2)]
        node_rows = pl.ds(pl.multiple_of(node * q_width, q_width), q_width)
        downs = [weight_rows(down_leaf_ref[child, node_rows, :]) for child in range(8)]
        nears = [near_ref[leaf] for leaf in leaves]
        blank = jnp.zeros((32, p_width), BF16)
        exponents = []
        for first in range(0, 8, 2):
            sides = []
            for child in (first, first + 1):
                lines = [features[child] if place == child % 4 else blank for place in range(4)]
                sides.append(jnp.concatenate(lines, axis=0))
            both = dot(turned[first // 4], jnp.concatenate(sides, axis=1))
            exponents += [both[:, :p_width], both[:, p_width:]]
        values = [halves(jnp.exp2(value)) for value in exponents]
        lefts = [jnp.concatenate(down, axis=0).astype(BF16) for down in downs]
        products = [dot(left, jnp.concatenate(value, axis=1)) for left, value in zip(lefts, values)]
        for child, leaf in enumerate(leaves):
            product = products[child]
            far = product[:q_width, :p_width] + product[q_width:, :p_width] + product[:q_width, p_width:]
            out_ref[leaf] = jnp.where(lane < counts_ref[leaf], far + nears[child], 0.0)
        return carry

    lax.fori_loop(0, node_count, node_step, 0)


def shifted(value, size):
    up = [(i, i + 1) for i in range(size - 1)]
    down = [(j, i) for i, j in up]
    return lax.ppermute(value, "oct", up), lax.ppermute(value, "oct", down)


def swapped(value, size, mask):
    return lax.ppermute(value, "oct", [(source, source ^ mask) for source in range(size)])


def local(
    points,
    dens,
    surface,
    counts,
    ulist,
    vlist,
    up_inverse,
    down_inverse,
    shift_up,
    shift_down,
    coarse,
    translate,
):
    leaf_count, q_width, p_width = dens.shape
    eq_width = surface.shape[2]
    node_count, type_count = vlist.shape
    node_rows = node_count * q_width
    size = lax.axis_size("oct")
    bits = size.bit_length() - 1
    level_count = -(-bits // 3)
    level_rows = level_count * q_width
    index = lax.axis_index("oct")
    vmem = pl.BlockSpec(memory_space=pltpu.VMEM)
    smem = pl.BlockSpec(memory_space=pltpu.SMEM)
    hbm = pl.BlockSpec(memory_space=pl.ANY)
    params = grant(56)
    points = jnp.transpose(points, (1, 0, 2))
    surface = jnp.transpose(surface, (1, 0, 2))
    ulist = ulist.T
    table = jnp.transpose(translate, (1, 2, 0))

    pack, send, slab = pl.pallas_call(
        lambda *refs: upward_kernel(level_count, *refs),
        out_shape=(
            jax.ShapeDtypeStruct((2 * leaf_count, PIECE, 128), BF16),
            jax.ShapeDtypeStruct((node_rows + 2 * level_rows + 16, eq_width), BF16),
            jax.ShapeDtypeStruct((level_rows, eq_width), F32),
        ),
        in_specs=[vmem, vmem, vmem, smem, vmem, vmem, vmem],
        out_specs=(vmem,) * 3,
        scratch_shapes=[pltpu.VMEM((8, node_rows, eq_width), F32)],
        compiler_params=params,
        name="upward",
    )(points, dens, surface, counts, counts.reshape(1, leaf_count), up_inverse, shift_up)

    send_lower, send_upper = shifted(send, size)
    features, turned, message = pl.pallas_call(
        outline_kernel,
        out_shape=(
            jax.ShapeDtypeStruct((2, 2 * leaf_count, 32, p_width), BF16),
            jax.ShapeDtypeStruct((leaf_count // 4, eq_width, 128), BF16),
            jax.ShapeDtypeStruct((leaf_count // 2, 2 * q_width + 8, p_width), F32),
        ),
        in_specs=[vmem, vmem, vmem, smem, hbm],
        out_specs=(vmem,) * 3,
        compiler_params=params,
        cost_estimate=pl.CostEstimate(flops=4 * 10**9, bytes_accessed=10**7, transcendentals=0),
        name="outline",
    )(points, dens, surface, counts, slab)
    lower, upper = shifted(message, size)
    send_lower, send_upper, features = lax.optimization_barrier((send_lower, send_upper, features))
    ends = slice(node_rows, node_rows + 2 * level_rows)
    partner = jnp.where(index & 1 == 1, send_lower[ends], send_upper[ends]).astype(F32)
    total = slab + (partner[:level_rows] + partner[level_rows:])
    total = total + swapped(total, size, 2)
    arrived = swapped(total, size, 4)
    send_lower, total = lax.optimization_barrier((send_lower, total))

    table = table.reshape(eq_width * eq_width, type_count)
    far_node, steps, piece_table, items = pl.pallas_call(
        far_kernel,
        out_shape=(
            jax.ShapeDtypeStruct((node_rows, eq_width), F32),
            jax.ShapeDtypeStruct((1, 128), jnp.int32),
            jax.ShapeDtypeStruct((32, 128), jnp.int32),
            jax.ShapeDtypeStruct((8, 128), jnp.int32),
        ),
        in_specs=[vmem, vmem, vmem, vmem, vmem, hbm],
        out_specs=(vmem,) * 4,
        scratch_shapes=[
            pltpu.VMEM((type_count // 128, eq_width * eq_width, 128), BF16),
            pltpu.VMEM((eq_width * eq_width, type_count % 128), BF16),
            pltpu.VMEM((eq_width * SOURCES, 128), F32),
            pltpu.VMEM((eq_width, node_rows), F32),
            pltpu.VMEM((CHUNK * eq_width, node_rows), F32),
            pltpu.SemaphoreType.DMA((eq_width // CHUNK, type_count // 128 + 1)),
        ],
        compiler_params=params,
        cost_estimate=pl.CostEstimate(flops=2 * 10**10, bytes_accessed=18 * 10**6, transcendentals=0),
        name="far",
    )(send_lower, send, send_upper, vlist, ulist, table)
    far_node, lower, upper = lax.optimization_barrier((far_node, lower, upper))

    far_node, total, arrived = lax.optimization_barrier((far_node, total, arrived))
    total = total + arrived
    shares = total[q_width:]
    others = [swapped(shares, size, mask << 3) for mask in range(1, size >> 3)]
    steps, shares = lax.optimization_barrier((steps, shares))
    near = pl.pallas_call(
        near_kernel,
        out_shape=jax.ShapeDtypeStruct((leaf_count, q_width, p_width), F32),
        in_specs=[smem, smem, smem, hbm, hbm, vmem, vmem],
        out_specs=vmem,
        scratch_shapes=[
            pltpu.VMEM((6 * leaf_count + 1, 2 * PIECE, 128), BF16),
            *[pltpu.VMEM((leaf_count + 1, p_width, 128), F32)] * TOTALS,
            pltpu.SemaphoreType.DMA((3,)),
        ],
        compiler_params=params,
        cost_estimate=pl.CostEstimate(flops=3 * 10**10, bytes_accessed=10**7, transcendentals=0),
        name="near",
    )(steps, piece_table.reshape(-1), items.reshape(-1), pack, features, lower, upper)

    tops = [total]
    for level in range(1, level_count):
        rows = slice((level - 1) * q_width, level * q_width)
        group = 1 << (min(3 * level + 3, bits) - 3)
        tops.append(sum([other[rows] for other in others[: group - 1]], shares[rows]))
    return pl.pallas_call(
        lambda *refs: final_kernel(level_count, *refs),
        out_shape=jax.ShapeDtypeStruct((leaf_count, q_width, p_width), F32),
        in_specs=[smem, hbm, hbm, hbm, vmem, hbm] + [vmem] * (2 + len(tops)),
        out_specs=vmem,
        scratch_shapes=[
            pltpu.VMEM((node_rows, eq_width), F32),
            pltpu.VMEM((8, node_rows, eq_width), F32),
            pltpu.VMEM((leaf_count, 32, p_width), BF16),
            pltpu.VMEM((leaf_count, 32, p_width), BF16),
            pltpu.VMEM((leaf_count // 4, eq_width, 128), BF16),
            pltpu.VMEM((leaf_count, q_width, p_width), F32),
            pltpu.VMEM((level_count, eq_width, eq_width), F32),
            pltpu.SemaphoreType.DMA((level_count + 4,)),
        ],
        compiler_params=params,
        name="final",
    )(counts, features.reshape(2, leaf_count, 2, 32, p_width), turned, near, far_node, coarse, shift_down, down_inverse, *tops)


def solution(mesh):
    placed = (
        P("oct", None, None),
        P("oct", None, None),
        P("oct", None, None),
        P("oct"),
        P("oct", None),
        P("oct", None),
        P(),
        P(),
        P(),
        P(),
        P(),
        P(),
    )
    return jax.shard_map(
        local, mesh=mesh, in_specs=placed, out_specs=P("oct", None, None), check_vma=False
    )
```

```python
import math

import jax
import jax.numpy as jnp
from jax import lax
from jax.experimental import pallas as pl
from jax.experimental.pallas import tpu as pltpu
from jax.sharding import PartitionSpec as P

F32 = jnp.float32
BF16 = jnp.bfloat16
HIGHEST = lax.Precision.HIGHEST
SCALE = math.sqrt(math.log2(math.e))
NT = (((1,), (1,)), ((), ()))
TN = (((0,), (0,)), ((), ()))
BLOCK = 256
UNROLL = 16
TOTALS = 2
PIECE = 64
CLASS_ROWS = (32, 64, 96, 128)
PLACES = 56
SOURCES = 32
CHUNK = 4
FIRST, SECOND = 16, 8


def dot(left, right):
    return jnp.dot(left, right, preferred_element_type=F32)


def dot_nt(left, right):
    return lax.dot_general(left, right, NT, preferred_element_type=F32)


def dot_tn(left, right):
    return lax.dot_general(left, right, TN, preferred_element_type=F32)


def halves(value):
    high = value.astype(BF16)
    low = (value - high.astype(F32)).astype(BF16)
    return high, low


def dot3(left, right):
    left_high, left_low = halves(left)
    right_high, right_low = halves(right)
    return dot(left_high, right_high) + dot(left_high, right_low) + dot(left_low, right_high)


def grant(mebibytes):
    return pltpu.CompilerParams(vmem_limit_bytes=mebibytes * 1024 * 1024)


def iota(shape, dim):
    return lax.broadcasted_iota(jnp.int32, shape, dim)


def coords_of(ref, leaf):
    width = ref.shape[2]
    row = iota((8, width), 0)
    value = jnp.zeros((8, width), F32)
    for dim in range(3):
        line = jnp.broadcast_to(ref[dim, pl.ds(leaf, 1), :], (8, width))
        value = jnp.where(row == dim, line, value)
    return value


def pieces(coords):
    row = iota(coords.shape, 0)
    used = row < 3
    scaled = jnp.where(used, coords, 0.0) * SCALE
    high = scaled.astype(BF16).astype(F32)
    rest = scaled - high
    mid = rest.astype(BF16).astype(F32)
    low = (rest - mid).astype(BF16).astype(F32)
    norm = -0.5 * jnp.sum(scaled * scaled, axis=0, keepdims=True)
    norm_high = norm.astype(BF16).astype(F32)
    norm_rest = norm - norm_high
    norm_mid = norm_rest.astype(BF16).astype(F32)
    norm_low = norm_rest - norm_mid
    norms = jnp.where(row == 0, norm_high, jnp.where(row == 1, norm_mid, jnp.where(row == 2, norm_low, 0.0)))
    ones = jnp.where(used, 1.0, 0.0)
    return high, mid, low, norms, ones


def paired(first, second):
    return first + pltpu.roll(second, 4, 0)


def left_rows(parts):
    high, mid, low, norms, ones = parts
    return jnp.concatenate([paired(high, high), paired(mid, mid), paired(high, low), paired(ones, norms)], axis=0)


def right_rows(parts):
    high, mid, low, norms, ones = parts
    both = paired(high, mid)
    return jnp.concatenate([both, both, paired(low, high), paired(norms, ones)], axis=0)


def weight_rows(weights):
    high = weights.astype(BF16).astype(F32)
    return [high, weights - high]


def feature_versions(rows):
    lower = iota(rows.shape, 1) < PIECE
    versions = []
    for half in range(2):
        alone = jnp.where(lower == (half == 0), rows, 0.0)
        versions.append((half, half, alone.astype(BF16)))
        versions.append((half, 1 - half, pltpu.roll(alone, PIECE, 1).astype(BF16)))
    return versions


def put_features(feature_ref, leaf, versions):
    for half, place, value in versions:
        feature_ref[place, 2 * leaf + half] = value


def put_pack(pack_ref, leaf, value):
    pack_ref[pl.ds(2 * leaf, 2)] = value.reshape(2, PIECE, 128)


def upward_kernel(
    level_count, points_ref, dens_ref, surface_ref, counts_ref, count_line_ref, up_ref, shift_ref, pack_ref, send_ref,
    slab_ref, check_ref
):
    leaf_count, q_width, p_width = dens_ref.shape
    eq_width = surface_ref.shape[2]
    node_count = leaf_count // 8
    lane = iota((q_width, p_width), 1)

    def node_step(node, carry):
        leaves = [node * 8 + child for child in range(8)]
        counts = [counts_ref[leaf] for leaf in leaves]
        weights = [jnp.where(lane < count, dens_ref[leaf], 0.0) for leaf, count in zip(leaves, counts)]
        coords = [coords_of(points_ref, leaf) for leaf in leaves]
        surfaces = [left_rows(pieces(coords_of(surface_ref, leaf))) for leaf in leaves]
        parts = [pieces(value) for value in coords]
        rights = [right_rows(value) for value in parts]
        lists = [weight_rows(value) for value in weights]
        packs = [
            jnp.concatenate([left_rows(part)] + split + [right], axis=0).astype(BF16).T
            for part, split, right in zip(parts, lists, rights)
        ]
        blank = jnp.zeros((96, eq_width), F32)
        wides = [jnp.concatenate([blank, value], axis=0).astype(BF16) for value in surfaces]
        exponents = [dot(pack, wide) for pack, wide in zip(packs, wides)]
        values = [halves(jnp.exp2(value)) for value in exponents]
        rows = [jnp.concatenate(split, axis=0).astype(BF16) for split in lists]
        firsts = [dot(row, value[0]) for row, value in zip(rows, values)]
        seconds = [dot(row[:q_width], value[1]) for row, value in zip(rows, values)]
        for child, leaf in enumerate(leaves):
            put_pack(pack_ref, leaf, packs[child])
            check = firsts[child][:q_width] + firsts[child][q_width:] + seconds[child]
            check_ref[child, pl.ds(pl.multiple_of(node * q_width, q_width), q_width), :] = check
        return carry

    lax.fori_loop(0, node_count, node_step, 0)

    node_eq = jnp.zeros((node_count * q_width, eq_width), F32)
    for child in range(8):
        node_eq = node_eq + dot3(dot3(check_ref[child], up_ref[...]), shift_ref[child])
    send_ref[: node_count * q_width, :] = node_eq.astype(BF16)
    slab_eq = jnp.zeros((q_width, eq_width), F32)
    for child in range(8):
        slab_eq = slab_eq + dot3(node_eq[child * q_width : (child + 1) * q_width], shift_ref[child])
    index = lax.axis_index("oct")
    slab = slab_eq
    start = node_count * q_width
    for level in range(level_count):
        slab = dot3(slab, shift_ref[jnp.right_shift(index, 3 * level) & 7])
        slab_ref[level * q_width : (level + 1) * q_width, :] = slab
        high, rest = halves(slab)
        for place, part in enumerate((high, rest)):
            first = start + (place * level_count + level) * q_width
            send_ref[first : first + q_width, :] = part
    start = start + 2 * level_count * q_width
    line = jnp.concatenate([count_line_ref[...].astype(F32), jnp.zeros((1, eq_width - leaf_count), F32)], axis=1)
    send_ref[start : start + 16, :] = jnp.broadcast_to(line, (16, eq_width)).astype(BF16)


def outline_kernel(
    points_ref, dens_ref, surface_ref, counts_ref, order_ref, feature_ref, turned_ref, message_ref
):
    leaf_count, q_width, p_width = dens_ref.shape
    lane = iota((q_width, p_width), 1)

    def node_step(node, carry):
        leaves = [node * 8 + child for child in range(8)]
        counts = [counts_ref[leaf] for leaf in leaves]
        weights = [jnp.where(lane < count, dens_ref[leaf], 0.0) for leaf, count in zip(leaves, counts)]
        coords = [coords_of(points_ref, leaf) for leaf in leaves]
        surfaces = [left_rows(pieces(coords_of(surface_ref, leaf))) for leaf in leaves]
        versions = [feature_versions(right_rows(pieces(value))) for value in coords]
        fours = [jnp.concatenate(surfaces[first : first + 4], axis=0).astype(BF16).T for first in range(0, 8, 4)]
        for number, four in enumerate(fours):
            turned_ref[2 * node + number] = four
        for child, leaf in enumerate(leaves):
            pair, side = node * 4 + child // 2, child % 2
            message_ref[pair, side * q_width : (side + 1) * q_width, :] = weights[child]
            put_features(feature_ref, leaf, versions[child])
        for number in range(4):
            message_ref[node * 4 + number, 2 * q_width :, :] = paired(coords[2 * number], coords[2 * number + 1])
        return carry

    lax.fori_loop(0, leaf_count // 8, node_step, 0)


def far_kernel(
    lower_ref, own_ref, upper_ref, vlist_ref, ulist_ref, table_hbm, out_ref, step_ref, piece_ref, item_ref, table_ref,
    tail_ref, wide_ref, total_ref, first_ref, sems
):
    node_count, type_count = vlist_ref.shape
    eq_width = own_ref.shape[1]
    q_width = out_ref.shape[0] // node_count
    lanes = node_count * q_width
    tile = 128 // q_width
    chunk = CHUNK
    chunk_rows = chunk * eq_width
    chunk_count = eq_width // chunk
    full = type_count // 128

    def copies_of(number):
        span = pl.ds(number * chunk_rows, chunk_rows)
        copies = []
        for part in range(full):
            source = table_hbm.at[span, pl.ds(part * 128, 128)]
            copies.append(pltpu.make_async_copy(source, table_ref.at[part, span], sems.at[number, part]))
        source = table_hbm.at[span, pl.ds(full * 128, type_count - full * 128)]
        copies.append(pltpu.make_async_copy(source, tail_ref.at[span], sems.at[number, full]))
        return copies

    for number in range(chunk_count):
        for copy in copies_of(number):
            copy.start()

    index = lax.axis_index("oct")
    repeat = (iota((q_width, 128), 1) % q_width == iota((q_width, 128), 0)).astype(BF16)
    for part, source in enumerate((lower_ref, own_ref, upper_ref)):
        for node in range(node_count):
            spread = dot_tn(source[node * q_width : (node + 1) * q_width, :], repeat)
            wide_ref[pl.ds(part * node_count + node, eq_width, stride=SOURCES), :] = spread
    for place in range(3 * node_count, SOURCES):
        wide_ref[pl.ds(place, eq_width, stride=SOURCES), :] = jnp.zeros((eq_width, 128), F32)

    ids = vlist_ref[...]
    places = jnp.where(ids >= 0, ids - (index - 1) * node_count, -1).astype(F32).astype(BF16)
    lane = iota((1, lanes), 1)
    second_half = jnp.bitwise_and(lane, 63)
    node_of = jnp.where(lane < 128, lane // FIRST, second_half // SECOND)
    source_of = jnp.where(lane < 128, lane % FIRST, FIRST + second_half % SECOND)
    spread = (jnp.broadcast_to(node_of, (node_count, lanes)) == iota((node_count, lanes), 0)).astype(BF16)
    wanted = dot_tn(places, spread)
    chosen = (wanted == source_of.astype(F32)).astype(F32)
    chosen_full = chosen[: full * 128].astype(BF16)
    chosen_tail = chosen[full * 128 :].astype(BF16)
    lane_node = iota((SOURCES, 128), 1) // q_width
    lower_lanes = iota((eq_width, 128), 1) < 64
    total_ref[...] = jnp.zeros_like(total_ref)

    leaf_count = ulist_ref.shape[1]
    start = own_ref.shape[0] - 16
    lines = [ref[start:, :].astype(F32)[:1, :leaf_count] for ref in (lower_ref, own_ref, upper_ref)]
    plan_of(ulist_ref, lines, step_ref, piece_ref, item_ref)

    def table_of(number):
        span = pl.ds(pl.multiple_of(number * chunk_rows, chunk_rows), chunk_rows)
        left = jnp.concatenate([table_ref[part, span, :] for part in range(full)], axis=1)
        return left, tail_ref[span, :]

    def first_product(left, tail):
        return dot(left, chosen_full) + dot(tail, chosen_tail)

    def block_rows(sents, first, count):
        lines = []
        for sent in sents:
            blank = jnp.zeros((count, 128), F32)
            for node in range(node_count):
                own = sent[node % tile][first : first + count]
                line = [own if place == node // tile else blank for place in range(node_count // tile)]
                lines.append(jnp.concatenate(line, axis=1))
        return lines

    def second_product(number, summed):
        lefts, rights = [], []
        for step in range(0, chunk, 2):
            sents = []
            for place in (step, step + 1):
                row = number * chunk + place
                sent = wide_ref[pl.ds(pl.multiple_of(row * SOURCES, SOURCES), SOURCES), :]
                sents.append([jnp.where(lane_node == part, sent, 0.0) for part in range(tile)])
            pair = [summed[place * eq_width : (place + 1) * eq_width] for place in (step, step + 1)]
            tiles = [pair[0][:, :128], pair[1][:, :128], jnp.where(lower_lanes, pair[0][:, 128:], pair[1][:, 128:])]
            for value in tiles:
                high = value.astype(BF16).astype(F32)
                lefts.append(jnp.concatenate([high, value - high], axis=0).astype(BF16))
            rights += block_rows(sents, 0, FIRST) + block_rows(sents, FIRST, SECOND)
        product = dot(jnp.concatenate(lefts, axis=1), jnp.concatenate(rights, axis=0).astype(BF16))
        return product[:eq_width] + product[eq_width:]

    def wait_for(number):
        for copy in copies_of(number):
            copy.wait()

    wait_for(0)
    first_ref[...] = first_product(*table_of(0))

    def pair_step(pair, carry):
        number = 2 * pair
        wait_for(number + 1)
        pl.when(pair < chunk_count // 2 - 1)(lambda: wait_for(number + 2))
        ahead = table_of(number + 1)
        behind = table_of(jnp.minimum(number + 2, chunk_count - 1))
        summed = first_ref[...]
        middle = first_product(*ahead)
        total = second_product(number, summed)
        following = first_product(*behind)
        total = total + second_product(number + 1, middle)
        first_ref[...] = following
        total_ref[...] += total
        return carry

    lax.fori_loop(0, chunk_count // 2, pair_step, 0)
    out_ref[...] = total_ref[...].T


def near_kernel(
    step_ref, piece_ref, item_ref, own_hbm, own_feature_hbm, lower_ref, upper_ref, out_ref, pack_ref, *rest
):
    total_refs, sems = rest[:TOTALS], rest[TOTALS]
    leaf_count, q_width, p_width = out_ref.shape
    own = pl.ds(0, 2 * leaf_count)
    ends = [(own_hbm, pack_ref.at[own, pl.ds(0, PIECE)])]
    ends += [(own_feature_hbm.at[half], pack_ref.at[own, pl.ds(PIECE + 32 * half, 32)]) for half in range(2)]
    copies = [pltpu.make_async_copy(*end, sems.at[number]) for number, end in enumerate(ends)]
    for copy in copies:
        copy.start()
    pack_ref[6 * leaf_count] = jnp.zeros((2 * PIECE, 128), BF16)
    for total_ref in total_refs:
        total_ref[...] = jnp.zeros_like(total_ref)
    def pack_step(step, carry):
        chosen = [(part, side) for side in range(2) for part in range(4)]
        sources = (lower_ref, upper_ref)
        weights, versions = [], []
        for part, side in chosen:
            place, half = step * 2 + part // 2, part % 2
            weights.append(weight_rows(sources[side][place, half * q_width : (half + 1) * q_width, :]))
            tail = sources[side][place, 2 * q_width :, :]
            tail = pltpu.roll(tail, 4, 0) if half else tail
            versions.append(feature_versions(right_rows(pieces(tail))))
        packs = []
        for part in range(0, len(chosen), 2):
            (high, low), (next_high, next_low) = weights[part : part + 2]
            both = jnp.concatenate([next_low, high, low, next_high], axis=0).astype(BF16).T
            packs += [both, pltpu.roll(both.astype(F32), 64, 1).astype(BF16)]
        for (part, side), pack, version in zip(chosen, packs, versions):
            place = (1 + side) * leaf_count + step * 4 + part
            pack_ref[pl.ds(2 * place, 2), :PIECE] = pack.reshape(2, PIECE, 128)
            for half, number, value in version:
                pack_ref[2 * place + half, PIECE + 32 * number : PIECE + 32 * (number + 1)] = value
        return carry

    lax.fori_loop(0, leaf_count // 4, pack_step, 0)
    for copy in copies:
        copy.wait()
    block_pieces = BLOCK // PIECE

    def items_of(step):
        first = step * UNROLL
        leaves = [item_ref[first + part] for part in range(UNROLL)]
        first = first * block_pieces
        pieces_of = [
            [piece_ref[first + part * block_pieces + number] for number in range(block_pieces)] for part in range(UNROLL)
        ]
        return list(zip(leaves, pieces_of))

    def sources_of(numbers):
        return jnp.concatenate([pack_ref[number, :PIECE] for number in numbers], axis=0)

    def features_of(numbers):
        tiles = []
        for tile in range(BLOCK // 128):
            lower = pack_ref[numbers[2 * tile], PIECE : PIECE + 32]
            tiles.append(lower + pack_ref[numbers[2 * tile + 1], PIECE + 32 :])
        return jnp.concatenate(tiles, axis=1)

    def targets_of(leaf, rows):
        first = 2 * leaf
        if rows <= PIECE:
            return pack_ref[first, :rows][:, :32]
        return jnp.concatenate([pack_ref[first, :PIECE][:, :32], pack_ref[first + 1, : rows - PIECE][:, :32]], axis=0)

    def run(rows, first, count):
        def blocks_step(step, carry):
            items = items_of(step)
            features = [features_of(numbers) for _, numbers in items]
            targets = [targets_of(leaf, rows) for leaf, _ in items]
            sources = [sources_of(numbers) for _, numbers in items]
            exponents = [dot(target, feature) for target, feature in zip(targets, features)]
            values = [jnp.exp2(value).astype(BF16) for value in exponents]
            products = []
            for part in range(0, UNROLL, 2):
                left = jnp.concatenate(values[part : part + 2], axis=0)
                both = dot(left, jnp.concatenate(sources[part : part + 2], axis=1))
                products += [both[:rows, :128], both[rows:, 128:]]
            for first in range(0, UNROLL, TOTALS):
                sums = [
                    total_refs[part][items[first + part][0], :rows] + products[first + part] for part in range(TOTALS)
                ]
                for part, value in enumerate(sums):
                    total_refs[part][items[first + part][0], :rows] = value
            return carry

        lax.fori_loop(first, first + count, blocks_step, 0)

    for number, rows in enumerate(CLASS_ROWS):
        run(rows, step_ref[0, 2 * number], step_ref[0, 2 * number + 1])

    def turn_step(step, carry):
        sums = [[total_ref[step * 8 + part] for total_ref in total_refs] for part in range(8)]
        sums = [sum(values[1:], values[0]) for values in sums]
        inner = (iota((p_width, 128), 1) >= 32) & (iota((p_width, 128), 1) < 96)
        for part in range(0, 8, 2):
            turned = jnp.where(inner, sums[part], pltpu.roll(sums[part + 1], 64, 1)).T
            out_ref[step * 8 + part] = turned[32 : 32 + q_width] + turned[32 + q_width : 32 + 2 * q_width]
            out_ref[step * 8 + part + 1] = turned[96 : 96 + q_width] + turned[:q_width]
        return carry

    lax.fori_loop(0, leaf_count // 8, turn_step, 0)


def as_column(line):
    width = line.shape[1]
    wide = jnp.concatenate([line, jnp.zeros((1, 128 - width), F32)], axis=1) if width < 128 else line
    return jnp.broadcast_to(wide, (128, 128)).T[:width, :width]


def plan_of(ulist_ref, counts, step_ref, piece_ref, item_ref):
    slot_count, leaf_count = ulist_ref.shape
    index = lax.axis_index("oct")
    shape = (leaf_count, leaf_count)
    row, column = iota(shape, 0), iota(shape, 1)
    tables = [as_column(line) for line in counts]
    own = jnp.broadcast_to(counts[1], shape)
    before = (tables[1] < own) | ((tables[1] == own) & (row < column))
    rank = jnp.sum(jnp.where(before, 1.0, 0.0), axis=0, keepdims=True)
    rank_column = as_column(rank).astype(jnp.int32)
    rank_wide = jnp.broadcast_to(rank, shape).astype(jnp.int32)

    block_pieces = BLOCK // PIECE
    empty = 6 * leaf_count
    place_shape = (PLACES, leaf_count)
    place_row = iota(place_shape, 0)
    listed = jnp.full(place_shape, empty, jnp.int32)
    offset = jnp.zeros((1, leaf_count), jnp.int32)
    for slot in range(slot_count):
        side = 1 if slot == 0 else (0 if slot < 9 else (1 if slot < 18 else 2))
        ids = ulist_ref[slot : slot + 1, :]
        place = jnp.where(ids >= 0, ids - (index + (side - 1)) * leaf_count, 0)
        found = jnp.sum(jnp.where(row == place, tables[side], 0.0), axis=0, keepdims=True).astype(jnp.int32)
        length = lax.shift_right_logical(found + (PIECE - 1), PIECE.bit_length() - 1)
        length = jnp.where(ids >= 0, length, 0)
        start = (place + (1, 0, 2)[side] * leaf_count) * 2
        inside = (place_row >= offset) & (place_row < offset + length)
        listed = jnp.where(inside, start + place_row - offset, listed)
        offset = offset + length

    blocks = lax.shift_right_logical(offset + (block_pieces - 1), block_pieces.bit_length() - 1)
    blocks_column = as_column(blocks.astype(F32))
    own_class = lax.shift_right_logical(counts[1].astype(jnp.int32) - 1, 5)
    class_column = as_column(own_class.astype(F32)).astype(jnp.int32)
    earlier = (class_column == jnp.broadcast_to(own_class, shape)) & (rank_column < rank_wide)
    first = jnp.sum(jnp.where(earlier, blocks_column, 0.0), axis=0, keepdims=True).astype(jnp.int32)
    lane = iota((1, 128), 1)
    steps_line = jnp.zeros((1, 128), jnp.int32)
    start = jnp.ones((1, 1), jnp.int32)
    for number in range(len(CLASS_ROWS)):
        inside = jnp.where(own_class == number, blocks.astype(F32), 0.0)
        items = jnp.sum(inside, axis=1, keepdims=True).astype(jnp.int32)
        steps = lax.shift_right_logical(items + (UNROLL - 1), UNROLL.bit_length() - 1)
        first = first + jnp.where(own_class == number, start * UNROLL, 0)
        steps_line = jnp.where(lane == 2 * number, start, jnp.where(lane == 2 * number + 1, steps, steps_line))
        start = start + steps
    step_ref[...] = steps_line

    first_column = as_column(first.astype(F32))[:, :1].astype(jnp.int32)
    blocks_column = blocks_column[:, :1].astype(jnp.int32)
    high = lax.shift_right_logical(listed, 8).astype(F32)
    low = jnp.bitwise_and(listed, 255).astype(F32)
    parts = jnp.concatenate([high, low], axis=0).astype(BF16)
    chunk = 1024
    wide = (leaf_count, chunk)
    column = iota(wide, 1)
    leaf_row = iota(wide, 0).astype(F32)
    for number in range(block_pieces):
        entry = column + chunk * number
        after = lax.shift_right_logical(entry, block_pieces.bit_length() - 1) - first_column
        inside = (after >= 0) & (after < blocks_column)
        place = after * block_pieces + jnp.bitwise_and(entry, block_pieces - 1)
        place = jnp.sum(jnp.where(inside, place.astype(F32), 0.0), axis=0, keepdims=True).astype(jnp.int32)
        found = jnp.sum(jnp.where(inside, 1.0, 0.0), axis=0, keepdims=True)
        both = dot(parts, jnp.where(inside, 1.0, 0.0).astype(BF16))
        value = both[:PLACES] * 256.0 + both[PLACES:]
        value = jnp.sum(jnp.where(iota((PLACES, chunk), 0) == place, value, 0.0), axis=0, keepdims=True)
        value = jnp.where(found > 0.0, value, float(empty)).astype(jnp.int32)
        for line in range(8):
            piece_ref[8 * number + line : 8 * number + line + 1, :] = value[:, line * 128 : (line + 1) * 128]
    after = column - first_column
    inside = (after >= 0) & (after < blocks_column)
    leaf = jnp.sum(jnp.where(inside, leaf_row - leaf_count, 0.0), axis=0, keepdims=True).astype(jnp.int32) + leaf_count
    for line in range(8):
        item_ref[line : line + 1, :] = leaf[:, line * 128 : (line + 1) * 128]


def final_kernel(
    level_count, counts_ref, feature_hbm, turned_hbm, near_hbm, far_ref, coarse_hbm, shift_ref, down_ref, *rest
):
    top_refs, rest = rest[:level_count], rest[level_count:]
    out_ref, node_ref, down_leaf_ref, lower_ref, upper_ref, turned_ref, near_ref, coarse_ref, sems = rest
    leaf_count, q_width, p_width = out_ref.shape
    eq_width = far_ref.shape[1]
    node_count = leaf_count // 8
    index = lax.axis_index("oct")
    ends = [(coarse_hbm.at[jnp.right_shift(index, 3 * level) & 7], coarse_ref.at[level]) for level in range(level_count)]
    ends += [(feature_hbm.at[0, :, 0], lower_ref), (feature_hbm.at[1, :, 1], upper_ref)]
    ends += [(turned_hbm, turned_ref), (near_hbm, near_ref)]
    copies = [pltpu.make_async_copy(*end, sems.at[number]) for number, end in enumerate(ends)]
    for copy in copies:
        copy.start()
    for copy in copies[:level_count]:
        copy.wait()
    slab_local = jnp.zeros((q_width, eq_width), F32)
    for level, top_ref in enumerate(top_refs):
        slab_local = slab_local + dot3(top_ref[:q_width, :], coarse_ref[level])
    for node in range(node_count):
        rows = slice(node * q_width, (node + 1) * q_width)
        node_ref[rows, :] = far_ref[rows, :] + dot3(slab_local, shift_ref[node])

    for child in range(8):
        down_leaf_ref[child] = dot3(dot3(node_ref[...], shift_ref[child]), down_ref[...])
    for copy in copies[level_count:]:
        copy.wait()
    lane = iota((q_width, p_width), 1)

    def node_step(node, carry):
        leaves = [node * 8 + child for child in range(8)]
        features = []
        for leaf in leaves:
            features.append(lower_ref[leaf] + upper_ref[leaf])
        turned = [turned_ref[2 * node + number] for number in range(2)]
        node_rows = pl.ds(pl.multiple_of(node * q_width, q_width), q_width)
        downs = [weight_rows(down_leaf_ref[child, node_rows, :]) for child in range(8)]
        nears = [near_ref[leaf] for leaf in leaves]
        blank = jnp.zeros((32, p_width), BF16)
        exponents = []
        for first in range(0, 8, 2):
            sides = []
            for child in (first, first + 1):
                lines = [features[child] if place == child % 4 else blank for place in range(4)]
                sides.append(jnp.concatenate(lines, axis=0))
            both = dot(turned[first // 4], jnp.concatenate(sides, axis=1))
            exponents += [both[:, :p_width], both[:, p_width:]]
        values = [halves(jnp.exp2(value)) for value in exponents]
        lefts = [jnp.concatenate(down, axis=0).astype(BF16) for down in downs]
        products = [dot(left, jnp.concatenate(value, axis=1)) for left, value in zip(lefts, values)]
        for child, leaf in enumerate(leaves):
            product = products[child]
            far = product[:q_width, :p_width] + product[q_width:, :p_width] + product[:q_width, p_width:]
            out_ref[leaf] = jnp.where(lane < counts_ref[leaf], far + nears[child], 0.0)
        return carry

    lax.fori_loop(0, node_count, node_step, 0)


def shifted(value, size):
    up = [(i, i + 1) for i in range(size - 1)]
    down = [(j, i) for i, j in up]
    return lax.ppermute(value, "oct", up), lax.ppermute(value, "oct", down)


def swapped(value, size, mask):
    return lax.ppermute(value, "oct", [(source, source ^ mask) for source in range(size)])


def local(
    points,
    dens,
    surface,
    counts,
    ulist,
    vlist,
    up_inverse,
    down_inverse,
    shift_up,
    shift_down,
    coarse,
    translate,
):
    leaf_count, q_width, p_width = dens.shape
    eq_width = surface.shape[2]
    node_count, type_count = vlist.shape
    node_rows = node_count * q_width
    size = lax.axis_size("oct")
    bits = size.bit_length() - 1
    level_count = -(-bits // 3)
    level_rows = level_count * q_width
    index = lax.axis_index("oct")
    vmem = pl.BlockSpec(memory_space=pltpu.VMEM)
    smem = pl.BlockSpec(memory_space=pltpu.SMEM)
    hbm = pl.BlockSpec(memory_space=pl.ANY)
    params = grant(56)
    points = jnp.transpose(points, (1, 0, 2))
    surface = jnp.transpose(surface, (1, 0, 2))
    ulist = ulist.T
    table = jnp.transpose(translate, (1, 2, 0))

    pack, send, slab = pl.pallas_call(
        lambda *refs: upward_kernel(level_count, *refs),
        out_shape=(
            jax.ShapeDtypeStruct((2 * leaf_count, PIECE, 128), BF16),
            jax.ShapeDtypeStruct((node_rows + 2 * level_rows + 16, eq_width), BF16),
            jax.ShapeDtypeStruct((level_rows, eq_width), F32),
        ),
        in_specs=[vmem, vmem, vmem, smem, vmem, vmem, vmem],
        out_specs=(vmem,) * 3,
        scratch_shapes=[pltpu.VMEM((8, node_rows, eq_width), F32)],
        compiler_params=params,
        name="upward",
    )(points, dens, surface, counts, counts.reshape(1, leaf_count), up_inverse, shift_up)

    send_lower, send_upper = shifted(send, size)
    features, turned, message = pl.pallas_call(
        outline_kernel,
        out_shape=(
            jax.ShapeDtypeStruct((2, 2 * leaf_count, 32, p_width), BF16),
            jax.ShapeDtypeStruct((leaf_count // 4, eq_width, 128), BF16),
            jax.ShapeDtypeStruct((leaf_count // 2, 2 * q_width + 8, p_width), F32),
        ),
        in_specs=[vmem, vmem, vmem, smem, hbm],
        out_specs=(vmem,) * 3,
        compiler_params=params,
        cost_estimate=pl.CostEstimate(flops=4 * 10**9, bytes_accessed=10**7, transcendentals=0),
        name="outline",
    )(points, dens, surface, counts, slab)
    lower, upper = shifted(message, size)
    send_lower, send_upper, features = lax.optimization_barrier((send_lower, send_upper, features))
    ends = slice(node_rows, node_rows + 2 * level_rows)
    partner = jnp.where(index & 1 == 1, send_lower[ends], send_upper[ends]).astype(F32)
    total = slab + (partner[:level_rows] + partner[level_rows:])
    total = total + swapped(total, size, 2)
    arrived = swapped(total, size, 4)
    send_lower, total = lax.optimization_barrier((send_lower, total))

    table = table.reshape(eq_width * eq_width, type_count)
    far_node, steps, piece_table, items = pl.pallas_call(
        far_kernel,
        out_shape=(
            jax.ShapeDtypeStruct((node_rows, eq_width), F32),
            jax.ShapeDtypeStruct((1, 128), jnp.int32),
            jax.ShapeDtypeStruct((32, 128), jnp.int32),
            jax.ShapeDtypeStruct((8, 128), jnp.int32),
        ),
        in_specs=[vmem, vmem, vmem, vmem, vmem, hbm],
        out_specs=(vmem,) * 4,
        scratch_shapes=[
            pltpu.VMEM((type_count // 128, eq_width * eq_width, 128), BF16),
            pltpu.VMEM((eq_width * eq_width, type_count % 128), BF16),
            pltpu.VMEM((eq_width * SOURCES, 128), F32),
            pltpu.VMEM((eq_width, node_rows), F32),
            pltpu.VMEM((CHUNK * eq_width, node_rows), F32),
            pltpu.SemaphoreType.DMA((eq_width // CHUNK, type_count // 128 + 1)),
        ],
        compiler_params=params,
        cost_estimate=pl.CostEstimate(flops=2 * 10**10, bytes_accessed=18 * 10**6, transcendentals=0),
        name="far",
    )(send_lower, send, send_upper, vlist, ulist, table)
    far_node, lower, upper = lax.optimization_barrier((far_node, lower, upper))

    far_node, total, arrived = lax.optimization_barrier((far_node, total, arrived))
    total = total + arrived
    shares = total[q_width:]
    others = [swapped(shares, size, mask << 3) for mask in range(1, size >> 3)]
    steps, shares = lax.optimization_barrier((steps, shares))
    near = pl.pallas_call(
        near_kernel,
        out_shape=jax.ShapeDtypeStruct((leaf_count, q_width, p_width), F32),
        in_specs=[smem, smem, smem, hbm, hbm, vmem, vmem],
        out_specs=vmem,
        scratch_shapes=[
            pltpu.VMEM((6 * leaf_count + 1, 2 * PIECE, 128), BF16),
            *[pltpu.VMEM((leaf_count + 1, p_width, 128), F32)] * TOTALS,
            pltpu.SemaphoreType.DMA((3,)),
        ],
        compiler_params=params,
        cost_estimate=pl.CostEstimate(flops=3 * 10**10, bytes_accessed=10**7, transcendentals=0),
        name="near",
    )(steps, piece_table.reshape(-1), items.reshape(-1), pack, features, lower, upper)

    tops = [total]
    for level in range(1, level_count):
        rows = slice((level - 1) * q_width, level * q_width)
        group = 1 << (min(3 * level + 3, bits) - 3)
        tops.append(sum([other[rows] for other in others[: group - 1]], shares[rows]))
    return pl.pallas_call(
        lambda *refs: final_kernel(level_count, *refs),
        out_shape=jax.ShapeDtypeStruct((leaf_count, q_width, p_width), F32),
        in_specs=[smem, hbm, hbm, hbm, vmem, hbm] + [vmem] * (2 + len(tops)),
        out_specs=vmem,
        scratch_shapes=[
            pltpu.VMEM((node_rows, eq_width), F32),
            pltpu.VMEM((8, node_rows, eq_width), F32),
            pltpu.VMEM((leaf_count, 32, p_width), BF16),
            pltpu.VMEM((leaf_count, 32, p_width), BF16),
            pltpu.VMEM((leaf_count // 4, eq_width, 128), BF16),
            pltpu.VMEM((leaf_count, q_width, p_width), F32),
            pltpu.VMEM((level_count, eq_width, eq_width), F32),
            pltpu.SemaphoreType.DMA((level_count + 4,)),
        ],
        compiler_params=params,
        name="final",
    )(counts, features.reshape(2, leaf_count, 2, 32, p_width), turned, near, far_node, coarse, shift_down, down_inverse, *tops)


def solution(mesh):
    placed = (
        P("oct", None, None),
        P("oct", None, None),
        P("oct", None, None),
        P("oct"),
        P("oct", None),
        P("oct", None),
        P(),
        P(),
        P(),
        P(),
        P(),
        P(),
    )
    return jax.shard_map(
        local, mesh=mesh, in_specs=placed, out_specs=P("oct", None, None), check_vma=False
    )
```
